32 devices in a mesh: batch: 8 (over z, x), fsdp: 2 (over y), seq: 2 (over core).
Axes of the slice: x: 2, y: 2, z: 4, core: 2. Of those that a mesh axis runs over, the one named last changes fastest.
Arguments:
- tokens: bfloat16 [16, 1024, 960], P(('batch', 'fsdp'), 'seq'), may hold values from -6 to 6
- attn_gain: bfloat16 [960], P('fsdp'), may hold values from 0.5 to 1.5
- w_query: bfloat16 [960, 960], P('fsdp'), may hold values from -0.25 to 0.25
- key_weight: bfloat16 [960, 320], P('fsdp'), may hold values from -0.1875 to 0.1875
- value_weight: bfloat16 [960, 320], P('fsdp'), may hold values from -0.1875 to 0.1875
- w_out: bfloat16 [960, 960], P('fsdp'), may hold values from -0.75 to 0.75
- ffn_gain: bfloat16 [960], P('fsdp'), may hold values from 0.5 to 1.5
- w_gate: bfloat16 [960, 2560], P('fsdp'), may hold values from -0.1875 to 0.1875
- w_up: bfloat16 [960, 2560], P('fsdp'), may hold values from -0.1875 to 0.1875
- w_down: bfloat16 [2560, 960], P('fsdp'), may hold values from -0.125 to 0.125
- cotangent: bfloat16 [16, 1024, 960], P(('batch', 'fsdp'), 'seq'), may hold values from -6 to 6
Outputs:
- layer_output: bfloat16 [16, 1024, 960], P(('batch', 'fsdp'), 'seq')
- grad_tokens: float32 [16, 1024, 960], P(('batch', 'fsdp'), 'seq')
- grad_attn_gain: float32 [960], P('fsdp')
- grad_query: float32 [960, 960], P('fsdp')
- grad_key: float32 [960, 320], P('fsdp')
- grad_value: float32 [960, 320], P('fsdp')
- grad_out: float32 [960, 960], P('fsdp')
- grad_ffn_gain: float32 [960], P('fsdp')
- grad_gate: float32 [960, 2560], P('fsdp')
- grad_up: float32 [960, 2560], P('fsdp')
- grad_down: float32 [2560, 960], P('fsdp')
The draws below stay inside these ranges and needn't reach their ends.
All inputs are finite; a program needn't handle non-finite values.
Results may differ from the reference program's by a relative error of at most 0.025.
Values may be sent and summed in bfloat16 or wider, within the bound.
No kernel may reach another device: no remote copies, remote signals or barrier semaphores. Data moves between devices by JAX's collectives and lax.ppermute only.
A program may use at most 320 MiB of HBM per device.

```python
import math
import jax
import jax.numpy as jnp
from jax import lax

MODEL_DIM = 960
QUERY_HEADS = 15
KEY_HEADS = 5
HEAD_DIM = 64
FF = 2560
LENGTH = 1024
SEQUENCES = 16


def level_of(rng, dims, cuts, low, top_value):
    level = 1.0
    for position, parts in cuts:
        steps = jax.random.uniform(jax.random.fold_in(jax.random.fold_in(rng, 6), position), (parts,), jnp.float32, low / len(cuts), top_value / len(cuts))
        level = level * jnp.repeat(jnp.exp(steps), dims[position] // parts).reshape((-1,) + (1,) * (len(dims) - 1 - position))
    return level


def centred(key, dims, deviation, reach, split=(), held_as=jnp.bfloat16):
    values = jax.random.normal(key, dims, jnp.float32) * deviation
    if len(split) > 0:
        values = level_of(key, dims, split, -0.22, 0.18) * values
    return jnp.clip(values, min=-reach, max=reach).astype(held_as)


def setup_inputs(seed: int = 0) -> dict:
    arg_keys = jax.random.split(jax.random.key(seed), 12)
    return {
        "tokens": centred(arg_keys[0], (SEQUENCES, LENGTH, MODEL_DIM), 1.0, 6.0, ((0, 16), (1, 2))),
        "attn_gain": jnp.clip(1.0 + 0.1 * jax.random.normal(arg_keys[1], (MODEL_DIM,), jnp.float32), 0.5, 1.5).astype(jnp.bfloat16),
        "w_query": centred(arg_keys[2], (MODEL_DIM, QUERY_HEADS * HEAD_DIM), (MODEL_DIM // 2) ** -0.5, 0.25, ((0, 2),)),
        "key_weight": centred(arg_keys[3], (MODEL_DIM, KEY_HEADS * HEAD_DIM), MODEL_DIM ** -0.5, 0.1875, ((0, 2),)),
        "value_weight": centred(arg_keys[4], (MODEL_DIM, KEY_HEADS * HEAD_DIM), MODEL_DIM ** -0.5, 0.1875, ((0, 2),)),
        "w_out": centred(arg_keys[5], (QUERY_HEADS * HEAD_DIM, MODEL_DIM), (max(QUERY_HEADS * HEAD_DIM // 16, 1)) ** -0.5, 0.75, ((0, 2),)),
        "ffn_gain": jnp.clip(1.0 + 0.1 * jax.random.normal(arg_keys[6], (MODEL_DIM,), jnp.float32), 0.5, 1.5).astype(jnp.bfloat16),
        "w_gate": centred(arg_keys[7], (MODEL_DIM, FF), MODEL_DIM ** -0.5, 0.1875, ((0, 2),)),
        "w_up": centred(arg_keys[8], (MODEL_DIM, FF), MODEL_DIM ** -0.5, 0.1875, ((0, 2),)),
        "w_down": centred(arg_keys[9], (FF, MODEL_DIM), FF ** -0.5, 0.125, ((0, 2),)),
        "cotangent": centred(arg_keys[10], (SEQUENCES, LENGTH, MODEL_DIM), 1.0, 6.0, ((0, 16), (1, 2))),
    }


@jax.custom_vjp
def low(v):
    return lax.optimization_barrier(v.astype(jnp.bfloat16)).astype(jnp.float32)

@jax.custom_vjp
def reduced_backward(v):
    return v

def low_keep(v):
    return (low(v), None)

def low_pass(kept, grad):
    return (grad,)

def back_keep(v):
    return (v, None)

def back_low(kept, grad):
    return (low(grad),)
low.defvjp(low_keep, low_pass)
reduced_backward.defvjp(back_keep, back_low)
EPSILON = 1e-05

def precise_product(left, right):
    return jnp.dot(left, right, precision=lax.Precision.HIGHEST, preferred_element_type=jnp.float32)

def rotary_tables(positions):
    half_dim = HEAD_DIM // 2
    frequency = jnp.exp(jnp.arange(half_dim, dtype=jnp.float32) * (-2.0 * math.log(10000.0) / HEAD_DIM))
    angles = positions[:, None] * frequency[None, :]
    return (jnp.cos(angles), jnp.sin(angles))

def apply_rotation(vectors, cosine_values, sine_values):
    half_dim = vectors.shape[-1] // 2
    first_half = vectors[..., :half_dim]
    second_half = vectors[..., half_dim:]
    cos_table = cosine_values[:, None, :]
    sin_table = sine_values[:, None, :]
    return jnp.concatenate([first_half * cos_table - second_half * sin_table, second_half * cos_table + first_half * sin_table], -1)

def norm_rows(values, gain):
    scales = lax.rsqrt(lax.optimization_barrier(jnp.mean(values * values, -1, keepdims=True)) + EPSILON)
    return values * scales * gain

def attention(query_rows, key_row_block, value_row_block):
    sequence_length = query_rows.shape[0]
    rows_per_block = min(512, sequence_length)
    number_of_blocks = sequence_length // rows_per_block
    query_groups = QUERY_HEADS // KEY_HEADS
    grouped_heads = query_rows.reshape(number_of_blocks, rows_per_block, KEY_HEADS, query_groups, HEAD_DIM)
    offsets = jnp.arange(number_of_blocks, dtype=jnp.int32) * rows_per_block
    key_pos = jnp.arange(sequence_length, dtype=jnp.int32)

    def one_block(inputs):
        query_part, offset = inputs
        scores = reduced_backward(jnp.einsum('qhgd,khd->hgqk', query_part, key_row_block, precision=lax.Precision.HIGHEST))
        query_pos = offset + jnp.arange(rows_per_block, dtype=jnp.int32)
        causal = key_pos[None, :] <= query_pos[:, None]
        scores = jnp.where(causal, scores, -1e+30)
        row_peak = lax.optimization_barrier(jnp.max(scores, -1, keepdims=True))
        exponent = jnp.exp(scores - row_peak)
        attn_probs = exponent / lax.optimization_barrier(jnp.sum(exponent, -1, keepdims=True))
        return jnp.einsum('hgqk,khd->qhgd', low(attn_probs), value_row_block, precision=lax.Precision.HIGHEST)
    outputs = lax.map(jax.checkpoint(one_block), (grouped_heads, offsets))
    return outputs.reshape(sequence_length, QUERY_HEADS * HEAD_DIM)

def layer_apply(values, params, cosine_values, sine_values):
    attn_gain, w_query, key_weight, value_weight, w_out, ffn_gain, w_gate, w_up, w_down = params
    sequence_length = values.shape[0]
    normalized_rows = low(norm_rows(values, attn_gain))
    query_rows = reduced_backward(precise_product(normalized_rows, w_query)).reshape(sequence_length, QUERY_HEADS, HEAD_DIM)
    key_row_block = reduced_backward(precise_product(normalized_rows, key_weight)).reshape(sequence_length, KEY_HEADS, HEAD_DIM)
    value_row_block = reduced_backward(precise_product(normalized_rows, value_weight)).reshape(sequence_length, KEY_HEADS, HEAD_DIM)
    query_rows = low(apply_rotation(query_rows, cosine_values, sine_values) * HEAD_DIM ** (-0.5))
    key_row_block = low(apply_rotation(key_row_block, cosine_values, sine_values))
    value_row_block = low(value_row_block)
    mixed = low(reduced_backward(attention(query_rows, key_row_block, value_row_block)))
    middle = values + reduced_backward(precise_product(mixed, w_out))
    normed_ffn = low(norm_rows(middle, ffn_gain))
    gate_act = reduced_backward(precise_product(normed_ffn, w_gate))
    up_act = reduced_backward(precise_product(normed_ffn, w_up))
    hidden = low(jax.nn.silu(gate_act) * up_act)
    return middle + reduced_backward(precise_product(hidden, w_down))

def reference(tokens, attn_gain, w_query, key_weight, value_weight, w_out, ffn_gain, w_gate, w_up, w_down, cotangent):
    params = tuple((array_in.astype(jnp.float32) for array_in in (attn_gain, w_query, key_weight, value_weight, w_out, ffn_gain, w_gate, w_up, w_down)))
    positions = jnp.arange(LENGTH, dtype=jnp.float32)
    cosine_values, sine_values = rotary_tables(positions)

    def forward(values, weights):
        return layer_apply(layer_apply(values, weights, cosine_values, sine_values), weights, cosine_values, sine_values)

    def per_sequence(totals, inputs):
        sequence, incoming = inputs
        output, pullback = jax.vjp(forward, sequence.astype(jnp.float32), params)
        grad_input, grad_params = pullback(incoming.astype(jnp.float32))
        totals = jax.tree.map(jnp.add, totals, grad_params)
        return (totals, (output.astype(jnp.bfloat16), grad_input))
    zero_grads = tuple((jnp.zeros_like(weight_item) for weight_item in params))
    totals, (outputs, grad_inputs) = lax.scan(per_sequence, zero_grads, (tokens, cotangent))
    return (outputs, grad_inputs, totals[0], totals[1], totals[2], totals[3], totals[4], totals[5], totals[6], totals[7], totals[8])
```

```python
import math

import jax
import jax.numpy as jnp
from jax import lax
from jax.sharding import PartitionSpec as P

QUERY_HEADS = 15
KEY_HEADS = 5
HEAD_DIM = 64


EPSILON = 1e-05


def rotary_tables(positions):
    half_dim = HEAD_DIM // 2
    frequency = jnp.exp(
        jnp.arange(half_dim, dtype=jnp.float32) * (-2.0 * math.log(10000.0) / HEAD_DIM)
    )
    angles = positions[:, None] * frequency[None, :]
    return (jnp.cos(angles), jnp.sin(angles))


def apply_rotation(vectors, cosine_values, sine_values):
    half_dim = vectors.shape[-1] // 2
    first_half = vectors[..., :half_dim]
    second_half = vectors[..., half_dim:]
    cos_table = cosine_values[:, None, :]
    sin_table = sine_values[:, None, :]
    return jnp.concatenate(
        [
            first_half * cos_table - second_half * sin_table,
            second_half * cos_table + first_half * sin_table,
        ],
        -1,
    )


def reverse_rotation(vectors, cosine_values, sine_values):
    return apply_rotation(vectors, cosine_values, -sine_values)


def norm_forward(values, gain):
    scales = lax.rsqrt(jnp.mean(values * values, -1, keepdims=True) + EPSILON)
    return (values * scales * gain, scales)


def norm_backward(values, scales, gain, incoming):
    weighted = gain * incoming
    inner = jnp.mean(values * weighted, -1, keepdims=True)
    grad_values = scales * weighted - values * scales * scales * scales * inner
    grad_gain = jnp.sum(incoming * values * scales, axis=(0, 1))
    return (grad_values, grad_gain)


def forward_layer(values, weights, tables, again):
    attn_gain, w_query, key_weight, value_weight, w_out, ffn_gain, w_gate, w_up, w_down = weights
    cosine_values, sine_values, query_pos, key_pos = tables
    sequence_count, block_extent, model_width = values.shape
    number_of_rows = sequence_count * block_extent
    query_groups = QUERY_HEADS // KEY_HEADS
    normalized_rows, scales_attn = norm_forward(values, attn_gain.astype(jnp.float32))
    normalized_rows = normalized_rows.astype(jnp.bfloat16).reshape(number_of_rows, model_width)
    query_rows = jnp.dot(normalized_rows, w_query, preferred_element_type=jnp.float32).reshape(
        sequence_count, block_extent, QUERY_HEADS, HEAD_DIM
    )
    key_row_block = jnp.dot(
        normalized_rows, key_weight, preferred_element_type=jnp.float32
    ).reshape(sequence_count, block_extent, KEY_HEADS, HEAD_DIM)
    value_row_block = jnp.dot(normalized_rows, value_weight, preferred_element_type=jnp.float32)
    query_rows = (
        apply_rotation(query_rows, cosine_values, sine_values) * HEAD_DIM ** (-0.5)
    ).astype(jnp.bfloat16)
    key_row_block = (
        apply_rotation(key_row_block, cosine_values, sine_values)
        .astype(jnp.bfloat16)
        .reshape(sequence_count, block_extent, KEY_HEADS * HEAD_DIM)
    )
    value_row_block = value_row_block.astype(jnp.bfloat16).reshape(
        sequence_count, block_extent, KEY_HEADS * HEAD_DIM
    )
    packed = jnp.concatenate([key_row_block, value_row_block], -1)
    if again:
        collected_rows = lax.all_gather(packed, "seq", axis=1, tiled=True)
    else:
        collected_rows = lax.all_gather(packed, "seq", axis=1, tiled=True)
    sequence_length = collected_rows.shape[1]
    every_key = collected_rows[..., : KEY_HEADS * HEAD_DIM].reshape(
        sequence_count, sequence_length, KEY_HEADS, HEAD_DIM
    )
    every_value = collected_rows[..., KEY_HEADS * HEAD_DIM :].reshape(
        sequence_count, sequence_length, KEY_HEADS, HEAD_DIM
    )
    grouped_heads = query_rows.reshape(
        sequence_count, block_extent, KEY_HEADS, query_groups, HEAD_DIM
    )
    scores = jnp.einsum(
        "sqhgd,skhd->shgqk", grouped_heads, every_key, preferred_element_type=jnp.float32
    )
    causal = key_pos[None, :] <= query_pos[:, None]
    scores = jnp.where(causal, scores, -1e30)
    row_peak = jnp.max(scores, -1, keepdims=True)
    exponent = jnp.exp(scores - row_peak)
    attn_probs = exponent / jnp.sum(exponent, -1, keepdims=True)
    probs_low = attn_probs.astype(jnp.bfloat16)
    mixed = jnp.einsum(
        "shgqk,skhd->sqhgd", probs_low, every_value, preferred_element_type=jnp.float32
    )
    mixed = mixed.astype(jnp.bfloat16).reshape(number_of_rows, QUERY_HEADS * HEAD_DIM)
    middle = values + jnp.dot(mixed, w_out, preferred_element_type=jnp.float32).reshape(
        sequence_count, block_extent, model_width
    )
    normed_ffn, scales_ffn = norm_forward(middle, ffn_gain.astype(jnp.float32))
    normed_ffn = normed_ffn.astype(jnp.bfloat16).reshape(number_of_rows, model_width)
    gate_act = jnp.dot(normed_ffn, w_gate, preferred_element_type=jnp.float32)
    up_act = jnp.dot(normed_ffn, w_up, preferred_element_type=jnp.float32)
    hidden = (jax.nn.silu(gate_act) * up_act).astype(jnp.bfloat16)
    output = middle + jnp.dot(hidden, w_down, preferred_element_type=jnp.float32).reshape(
        sequence_count, block_extent, model_width
    )
    saved = (
        values,
        scales_attn,
        normalized_rows,
        grouped_heads,
        every_key,
        every_value,
        attn_probs,
        probs_low,
        mixed,
        middle,
        scales_ffn,
        normed_ffn,
        gate_act,
        up_act,
        hidden,
    )
    return (output, saved)


def backward_layer(incoming, saved, weights, tables):
    attn_gain, w_query, key_weight, value_weight, w_out, ffn_gain, w_gate, w_up, w_down = weights
    cosine_values, sine_values, query_pos, key_pos = tables
    (
        values,
        scales_attn,
        normalized_rows,
        grouped_heads,
        every_key,
        every_value,
        attn_probs,
        probs_low,
        mixed,
        middle,
        scales_ffn,
        normed_ffn,
        gate_act,
        up_act,
        hidden,
    ) = saved
    sequence_count, block_extent, model_width = values.shape
    number_of_rows = sequence_count * block_extent
    sequence_length = every_key.shape[1]
    branch_grad = incoming.astype(jnp.bfloat16).reshape(number_of_rows, model_width)
    grad_down = jnp.einsum("rf,rd->fd", hidden, branch_grad, preferred_element_type=jnp.float32)
    grad_hidden = jnp.einsum("rd,fd->rf", branch_grad, w_down, preferred_element_type=jnp.float32)
    sigmoid_gate = jax.nn.sigmoid(gate_act)
    silu_gate = gate_act * sigmoid_gate
    gate_grad = (
        grad_hidden * up_act * sigmoid_gate * (1.0 + gate_act * (1.0 - sigmoid_gate))
    ).astype(jnp.bfloat16)
    up_grad = (grad_hidden * silu_gate).astype(jnp.bfloat16)
    grad_gate = jnp.einsum("rd,rf->df", normed_ffn, gate_grad, preferred_element_type=jnp.float32)
    grad_up = jnp.einsum("rd,rf->df", normed_ffn, up_grad, preferred_element_type=jnp.float32)
    grad_normed_ffn = jnp.einsum("rf,df->rd", gate_grad, w_gate, preferred_element_type=jnp.float32)
    grad_normed_ffn = grad_normed_ffn + jnp.einsum(
        "rf,df->rd", up_grad, w_up, preferred_element_type=jnp.float32
    )
    back_ffn, grad_ffn_gain = norm_backward(
        middle,
        scales_ffn,
        ffn_gain.astype(jnp.float32),
        grad_normed_ffn.reshape(sequence_count, block_extent, model_width),
    )
    grad_middle = incoming + back_ffn
    attn_grad = grad_middle.astype(jnp.bfloat16).reshape(number_of_rows, model_width)
    grad_out = jnp.einsum("rc,rd->cd", mixed, attn_grad, preferred_element_type=jnp.float32)
    blended_gradient = jnp.einsum("rd,cd->rc", attn_grad, w_out, preferred_element_type=jnp.float32)
    blended_gradient = blended_gradient.astype(jnp.bfloat16).reshape(
        sequence_count, block_extent, KEY_HEADS, QUERY_HEADS // KEY_HEADS, HEAD_DIM
    )
    probs_grad = jnp.einsum(
        "sqhgd,skhd->shgqk", blended_gradient, every_value, preferred_element_type=jnp.float32
    )
    score_grad = attn_probs * (probs_grad - jnp.sum(attn_probs * probs_grad, -1, keepdims=True))
    score_grad = score_grad.astype(jnp.bfloat16)
    query_grad = jnp.einsum(
        "shgqk,skhd->sqhgd", score_grad, every_key, preferred_element_type=jnp.float32
    )
    key_gradient = jnp.einsum(
        "shgqk,sqhgd->skhd", score_grad, grouped_heads, preferred_element_type=jnp.float32
    )
    value_gradient = jnp.einsum(
        "shgqk,sqhgd->skhd", probs_low, blended_gradient, preferred_element_type=jnp.float32
    )
    packed_grad = jnp.concatenate(
        [
            key_gradient.reshape(sequence_count, sequence_length, KEY_HEADS * HEAD_DIM),
            value_gradient.reshape(sequence_count, sequence_length, KEY_HEADS * HEAD_DIM),
        ],
        -1,
    )
    local_gradient = lax.psum_scatter(packed_grad, "seq", scatter_dimension=1, tiled=True)
    local_keys = local_gradient[..., : KEY_HEADS * HEAD_DIM].reshape(
        sequence_count, block_extent, KEY_HEADS, HEAD_DIM
    )
    value_reduced = (
        local_gradient[..., KEY_HEADS * HEAD_DIM :]
        .reshape(number_of_rows, KEY_HEADS * HEAD_DIM)
        .astype(jnp.bfloat16)
    )
    query_low = (
        (
            reverse_rotation(
                query_grad.reshape(sequence_count, block_extent, QUERY_HEADS, HEAD_DIM),
                cosine_values,
                sine_values,
            )
            * HEAD_DIM ** (-0.5)
        )
        .astype(jnp.bfloat16)
        .reshape(number_of_rows, QUERY_HEADS * HEAD_DIM)
    )
    key_reduced = (
        reverse_rotation(local_keys, cosine_values, sine_values)
        .astype(jnp.bfloat16)
        .reshape(number_of_rows, KEY_HEADS * HEAD_DIM)
    )
    grad_query = jnp.einsum(
        "rd,rc->dc", normalized_rows, query_low, preferred_element_type=jnp.float32
    )
    grad_key = jnp.einsum(
        "rd,rc->dc", normalized_rows, key_reduced, preferred_element_type=jnp.float32
    )
    grad_value = jnp.einsum(
        "rd,rc->dc", normalized_rows, value_reduced, preferred_element_type=jnp.float32
    )
    grad_normed = jnp.einsum("rc,dc->rd", query_low, w_query, preferred_element_type=jnp.float32)
    grad_normed = grad_normed + jnp.einsum(
        "rc,dc->rd", key_reduced, key_weight, preferred_element_type=jnp.float32
    )
    grad_normed = grad_normed + jnp.einsum(
        "rc,dc->rd", value_reduced, value_weight, preferred_element_type=jnp.float32
    )
    back_attn, grad_attn_gain = norm_backward(
        values,
        scales_attn,
        attn_gain.astype(jnp.float32),
        grad_normed.reshape(sequence_count, block_extent, model_width),
    )
    return (
        grad_middle + back_attn,
        (
            grad_attn_gain,
            grad_query,
            grad_key,
            grad_value,
            grad_out,
            grad_ffn_gain,
            grad_gate,
            grad_up,
            grad_down,
        ),
    )


def swap(values, axis, bit):
    size = lax.axis_size(axis)
    return lax.ppermute(values, axis, [(i, i ^ bit) for i in range(size)])


def bits_of(axis):
    size = lax.axis_size(axis)
    assert size & (size - 1) == 0
    return [1 << i for i in range(size.bit_length() - 1)]


def high(axis, bit):
    return (lax.axis_index(axis) // bit) % 2


def halves(values, dim, which):
    half = values.shape[dim] // 2
    return lax.dynamic_slice_in_dim(values, which * half, half, dim)


def joined(mine, other, dim, which):
    return jnp.where(
        which == 0,
        jnp.concatenate([mine, other], dim),
        jnp.concatenate([other, mine], dim),
    )


def gather_rows(shard):
    rows = shard.shape[0]
    quarter = rows // 4
    mine = lax.axis_index("fsdp")
    low_batch, low_seq = high("batch", 1), high("seq", 1)
    number = 2 * low_batch + low_seq
    sent = lax.dynamic_slice_in_dim(shard, number * quarter, quarter, 0)
    first = swap(sent, "fsdp", 1)
    second = swap(first, "batch", 1)
    third = swap(first, "seq", 1)
    fourth = swap(second, "seq", 1)
    whole = jnp.zeros((2 * rows,) + shard.shape[1:], shard.dtype)
    whole = lax.dynamic_update_slice_in_dim(whole, shard, mine * rows, 0)
    base = (1 - mine) * rows
    for piece, number in (
        (first, 2 * low_batch + low_seq),
        (second, 2 * (1 - low_batch) + low_seq),
        (third, 2 * low_batch + (1 - low_seq)),
        (fourth, 2 * (1 - low_batch) + (1 - low_seq)),
    ):
        whole = lax.dynamic_update_slice_in_dim(whole, piece, base + number * quarter, 0)
    return whole


def split_dim(shape):
    if shape[0] % 16 == 0:
        return 0
    if shape[1] % 256 == 0:
        return 1
    return 0 if shape[0] % 2 == 0 else 1


def reduce_rows(partial):
    rows, columns = partial.shape
    held = partial.reshape(2, rows // 2, columns)
    stages = []
    for bit in bits_of("seq"):
        which = high("seq", bit)
        kept, sent = halves(held, 1, which), halves(held, 1, 1 - which)
        arrived = swap(sent.astype(jnp.bfloat16), "seq", bit)
        held = kept.astype(jnp.float32) + arrived.astype(jnp.float32)
        stages.append(("seq", bit, 0, which))
    mine = lax.axis_index("fsdp")
    kept, sent = halves(held, 0, mine)[0], halves(held, 0, 1 - mine)[0]
    arrived = swap(sent.astype(jnp.bfloat16), "fsdp", 1)
    held = kept + arrived.astype(jnp.float32)
    for bit in bits_of("batch"):
        which = high("batch", bit)
        dim = split_dim(held.shape)
        kept, sent = halves(held, dim, which), halves(held, dim, 1 - which)
        arrived = swap(sent.astype(jnp.bfloat16), "batch", bit)
        held = kept + arrived.astype(jnp.float32)
        stages.append(("batch", bit, dim, which))
    held = held.astype(jnp.bfloat16)
    for axis, bit, dim, which in reversed(stages):
        held = joined(held, swap(held, axis, bit), dim, which)
    return held.astype(jnp.float32)


def per_device(
    tokens,
    attn_gain,
    w_query,
    key_weight,
    value_weight,
    w_out,
    ffn_gain,
    w_gate,
    w_up,
    w_down,
    cotangent,
):
    gains = jnp.stack([attn_gain, ffn_gain])
    both = swap(gains, "fsdp", 1)
    gains = joined(gains, both, 1, lax.axis_index("fsdp"))
    projections = gather_rows(jnp.concatenate([w_query, key_weight, value_weight], 1))
    width, narrow = w_query.shape[1], key_weight.shape[1]
    weights = (
        gains[0],
        projections[:, :width],
        projections[:, width : width + narrow],
        projections[:, width + narrow :],
        gather_rows(w_out),
        gains[1],
        gather_rows(w_gate),
        gather_rows(w_up),
        gather_rows(w_down),
    )
    block_extent = tokens.shape[1]
    seq_devices = lax.axis_size("seq")
    query_pos = lax.axis_index("seq") * block_extent + jnp.arange(block_extent, dtype=jnp.int32)
    key_pos = jnp.arange(block_extent * seq_devices, dtype=jnp.int32)
    cosine_values, sine_values = rotary_tables(query_pos.astype(jnp.float32))
    tables = (cosine_values, sine_values, query_pos, key_pos)
    start_in = tokens.astype(jnp.float32)
    middle_in, saved_lower = forward_layer(start_in, weights, tables, False)
    final_out, saved_upper = forward_layer(middle_in, weights, tables, False)
    grad_middle, grads_upper = backward_layer(
        cotangent.astype(jnp.float32), saved_upper, weights, tables
    )
    grad_start, grads_lower = backward_layer(grad_middle, saved_lower, weights, tables)
    summed = tuple(
        (upper_term + lower_term for upper_term, lower_term in zip(grads_upper, grads_lower))
    )
    gain_grads = lax.psum(jnp.stack([summed[0], summed[5]]), ("batch", "fsdp", "seq"))
    gain_grads = halves(gain_grads, 1, lax.axis_index("fsdp"))
    down = reduce_rows(summed[8])
    gate = reduce_rows(summed[6])
    up = reduce_rows(summed[7])
    pack = reduce_rows(jnp.concatenate([summed[4], summed[1], summed[2], summed[3]], 1))
    return (
        final_out.astype(jnp.bfloat16),
        grad_start,
        gain_grads[0],
        pack[:, width : 2 * width],
        pack[:, 2 * width : 2 * width + narrow],
        pack[:, 2 * width + narrow :],
        pack[:, :width],
        gain_grads[1],
        gate,
        up,
        down,
    )


def solution(mesh):
    return jax.shard_map(
        per_device,
        mesh=mesh,
        in_specs=(
            P(("batch", "fsdp"), "seq", None),
            P("fsdp"),
            P("fsdp", None),
            P("fsdp", None),
            P("fsdp", None),
            P("fsdp", None),
            P("fsdp"),
            P("fsdp", None),
            P("fsdp", None),
            P("fsdp", None),
            P(("batch", "fsdp"), "seq", None),
        ),
        out_specs=(
            P(("batch", "fsdp"), "seq", None),
            P(("batch", "fsdp"), "seq", None),
            P("fsdp"),
            P("fsdp", None),
            P("fsdp", None),
            P("fsdp", None),
            P("fsdp", None),
            P("fsdp"),
            P("fsdp", None),
            P("fsdp", None),
            P("fsdp", None),
        ),
        check_vma=False,
    )
```

```python
import functools
import math

import jax
import jax.numpy as jnp
from jax import lax
from jax.experimental import pallas as pl
from jax.experimental.pallas import tpu as pltpu
from jax.sharding import PartitionSpec as P

QUERY_HEADS = 15
KEY_HEADS = 5
HEAD_DIM = 64
GROUP = QUERY_HEADS // KEY_HEADS
EPSILON = 1e-05
VMEM_BYTES = 56 * 1024 * 1024
F32 = jnp.float32
BF16 = jnp.bfloat16


def dot(left, right, left_dim, right_dim):
    return lax.dot_general(
        left, right, (((left_dim,), (right_dim,)), ((), ())), preferred_element_type=F32
    )


def spans(total, size):
    return [(start, min(size, total - start)) for start in range(0, total, size)]


def call(kernel, name, grid, in_specs, out_specs, out_shape, scratch=(), flops=0, moved=0):
    return pl.pallas_call(
        kernel,
        name=name,
        out_shape=out_shape,
        grid_spec=pltpu.PrefetchScalarGridSpec(
            num_scalar_prefetch=1,
            grid=grid,
            in_specs=in_specs,
            out_specs=out_specs,
            scratch_shapes=list(scratch),
        ),
        compiler_params=pltpu.CompilerParams(vmem_limit_bytes=VMEM_BYTES),
        cost_estimate=pl.CostEstimate(flops=flops, bytes_accessed=moved, transcendentals=0),
    )


def whole(shape):
    return pl.BlockSpec(shape, lambda *_: (0,) * len(shape))


def shaped(shape, dtype):
    return jax.ShapeDtypeStruct(shape, dtype)


def scale_of(values):
    return lax.rsqrt(jnp.mean(values * values, 0, keepdims=True) + EPSILON)


def norm_back(values, gain, incoming):
    scales = scale_of(values)
    weighted = gain * incoming
    inner = jnp.mean(values * weighted, 0, keepdims=True)
    grad = scales * weighted - values * (scales * scales * scales * inner)
    return grad, jnp.sum(incoming * values * scales, 1, keepdims=True)


def rotate(values, cosine, sine):
    half = HEAD_DIM // 2
    first, second = values[:half], values[half:]
    return first * cosine - second * sine, second * cosine + first * sine


def project_kernel(
    info, x, gain, q_own, q_oth, k_own, k_oth, v_own, v_oth, cosine, sine, normed, out
):
    width = x.shape[0]
    half = width // 2
    values = x[...].astype(F32)
    normed[...] = (values * scale_of(values) * gain[...]).astype(BF16)
    own = normed[pl.ds(pl.multiple_of(info[0] * half, half), half), :]
    oth = normed[pl.ds(pl.multiple_of((1 - info[0]) * half, half), half), :]
    cos, sin = cosine[...], sine[...]
    hd = HEAD_DIM

    def turned(rows, base, factor):
        for head in range(rows.shape[0] // hd):
            first, second = rotate(rows[head * hd : (head + 1) * hd], cos, sin)
            at = base + head * hd
            out[at : at + hd // 2, :] = (first * factor).astype(BF16)
            out[at + hd // 2 : at + hd, :] = (second * factor).astype(BF16)

    q_width = q_own.shape[1]
    for start, size in spans(q_width, 256):
        part = slice(start, start + size)
        rows = dot(q_own[:, part], own, 0, 0) + dot(q_oth[:, part], oth, 0, 0)
        turned(rows, start, hd**-0.5)
    kv = k_own.shape[0]
    turned(dot(k_own[...], own, 1, 0) + dot(k_oth[...], oth, 1, 0), q_width, 1.0)
    rows = dot(v_own[...], own, 1, 0) + dot(v_oth[...], oth, 1, 0)
    out[q_width + kv : q_width + 2 * kv, :] = rows.astype(BF16)


def project(info, x, gain, weights, tables):
    width, rows = x.shape
    q, k, v = weights
    total = q[0].shape[1] + 2 * k[0].shape[0]
    operands = (x, gain, *q, *k, *v, *tables)
    return call(
        project_kernel,
        "project",
        (1,),
        [whole(item.shape) for item in operands],
        [whole((width, rows)), whole((total, rows))],
        [shaped((width, rows), BF16), shaped((total, rows), BF16)],
        flops=2 * width * total * rows,
        moved=8_000_000,
    )(info, *operands)


def attend_kernel(info, q, k_own, v_own, k_past, v_past, out, lse):
    rows = q.shape[1]
    block = min(256, rows)
    hd = HEAD_DIM

    def step(state, queries, keys, values, first_row):
        fresh = []
        for group in range(GROUP):
            scores = dot(keys, queries[group], 0, 0)
            if first_row is not None:
                key_row = lax.broadcasted_iota(jnp.int32, scores.shape, 0)
                query_row = lax.broadcasted_iota(jnp.int32, scores.shape, 1) + first_row
                scores = jnp.where(key_row <= query_row, scores, -1e30)
            peak = jnp.max(scores, 0, keepdims=True)
            if state is not None:
                old_peak, old_sum, old_out = state[group]
                peak = jnp.maximum(peak, old_peak)
            exponent = jnp.exp(scores - peak)
            total = jnp.sum(exponent, 0, keepdims=True)
            mixed = dot(values, exponent.astype(BF16), 1, 0)
            if state is not None:
                shrink = jnp.exp(old_peak - peak)
                total = total + shrink * old_sum
                mixed = mixed + shrink * old_out
            fresh.append((peak, total, mixed))
        return tuple(fresh)

    for start in range(0, rows, block):
        part = slice(start, start + block)
        queries = [q[group * hd : (group + 1) * hd, part] for group in range(GROUP)]
        seen = start + block
        state = step(None, queries, k_own[:, :seen], v_own[:, :seen], start)
        state = lax.fori_loop(
            0,
            info[1],
            lambda device, held: step(held, queries, k_past[device], v_past[device], None),
            state,
        )
        for group in range(GROUP):
            peak, total, mixed = state[group]
            out[group * hd : (group + 1) * hd, part] = (mixed / total).astype(BF16)
            lse[0, group : group + 1, part] = peak + jnp.log(total)


def attention_specs(rows, past, order):
    hd = HEAD_DIM
    return [
        pl.BlockSpec((GROUP * hd, rows), lambda h, info: (h, 0)),
        pl.BlockSpec((hd, rows), lambda h, info: (QUERY_HEADS + h, 0)),
        pl.BlockSpec((hd, rows), lambda h, info: (QUERY_HEADS + KEY_HEADS + h, 0)),
        pl.BlockSpec((past, hd, rows), lambda h, info: (0, h, 0)),
        pl.BlockSpec((past, hd, rows), lambda h, info: (0, KEY_HEADS + h, 0)),
    ]


def attend(info, qkv, past):
    rows = qkv.shape[1]
    count = past.shape[0]
    return call(
        attend_kernel,
        "attend",
        (KEY_HEADS,),
        attention_specs(rows, count, None),
        [
            pl.BlockSpec((GROUP * HEAD_DIM, rows), lambda h, info: (h, 0)),
            pl.BlockSpec((1, 8, rows), lambda h, info: (h, 0, 0)),
        ],
        [shaped((QUERY_HEADS * HEAD_DIM, rows), BF16), shaped((KEY_HEADS, 8, rows), F32)],
        flops=16 * QUERY_HEADS * HEAD_DIM * rows * rows,
        moved=4_000_000,
    )(info, qkv, qkv, qkv, past, past)


def mix_kernel(info, x, mixed, o_own, o_oth, gain, middle, normed):
    width = x.shape[0]
    half = mixed.shape[0] // 2
    own = mixed[pl.ds(pl.multiple_of(info[0] * half, half), half), :]
    oth = mixed[pl.ds(pl.multiple_of((1 - info[0]) * half, half), half), :]
    for start, size in spans(width, 256):
        part = slice(start, start + size)
        added = dot(o_own[:, part], own, 0, 0) + dot(o_oth[:, part], oth, 0, 0)
        middle[part, :] = x[part, :].astype(F32) + added
    values = middle[...]
    normed[...] = (values * scale_of(values) * gain[...]).astype(BF16)


def mix(info, x, mixed, weights, gain):
    width, rows = x.shape
    operands = (x, mixed, *weights, gain)
    return call(
        mix_kernel,
        "mix",
        (1,),
        [whole(item.shape) for item in operands],
        [whole((width, rows)), whole((width, rows))],
        [shaped((width, rows), F32), shaped((width, rows), BF16)],
        flops=2 * width * width * rows,
        moved=8_000_000,
    )(info, *operands)


def expand_kernel(info, normed, g_own, g_oth, u_own, u_oth, hidden, silu, slope, own, oth):
    half = normed.shape[0] // 2

    @pl.when(pl.program_id(0) == 0)
    def _():
        own[...] = normed[pl.ds(pl.multiple_of(info[0] * half, half), half), :].T
        oth[...] = normed[pl.ds(pl.multiple_of((1 - info[0]) * half, half), half), :].T

    rows = own.shape[0]
    block = min(256, rows)
    for start in range(0, rows, block):
        part = slice(start, start + block)
        gate = dot(own[part, :], g_own[...], 1, 0) + dot(oth[part, :], g_oth[...], 1, 0)
        up = dot(own[part, :], u_own[...], 1, 0) + dot(oth[part, :], u_oth[...], 1, 0)
        sigmoid = jax.nn.sigmoid(gate)
        active = gate * sigmoid
        hidden[part, :] = (active * up).astype(BF16)
        silu[part, :] = active.astype(BF16)
        slope[part, :] = (up * (sigmoid + active * (1.0 - sigmoid))).astype(BF16)


def expand(info, normed, gate, up):
    width, rows = normed.shape
    ff = gate[0].shape[1]
    tile = ff // 5
    half = width // 2
    weight = pl.BlockSpec((half, tile), lambda t, info: (0, t))
    result = pl.BlockSpec((rows, tile), lambda t, info: (0, t))
    return call(
        expand_kernel,
        "expand",
        (ff // tile,),
        [whole((width, rows))] + [weight] * 4,
        [result] * 3,
        [shaped((rows, ff), BF16)] * 3,
        [pltpu.VMEM((rows, half), BF16)] * 2,
        flops=4 * width * ff * rows,
        moved=20_000_000,
    )(info, normed, *gate, *up)


def shrink_kernel(info, middle, hidden, d_own, d_oth, out):
    half = hidden.shape[1] // 2
    own = hidden[:, pl.ds(pl.multiple_of(info[0] * half, half), half)]
    oth = hidden[:, pl.ds(pl.multiple_of((1 - info[0]) * half, half), half)]
    added = dot(d_own[...], own, 1, 1) + dot(d_oth[...], oth, 1, 1)
    out[...] = (middle[...] + added).astype(out.dtype)


def shrink(info, middle, hidden, down, dtype):
    width, rows = middle.shape
    ff = hidden.shape[1]
    tile = width // 5
    return call(
        shrink_kernel,
        "shrink",
        (width // tile,),
        [
            pl.BlockSpec((tile, rows), lambda t, info: (t, 0)),
            whole((rows, ff)),
            pl.BlockSpec((tile, ff // 2), lambda t, info: (t, 0)),
            pl.BlockSpec((tile, ff // 2), lambda t, info: (t, 0)),
        ],
        [pl.BlockSpec((tile, rows), lambda t, info: (t, 0))],
        [shaped((width, rows), dtype)],
        flops=2 * width * ff * rows,
        moved=11_000_000,
    )(info, middle, hidden, *down)[0]


def ffn_back_kernel(
    info,
    grad,
    middle,
    gain,
    silu,
    slope,
    d_own,
    d_oth,
    g_own,
    g_oth,
    u_own,
    u_oth,
    o_own,
    o_oth,
    gate_grad,
    up_grad,
    branch,
    grad_middle,
    attn_grad,
    mixed_grad,
    gain_grad,
    branch_rows,
    hidden_grad,
    total,
):
    step = pl.program_id(0)
    steps = pl.num_programs(0)
    half = total.shape[0] // 2
    own = pl.ds(pl.multiple_of(info[0] * half, half), half)
    oth = pl.ds(pl.multiple_of((1 - info[0]) * half, half), half)

    @pl.when(step == 0)
    def _():
        branch[...] = grad[...].astype(BF16)
        branch_rows[...] = branch[...].T

    @pl.when(step < steps // 2)
    def _():
        hidden_grad[...] = dot(branch_rows[...], d_own[...], 1, 0)

    @pl.when(step >= steps // 2)
    def _():
        hidden_grad[...] = dot(branch_rows[...], d_oth[...], 1, 0)

    incoming = hidden_grad[...]
    gate_grad[...] = (incoming * slope[...].astype(F32)).astype(BF16)
    up_grad[...] = (incoming * silu[...].astype(F32)).astype(BF16)
    own_part = dot(g_own[...], gate_grad[...], 1, 1) + dot(u_own[...], up_grad[...], 1, 1)
    oth_part = dot(g_oth[...], gate_grad[...], 1, 1) + dot(u_oth[...], up_grad[...], 1, 1)

    @pl.when(step == 0)
    def _():
        total[own, :] = own_part
        total[oth, :] = oth_part

    @pl.when(step > 0)
    def _():
        total[own, :] += own_part
        total[oth, :] += oth_part

    @pl.when(step == steps - 1)
    def _():
        back, gain_sum = norm_back(middle[...], gain[...], total[...])
        gain_grad[...] = gain_sum
        result = grad[...].astype(F32) + back
        grad_middle[...] = result
        attn_grad[...] = result.astype(BF16)
        low = attn_grad[...]
        mixed_grad[own, :] = dot(o_own[...], low, 1, 0).astype(BF16)
        mixed_grad[oth, :] = dot(o_oth[...], low, 1, 0).astype(BF16)


def ffn_back(info, grad, middle, gain, silu, slope, down, gate, up, out):
    width, rows = middle.shape
    ff = silu.shape[1]
    tile = ff // 4
    half = width // 2
    steps = ff // tile

    def column(t, info):
        own = info[0] * (steps // 2) + t
        return jnp.where(t < steps // 2, own, (1 - info[0]) * (steps // 2) + t - steps // 2)

    token = pl.BlockSpec((rows, tile), lambda t, info: (0, column(t, info)))
    weight = pl.BlockSpec((half, tile), lambda t, info: (0, column(t, info)))
    return call(
        ffn_back_kernel,
        "ffn_back",
        (steps,),
        [
            whole((width, rows)),
            whole((width, rows)),
            whole((width, 1)),
            token,
            token,
            pl.BlockSpec((width, tile), lambda t, info: (0, jnp.minimum(t, steps // 2 - 1))),
            pl.BlockSpec((width, tile), lambda t, info: (0, jnp.maximum(t - steps // 2, 0))),
            weight,
            weight,
            weight,
            weight,
            whole(out[0].shape),
            whole(out[1].shape),
        ],
        [
            token,
            token,
            whole((width, rows)),
            whole((width, rows)),
            whole((width, rows)),
            whole((2 * out[0].shape[0], rows)),
            whole((width, 1)),
        ],
        [
            shaped((rows, ff), BF16),
            shaped((rows, ff), BF16),
            shaped((width, rows), BF16),
            shaped((width, rows), F32),
            shaped((width, rows), BF16),
            shaped((2 * out[0].shape[0], rows), BF16),
            shaped((width, 1), F32),
        ],
        [
            pltpu.VMEM((rows, width), BF16),
            pltpu.VMEM((rows, tile), F32),
            pltpu.VMEM((width, rows), F32),
        ],
        flops=6 * width * ff * rows + 2 * width * width * rows,
        moved=32_000_000,
    )(info, grad, middle, gain, silu, slope, *down, *gate, *up, *out)


def attend_back_kernel(
    info,
    q,
    k_own,
    v_own,
    k_past,
    v_past,
    mixed_grad,
    mixed,
    lse,
    cosine,
    sine,
    q_grad,
    own_grad,
    past_grad,
):
    rows = q.shape[1]
    block = min(256, rows)
    hd = HEAD_DIM
    own_grad[...] = jnp.zeros_like(own_grad)
    past_grad[...] = jnp.zeros_like(past_grad)

    def step(state, tiles, keys, values, first_row):
        key_sum = value_sum = None
        fresh = []
        for group in range(GROUP):
            query, incoming, level, inner = tiles[group]
            scores = dot(keys, query, 0, 0)
            if first_row is not None:
                key_row = lax.broadcasted_iota(jnp.int32, scores.shape, 0)
                query_row = lax.broadcasted_iota(jnp.int32, scores.shape, 1) + first_row
                scores = jnp.where(key_row <= query_row, scores, -1e30)
            probs = jnp.exp(scores - level)
            slopes = dot(values, incoming, 0, 0)
            low = (probs * (slopes - inner)).astype(BF16)
            value_part = dot(incoming, probs.astype(BF16), 1, 1)
            key_part = dot(query, low, 1, 1)
            key_sum = key_part if key_sum is None else key_sum + key_part
            value_sum = value_part if value_sum is None else value_sum + value_part
            query_part = dot(keys, low, 1, 0)
            fresh.append(query_part if state is None else state[group] + query_part)
        return tuple(fresh), key_sum, value_sum

    for start in range(0, rows, block):
        part = slice(start, start + block)
        tiles = []
        for group in range(GROUP):
            head = slice(group * hd, (group + 1) * hd)
            incoming = mixed_grad[head, part]
            inner = jnp.sum(
                incoming.astype(F32) * mixed[head, part].astype(F32), 0, keepdims=True
            )
            tiles.append((q[head, part], incoming, lse[0, group : group + 1, part], inner))
        seen = start + block
        state, key_sum, value_sum = step(None, tiles, k_own[:, :seen], v_own[:, :seen], start)
        own_grad[0, :hd, :seen] += key_sum
        own_grad[0, hd:, :seen] += value_sum

        def past_step(device, held):
            held, key_sum, value_sum = step(held, tiles, k_past[device], v_past[device], None)
            past_grad[device, 0, :hd, :] += key_sum
            past_grad[device, 0, hd:, :] += value_sum
            return held

        state = lax.fori_loop(0, info[1], past_step, state)
        cos, sin = cosine[:, part], -sine[:, part]
        for group in range(GROUP):
            first, second = rotate(state[group], cos, sin)
            at = group * hd
            q_grad[at : at + hd // 2, part] = (first * hd**-0.5).astype(BF16)
            q_grad[at + hd // 2 : at + hd, part] = (second * hd**-0.5).astype(BF16)


def attend_back(info, qkv, past, mixed_grad, mixed, lse, tables):
    rows = qkv.shape[1]
    count = past.shape[0]
    hd = HEAD_DIM
    group = pl.BlockSpec((GROUP * hd, rows), lambda h, info: (h, 0))
    return call(
        attend_back_kernel,
        "attend_back",
        (KEY_HEADS,),
        attention_specs(rows, count, None)
        + [
            group,
            group,
            pl.BlockSpec((1, 8, rows), lambda h, info: (h, 0, 0)),
            whole(tables[0].shape),
            whole(tables[1].shape),
        ],
        [
            group,
            pl.BlockSpec((1, 2 * hd, rows), lambda h, info: (h, 0, 0)),
            pl.BlockSpec((count, 1, 2 * hd, rows), lambda h, info: (0, h, 0, 0)),
        ],
        [
            shaped((QUERY_HEADS * hd, rows), BF16),
            shaped((KEY_HEADS, 2 * hd, rows), F32),
            shaped((count, KEY_HEADS, 2 * hd, rows), F32),
        ],
        flops=40 * QUERY_HEADS * hd * rows * rows,
        moved=10_000_000,
    )(info, qkv, qkv, qkv, past, past, mixed_grad, mixed, lse, *tables)


def project_back_kernel(
    info,
    x,
    gain,
    grad_middle,
    q_grad,
    own_grad,
    arrived,
    q_own,
    q_oth,
    k_own,
    k_oth,
    v_own,
    v_oth,
    cosine,
    sine,
    kv_grad,
    out,
    gain_grad,
    total,
):
    half = x.shape[0] // 2
    hd = HEAD_DIM
    kv = KEY_HEADS * hd
    cos, sin = cosine[...], -sine[...]
    for head in range(KEY_HEADS):
        both = own_grad[head] + arrived[head].astype(F32)
        first, second = rotate(both[:hd], cos, sin)
        at = head * hd
        kv_grad[at : at + hd // 2, :] = first.astype(BF16)
        kv_grad[at + hd // 2 : at + hd, :] = second.astype(BF16)
        kv_grad[kv + at : kv + at + hd, :] = both[hd:].astype(BF16)
    for mine, q, k, v in (
        (info[0], q_own, k_own, v_own),
        (1 - info[0], q_oth, k_oth, v_oth),
    ):
        total[pl.ds(pl.multiple_of(mine * half, half), half), :] = (
            dot(q[...], q_grad[...], 1, 0)
            + dot(k[...], kv_grad[:kv, :], 0, 0)
            + dot(v[...], kv_grad[kv:, :], 0, 0)
        )
    back, gain_sum = norm_back(x[...].astype(F32), gain[...], total[...])
    gain_grad[...] = gain_sum
    out[...] = grad_middle[...] + back


def project_back(info, x, gain, grad_middle, q_grad, own_grad, arrived, weights, tables):
    width, rows = x.shape
    q, k, v = weights
    kv = 2 * KEY_HEADS * HEAD_DIM
    operands = (x, gain, grad_middle, q_grad, own_grad, arrived, *q, *k, *v, *tables)
    return call(
        project_back_kernel,
        "project_back",
        (1,),
        [whole(item.shape) for item in operands],
        [whole((kv, rows)), whole((width, rows)), whole((width, 1))],
        [shaped((kv, rows), BF16), shaped((width, rows), F32), shaped((width, 1), F32)],
        [pltpu.VMEM((width, rows), F32)],
        flops=2 * width * (width + kv) * rows,
        moved=13_000_000,
    )(info, *operands)


def outer_send_kernel(info, left_a, right_a, left_b, right_b, out):
    count, size = out.shape[0], out.shape[1]
    other = 1 - info[2]
    for half in range(count):
        rows = pl.ds(pl.multiple_of((2 * half + other) * size, size), size)
        out[half] = (
            dot(left_a[rows, :], right_a[...], 1, 0) + dot(left_b[rows, :], right_b[...], 1, 0)
        ).astype(BF16)


def outer_keep_kernel(info, left_a, right_a, left_b, right_b, arrived, sent, kept):
    size = sent.shape[0]
    for half, out in ((1 - info[0], sent), (info[0], kept)):
        rows = pl.ds(pl.multiple_of((2 * half + info[2]) * size, size), size)
        out[...] = (
            dot(left_a[rows, :], right_a[...], 1, 0)
            + dot(left_b[rows, :], right_b[...], 1, 0)
            + arrived[half].astype(F32)
        ).astype(BF16)


def column_tile(columns):
    return columns // 5


def outer_send(info, parts, count):
    left_a, right_a, left_b, right_b = parts
    width, rows = left_a.shape
    columns = right_a.shape[1]
    size = width // (2 * count)
    tile = column_tile(columns)
    right = pl.BlockSpec((rows, tile), lambda t, info: (0, t))
    return call(
        outer_send_kernel,
        "outer_send",
        (columns // tile,),
        [whole((width, rows)), right, whole((width, rows)), right],
        [pl.BlockSpec((count, size, tile), lambda t, info: (0, 0, t))],
        [shaped((count, size, columns), BF16)],
        flops=2 * width * columns * rows,
        moved=10_000_000,
    )(info, *parts)[0]


def outer_keep(info, parts, arrived):
    left_a, right_a, left_b, right_b = parts
    width, rows = left_a.shape
    columns = right_a.shape[1]
    size = width // 4
    tile = column_tile(columns)
    right = pl.BlockSpec((rows, tile), lambda t, info: (0, t))
    result = pl.BlockSpec((size, tile), lambda t, info: (0, t))
    return call(
        outer_keep_kernel,
        "outer_keep",
        (columns // tile,),
        [
            whole((width, rows)),
            right,
            whole((width, rows)),
            right,
            pl.BlockSpec((2, size, tile), lambda t, info: (0, 0, t)),
        ],
        [result, result],
        [shaped((size, columns), BF16)] * 2,
        flops=2 * width * columns * rows,
        moved=13_000_000,
    )(info, *parts, arrived)


def down_keep_kernel(info, left_a, right_a, left_b, right_b, arrived, sent, kept):
    size = sent.shape[0]
    rows = pl.ds(pl.multiple_of(info[2] * size, size), size)
    result = (
        dot(left_a[rows, :], right_a[...], 1, 0)
        + dot(left_b[rows, :], right_b[...], 1, 0)
        + arrived[0].astype(F32)
    ).astype(BF16)

    @pl.when(pl.program_id(0) < pl.num_programs(0) // 2)
    def _():
        sent[...] = result

    @pl.when(pl.program_id(0) >= pl.num_programs(0) // 2)
    def _():
        kept[...] = result


def down_keep(info, parts, arrived):
    left_a, right_a, left_b, right_b = parts
    width, rows = left_a.shape
    columns = right_a.shape[1]
    size, tile = width // 2, columns // 4

    def column(t, info):
        return jnp.where(t < 2, (1 - info[0]) * 2 + t, info[0] * 2 + t - 2)

    right = pl.BlockSpec((rows, tile), lambda t, info: (0, column(t, info)))
    return call(
        down_keep_kernel,
        "down_keep",
        (4,),
        [
            whole((width, rows)),
            right,
            whole((width, rows)),
            right,
            pl.BlockSpec((1, size, tile), lambda t, info: (0, 0, column(t, info))),
        ],
        [
            pl.BlockSpec((size, tile), lambda t, info: (0, jnp.minimum(t, 1))),
            pl.BlockSpec((size, tile), lambda t, info: (0, jnp.maximum(t - 2, 0))),
        ],
        [shaped((size, columns // 2), BF16)] * 2,
        flops=2 * width * columns * rows,
        moved=13_000_000,
    )(info, *parts, arrived)


def pack_parts(operands, rows):
    at = 0
    for left_a, right_a, left_b, right_b in operands:
        size = right_a.shape[0]
        product = dot(left_a[rows, :], right_a[...], 1, 1) + dot(
            left_b[rows, :], right_b[...], 1, 1
        )
        yield slice(at, at + size), product
        at += size


def pack_send_kernel(info, *refs):
    operands, out = [refs[:4], refs[4:8], refs[8:12]], refs[12]
    size = out.shape[1]
    for half in range(2):
        rows = pl.ds(pl.multiple_of((2 * half + 1 - info[2]) * size, size), size)
        for part, product in pack_parts(operands, rows):
            out[half, :, part] = product.astype(BF16)


def pack_keep_kernel(info, *refs):
    operands, arrived, sent, kept = [refs[:4], refs[4:8], refs[8:12]], *refs[12:]
    size = sent.shape[0]
    for half, out in ((1 - info[0], sent), (info[0], kept)):
        rows = pl.ds(pl.multiple_of((2 * half + info[2]) * size, size), size)
        for part, product in pack_parts(operands, rows):
            out[:, part] = (product + arrived[half, :, part].astype(F32)).astype(BF16)


def pack_send(info, parts):
    width, rows = parts[0].shape
    columns = parts[1].shape[0] + parts[5].shape[0] + parts[9].shape[0]
    return call(
        pack_send_kernel,
        "pack_send",
        (1,),
        [whole(item.shape) for item in parts],
        [whole((2, width // 4, columns))],
        [shaped((2, width // 4, columns), BF16)],
        flops=2 * width * columns * rows,
        moved=14_000_000,
    )(info, *parts)[0]


def pack_keep(info, parts, arrived):
    width, rows = parts[0].shape
    columns = arrived.shape[2]
    return call(
        pack_keep_kernel,
        "pack_keep",
        (1,),
        [whole(item.shape) for item in (*parts, arrived)],
        [whole((width // 4, columns))] * 2,
        [shaped((width // 4, columns), BF16)] * 2,
        flops=2 * width * columns * rows,
        moved=17_000_000,
    )(info, *parts, arrived)


def swap(values, axis, bit):
    size = lax.axis_size(axis)
    return lax.ppermute(values, axis, [(i, i ^ bit) for i in range(size)])


def bits_of(axis):
    size = lax.axis_size(axis)
    assert size & (size - 1) == 0
    return [1 << i for i in range(size.bit_length() - 1)]


def high(axis, bit):
    return (lax.axis_index(axis) // bit) % 2


def halves(values, dim, which):
    half = values.shape[dim] // 2
    return lax.dynamic_slice_in_dim(values, which * half, half, dim)


def joined(mine, other, dim, which):
    return jnp.where(
        which == 0,
        jnp.concatenate([mine, other], dim),
        jnp.concatenate([other, mine], dim),
    )


def fetch(shard, row_parts, column_parts):
    low_batch, low_seq = high("batch", 1), high("seq", 1)
    piece = halves(shard, row_parts, low_batch)
    piece = halves(piece, column_parts, low_seq)
    first = swap(piece, "fsdp", 1)
    second = swap(first, "batch", 1)
    mine = joined(first, second, row_parts, low_batch)
    theirs = swap(mine, "seq", 1)
    return joined(mine, theirs, column_parts, low_seq)


def fetch_pair(shard_a, shard_b):
    low_batch, low_seq = high("batch", 1), high("seq", 1)
    piece = halves(jnp.where(low_seq == 0, shard_a, shard_b), 0, low_batch)
    first = swap(piece, "fsdp", 1)
    second = swap(first, "batch", 1)
    mine = joined(first, second, 0, low_batch)
    theirs = swap(mine, "seq", 1)
    return (
        jnp.where(low_seq == 0, mine, theirs),
        jnp.where(low_seq == 0, theirs, mine),
    )


def split_dim(shape):
    if shape[0] % 16 == 0:
        return 0
    if shape[1] % 256 == 0:
        return 1
    return 0 if shape[0] % 2 == 0 else 1


def share_out(sent, kept):
    held = kept.astype(F32) + swap(sent, "fsdp", 1).astype(F32)
    stages = []
    for axis in ("seq", "batch"):
        for bit in bits_of(axis):
            if axis == "seq" and bit == 1:
                continue
            which = high(axis, bit)
            dim = split_dim(held.shape)
            low = held.astype(BF16)
            arrived = swap(halves(low, dim, 1 - which), axis, bit)
            held = halves(held, dim, which) + arrived.astype(F32)
            stages.append((axis, bit, dim, which))
    held = held.astype(BF16)
    stages.insert(0, ("seq", 1, 0, high("seq", 1)))
    for axis, bit, dim, which in reversed(stages):
        held = joined(held, swap(held, axis, bit), dim, which)
    return held.astype(F32)


def per_device(
    tokens,
    attn_gain,
    w_query,
    key_weight,
    value_weight,
    w_out,
    ffn_gain,
    w_gate,
    w_up,
    w_down,
    cotangent,
):
    assert tokens.shape[0] == 1 and lax.axis_size("fsdp") == 2
    mine, place, core = lax.axis_index("fsdp"), lax.axis_index("seq"), high("seq", 1)
    devices = lax.axis_size("seq")
    info = jnp.stack([mine, place, core]).astype(jnp.int32)
    start_in = tokens[0].T
    incoming = cotangent[0].T
    width, rows = start_in.shape

    gains = jnp.stack([attn_gain, ffn_gain])
    gains = joined(gains, swap(gains, "fsdp", 1), 1, mine).astype(F32)[..., None]
    key_weight, value_weight, w_down = key_weight.T, value_weight.T, w_down.T
    q_oth, o_oth = fetch_pair(w_query, w_out)
    k_oth, v_oth = fetch_pair(key_weight, value_weight)
    qkv_weights = ((w_query, q_oth), (key_weight, k_oth), (value_weight, v_oth))
    out = (w_out, o_oth)
    gate = (w_gate, fetch(w_gate, 0, 1))
    up = (w_up, fetch(w_up, 0, 1))
    down = (w_down, fetch(w_down, 0, 1))

    positions = (place * rows + jnp.arange(rows, dtype=jnp.int32)).astype(F32)
    frequency = jnp.exp(
        jnp.arange(HEAD_DIM // 2, dtype=F32) * (-2.0 * math.log(10000.0) / HEAD_DIM)
    )
    angles = frequency[:, None] * positions[None, :]
    tables = (jnp.cos(angles), jnp.sin(angles))

    def forward(x, dtype):
        normed, qkv = project(info, x, gains[0], qkv_weights, tables)
        kv = qkv[QUERY_HEADS * HEAD_DIM :]
        if devices == 2:
            past = swap(kv, "seq", 1)[None]
        else:
            past = lax.all_gather(kv, "seq")
        mixed, lse = attend(info, qkv, past)
        middle, normed_ffn = mix(info, x, mixed, out, gains[1])
        hidden, silu, slope = expand(info, normed_ffn, gate, up)
        result = shrink(info, middle, hidden, down, dtype)
        return result, (
            x, normed, qkv, past, mixed, lse, middle, normed_ffn, hidden, silu, slope
        )

    def backward(grad, saved):
        x, normed, qkv, past, mixed, lse, middle, normed_ffn, hidden, silu, slope = saved
        gate_grad, up_grad, branch, grad_middle, attn_grad, mixed_grad, ffn_gain_grad = ffn_back(
            info, grad, middle, gains[1], silu, slope, down, gate, up, out
        )
        q_grad, own_grad, past_grad = attend_back(
            info, qkv, past, mixed_grad, mixed, lse, tables
        )
        if devices == 2:
            arrived = swap(past_grad[0].astype(BF16), "seq", 1)
        else:
            arrived = lax.psum_scatter(past_grad, "seq", scatter_dimension=0)
        kv_grad, result, attn_gain_grad = project_back(
            info, x, gains[0], grad_middle, q_grad, own_grad, arrived, qkv_weights, tables
        )
        return result, (
            (branch, hidden),
            (normed_ffn, gate_grad),
            (normed_ffn, up_grad),
            (mixed, attn_grad),
            (normed, q_grad),
            (normed, kv_grad),
        ), jnp.stack([attn_gain_grad[:, 0], ffn_gain_grad[:, 0]])

    middle_in, saved_lower = forward(start_in, F32)
    final_out, saved_upper = forward(middle_in, BF16)
    grad_between, upper, upper_gains = backward(incoming, saved_upper)
    grad_start, lower, lower_gains = backward(grad_between, saved_lower)

    terms = [(*high_term, *low_term) for high_term, low_term in zip(upper, lower)]
    pack_terms = (*terms[5], *terms[3], *terms[4])
    down_arrived = swap(outer_send(info, terms[0], 1), "seq", 1)
    gate_arrived = swap(outer_send(info, terms[1], 2), "seq", 1)
    up_arrived = swap(outer_send(info, terms[2], 2), "seq", 1)
    pack_arrived = swap(pack_send(info, pack_terms), "seq", 1)
    down_grad = share_out(*down_keep(info, terms[0], down_arrived))
    gate_grad = share_out(*outer_keep(info, terms[1], gate_arrived))
    up_grad = share_out(*outer_keep(info, terms[2], up_arrived))
    pack = share_out(*pack_keep(info, pack_terms, pack_arrived))
    gain_grads = lax.psum(upper_gains + lower_gains, ("batch", "fsdp", "seq"))
    gain_grads = halves(gain_grads, 1, mine)
    narrow = KEY_HEADS * HEAD_DIM
    key_part, value_part, out_part, query_part = jnp.split(
        pack, [narrow, 2 * narrow, 2 * narrow + width], 1
    )
    return (
        final_out.T[None],
        grad_start.T[None],
        gain_grads[0],
        query_part,
        key_part,
        value_part,
        out_part,
        gain_grads[1],
        gate_grad,
        up_grad,
        down_grad.T,
    )


def solution(mesh):
    return jax.shard_map(
        per_device,
        mesh=mesh,
        in_specs=(
            P(("batch", "fsdp"), "seq", None),
            P("fsdp"),
            P("fsdp", None),
            P("fsdp", None),
            P("fsdp", None),
            P("fsdp", None),
            P("fsdp"),
            P("fsdp", None),
            P("fsdp", None),
            P("fsdp", None),
            P(("batch", "fsdp"), "seq", None),
        ),
        out_specs=(
            P(("batch", "fsdp"), "seq", None),
            P(("batch", "fsdp"), "seq", None),
            P("fsdp"),
            P("fsdp", None),
            P("fsdp", None),
            P("fsdp", None),
            P("fsdp", None),
            P("fsdp"),
            P("fsdp", None),
            P("fsdp", None),
            P("fsdp", None),
        ),
        check_vma=False,
    )
```

```python
import functools
import math

import jax
import jax.numpy as jnp
from jax import lax
from jax.experimental import pallas as pl
from jax.experimental.pallas import tpu as pltpu
from jax.sharding import PartitionSpec as P

QUERY_HEADS = 15
KEY_HEADS = 5
HEAD_DIM = 64
GROUP = QUERY_HEADS // KEY_HEADS
EPSILON = 1e-05
VMEM_BYTES = 56 * 1024 * 1024
F32 = jnp.float32
BF16 = jnp.bfloat16


def dot(left, right, left_dim, right_dim):
    return lax.dot_general(
        left, right, (((left_dim,), (right_dim,)), ((), ())), preferred_element_type=F32
    )


def spans(total, size):
    return [(start, min(size, total - start)) for start in range(0, total, size)]


def call(kernel, name, grid, in_specs, out_specs, out_shape, scratch=(), flops=0, moved=0):
    return pl.pallas_call(
        kernel,
        name=name,
        out_shape=out_shape,
        grid_spec=pltpu.PrefetchScalarGridSpec(
            num_scalar_prefetch=1,
            grid=grid,
            in_specs=in_specs,
            out_specs=out_specs,
            scratch_shapes=list(scratch),
        ),
        compiler_params=pltpu.CompilerParams(vmem_limit_bytes=VMEM_BYTES),
        cost_estimate=pl.CostEstimate(flops=flops, bytes_accessed=moved, transcendentals=0),
    )


def whole(shape):
    return pl.BlockSpec(shape, lambda *_: (0,) * len(shape))


def shaped(shape, dtype):
    return jax.ShapeDtypeStruct(shape, dtype)


def scale_of(values):
    return lax.rsqrt(jnp.mean(values * values, 0, keepdims=True) + EPSILON)


def norm_back(values, gain, incoming):
    scales = scale_of(values)
    weighted = gain * incoming
    inner = jnp.mean(values * weighted, 0, keepdims=True)
    grad = scales * weighted - values * (scales * scales * scales * inner)
    return grad, jnp.sum(incoming * values * scales, 1, keepdims=True)


def rotate(values, cosine, sine):
    half = HEAD_DIM // 2
    first, second = values[:half], values[half:]
    return first * cosine - second * sine, second * cosine + first * sine


def project_kernel(
    info, x, gain, q_weight, k_own, k_oth, v_own, v_oth, cosine, sine, normed, out
):
    width = x.shape[0]
    half = width // 2
    values = x[...].astype(F32)
    normed[...] = (values * scale_of(values) * gain[...]).astype(BF16)
    own = normed[pl.ds(pl.multiple_of(info[0] * half, half), half), :]
    oth = normed[pl.ds(pl.multiple_of((1 - info[0]) * half, half), half), :]
    cos, sin = cosine[...], sine[...]
    hd = HEAD_DIM

    def turned(rows, base, factor):
        for head in range(rows.shape[0] // hd):
            first, second = rotate(rows[head * hd : (head + 1) * hd], cos, sin)
            at = base + head * hd
            out[at : at + hd // 2, :] = (first * factor).astype(BF16)
            out[at + hd // 2 : at + hd, :] = (second * factor).astype(BF16)

    q_width = q_weight.shape[2]
    turned(dot(q_weight[0], normed[...], 0, 0), 0, hd**-0.5)
    kv = k_own.shape[0]
    turned(dot(k_own[...], own, 1, 0) + dot(k_oth[...], oth, 1, 0), q_width, 1.0)
    rows = dot(v_own[...], own, 1, 0) + dot(v_oth[...], oth, 1, 0)
    out[q_width + kv : q_width + 2 * kv, :] = rows.astype(BF16)


def project(info, x, gain, weights, tables):
    width, rows = x.shape
    square, k, v = weights
    total = square.shape[2] + 2 * k[0].shape[0]
    operands = (x, gain, square, *k, *v, *tables)
    specs = [whole(item.shape) for item in operands]
    specs[2] = pl.BlockSpec((1, *square.shape[1:]), lambda t, info: (0, 0, 0))
    return call(
        project_kernel,
        "project",
        (1,),
        specs,
        [whole((width, rows)), whole((total, rows))],
        [shaped((width, rows), BF16), shaped((total, rows), BF16)],
        flops=2 * width * total * rows,
        moved=8_000_000,
    )(info, *operands)


def attend_kernel(info, q, k_own, v_own, k_past, v_past, out, lse, keys_own, keys_past):
    rows = q.shape[1]
    block = min(256, rows)
    hd = HEAD_DIM
    groups = range(GROUP)
    keys_own[...] = k_own[...].T

    @pl.loop(0, info[1])
    def _(device):
        keys_past[device] = k_past[device].T

    def scores_of(keys, query, first_row):
        scores = dot(keys, query, 1, 0)
        if first_row is None:
            return scores
        key_row = lax.broadcasted_iota(jnp.int32, scores.shape, 0)
        query_row = lax.broadcasted_iota(jnp.int32, scores.shape, 1) + first_row
        return jnp.where(key_row <= query_row, scores, -1e30)

    for start in range(0, rows, block):
        part = slice(start, start + block)
        seen = start + block
        queries = [q[group * hd : (group + 1) * hd, part] for group in groups]

        def peaks(keys, first_row):
            return [
                jnp.max(scores_of(keys, query, first_row), 0, keepdims=True) for query in queries
            ]

        def past_peaks(device, held):
            fresh = peaks(keys_past[device], None)
            return tuple(jnp.maximum(old, new) for old, new in zip(held, fresh))

        peak = lax.fori_loop(0, info[1], past_peaks, tuple(peaks(keys_own[:seen, :], start)))

        def sums(keys, values, first_row):
            result = []
            for group in groups:
                exponent = jnp.exp(scores_of(keys, queries[group], first_row) - peak[group])
                total = jnp.sum(exponent, 0, keepdims=True)
                result.append((total, dot(values, exponent.astype(BF16), 1, 0)))
            return tuple(result)

        def past_sums(device, held):
            fresh = sums(keys_past[device], v_past[device], None)
            return tuple(
                (old[0] + new[0], old[1] + new[1]) for old, new in zip(held, fresh)
            )

        state = lax.fori_loop(
            0, info[1], past_sums, sums(keys_own[:seen, :], v_own[:, :seen], start)
        )
        for group in groups:
            total, mixed = state[group]
            out[group * hd : (group + 1) * hd, part] = (mixed / total).astype(BF16)
            lse[0, group : group + 1, part] = peak[group] + jnp.log(total)


def attention_specs(rows, past, base):
    hd = HEAD_DIM
    return [
        pl.BlockSpec((GROUP * hd, rows), lambda h, info: (base + h, 0)),
        pl.BlockSpec((hd, rows), lambda h, info: (QUERY_HEADS + base + h, 0)),
        pl.BlockSpec((hd, rows), lambda h, info: (QUERY_HEADS + KEY_HEADS + base + h, 0)),
        pl.BlockSpec((past, hd, rows), lambda h, info: (0, base + h, 0)),
        pl.BlockSpec((past, hd, rows), lambda h, info: (0, KEY_HEADS + base + h, 0)),
    ]


def attend(info, qkv, past):
    rows = qkv.shape[1]
    count = past.shape[0]
    return call(
        attend_kernel,
        "attend",
        (KEY_HEADS,),
        attention_specs(rows, count, 0),
        [
            pl.BlockSpec((GROUP * HEAD_DIM, rows), lambda h, info: (h, 0)),
            pl.BlockSpec((1, 8, rows), lambda h, info: (h, 0, 0)),
        ],
        [shaped((QUERY_HEADS * HEAD_DIM, rows), BF16), shaped((KEY_HEADS, 8, rows), F32)],
        [pltpu.VMEM((rows, HEAD_DIM), BF16), pltpu.VMEM((count, rows, HEAD_DIM), BF16)],
        flops=16 * QUERY_HEADS * HEAD_DIM * rows * rows,
        moved=4_000_000,
    )(info, qkv, qkv, qkv, past, past)


def mix_kernel(info, x, mixed, weight, gain, middle, normed):
    middle[...] = x[...].astype(F32) + dot(weight[0], mixed[...], 0, 0)
    values = middle[...]
    normed[...] = (values * scale_of(values) * gain[...]).astype(BF16)


def mix(info, x, mixed, square, gain):
    width, rows = x.shape
    operands = (x, mixed, square, gain)
    specs = [whole(item.shape) for item in operands]
    specs[2] = pl.BlockSpec((1, *square.shape[1:]), lambda t, info: (1, 0, 0))
    return call(
        mix_kernel,
        "mix",
        (1,),
        specs,
        [whole((width, rows)), whole((width, rows))],
        [shaped((width, rows), F32), shaped((width, rows), BF16)],
        flops=2 * width * width * rows,
        moved=8_000_000,
    )(info, *operands)


def expand_kernel(info, normed, gate_weight, up_weight, hidden, silu, slope, token_rows):
    @pl.when(pl.program_id(0) == 0)
    def _():
        token_rows[...] = normed[...].T

    tile = gate_weight.shape[1]
    for start, size in spans(tile, 256):
        part = slice(start, start + size)
        gate = dot(token_rows[...], gate_weight[:, part], 1, 0)
        up = dot(token_rows[...], up_weight[:, part], 1, 0)
        sigmoid = 0.5 * jnp.tanh(0.5 * gate) + 0.5
        active = gate * sigmoid
        hidden[:, part] = (active * up).astype(BF16)
        silu[:, part] = active.astype(BF16)
        slope[:, part] = (up * (sigmoid + active * (1.0 - sigmoid))).astype(BF16)


def expand(info, normed, gate, up):
    width, rows = normed.shape
    ff = gate.shape[1]
    tile = ff // 5
    weight = pl.BlockSpec((width, tile), lambda t, info: (0, t))
    result = pl.BlockSpec((rows, tile), lambda t, info: (0, t))
    return call(
        expand_kernel,
        "expand",
        (ff // tile,),
        [whole((width, rows)), weight, weight],
        [result] * 3,
        [shaped((rows, ff), BF16)] * 3,
        [pltpu.VMEM((rows, width), BF16)],
        flops=4 * width * ff * rows,
        moved=20_000_000,
    )(info, normed, gate, up)


def shrink_kernel(info, middle, hidden, weight, out):
    out[...] = (middle[...] + dot(weight[...], hidden[...], 1, 1)).astype(out.dtype)


def shrink(info, middle, hidden, down, dtype):
    width, rows = middle.shape
    ff = hidden.shape[1]
    tile = width // 2
    return call(
        shrink_kernel,
        "shrink",
        (width // tile,),
        [
            pl.BlockSpec((tile, rows), lambda t, info: (t, 0)),
            whole((rows, ff)),
            pl.BlockSpec((tile, ff), lambda t, info: (t, 0)),
        ],
        [pl.BlockSpec((tile, rows), lambda t, info: (t, 0))],
        [shaped((width, rows), dtype)],
        flops=2 * width * ff * rows,
        moved=11_000_000,
    )(info, middle, hidden, down)[0]


def ffn_back_kernel(
    info,
    grad,
    middle,
    gain,
    silu,
    slope,
    down,
    gate,
    up,
    square,
    gate_grad,
    up_grad,
    branch,
    grad_middle,
    attn_grad,
    mixed_grad,
    gain_grad,
    branch_rows,
    total,
):
    step = pl.program_id(0)
    steps = pl.num_programs(0)

    @pl.when(step == 0)
    def _():
        branch[...] = grad[...].astype(BF16)
        branch_rows[...] = branch[...].T
        total[...] = jnp.zeros_like(total)

    for start, size in spans(down.shape[1], 256):
        part = slice(start, start + size)
        incoming = dot(branch_rows[...], down[:, part], 1, 0)
        gate_grad[:, part] = (incoming * slope[:, part].astype(F32)).astype(BF16)
        up_grad[:, part] = (incoming * silu[:, part].astype(F32)).astype(BF16)
    total[...] += dot(gate[...], gate_grad[...], 1, 1) + dot(up[...], up_grad[...], 1, 1)

    @pl.when(step == steps - 1)
    def _():
        back, gain_sum = norm_back(middle[...], gain[...], total[...])
        gain_grad[...] = gain_sum
        result = grad[...].astype(F32) + back
        grad_middle[...] = result
        attn_grad[...] = result.astype(BF16)
        mixed_grad[...] = dot(square[0], attn_grad[...], 1, 0).astype(BF16)


def ffn_back(info, grad, middle, gain, silu, slope, down, gate, up, square):
    width, rows = middle.shape
    ff = silu.shape[1]
    tile = ff // 5
    heads = square.shape[1]
    token = pl.BlockSpec((rows, tile), lambda t, info: (0, t))
    weight = pl.BlockSpec((width, tile), lambda t, info: (0, t))
    return call(
        ffn_back_kernel,
        "ffn_back",
        (ff // tile,),
        [
            whole((width, rows)),
            whole((width, rows)),
            whole((width, 1)),
            token,
            token,
            weight,
            weight,
            weight,
            pl.BlockSpec((1, heads, width), lambda t, info: (1, 0, 0)),
        ],
        [
            token,
            token,
            whole((width, rows)),
            whole((width, rows)),
            whole((width, rows)),
            whole((heads, rows)),
            whole((width, 1)),
        ],
        [
            shaped((rows, ff), BF16),
            shaped((rows, ff), BF16),
            shaped((width, rows), BF16),
            shaped((width, rows), F32),
            shaped((width, rows), BF16),
            shaped((heads, rows), BF16),
            shaped((width, 1), F32),
        ],
        [pltpu.VMEM((rows, width), BF16), pltpu.VMEM((width, rows), F32)],
        flops=6 * width * ff * rows + 2 * width * width * rows,
        moved=32_000_000,
    )(info, grad, middle, gain, silu, slope, down, gate, up, square)


def attend_back_kernel(
    info,
    q,
    k_own,
    v_own,
    k_past,
    v_past,
    mixed_grad,
    mixed,
    lse,
    cosine,
    sine,
    q_grad,
    own_grad,
    past_grad,
    keys_own,
    values_own,
    keys_past,
    values_past,
):
    rows = q.shape[1]
    block = min(256, rows)
    hd = HEAD_DIM
    own_grad[...] = jnp.zeros_like(own_grad)
    past_grad[...] = jnp.zeros_like(past_grad)
    keys_own[...] = k_own[...].T
    values_own[...] = v_own[...].T

    @pl.loop(0, info[1])
    def _(device):
        keys_past[device] = k_past[device].T
        values_past[device] = v_past[device].T

    def step(state, tiles, keys, key_rows, value_rows, first_row):
        key_sum = value_sum = None
        fresh = []
        for group in range(GROUP):
            query, incoming, level, inner = tiles[group]
            scores = dot(key_rows, query, 1, 0)
            if first_row is not None:
                key_row = lax.broadcasted_iota(jnp.int32, scores.shape, 0)
                query_row = lax.broadcasted_iota(jnp.int32, scores.shape, 1) + first_row
                scores = jnp.where(key_row <= query_row, scores, -1e30)
            probs = jnp.exp(scores - level)
            slopes = dot(value_rows, incoming, 1, 0)
            low = (probs * (slopes - inner)).astype(BF16)
            value_part = dot(incoming, probs.astype(BF16), 1, 1)
            key_part = dot(query, low, 1, 1)
            key_sum = key_part if key_sum is None else key_sum + key_part
            value_sum = value_part if value_sum is None else value_sum + value_part
            query_part = dot(keys, low, 1, 0)
            fresh.append(query_part if state is None else state[group] + query_part)
        return tuple(fresh), key_sum, value_sum

    for start in range(0, rows, block):
        part = slice(start, start + block)
        tiles = []
        for group in range(GROUP):
            head = slice(group * hd, (group + 1) * hd)
            incoming = mixed_grad[head, part]
            inner = jnp.sum(
                incoming.astype(F32) * mixed[head, part].astype(F32), 0, keepdims=True
            )
            tiles.append((q[head, part], incoming, lse[0, group : group + 1, part], inner))
        seen = start + block
        state, key_sum, value_sum = step(
            None, tiles, k_own[:, :seen], keys_own[:seen, :], values_own[:seen, :], start
        )
        own_grad[0, :hd, :seen] += key_sum
        own_grad[0, hd:, :seen] += value_sum

        def past_step(device, held):
            held, key_sum, value_sum = step(
                held, tiles, k_past[device], keys_past[device], values_past[device], None
            )
            past_grad[device, 0, :hd, :] += key_sum
            past_grad[device, 0, hd:, :] += value_sum
            return held

        state = lax.fori_loop(0, info[1], past_step, state)
        cos, sin = cosine[:, part], -sine[:, part]
        for group in range(GROUP):
            first, second = rotate(state[group], cos, sin)
            at = group * hd
            q_grad[at : at + hd // 2, part] = (first * hd**-0.5).astype(BF16)
            q_grad[at + hd // 2 : at + hd, part] = (second * hd**-0.5).astype(BF16)


def attend_back(info, qkv, past, mixed_grad, mixed, lse, tables, base, heads):
    rows = qkv.shape[1]
    count = past.shape[0]
    hd = HEAD_DIM
    group = pl.BlockSpec((GROUP * hd, rows), lambda h, info: (base + h, 0))
    return call(
        attend_back_kernel,
        "attend_back",
        (heads,),
        attention_specs(rows, count, base)
        + [
            group,
            group,
            pl.BlockSpec((1, 8, rows), lambda h, info: (base + h, 0, 0)),
            whole(tables[0].shape),
            whole(tables[1].shape),
        ],
        [
            pl.BlockSpec((GROUP * hd, rows), lambda h, info: (h, 0)),
            pl.BlockSpec((1, 2 * hd, rows), lambda h, info: (h, 0, 0)),
            pl.BlockSpec((count, 1, 2 * hd, rows), lambda h, info: (0, h, 0, 0)),
        ],
        [
            shaped((heads * GROUP * hd, rows), BF16),
            shaped((heads, 2 * hd, rows), F32),
            shaped((count, heads, 2 * hd, rows), F32),
        ],
        [
            pltpu.VMEM((rows, hd), BF16),
            pltpu.VMEM((rows, hd), BF16),
            pltpu.VMEM((count, rows, hd), BF16),
            pltpu.VMEM((count, rows, hd), BF16),
        ],
        flops=40 * GROUP * heads * hd * rows * rows,
        moved=2_000_000 * heads,
    )(info, qkv, qkv, qkv, past, past, mixed_grad, mixed, lse, *tables)


def project_back_kernel(parts, info, x, gain, grad_middle, *refs):
    q_grads, own_grads, arrived = refs[:parts], refs[parts : 2 * parts], refs[2 * parts : 3 * parts]
    (
        square,
        k_own,
        k_oth,
        v_own,
        v_oth,
        cosine,
        sine,
        q_grad,
        kv_grad,
        out,
        gain_grad,
        total,
    ) = refs[3 * parts :]
    half = x.shape[0] // 2
    hd = HEAD_DIM
    kv = KEY_HEADS * hd
    cos, sin = cosine[...], -sine[...]
    head = 0
    for piece, own, far in zip(q_grads, own_grads, arrived):
        q_grad[head * GROUP * hd : head * GROUP * hd + piece.shape[0], :] = piece[...]
        for item in range(own.shape[0]):
            both = own[item] + far[item].astype(F32)
            first, second = rotate(both[:hd], cos, sin)
            at = head * hd
            kv_grad[at : at + hd // 2, :] = first.astype(BF16)
            kv_grad[at + hd // 2 : at + hd, :] = second.astype(BF16)
            kv_grad[kv + at : kv + at + hd, :] = both[hd:].astype(BF16)
            head += 1
    total[...] = dot(square[0], q_grad[...], 1, 0)
    for mine, k, v in ((info[0], k_own, v_own), (1 - info[0], k_oth, v_oth)):
        total[pl.ds(pl.multiple_of(mine * half, half), half), :] += dot(
            k[...], kv_grad[:kv, :], 0, 0
        ) + dot(v[...], kv_grad[kv:, :], 0, 0)
    back, gain_sum = norm_back(x[...].astype(F32), gain[...], total[...])
    gain_grad[...] = gain_sum
    out[...] = grad_middle[...] + back


def project_back(info, x, gain, grad_middle, q_grads, own_grads, arrived, weights, tables):
    width, rows = x.shape
    square, k, v = weights
    heads = square.shape[2]
    kv = 2 * KEY_HEADS * HEAD_DIM
    operands = (x, gain, grad_middle, *q_grads, *own_grads, *arrived, square, *k, *v, *tables)
    specs = [whole(item.shape) for item in operands]
    specs[3 + 3 * len(q_grads)] = pl.BlockSpec((1, width, heads), lambda t, info: (0, 0, 0))
    return call(
        functools.partial(project_back_kernel, len(q_grads)),
        "project_back",
        (1,),
        specs,
        [whole((heads, rows)), whole((kv, rows)), whole((width, rows)), whole((width, 1))],
        [
            shaped((heads, rows), BF16),
            shaped((kv, rows), BF16),
            shaped((width, rows), F32),
            shaped((width, 1), F32),
        ],
        [pltpu.VMEM((width, rows), F32)],
        flops=2 * width * (width + kv) * rows,
        moved=13_000_000,
    )(info, *operands)


def order_rows(info, target, sources):
    rows = sources[0].shape[1]
    size = target.shape[0] // 4
    at = 0
    for core in (1 - info[2], info[2]):
        for half in (1 - info[0], info[0]):
            start = pl.multiple_of((2 * half + core) * size, size)
            for index, source in enumerate(sources):
                target[at : at + size, index * rows : (index + 1) * rows] = source[
                    pl.ds(start, size), :
                ]
            at += size


def order_halves(info, target, sources):
    rows = sources[0].shape[1]
    size = target.shape[0] // 2
    for at, core in ((0, 1 - info[2]), (size, info[2])):
        start = pl.multiple_of(core * size, size)
        for index, source in enumerate(sources):
            target[at : at + size, index * rows : (index + 1) * rows] = source[pl.ds(start, size), :]


def outer_kernel(split_columns, info, left_a, right_a, left_b, right_b, sent, kept, left, right):
    rows = left_a.shape[1]

    @pl.when(pl.program_id(0) == 0)
    def _():
        order = order_halves if split_columns else order_rows
        order(info, left, (left_a, left_b))

    right[:rows, :] = right_a[...]
    right[rows:, :] = right_b[...]
    count, size = sent.shape[0], sent.shape[1]
    for at, out in ((0, sent), (count * size, kept)):
        product = dot(left[at : at + count * size, :], right[...], 1, 0).astype(BF16)
        for index in range(count):
            out[index] = product[index * size : (index + 1) * size]


def outer(info, parts, split_columns):
    left_a, right_a, left_b, right_b = parts
    width, rows = left_a.shape
    columns = right_a.shape[1]
    if split_columns:
        tile = columns // 4

        def column(t, info):
            return jnp.where(t < 2, (1 - info[0]) * 2 + t, info[0] * 2 + t - 2)

        right = pl.BlockSpec((rows, tile), lambda t, info: (0, column(t, info)))
        result = pl.BlockSpec((1, width // 2, tile), lambda t, info: (t // 2, 0, t % 2))
        shape = shaped((2, width // 2, columns // 2), BF16)
    else:
        tile = columns // 5
        right = pl.BlockSpec((rows, tile), lambda t, info: (0, t))
        result = pl.BlockSpec((2, width // 4, tile), lambda t, info: (0, 0, t))
        shape = shaped((2, width // 4, columns), BF16)
    return call(
        functools.partial(outer_kernel, split_columns),
        "outer",
        (columns // tile,),
        [whole((width, rows)), right, whole((width, rows)), right],
        [result, result],
        [shape, shape],
        [pltpu.VMEM((width, 2 * rows), BF16), pltpu.VMEM((2 * rows, tile), BF16)],
        flops=4 * width * columns * rows,
        moved=14_000_000,
    )(info, *parts)


def pack_kernel(info, left_a, *refs):
    sent, kept, left, right = refs[-4:]
    left_b, rights_a, rights_b = refs[0], refs[1:-4:2], refs[2:-4:2]
    rows = left_a.shape[1]
    order_rows(info, left, (left_a, left_b))
    at = 0
    for right_a, right_b in zip(rights_a, rights_b):
        right[at : at + right_a.shape[0], :rows] = right_a[...]
        right[at : at + right_a.shape[0], rows:] = right_b[...]
        at += right_a.shape[0]
    count, size = sent.shape[0], sent.shape[1]
    for base, out in ((0, sent), (count * size, kept)):
        for start, span in spans(right.shape[0], 512):
            product = dot(left[base : base + count * size, :], right[start : start + span, :], 1, 1)
            for index in range(count):
                out[index, :, start : start + span] = product[
                    index * size : (index + 1) * size
                ].astype(BF16)


def pack(info, left_a, left_b, rights):
    width, rows = left_a.shape
    columns = sum(item.shape[0] for item in rights[::2])
    operands = (left_a, left_b, *rights)
    shape = shaped((2, width // 4, columns), BF16)
    return call(
        pack_kernel,
        "pack",
        (1,),
        [whole(item.shape) for item in operands],
        [whole(shape.shape)] * 2,
        [shape, shape],
        [pltpu.VMEM((width, 2 * rows), BF16), pltpu.VMEM((columns, 2 * rows), BF16)],
        flops=4 * width * columns * rows,
        moved=14_000_000,
    )(info, *operands)


def swap(values, axis, bit):
    size = lax.axis_size(axis)
    return lax.ppermute(values, axis, [(i, i ^ bit) for i in range(size)])


def bits_of(axis):
    size = lax.axis_size(axis)
    assert size & (size - 1) == 0
    return [1 << i for i in range(size.bit_length() - 1)]


def high(axis, bit):
    return (lax.axis_index(axis) // bit) % 2


def halves(values, dim, which):
    half = values.shape[dim] // 2
    return lax.dynamic_slice_in_dim(values, which * half, half, dim)


def joined(mine, other, dim, which):
    return jnp.where(
        which == 0,
        jnp.concatenate([mine, other], dim),
        jnp.concatenate([other, mine], dim),
    )


def after(values, *others):
    return lax.optimization_barrier((values, *others))[0]


def shared(piece):
    first = swap(piece, "fsdp", 1)
    second = swap(first, "batch", 1)
    return first, second, swap(first, "seq", 1), swap(second, "seq", 1)


def place_kernel(split_columns, info, *refs):
    own, pieces, out, sems = refs[0], refs[1:5], refs[5], refs[6]
    mine, core, low_batch = info[0], info[2], info[3]
    rows, columns = pieces[0].shape
    if split_columns:
        full = own.shape[1]
        copies = [(own, out.at[:, pl.ds(pl.multiple_of(mine * full, full), full)])]
    else:
        full = own.shape[0]
        copies = [(own, out.at[pl.ds(pl.multiple_of(mine * full, full), full), :])]
    number = 0
    for other_core in (0, 1):
        for other_batch in (0, 1):
            at_core = core if other_core == 0 else 1 - core
            at_batch = low_batch if other_batch == 0 else 1 - low_batch
            if split_columns:
                row = (2 * at_batch + at_core) * rows
                column = (1 - mine) * columns
            else:
                row = (1 - mine) * full + at_batch * rows
                column = at_core * columns
            target = out.at[
                pl.ds(pl.multiple_of(row, rows), rows),
                pl.ds(pl.multiple_of(column, columns), columns),
            ]
            copies.append((pieces[number], target))
            number += 1
    running = [
        pltpu.make_async_copy(source, target, sems.at[index])
        for index, (source, target) in enumerate(copies)
    ]
    for copy in running:
        copy.start()
    for copy in running:
        copy.wait()


def place(info, own, pieces, split_columns):
    rows, columns = own.shape
    shape = (rows, 2 * columns) if split_columns else (2 * rows, columns)
    anywhere = pl.BlockSpec(memory_space=pl.ANY)
    return call(
        functools.partial(place_kernel, split_columns),
        "place",
        (1,),
        [anywhere] * 5,
        [anywhere],
        [shaped(shape, own.dtype)],
        [pltpu.SemaphoreType.DMA((5,))],
        moved=10_000_000,
    )(info, own, *pieces)[0]


def place_pair_kernel(info, *refs):
    own_a, own_b, pieces, out, sems = refs[0], refs[1], refs[2:6], refs[6], refs[7]
    mine, core, low_batch = info[0], info[2], info[3]
    full, rows = own_a.shape[0], pieces[0].shape[0]
    at_own = pl.ds(pl.multiple_of(mine * full, full), full)
    copies = [(own_a, out.at[0, at_own, :]), (own_b, out.at[1, at_own, :])]
    number = 0
    for at_core in (core, 1 - core):
        for at_batch in (low_batch, 1 - low_batch):
            row = (1 - mine) * full + at_batch * rows
            target = out.at[at_core, pl.ds(pl.multiple_of(row, rows), rows), :]
            copies.append((pieces[number], target))
            number += 1
    running = [
        pltpu.make_async_copy(source, target, sems.at[index])
        for index, (source, target) in enumerate(copies)
    ]
    for copy in running:
        copy.start()
    for copy in running:
        copy.wait()


def place_pair(info, own_a, own_b, pieces):
    rows, columns = own_a.shape
    anywhere = pl.BlockSpec(memory_space=pl.ANY)
    return call(
        place_pair_kernel,
        "place_pair",
        (1,),
        [anywhere] * 6,
        [anywhere],
        [shaped((2, 2 * rows, columns), own_a.dtype)],
        [pltpu.SemaphoreType.DMA((6,))],
        moved=8_000_000,
    )(info, own_a, own_b, *pieces)[0]


def split_dim(shape):
    if shape[0] % 16 == 0:
        return 0
    if shape[1] % 256 == 0:
        return 1
    return 0 if shape[0] % 2 == 0 else 1


def share_out(sent, kept, earlier):
    arrived = swap(after(sent, earlier), "fsdp", 1)
    held = kept.astype(F32) + arrived.astype(F32)
    stages = []
    for axis in ("seq", "batch"):
        for bit in bits_of(axis):
            if axis == "seq" and bit == 1:
                continue
            which = high(axis, bit)
            dim = split_dim(held.shape)
            low = held.astype(BF16)
            travelled = swap(halves(low, dim, 1 - which), axis, bit)
            held = halves(held, dim, which) + travelled.astype(F32)
            stages.append((axis, bit, dim, which))
    held = held.astype(BF16)
    stages.insert(0, ("seq", 1, 0, high("seq", 1)))
    for axis, bit, dim, which in reversed(stages):
        held = joined(held, swap(held, axis, bit), dim, which)
    return held.astype(F32), arrived


def per_device(
    tokens,
    attn_gain,
    w_query,
    key_weight,
    value_weight,
    w_out,
    ffn_gain,
    w_gate,
    w_up,
    w_down,
    cotangent,
):
    assert tokens.shape[0] == 1 and lax.axis_size("fsdp") == 2
    mine, spot, core = lax.axis_index("fsdp"), lax.axis_index("seq"), high("seq", 1)
    low_batch = high("batch", 1)
    devices = lax.axis_size("seq")
    info = jnp.stack([mine, spot, core, low_batch]).astype(jnp.int32)
    start_in = tokens[0].T
    incoming = cotangent[0].T
    width, rows = start_in.shape

    gains = jnp.stack([attn_gain, ffn_gain])
    gains = joined(gains, swap(gains, "fsdp", 1), 1, mine).astype(F32)[..., None]
    key_weight, value_weight, w_down = key_weight.T, value_weight.T, w_down.T
    piece = halves(jnp.where(core == 0, w_query, w_out), 0, low_batch)
    square_pieces = shared(piece)
    piece = halves(jnp.where(core == 0, key_weight, value_weight), 0, low_batch)
    kv_pieces = shared(piece)
    piece = halves(halves(w_gate, 0, low_batch), 1, core)
    gate_pieces = shared(after(piece, square_pieces[0], kv_pieces[0]))
    piece = halves(halves(w_up, 0, low_batch), 1, core)
    up_pieces = shared(after(piece, gate_pieces[0]))
    piece = halves(halves(w_down, 0, low_batch), 0, core)
    down_pieces = shared(after(piece, up_pieces[0]))

    square = place_pair(info, w_query, w_out, square_pieces)
    held = joined(kv_pieces[0], kv_pieces[1], 0, low_batch)
    other = joined(kv_pieces[2], kv_pieces[3], 0, low_batch)
    k_oth, v_oth = jnp.where(core == 0, held, other), jnp.where(core == 0, other, held)
    qkv_weights = (square, (key_weight, k_oth), (value_weight, v_oth))
    gate = place(info, w_gate, gate_pieces, False)
    up = place(info, w_up, up_pieces, False)
    down = place(info, w_down, down_pieces, True)

    positions = (spot * rows + jnp.arange(rows, dtype=jnp.int32)).astype(F32)
    frequency = jnp.exp(
        jnp.arange(HEAD_DIM // 2, dtype=F32) * (-2.0 * math.log(10000.0) / HEAD_DIM)
    )
    angles = frequency[:, None] * positions[None, :]
    tables = (jnp.cos(angles), jnp.sin(angles))

    def forward(x, dtype):
        normed, qkv = project(info, x, gains[0], qkv_weights, tables)
        kv = qkv[QUERY_HEADS * HEAD_DIM :]
        if devices == 2:
            past = swap(kv, "seq", 1)[None]
        else:
            past = lax.all_gather(kv, "seq")
        mixed, lse = attend(info, qkv, past)
        middle, normed_ffn = mix(info, x, mixed, square, gains[1])
        hidden, silu, slope = expand(info, normed_ffn, gate, up)
        result = shrink(info, middle, hidden, down, dtype)
        return result, (
            x, normed, qkv, past, mixed, lse, middle, normed_ffn, hidden, silu, slope
        )

    def backward_ffn(grad, saved):
        return ffn_back(
            info, grad, saved[6], gains[1], saved[9], saved[10], down, gate, up, square
        )

    def backward_attention(saved, grad_middle, mixed_grad):
        x, normed, qkv, past, mixed, lse = saved[:6]
        pieces, travelled = [], []
        for base, heads in ((0, 2), (2, 2), (4, 1)):
            pieces.append(
                attend_back(info, qkv, past, mixed_grad, mixed, lse, tables, base, heads)
            )
            past_grad = pieces[-1][2]
            if devices == 2:
                travelled.append(swap(past_grad[0].astype(BF16), "seq", 1))
            else:
                travelled.append(lax.psum_scatter(past_grad, "seq", scatter_dimension=0))
        return project_back(
            info,
            x,
            gains[0],
            grad_middle,
            [item[0] for item in pieces],
            [item[1] for item in pieces],
            travelled,
            qkv_weights,
            tables,
        )

    middle_in, saved_low = forward(start_in, F32)
    final_out, saved_high = forward(middle_in, BF16)
    high_gate, high_up, high_branch, grad_middle, high_attn, mixed_grad, high_ffn_gain = (
        backward_ffn(incoming, saved_high)
    )
    high_q, high_kv, grad_between, high_attn_gain = backward_attention(
        saved_high, grad_middle, mixed_grad
    )
    low_gate, low_up, low_branch, grad_middle, low_attn, mixed_grad, low_ffn_gain = (
        backward_ffn(grad_between, saved_low)
    )

    def with_core(pair):
        both = pair[1].astype(F32) + swap(pair[0], "seq", 1).astype(F32)
        return both[0].astype(BF16), both[1]

    down_terms = (high_branch, saved_high[8], low_branch, saved_low[8])
    down_sent, down_kept = with_core(outer(info, down_terms, True))
    gate_terms = (saved_high[7], high_gate, saved_low[7], low_gate)
    gate_sent, gate_kept = with_core(outer(info, gate_terms, False))
    up_terms = (saved_high[7], high_up, saved_low[7], low_up)
    up_sent, up_kept = with_core(outer(info, up_terms, False))
    out_sent, out_kept = with_core(
        pack(info, saved_high[4], saved_low[4], (high_attn, low_attn))
    )
    mixed_grad = after(mixed_grad, down_sent, gate_sent)
    low_q, low_kv, grad_start, low_attn_gain = backward_attention(
        saved_low, grad_middle, mixed_grad
    )
    qkv_sent, qkv_kept = with_core(
        pack(info, saved_high[1], saved_low[1], (high_q, low_q, high_kv, low_kv))
    )
    down_grad, earlier = share_out(down_sent, down_kept, info)
    gate_grad, earlier = share_out(gate_sent, gate_kept, earlier)
    up_grad, earlier = share_out(up_sent, up_kept, earlier)
    out_grad, earlier = share_out(out_sent, out_kept, earlier)
    qkv_grad, earlier = share_out(qkv_sent, qkv_kept, earlier)
    gain_grads = jnp.stack(
        [(high_attn_gain + low_attn_gain)[:, 0], (high_ffn_gain + low_ffn_gain)[:, 0]]
    )
    for axis in ("seq", "fsdp", "batch"):
        for bit in bits_of(axis):
            gain_grads = gain_grads + swap(gain_grads, axis, bit)
    gain_grads = halves(gain_grads, 1, mine)
    narrow = KEY_HEADS * HEAD_DIM
    query_part, key_part, value_part = jnp.split(qkv_grad, [width, width + narrow], 1)
    return (
        final_out.T[None],
        grad_start.T[None],
        gain_grads[0],
        query_part,
        key_part,
        value_part,
        out_grad,
        gain_grads[1],
        gate_grad,
        up_grad,
        down_grad.T,
    )


def solution(mesh):
    return jax.shard_map(
        per_device,
        mesh=mesh,
        in_specs=(
            P(("batch", "fsdp"), "seq", None),
            P("fsdp"),
            P("fsdp", None),
            P("fsdp", None),
            P("fsdp", None),
            P("fsdp", None),
            P("fsdp"),
            P("fsdp", None),
            P("fsdp", None),
            P("fsdp", None),
            P(("batch", "fsdp"), "seq", None),
        ),
        out_specs=(
            P(("batch", "fsdp"), "seq", None),
            P(("batch", "fsdp"), "seq", None),
            P("fsdp"),
            P("fsdp", None),
            P("fsdp", None),
            P("fsdp", None),
            P("fsdp", None),
            P("fsdp"),
            P("fsdp", None),
            P("fsdp", None),
            P("fsdp", None),
        ),
        check_vma=False,
    )
```

```python
import functools
import math

import jax
import jax.numpy as jnp
from jax import lax
from jax.experimental import pallas as pl
from jax.experimental.pallas import tpu as pltpu
from jax.sharding import PartitionSpec as P

QUERY_HEADS = 15
KEY_HEADS = 5
HEAD_DIM = 64
GROUP = QUERY_HEADS // KEY_HEADS
EPSILON = 1e-05
VMEM_BYTES = 56 * 1024 * 1024
F32 = jnp.float32
BF16 = jnp.bfloat16


def dot(left, right, left_dim, right_dim):
    return lax.dot_general(
        left, right, (((left_dim,), (right_dim,)), ((), ())), preferred_element_type=F32
    )


def spans(total, size):
    return [(start, min(size, total - start)) for start in range(0, total, size)]


def call(kernel, name, grid, in_specs, out_specs, out_shape, scratch=(), flops=0, moved=0):
    return pl.pallas_call(
        kernel,
        name=name,
        out_shape=out_shape,
        grid_spec=pltpu.PrefetchScalarGridSpec(
            num_scalar_prefetch=1,
            grid=grid,
            in_specs=in_specs,
            out_specs=out_specs,
            scratch_shapes=list(scratch),
        ),
        compiler_params=pltpu.CompilerParams(vmem_limit_bytes=VMEM_BYTES),
        cost_estimate=pl.CostEstimate(flops=flops, bytes_accessed=moved, transcendentals=0),
    )


def whole(shape):
    return pl.BlockSpec(shape, lambda *_: (0,) * len(shape))


def shaped(shape, dtype):
    return jax.ShapeDtypeStruct(shape, dtype)


def scale_of(values):
    return lax.rsqrt(jnp.mean(values * values, 0, keepdims=True) + EPSILON)


def norm_back(values, gain, incoming):
    scales = scale_of(values)
    weighted = gain * incoming
    inner = jnp.mean(values * weighted, 0, keepdims=True)
    grad = scales * weighted - values * (scales * scales * scales * inner)
    return grad, jnp.sum(incoming * values * scales, 1, keepdims=True)


def rotate(values, cosine, sine):
    half = HEAD_DIM // 2
    first, second = values[:half], values[half:]
    return first * cosine - second * sine, second * cosine + first * sine


def project_kernel(
    info, x, gain, q_weight, k_own, k_oth, v_own, v_oth, cosine, sine, normed, out
):
    width = x.shape[0]
    half = width // 2
    values = x[...].astype(F32)
    normed[...] = (values * scale_of(values) * gain[...]).astype(BF16)
    own = normed[pl.ds(pl.multiple_of(info[0] * half, half), half), :]
    oth = normed[pl.ds(pl.multiple_of((1 - info[0]) * half, half), half), :]
    cos, sin = cosine[...], sine[...]
    hd = HEAD_DIM

    def turned(rows, base, factor):
        for head in range(rows.shape[0] // hd):
            first, second = rotate(rows[head * hd : (head + 1) * hd], cos, sin)
            at = base + head * hd
            out[at : at + hd // 2, :] = (first * factor).astype(BF16)
            out[at + hd // 2 : at + hd, :] = (second * factor).astype(BF16)

    q_width = q_weight.shape[2]
    turned(dot(q_weight[0], normed[...], 0, 0), 0, hd**-0.5)
    kv = k_own.shape[0]
    turned(dot(k_own[...], own, 1, 0) + dot(k_oth[...], oth, 1, 0), q_width, 1.0)
    rows = dot(v_own[...], own, 1, 0) + dot(v_oth[...], oth, 1, 0)
    out[q_width + kv : q_width + 2 * kv, :] = rows.astype(BF16)


def project(info, x, gain, weights, tables):
    width, rows = x.shape
    square, k, v = weights
    total = square.shape[2] + 2 * k[0].shape[0]
    operands = (x, gain, square, *k, *v, *tables)
    specs = [whole(item.shape) for item in operands]
    specs[2] = pl.BlockSpec((1, *square.shape[1:]), lambda t, info: (0, 0, 0))
    return call(
        project_kernel,
        "project",
        (1,),
        specs,
        [whole((width, rows)), whole((total, rows))],
        [shaped((width, rows), BF16), shaped((total, rows), BF16)],
        flops=2 * width * total * rows,
        moved=8_000_000,
    )(info, *operands)


def attend_kernel(info, q, k_own, v_own, k_past, v_past, out, lse, keys_own, keys_past):
    rows = q.shape[1]
    block = min(256, rows)
    hd = HEAD_DIM
    groups = range(GROUP)
    keys_own[...] = k_own[...].T

    @pl.loop(0, info[1])
    def _(device):
        keys_past[device] = k_past[device].T

    def scores_of(keys, query, first_row):
        scores = dot(keys, query, 1, 0)
        if first_row is None:
            return scores
        key_row = lax.broadcasted_iota(jnp.int32, scores.shape, 0)
        query_row = lax.broadcasted_iota(jnp.int32, scores.shape, 1) + first_row
        return jnp.where(key_row <= query_row, scores, -1e30)

    for start in range(0, rows, block):
        part = slice(start, start + block)
        seen = start + block
        queries = [q[group * hd : (group + 1) * hd, part] for group in groups]

        def peaks(keys, first_row):
            return [
                jnp.max(scores_of(keys, query, first_row), 0, keepdims=True) for query in queries
            ]

        def past_peaks(device, held):
            fresh = peaks(keys_past[device], None)
            return tuple(jnp.maximum(old, new) for old, new in zip(held, fresh))

        peak = lax.fori_loop(0, info[1], past_peaks, tuple(peaks(keys_own[:seen, :], start)))

        def sums(keys, values, first_row):
            result = []
            for group in groups:
                exponent = jnp.exp(scores_of(keys, queries[group], first_row) - peak[group])
                total = jnp.sum(exponent, 0, keepdims=True)
                result.append((total, dot(values, exponent.astype(BF16), 1, 0)))
            return tuple(result)

        def past_sums(device, held):
            fresh = sums(keys_past[device], v_past[device], None)
            return tuple(
                (old[0] + new[0], old[1] + new[1]) for old, new in zip(held, fresh)
            )

        state = lax.fori_loop(
            0, info[1], past_sums, sums(keys_own[:seen, :], v_own[:, :seen], start)
        )
        for group in groups:
            total, mixed = state[group]
            out[group * hd : (group + 1) * hd, part] = (mixed / total).astype(BF16)
            lse[0, group : group + 1, part] = peak[group] + jnp.log(total)


def attention_specs(rows, past, base):
    hd = HEAD_DIM
    return [
        pl.BlockSpec((GROUP * hd, rows), lambda h, info: (base + h, 0)),
        pl.BlockSpec((hd, rows), lambda h, info: (QUERY_HEADS + base + h, 0)),
        pl.BlockSpec((hd, rows), lambda h, info: (QUERY_HEADS + KEY_HEADS + base + h, 0)),
        pl.BlockSpec((past, hd, rows), lambda h, info: (0, base + h, 0)),
        pl.BlockSpec((past, hd, rows), lambda h, info: (0, KEY_HEADS + base + h, 0)),
    ]


def attend(info, qkv, past):
    rows = qkv.shape[1]
    count = past.shape[0]
    return call(
        attend_kernel,
        "attend",
        (KEY_HEADS,),
        attention_specs(rows, count, 0),
        [
            pl.BlockSpec((GROUP * HEAD_DIM, rows), lambda h, info: (h, 0)),
            pl.BlockSpec((1, 8, rows), lambda h, info: (h, 0, 0)),
        ],
        [shaped((QUERY_HEADS * HEAD_DIM, rows), BF16), shaped((KEY_HEADS, 8, rows), F32)],
        [pltpu.VMEM((rows, HEAD_DIM), BF16), pltpu.VMEM((count, rows, HEAD_DIM), BF16)],
        flops=16 * QUERY_HEADS * HEAD_DIM * rows * rows,
        moved=4_000_000,
    )(info, qkv, qkv, qkv, past, past)


def mix_kernel(info, x, mixed, weight, gain, middle, normed):
    middle[...] = x[...].astype(F32) + dot(weight[0], mixed[...], 0, 0)
    values = middle[...]
    normed[...] = (values * scale_of(values) * gain[...]).astype(BF16)


def mix(info, x, mixed, square, gain):
    width, rows = x.shape
    operands = (x, mixed, square, gain)
    specs = [whole(item.shape) for item in operands]
    specs[2] = pl.BlockSpec((1, *square.shape[1:]), lambda t, info: (1, 0, 0))
    return call(
        mix_kernel,
        "mix",
        (1,),
        specs,
        [whole((width, rows)), whole((width, rows))],
        [shaped((width, rows), F32), shaped((width, rows), BF16)],
        flops=2 * width * width * rows,
        moved=8_000_000,
    )(info, *operands)


def expand_kernel(info, normed, gate_weight, up_weight, hidden, silu, slope, token_rows):
    @pl.when(pl.program_id(0) == 0)
    def _():
        token_rows[...] = normed[...].T

    tile = gate_weight.shape[1]
    for start, size in spans(tile, 256):
        part = slice(start, start + size)
        gate = dot(token_rows[...], gate_weight[:, part], 1, 0)
        up = dot(token_rows[...], up_weight[:, part], 1, 0)
        sigmoid = 0.5 * jnp.tanh(0.5 * gate) + 0.5
        active = gate * sigmoid
        hidden[:, part] = (active * up).astype(BF16)
        silu[:, part] = active.astype(BF16)
        slope[:, part] = (up * (sigmoid + active * (1.0 - sigmoid))).astype(BF16)


def expand(info, normed, gate, up):
    width, rows = normed.shape
    ff = gate.shape[1]
    tile = ff // 5
    weight = pl.BlockSpec((width, tile), lambda t, info: (0, t))
    result = pl.BlockSpec((rows, tile), lambda t, info: (0, t))
    return call(
        expand_kernel,
        "expand",
        (ff // tile,),
        [whole((width, rows)), weight, weight],
        [result] * 3,
        [shaped((rows, ff), BF16)] * 3,
        [pltpu.VMEM((rows, width), BF16)],
        flops=4 * width * ff * rows,
        moved=20_000_000,
    )(info, normed, gate, up)


def shrink_kernel(info, middle, hidden, weight, out):
    out[...] = (middle[...] + dot(weight[...], hidden[...], 1, 1)).astype(out.dtype)


def shrink(info, middle, hidden, down, dtype):
    width, rows = middle.shape
    ff = hidden.shape[1]
    tile = width // 2
    return call(
        shrink_kernel,
        "shrink",
        (width // tile,),
        [
            pl.BlockSpec((tile, rows), lambda t, info: (t, 0)),
            whole((rows, ff)),
            pl.BlockSpec((tile, ff), lambda t, info: (t, 0)),
        ],
        [pl.BlockSpec((tile, rows), lambda t, info: (t, 0))],
        [shaped((width, rows), dtype)],
        flops=2 * width * ff * rows,
        moved=11_000_000,
    )(info, middle, hidden, down)[0]


def ffn_back_kernel(
    info,
    grad,
    middle,
    gain,
    silu,
    slope,
    down,
    gate,
    up,
    square,
    gate_grad,
    up_grad,
    branch,
    grad_middle,
    attn_grad,
    mixed_grad,
    gain_grad,
    branch_rows,
    total,
):
    step = pl.program_id(0)
    steps = pl.num_programs(0)

    @pl.when(step == 0)
    def _():
        branch[...] = grad[...].astype(BF16)
        branch_rows[...] = branch[...].T
        total[...] = jnp.zeros_like(total)

    for start, size in spans(down.shape[1], 256):
        part = slice(start, start + size)
        incoming = dot(branch_rows[...], down[:, part], 1, 0)
        gate_grad[:, part] = (incoming * slope[:, part].astype(F32)).astype(BF16)
        up_grad[:, part] = (incoming * silu[:, part].astype(F32)).astype(BF16)
    total[...] += dot(gate[...], gate_grad[...], 1, 1) + dot(up[...], up_grad[...], 1, 1)

    @pl.when(step == steps - 1)
    def _():
        back, gain_sum = norm_back(middle[...], gain[...], total[...])
        gain_grad[...] = gain_sum
        result = grad[...].astype(F32) + back
        grad_middle[...] = result
        attn_grad[...] = result.astype(BF16)
        mixed_grad[...] = dot(square[0], attn_grad[...], 1, 0).astype(BF16)


def ffn_back(info, grad, middle, gain, silu, slope, down, gate, up, square):
    width, rows = middle.shape
    ff = silu.shape[1]
    tile = ff // 5
    heads = square.shape[1]
    token = pl.BlockSpec((rows, tile), lambda t, info: (0, t))
    weight = pl.BlockSpec((width, tile), lambda t, info: (0, t))
    return call(
        ffn_back_kernel,
        "ffn_back",
        (ff // tile,),
        [
            whole((width, rows)),
            whole((width, rows)),
            whole((width, 1)),
            token,
            token,
            weight,
            weight,
            weight,
            pl.BlockSpec((1, heads, width), lambda t, info: (1, 0, 0)),
        ],
        [
            token,
            token,
            whole((width, rows)),
            whole((width, rows)),
            whole((width, rows)),
            whole((heads, rows)),
            whole((width, 1)),
        ],
        [
            shaped((rows, ff), BF16),
            shaped((rows, ff), BF16),
            shaped((width, rows), BF16),
            shaped((width, rows), F32),
            shaped((width, rows), BF16),
            shaped((heads, rows), BF16),
            shaped((width, 1), F32),
        ],
        [pltpu.VMEM((rows, width), BF16), pltpu.VMEM((width, rows), F32)],
        flops=6 * width * ff * rows + 2 * width * width * rows,
        moved=32_000_000,
    )(info, grad, middle, gain, silu, slope, down, gate, up, square)


def attend_back_kernel(
    info,
    q,
    k_own,
    v_own,
    k_past,
    v_past,
    mixed_grad,
    mixed,
    lse,
    cosine,
    sine,
    q_grad,
    own_grad,
    past_grad,
    keys_own,
    values_own,
    keys_past,
    values_past,
):
    rows = q.shape[1]
    block = min(256, rows)
    hd = HEAD_DIM
    own_grad[...] = jnp.zeros_like(own_grad)
    past_grad[...] = jnp.zeros_like(past_grad)
    keys_own[...] = k_own[...].T
    values_own[...] = v_own[...].T

    @pl.loop(0, info[1])
    def _(device):
        keys_past[device] = k_past[device].T
        values_past[device] = v_past[device].T

    def step(state, tiles, keys, key_rows, value_rows, first_row):
        key_sum = value_sum = None
        fresh = []
        for group in range(GROUP):
            query, incoming, level, inner = tiles[group]
            scores = dot(key_rows, query, 1, 0)
            if first_row is not None:
                key_row = lax.broadcasted_iota(jnp.int32, scores.shape, 0)
                query_row = lax.broadcasted_iota(jnp.int32, scores.shape, 1) + first_row
                scores = jnp.where(key_row <= query_row, scores, -1e30)
            probs = jnp.exp(scores - level)
            slopes = dot(value_rows, incoming, 1, 0)
            low = (probs * (slopes - inner)).astype(BF16)
            value_part = dot(incoming, probs.astype(BF16), 1, 1)
            key_part = dot(query, low, 1, 1)
            key_sum = key_part if key_sum is None else key_sum + key_part
            value_sum = value_part if value_sum is None else value_sum + value_part
            query_part = dot(keys, low, 1, 0)
            fresh.append(query_part if state is None else state[group] + query_part)
        return tuple(fresh), key_sum, value_sum

    for start in range(0, rows, block):
        part = slice(start, start + block)
        tiles = []
        for group in range(GROUP):
            head = slice(group * hd, (group + 1) * hd)
            incoming = mixed_grad[head, part]
            inner = jnp.sum(
                incoming.astype(F32) * mixed[head, part].astype(F32), 0, keepdims=True
            )
            tiles.append((q[head, part], incoming, lse[0, group : group + 1, part], inner))
        seen = start + block
        state, key_sum, value_sum = step(
            None, tiles, k_own[:, :seen], keys_own[:seen, :], values_own[:seen, :], start
        )
        own_grad[0, :hd, :seen] += key_sum
        own_grad[0, hd:, :seen] += value_sum

        def past_step(device, held):
            held, key_sum, value_sum = step(
                held, tiles, k_past[device], keys_past[device], values_past[device], None
            )
            past_grad[device, 0, :hd, :] += key_sum
            past_grad[device, 0, hd:, :] += value_sum
            return held

        state = lax.fori_loop(0, info[1], past_step, state)
        cos, sin = cosine[:, part], -sine[:, part]
        for group in range(GROUP):
            first, second = rotate(state[group], cos, sin)
            at = group * hd
            q_grad[at : at + hd // 2, part] = (first * hd**-0.5).astype(BF16)
            q_grad[at + hd // 2 : at + hd, part] = (second * hd**-0.5).astype(BF16)


def attend_back(info, qkv, past, mixed_grad, mixed, lse, tables, base, heads):
    rows = qkv.shape[1]
    count = past.shape[0]
    hd = HEAD_DIM
    group = pl.BlockSpec((GROUP * hd, rows), lambda h, info: (base + h, 0))
    return call(
        attend_back_kernel,
        "attend_back",
        (heads,),
        attention_specs(rows, count, base)
        + [
            group,
            group,
            pl.BlockSpec((1, 8, rows), lambda h, info: (base + h, 0, 0)),
            whole(tables[0].shape),
            whole(tables[1].shape),
        ],
        [
            pl.BlockSpec((GROUP * hd, rows), lambda h, info: (h, 0)),
            pl.BlockSpec((1, 2 * hd, rows), lambda h, info: (h, 0, 0)),
            pl.BlockSpec((count, 1, 2 * hd, rows), lambda h, info: (0, h, 0, 0)),
        ],
        [
            shaped((heads * GROUP * hd, rows), BF16),
            shaped((heads, 2 * hd, rows), F32),
            shaped((count, heads, 2 * hd, rows), F32),
        ],
        [
            pltpu.VMEM((rows, hd), BF16),
            pltpu.VMEM((rows, hd), BF16),
            pltpu.VMEM((count, rows, hd), BF16),
            pltpu.VMEM((count, rows, hd), BF16),
        ],
        flops=40 * GROUP * heads * hd * rows * rows,
        moved=2_000_000 * heads,
    )(info, qkv, qkv, qkv, past, past, mixed_grad, mixed, lse, *tables)


def project_back_kernel(parts, info, x, gain, grad_middle, *refs):
    q_grads, own_grads, arrived = refs[:parts], refs[parts : 2 * parts], refs[2 * parts : 3 * parts]
    (
        square,
        k_own,
        k_oth,
        v_own,
        v_oth,
        cosine,
        sine,
        q_grad,
        kv_grad,
        out,
        gain_grad,
        total,
    ) = refs[3 * parts :]
    half = x.shape[0] // 2
    hd = HEAD_DIM
    kv = KEY_HEADS * hd
    cos, sin = cosine[...], -sine[...]
    head = 0
    for piece, own, far in zip(q_grads, own_grads, arrived):
        q_grad[head * GROUP * hd : head * GROUP * hd + piece.shape[0], :] = piece[...]
        for item in range(own.shape[0]):
            both = own[item] + far[item].astype(F32)
            first, second = rotate(both[:hd], cos, sin)
            at = head * hd
            kv_grad[at : at + hd // 2, :] = first.astype(BF16)
            kv_grad[at + hd // 2 : at + hd, :] = second.astype(BF16)
            kv_grad[kv + at : kv + at + hd, :] = both[hd:].astype(BF16)
            head += 1
    total[...] = dot(square[0], q_grad[...], 1, 0)
    for mine, k, v in ((info[0], k_own, v_own), (1 - info[0], k_oth, v_oth)):
        total[pl.ds(pl.multiple_of(mine * half, half), half), :] += dot(
            k[...], kv_grad[:kv, :], 0, 0
        ) + dot(v[...], kv_grad[kv:, :], 0, 0)
    back, gain_sum = norm_back(x[...].astype(F32), gain[...], total[...])
    gain_grad[...] = gain_sum
    out[...] = grad_middle[...] + back


def project_back(info, x, gain, grad_middle, q_grads, own_grads, arrived, weights, tables):
    width, rows = x.shape
    square, k, v = weights
    heads = square.shape[2]
    kv = 2 * KEY_HEADS * HEAD_DIM
    operands = (x, gain, grad_middle, *q_grads, *own_grads, *arrived, square, *k, *v, *tables)
    specs = [whole(item.shape) for item in operands]
    specs[3 + 3 * len(q_grads)] = pl.BlockSpec((1, width, heads), lambda t, info: (0, 0, 0))
    return call(
        functools.partial(project_back_kernel, len(q_grads)),
        "project_back",
        (1,),
        specs,
        [whole((heads, rows)), whole((kv, rows)), whole((width, rows)), whole((width, 1))],
        [
            shaped((heads, rows), BF16),
            shaped((kv, rows), BF16),
            shaped((width, rows), F32),
            shaped((width, 1), F32),
        ],
        [pltpu.VMEM((width, rows), F32)],
        flops=2 * width * (width + kv) * rows,
        moved=13_000_000,
    )(info, *operands)


def order_rows(info, target, sources):
    rows = sources[0].shape[1]
    size = target.shape[0] // 4
    at = 0
    for core in (1 - info[2], info[2]):
        for half in (1 - info[0], info[0]):
            start = pl.multiple_of((2 * half + core) * size, size)
            for index, source in enumerate(sources):
                target[at : at + size, index * rows : (index + 1) * rows] = source[
                    pl.ds(start, size), :
                ]
            at += size


def order_halves(info, target, sources):
    rows = sources[0].shape[1]
    size = target.shape[0] // 2
    for at, core in ((0, 1 - info[2]), (size, info[2])):
        start = pl.multiple_of(core * size, size)
        for index, source in enumerate(sources):
            target[at : at + size, index * rows : (index + 1) * rows] = source[pl.ds(start, size), :]


def outer_kernel(split_columns, info, left_a, right_a, left_b, right_b, sent, kept, left, right):
    rows = left_a.shape[1]

    @pl.when(pl.program_id(0) == 0)
    def _():
        order = order_halves if split_columns else order_rows
        order(info, left, (left_a, left_b))

    right[:rows, :] = right_a[...]
    right[rows:, :] = right_b[...]
    count, size = sent.shape[0], sent.shape[1]
    for at, out in ((0, sent), (count * size, kept)):
        product = dot(left[at : at + count * size, :], right[...], 1, 0).astype(BF16)
        for index in range(count):
            out[index] = product[index * size : (index + 1) * size]


def outer(info, parts, split_columns):
    left_a, right_a, left_b, right_b = parts
    width, rows = left_a.shape
    columns = right_a.shape[1]
    if split_columns:
        tile = columns // 4

        def column(t, info):
            return jnp.where(t < 2, (1 - info[0]) * 2 + t, info[0] * 2 + t - 2)

        right = pl.BlockSpec((rows, tile), lambda t, info: (0, column(t, info)))
        result = pl.BlockSpec((1, width // 2, tile), lambda t, info: (t // 2, 0, t % 2))
        shape = shaped((2, width // 2, columns // 2), BF16)
    else:
        tile = columns // 5
        right = pl.BlockSpec((rows, tile), lambda t, info: (0, t))
        result = pl.BlockSpec((2, width // 4, tile), lambda t, info: (0, 0, t))
        shape = shaped((2, width // 4, columns), BF16)
    return call(
        functools.partial(outer_kernel, split_columns),
        "outer",
        (columns // tile,),
        [whole((width, rows)), right, whole((width, rows)), right],
        [result, result],
        [shape, shape],
        [pltpu.VMEM((width, 2 * rows), BF16), pltpu.VMEM((2 * rows, tile), BF16)],
        flops=4 * width * columns * rows,
        moved=14_000_000,
    )(info, *parts)


def pack_kernel(info, left_a, *refs):
    sent, kept, left, right = refs[-4:]
    left_b, rights_a, rights_b = refs[0], refs[1:-4:2], refs[2:-4:2]
    rows = left_a.shape[1]
    order_rows(info, left, (left_a, left_b))
    at = 0
    for right_a, right_b in zip(rights_a, rights_b):
        right[at : at + right_a.shape[0], :rows] = right_a[...]
        right[at : at + right_a.shape[0], rows:] = right_b[...]
        at += right_a.shape[0]
    count, size = sent.shape[0], sent.shape[1]
    for base, out in ((0, sent), (count * size, kept)):
        for start, span in spans(right.shape[0], 512):
            product = dot(left[base : base + count * size, :], right[start : start + span, :], 1, 1)
            for index in range(count):
                out[index, :, start : start + span] = product[
                    index * size : (index + 1) * size
                ].astype(BF16)


def pack(info, left_a, left_b, rights):
    width, rows = left_a.shape
    columns = sum(item.shape[0] for item in rights[::2])
    operands = (left_a, left_b, *rights)
    shape = shaped((2, width // 4, columns), BF16)
    return call(
        pack_kernel,
        "pack",
        (1,),
        [whole(item.shape) for item in operands],
        [whole(shape.shape)] * 2,
        [shape, shape],
        [pltpu.VMEM((width, 2 * rows), BF16), pltpu.VMEM((columns, 2 * rows), BF16)],
        flops=4 * width * columns * rows,
        moved=14_000_000,
    )(info, *operands)


def swap(values, axis, bit):
    size = lax.axis_size(axis)
    return lax.ppermute(values, axis, [(i, i ^ bit) for i in range(size)])


def bits_of(axis):
    size = lax.axis_size(axis)
    assert size & (size - 1) == 0
    return [1 << i for i in range(size.bit_length() - 1)]


def high(axis, bit):
    return (lax.axis_index(axis) // bit) % 2


def halves(values, dim, which):
    half = values.shape[dim] // 2
    return lax.dynamic_slice_in_dim(values, which * half, half, dim)


def joined(mine, other, dim, which):
    return jnp.where(
        which == 0,
        jnp.concatenate([mine, other], dim),
        jnp.concatenate([other, mine], dim),
    )


def tied(values, others):
    return lax.optimization_barrier((values, others))[0]


def place_kernel(owned, info, *refs):
    pieces, out = refs[owned : owned + 4], refs[-1]
    step = pl.program_id(0)
    per = 4 // owned
    for index in range(owned):

        @pl.when((step >= index * per) & (step < (index + 1) * per))
        def _():
            out[...] = refs[index][...].reshape(out.shape)

    for index in range(4):

        @pl.when(step == 4 + index)
        def _():
            out[...] = pieces[index][...].reshape(out.shape)


def place(info, own, pieces, kind):
    piece = pl.BlockSpec(pieces[0].shape, lambda t, info: (0, 0))
    block = pieces[0].shape
    rows, columns = own[0].shape

    def where_piece(t, info):
        number = jnp.maximum(t - 4, 0)
        batch = jnp.where(number % 2 == 0, info[3], 1 - info[3])
        core = jnp.where(number < 2, info[2], 1 - info[2])
        return batch, core

    if kind == "rows":
        shape, spec = (2 * rows, columns), block
        own_maps = [lambda t, info: (jnp.minimum(t, 3) // 2, jnp.minimum(t, 3) % 2)]

        def out_map(t, info):
            batch, core = where_piece(t, info)
            return (
                jnp.where(t < 4, info[0] * 2 + t // 2, (1 - info[0]) * 2 + batch),
                jnp.where(t < 4, t % 2, core),
            )
    elif kind == "columns":
        shape, spec = (rows, 2 * columns), block
        own_maps = [lambda t, info: (jnp.minimum(t, 3), 0)]

        def out_map(t, info):
            batch, core = where_piece(t, info)
            return (
                jnp.where(t < 4, t, 2 * batch + core),
                jnp.where(t < 4, info[0], 1 - info[0]),
            )
    else:
        shape, spec = (2, 2 * rows, columns), (1, *block)
        own_maps = [
            lambda t, info: (jnp.minimum(t, 1), 0),
            lambda t, info: (jnp.clip(t - 2, 0, 1), 0),
        ]

        def out_map(t, info):
            batch, core = where_piece(t, info)
            return (
                jnp.where(t < 4, t // 2, core),
                jnp.where(t < 4, info[0] * 2 + t % 2, (1 - info[0]) * 2 + batch),
                0,
            )

    return call(
        functools.partial(place_kernel, len(own)),
        "place",
        (8,),
        [pl.BlockSpec(block, item) for item in own_maps] + [piece] * 4,
        [pl.BlockSpec(spec, out_map)],
        [shaped(shape, own[0].dtype)],
        moved=10_000_000,
    )(info, *own, *pieces)[0]


def split_dim(shape):
    if shape[0] % 16 == 0:
        return 0
    if shape[1] % 256 == 0:
        return 1
    return 0 if shape[0] % 2 == 0 else 1


def over_fsdp(values):
    return swap(values, "fsdp", 1)


class Chain:
    def __init__(self, sent, kept):
        self.sent, self.held, self.stages = sent, kept, []
        self.todo = [("fsdp", 1)]
        self.todo += [("seq", bit) for bit in bits_of("seq")[1:]]
        self.todo += [("batch", bit) for bit in bits_of("batch")]
        self.back = None

    def step(self, wait=()):
        if self.todo:
            axis, bit = self.todo.pop(0)
            if axis == "fsdp":
                arrived = swap(tied(self.sent, wait), axis, bit)
                self.held = self.held.astype(F32) + arrived.astype(F32)
                return arrived
            which = high(axis, bit)
            dim = split_dim(self.held.shape)
            low = self.held.astype(BF16)
            arrived = swap(tied(halves(low, dim, 1 - which), wait), axis, bit)
            self.held = halves(self.held, dim, which) + arrived.astype(F32)
            self.stages.append((axis, bit, dim, which))
            return arrived
        if self.back is None:
            self.held = self.held.astype(BF16)
            self.back = [("seq", 1, 0, high("seq", 1))] + self.stages
        axis, bit, dim, which = self.back.pop()
        arrived = swap(tied(self.held, wait), axis, bit)
        self.held = joined(self.held, arrived, dim, which)
        return arrived

    def finish(self):
        while self.back is None or self.back:
            self.step()
        return self.held.astype(F32)


def per_device(
    tokens,
    attn_gain,
    w_query,
    key_weight,
    value_weight,
    w_out,
    ffn_gain,
    w_gate,
    w_up,
    w_down,
    cotangent,
):
    assert tokens.shape[0] == 1 and lax.axis_size("fsdp") == 2
    mine, spot, core = lax.axis_index("fsdp"), lax.axis_index("seq"), high("seq", 1)
    low_batch = high("batch", 1)
    devices = lax.axis_size("seq")
    info = jnp.stack([mine, spot, core, low_batch]).astype(jnp.int32)
    start_in = tokens[0].T
    incoming = cotangent[0].T
    width, rows = start_in.shape

    gains = jnp.stack([attn_gain, ffn_gain])
    gains = joined(gains, swap(gains, "fsdp", 1), 1, mine).astype(F32)[..., None]
    key_weight, value_weight, w_down = key_weight.T, value_weight.T, w_down.T
    def fsdp(values):
        return swap(values, "fsdp", 1)

    def pair(values):
        return swap(values, "batch", 1)

    def cores(values):
        return swap(values, "seq", 1)

    square_piece = halves(jnp.where(core == 0, w_query, w_out), 0, low_batch)
    kv_piece = halves(jnp.where(core == 0, key_weight, value_weight), 0, low_batch)
    square_0, kv_0 = fsdp(square_piece), fsdp(kv_piece)
    gate_piece = tied(halves(halves(w_gate, 0, low_batch), 1, core), (square_0, kv_0))
    gate_0, square_1, kv_1 = fsdp(gate_piece), pair(square_0), pair(kv_0)
    square_2, kv_2 = cores(square_0), cores(kv_0)
    done = (gate_0, square_1, kv_1, square_2, kv_2)
    up_piece, gate_0, square_1, kv_1 = tied(
        (halves(halves(w_up, 0, low_batch), 1, core), gate_0, square_1, kv_1), done
    )
    square_3, kv_3 = cores(square_1), cores(kv_1)
    up_0, gate_1, gate_2 = fsdp(up_piece), pair(gate_0), cores(gate_0)
    second_round = (up_0, gate_1, gate_2)

    square = place(info, (w_query, w_out), (square_0, square_1, square_2, square_3), "pair")
    held = joined(kv_0, kv_1, 0, low_batch)
    other = joined(kv_2, kv_3, 0, low_batch)
    k_oth, v_oth = jnp.where(core == 0, held, other), jnp.where(core == 0, other, held)
    qkv_weights = (square, (key_weight, k_oth), (value_weight, v_oth))

    positions = (spot * rows + jnp.arange(rows, dtype=jnp.int32)).astype(F32)
    frequency = jnp.exp(
        jnp.arange(HEAD_DIM // 2, dtype=F32) * (-2.0 * math.log(10000.0) / HEAD_DIM)
    )
    angles = frequency[:, None] * positions[None, :]
    tables = (jnp.cos(angles), jnp.sin(angles))

    def to_attention(x):
        normed, qkv = project(info, x, gains[0], qkv_weights, tables)
        kv = qkv[QUERY_HEADS * HEAD_DIM :]
        if devices == 2:
            past = cores(kv)[None]
        else:
            past = lax.all_gather(kv, "seq")
        return normed, qkv, past

    low_normed, low_qkv, low_past = to_attention(start_in)
    low_past, up_0, gate_1, gate_2 = tied((low_past, up_0, gate_1, gate_2), second_round)
    down_piece = tied(halves(halves(w_down, 0, low_batch), 0, core), second_round)
    down_0, up_1, gate_3, up_2 = fsdp(down_piece), pair(up_0), cores(gate_1), cores(up_0)
    third_round = (down_0, up_1, gate_3, up_2)
    low_mixed, low_lse = attend(info, low_qkv, low_past)
    low_mixed, down_0, up_1 = tied((low_mixed, down_0, up_1), third_round)
    down_1, up_3, down_2 = pair(down_0), cores(up_1), cores(down_0)
    low_middle, low_normed_ffn = mix(info, start_in, low_mixed, square, gains[1])
    gate = place(info, (w_gate,), (gate_0, gate_1, gate_2, gate_3), "rows")
    up = place(info, (w_up,), (up_0, up_1, up_2, up_3), "rows")
    low_hidden, low_silu, low_slope = expand(info, low_normed_ffn, gate, up)
    down_3 = cores(down_1)
    down = place(info, (w_down,), (down_0, down_1, down_2, down_3), "columns")
    middle_in = shrink(info, low_middle, low_hidden, down, F32)

    high_normed, high_qkv, high_past = to_attention(middle_in)
    high_mixed, high_lse = attend(info, high_qkv, high_past)
    high_middle, high_normed_ffn = mix(info, middle_in, high_mixed, square, gains[1])
    high_hidden, high_silu, high_slope = expand(info, high_normed_ffn, gate, up)

    def attention_back(qkv, past, mixed_grad, mixed, lse, base, heads):
        q_grad, own_grad, past_grad = attend_back(
            info, qkv, past, mixed_grad, mixed, lse, tables, base, heads
        )
        if devices == 2:
            return q_grad, own_grad, cores(past_grad[0].astype(BF16))
        return q_grad, own_grad, lax.psum_scatter(past_grad, "seq", scatter_dimension=0)

    def to_input(x, grad_middle, parts):
        return project_back(
            info, x, gains[0], grad_middle, *zip(*parts), qkv_weights, tables
        )

    high_gate, high_up, high_branch, grad_middle, high_attn, mixed_grad, high_ffn_gain = ffn_back(
        info, incoming, high_middle, gains[1], high_silu, high_slope, down, gate, up, square
    )
    parts = [
        attention_back(high_qkv, high_past, mixed_grad, high_mixed, high_lse, base, heads)
        for base, heads in ((0, 3), (3, 2))
    ]
    high_q, high_kv, grad_between, high_attn_gain = to_input(middle_in, grad_middle, parts)

    def with_core(kept, arrived):
        both = kept.astype(F32) + arrived.astype(F32)
        return both[0].astype(BF16), both[1]

    low_branch = grad_between.astype(BF16)
    down_away, down_kept = outer(info, (high_branch, high_hidden, low_branch, low_hidden), True)
    down_core = cores(down_away)
    final_out = shrink(info, tied(high_middle, down_away), high_hidden, down, BF16)
    grad_between, down_core = tied((grad_between, down_core), final_out)
    down_chain = Chain(*with_core(down_kept, down_core))
    grad_between, down_chain.sent = tied((grad_between, down_chain.sent), ())
    grad_between = tied(grad_between, down_chain.sent)
    low_gate, low_up, _, grad_middle, low_attn, mixed_grad, low_ffn_gain = ffn_back(
        info, grad_between, low_middle, gains[1], low_silu, low_slope, down, gate, up, square
    )
    gate_away, gate_kept = outer(info, (high_normed_ffn, high_gate, low_normed_ffn, low_gate), False)
    gate_core = cores(gate_away)
    down_y = down_chain.step()
    low_up = tied(low_up, (down_y, gate_away))
    up_away, up_kept = outer(info, (high_normed_ffn, high_up, low_normed_ffn, low_up), False)
    down_x = down_chain.step()
    up_core = cores(up_away)
    low_attn, gate_core = tied((low_attn, gate_core), (up_away, gate_core))
    gate_chain = Chain(*with_core(gate_kept, gate_core))
    low_attn = tied(low_attn, gate_chain.sent)
    out_away, out_kept = pack(info, high_mixed, low_mixed, (high_attn, low_attn))
    out_core = cores(out_away)
    mixed_grad = tied(mixed_grad, (out_away, down_x, up_core))
    up_chain = Chain(*with_core(up_kept, up_core))
    parts = []

    def low_part(base, heads):
        parts.append(
            attention_back(low_qkv, low_past, mixed_grad, low_mixed, low_lse, base, heads)
        )
        return parts[-1][0]

    gate_y = gate_chain.step()
    down_z = down_chain.step()
    grown = low_part(0, 2)
    mixed_grad = tied(mixed_grad, (grown, down_z, out_core))
    out_chain = Chain(*with_core(out_kept, out_core))
    down_z = down_chain.step((grown,))
    grown = low_part(2, 2)
    mixed_grad = tied(mixed_grad, (grown, down_z, gate_y))
    up_y = up_chain.step((gate_y,))
    gate_x = gate_chain.step()
    down_z = down_chain.step((grown,))
    grown = low_part(4, 1)
    grad_middle = tied(grad_middle, (grown, down_z, gate_x))
    down_z = down_chain.step((grown,))
    gate_z = gate_chain.step()
    low_q, low_kv, grad_start, low_attn_gain = to_input(start_in, grad_middle, parts)
    low_q = tied(low_q, (low_kv, gate_z, down_z))
    gate_z = gate_chain.step((low_kv,))
    down_x = down_chain.step((low_kv,))
    qkv_away, qkv_kept = pack(info, high_normed, low_normed, (high_q, low_q, high_kv, low_kv))
    qkv_core = cores(tied(qkv_away, (up_y,)))
    qkv_chain = Chain(*with_core(qkv_kept, qkv_core))
    out_y = out_chain.step((up_y,))
    up_x = up_chain.step((down_x,))
    gate_z = gate_chain.step()
    qkv_y = qkv_chain.step((out_y,))
    gate_z = gate_chain.step()
    gate_x = gate_chain.step((up_x,))
    down_grad = down_chain.finish()
    out_x = out_chain.step((gate_x,))
    for _ in range(4):
        up_chain.step()
    up_x = up_chain.step((out_x,))
    qkv_x = qkv_chain.step((up_x,))
    up_grad, gate_grad = up_chain.finish(), gate_chain.finish()
    for _ in range(4):
        out_chain.step()
    out_chain.step((qkv_x,))
    out_grad, qkv_grad = out_chain.finish(), qkv_chain.finish()
    gain_grads = jnp.stack(
        [(high_attn_gain + low_attn_gain)[:, 0], (high_ffn_gain + low_ffn_gain)[:, 0]]
    )
    for axis in ("seq", "fsdp", "batch"):
        for bit in bits_of(axis):
            gain_grads = gain_grads + swap(gain_grads, axis, bit)
    gain_grads = halves(gain_grads, 1, mine)
    narrow = KEY_HEADS * HEAD_DIM
    query_part, key_part, value_part = jnp.split(qkv_grad, [width, width + narrow], 1)
    return (
        final_out.T[None],
        grad_start.T[None],
        gain_grads[0],
        query_part,
        key_part,
        value_part,
        out_grad,
        gain_grads[1],
        gate_grad,
        up_grad,
        down_grad.T,
    )


def solution(mesh):
    return jax.shard_map(
        per_device,
        mesh=mesh,
        in_specs=(
            P(("batch", "fsdp"), "seq", None),
            P("fsdp"),
            P("fsdp", None),
            P("fsdp", None),
            P("fsdp", None),
            P("fsdp", None),
            P("fsdp"),
            P("fsdp", None),
            P("fsdp", None),
            P("fsdp", None),
            P(("batch", "fsdp"), "seq", None),
        ),
        out_specs=(
            P(("batch", "fsdp"), "seq", None),
            P(("batch", "fsdp"), "seq", None),
            P("fsdp"),
            P("fsdp", None),
            P("fsdp", None),
            P("fsdp", None),
            P("fsdp", None),
            P("fsdp"),
            P("fsdp", None),
            P("fsdp", None),
            P("fsdp", None),
        ),
        check_vma=False,
    )
```

```python
import functools
import math

import jax
import jax.numpy as jnp
from jax import lax
from jax.experimental import pallas as pl
from jax.experimental.pallas import tpu as pltpu
from jax.sharding import PartitionSpec as P

QUERY_HEADS = 15
KEY_HEADS = 5
HEAD_DIM = 64
GROUP = QUERY_HEADS // KEY_HEADS
EPSILON = 1e-05
VMEM_BYTES = 56 * 1024 * 1024
F32 = jnp.float32
BF16 = jnp.bfloat16


def dot(left, right, left_dim, right_dim):
    return lax.dot_general(
        left, right, (((left_dim,), (right_dim,)), ((), ())), preferred_element_type=F32
    )


def spans(total, size):
    return [(start, min(size, total - start)) for start in range(0, total, size)]


COSTS = {
    "project": 6.0,
    "attend": 20.0,
    "mix": 5.5,
    "expand": 10.0,
    "expand_first": 14.0,
    "shrink": 6.5,
    "shrink_first": 8.0,
    "ffn_back": 18.0,
    "attend_back": 6.5,
    "project_back": 9.5,
    "outer": 10.0,
    "pack": 7.0,
}


def call(kernel, name, grid, in_specs, out_specs, out_shape, scratch=()):
    cost = int(COSTS[name] * 0.45e9 * (grid[0] if name == "attend_back" else 1))
    return pl.pallas_call(
        kernel,
        name=name,
        out_shape=out_shape,
        grid_spec=pltpu.PrefetchScalarGridSpec(
            num_scalar_prefetch=1,
            grid=grid,
            in_specs=in_specs,
            out_specs=out_specs,
            scratch_shapes=list(scratch),
        ),
        compiler_params=pltpu.CompilerParams(vmem_limit_bytes=VMEM_BYTES),
        cost_estimate=pl.CostEstimate(flops=cost, bytes_accessed=1, transcendentals=0),
    )


def whole(shape):
    return pl.BlockSpec(shape, lambda *_: (0,) * len(shape))


def shaped(shape, dtype):
    return jax.ShapeDtypeStruct(shape, dtype)


def scale_of(values):
    return lax.rsqrt(jnp.mean(values * values, 0, keepdims=True) + EPSILON)


def norm_back(values, gain, incoming):
    scales = scale_of(values)
    weighted = gain * incoming
    inner = jnp.mean(values * weighted, 0, keepdims=True)
    grad = scales * weighted - values * (scales * scales * scales * inner)
    return grad, jnp.sum(incoming * values * scales, 1, keepdims=True)


def rotate(values, cosine, sine):
    half = HEAD_DIM // 2
    first, second = values[:half], values[half:]
    return first * cosine - second * sine, second * cosine + first * sine


def project_kernel(
    info, x, gain, q_weight, k_own, k_oth, v_own, v_oth, cosine, sine, normed, out
):
    width = x.shape[0]
    half = width // 2
    values = x[...].astype(F32)
    normed[...] = (values * scale_of(values) * gain[...]).astype(BF16)
    own = normed[pl.ds(pl.multiple_of(info[0] * half, half), half), :]
    oth = normed[pl.ds(pl.multiple_of((1 - info[0]) * half, half), half), :]
    cos, sin = cosine[...], sine[...]
    hd = HEAD_DIM

    def turned(rows, base, factor):
        for head in range(rows.shape[0] // hd):
            first, second = rotate(rows[head * hd : (head + 1) * hd], cos, sin)
            at = base + head * hd
            out[at : at + hd // 2, :] = (first * factor).astype(BF16)
            out[at + hd // 2 : at + hd, :] = (second * factor).astype(BF16)

    q_width = q_weight.shape[1]
    turned(dot(q_weight[...], normed[...], 0, 0), 0, hd**-0.5)
    kv = k_own.shape[0]
    turned(dot(k_own[...], own, 1, 0) + dot(k_oth[...], oth, 1, 0), q_width, 1.0)
    rows = dot(v_own[...], own, 1, 0) + dot(v_oth[...], oth, 1, 0)
    out[q_width + kv : q_width + 2 * kv, :] = rows.astype(BF16)


def project(info, x, gain, weights, tables):
    width, rows = x.shape
    q, k, v = weights
    total = q.shape[1] + 2 * k[0].shape[0]
    operands = (x, gain, q, *k, *v, *tables)
    return call(
        project_kernel,
        "project",
        (1,),
        [whole(item.shape) for item in operands],
        [whole((width, rows)), whole((total, rows))],
        [shaped((width, rows), BF16), shaped((total, rows), BF16)],
    )(info, *operands)


def scores_of(keys, queries, masked):
    scores = dot(keys, queries, 1, 0)
    if not masked:
        return scores
    key_row = lax.broadcasted_iota(jnp.int32, scores.shape, 0)
    query_row = lax.broadcasted_iota(jnp.int32, scores.shape, 1)
    return jnp.where(key_row <= query_row, scores, -1e30)


def attend_kernel(
    info, q, k_own, v_own, k_past, v_past, out, lse, keys_own, keys_past, peak, total, mixed
):
    rows = q.shape[1]
    block = min(256, rows)
    hd = HEAD_DIM
    groups = [(group, slice(group * hd, (group + 1) * hd)) for group in range(GROUP)]
    keys_own[...] = k_own[...].T

    @pl.loop(0, info[1])
    def _(device):
        keys_past[device] = k_past[device].T

    for start in range(0, rows, block):
        for group, head in groups:
            scores = scores_of(keys_own[start : start + block, :], q[head, start:], True)
            fresh = jnp.max(scores, 0, keepdims=True)
            if start > 0:
                fresh = jnp.maximum(fresh, peak[group : group + 1, start:])
            peak[group : group + 1, start:] = fresh

    @pl.loop(0, info[1])
    def _(device):
        for group, head in groups:
            scores = scores_of(keys_past[device], q[head, :], False)
            peak[group : group + 1, :] = jnp.maximum(
                peak[group : group + 1, :], jnp.max(scores, 0, keepdims=True)
            )

    def add(group, head, keys, values, start, masked, first):
        scores = scores_of(keys, q[head, start:], masked)
        exponent = jnp.exp(scores - peak[group : group + 1, start:])
        sums = jnp.sum(exponent, 0, keepdims=True)
        product = dot(values, exponent.astype(BF16), 1, 0)
        if first:
            total[group : group + 1, :] = sums
            mixed[head, :] = product
        else:
            total[group : group + 1, start:] += sums
            mixed[head, start:] += product

    for start in range(0, rows, block):
        part = slice(start, start + block)
        for group, head in groups:
            add(group, head, keys_own[part, :], v_own[:, part], start, True, start == 0)

    @pl.loop(0, info[1])
    def _(device):
        for group, head in groups:
            add(group, head, keys_past[device], v_past[device], 0, False, False)

    for group, head in groups:
        sums = total[group : group + 1, :]
        out[head, :] = (mixed[head, :] / sums).astype(BF16)
        lse[0, group : group + 1, :] = peak[group : group + 1, :] + jnp.log(sums)


def attention_specs(rows, past, base):
    hd = HEAD_DIM
    return [
        pl.BlockSpec((GROUP * hd, rows), lambda h, info: (base + h, 0)),
        pl.BlockSpec((hd, rows), lambda h, info: (QUERY_HEADS + base + h, 0)),
        pl.BlockSpec((hd, rows), lambda h, info: (QUERY_HEADS + KEY_HEADS + base + h, 0)),
        pl.BlockSpec((past, hd, rows), lambda h, info: (0, base + h, 0)),
        pl.BlockSpec((past, hd, rows), lambda h, info: (0, KEY_HEADS + base + h, 0)),
    ]


def attend(info, qkv, past):
    rows = qkv.shape[1]
    count = past.shape[0]
    return call(
        attend_kernel,
        "attend",
        (KEY_HEADS,),
        attention_specs(rows, count, 0),
        [
            pl.BlockSpec((GROUP * HEAD_DIM, rows), lambda h, info: (h, 0)),
            pl.BlockSpec((1, 8, rows), lambda h, info: (h, 0, 0)),
        ],
        [shaped((QUERY_HEADS * HEAD_DIM, rows), BF16), shaped((KEY_HEADS, 8, rows), F32)],
        [
            pltpu.VMEM((rows, HEAD_DIM), BF16),
            pltpu.VMEM((count, rows, HEAD_DIM), BF16),
            pltpu.VMEM((8, rows), F32),
            pltpu.VMEM((8, rows), F32),
            pltpu.VMEM((GROUP * HEAD_DIM, rows), F32),
        ],
    )(info, qkv, qkv, qkv, past, past)


def mix_kernel(info, x, mixed, weight, gain, middle, normed):
    middle[...] = x[...].astype(F32) + dot(weight[...], mixed[...], 0, 0)
    values = middle[...]
    normed[...] = (values * scale_of(values) * gain[...]).astype(BF16)


def mix(info, x, mixed, weight, gain):
    width, rows = x.shape
    operands = (x, mixed, weight, gain)
    return call(
        mix_kernel,
        "mix",
        (1,),
        [whole(item.shape) for item in operands],
        [whole((width, rows)), whole((width, rows))],
        [shaped((width, rows), F32), shaped((width, rows), BF16)],
    )(info, *operands)


def activate(token_rows, gate_weight, up_weight, hidden, silu, slope):
    gate = dot(token_rows[...], gate_weight[...], 1, 0)
    up = dot(token_rows[...], up_weight[...], 1, 0)
    sigmoid = 0.5 * jnp.tanh(0.5 * gate) + 0.5
    active = gate * sigmoid
    hidden[...] = (active * up).astype(BF16)
    silu[...] = active.astype(BF16)
    slope[...] = (up * (sigmoid + active * (1.0 - sigmoid))).astype(BF16)


def expand_kernel(info, normed, gate_weight, up_weight, hidden, silu, slope, token_rows):
    @pl.when(pl.program_id(0) == 0)
    def _():
        token_rows[...] = normed[...].T

    activate(token_rows, gate_weight, up_weight, hidden, silu, slope)


def expand(info, normed, gate, up):
    width, rows = normed.shape
    ff = gate.shape[1]
    tile = ff // 5
    weight = pl.BlockSpec((width, tile), lambda t, info: (0, t))
    result = pl.BlockSpec((rows, tile), lambda t, info: (0, t))
    return call(
        expand_kernel,
        "expand",
        (ff // tile,),
        [whole((width, rows)), weight, weight],
        [result] * 3,
        [shaped((rows, ff), BF16)] * 3,
        [pltpu.VMEM((rows, width), BF16)],
    )(info, normed, gate, up)


def expand_first_kernel(info, normed, *refs):
    gate_parts, up_parts = refs[:5], refs[5:10]
    hidden, silu, slope, gate_weight, up_weight, token_rows = refs[10:]
    step = pl.program_id(0)
    steps = pl.num_programs(0)

    @pl.when(step == 0)
    def _():
        token_rows[...] = normed[...].T

    for (own, *pieces), target in ((gate_parts, gate_weight), (up_parts, up_weight)):
        half, quarter = own.shape[0], pieces[0].shape[0]
        target[pl.ds(pl.multiple_of(info[0] * half, half), half), :] = own[...]
        other = (1 - info[0]) * half
        near = pl.ds(pl.multiple_of(other + info[3] * quarter, quarter), quarter)
        far = pl.ds(pl.multiple_of(other + (1 - info[3]) * quarter, quarter), quarter)

        @pl.when(step < steps // 2)
        def _():
            target[near, :] = pieces[0][...]
            target[far, :] = pieces[1][...]

        @pl.when(step >= steps // 2)
        def _():
            target[near, :] = pieces[2][...]
            target[far, :] = pieces[3][...]

    activate(token_rows, gate_weight, up_weight, hidden, silu, slope)


def expand_first(info, normed, gate, up):
    width, rows = normed.shape
    half, ff = gate[0].shape
    steps = 4
    tile = ff // steps
    quarter = half // 2

    def column(t, info):
        own = info[2] * (steps // 2) + t
        return jnp.where(t < steps // 2, own, (1 - info[2]) * (steps // 2) + t - steps // 2)

    early = pl.BlockSpec((quarter, tile), lambda t, info: (0, jnp.minimum(t, steps // 2 - 1)))
    late = pl.BlockSpec((quarter, tile), lambda t, info: (0, jnp.maximum(t - steps // 2, 0)))
    parts = [pl.BlockSpec((half, tile), lambda t, info: (0, column(t, info)))]
    parts += [early, early, late, late]
    result = pl.BlockSpec((rows, tile), lambda t, info: (0, column(t, info)))
    weight = pl.BlockSpec((width, tile), lambda t, info: (0, column(t, info)))
    return call(
        expand_first_kernel,
        "expand_first",
        (steps,),
        [whole((width, rows))] + parts * 2,
        [result] * 3 + [weight] * 2,
        [shaped((rows, ff), BF16)] * 3 + [shaped((width, ff), BF16)] * 2,
        [pltpu.VMEM((rows, width), BF16)],
    )(info, normed, *gate, *up)


def shrink_kernel(info, middle, hidden, weight, out):
    out[...] = (middle[...] + dot(weight[...], hidden[...], 1, 1)).astype(out.dtype)


def shrink(info, middle, hidden, down, dtype):
    width, rows = middle.shape
    ff = hidden.shape[1]
    tile = width // 2
    return call(
        shrink_kernel,
        "shrink",
        (width // tile,),
        [
            pl.BlockSpec((tile, rows), lambda t, info: (t, 0)),
            whole((rows, ff)),
            pl.BlockSpec((tile, ff), lambda t, info: (t, 0)),
        ],
        [pl.BlockSpec((tile, rows), lambda t, info: (t, 0))],
        [shaped((width, rows), dtype)],
    )(info, middle, hidden, down)[0]


def shrink_first_kernel(info, middle, hidden, own, near_0, far_0, near_1, far_1, out, weight):
    half, quarter = own.shape[1], near_0.shape[0]
    weight[:, pl.ds(pl.multiple_of(info[0] * half, half), half)] = own[...]
    other = pl.ds(pl.multiple_of((1 - info[0]) * half, half), half)
    at_near = pl.ds(pl.multiple_of(info[2] * quarter, quarter), quarter)
    at_far = pl.ds(pl.multiple_of((1 - info[2]) * quarter, quarter), quarter)
    for step, near, far in ((0, near_0, far_0), (1, near_1, far_1)):

        @pl.when(pl.program_id(0) == step)
        def _():
            weight[at_near, other] = near[...]
            weight[at_far, other] = far[...]

    out[...] = middle[...] + dot(weight[...], hidden[...], 1, 1)


def shrink_first(info, middle, hidden, parts):
    width, rows = middle.shape
    ff = hidden.shape[1]
    tile = width // 2
    own, first, second, third, fourth = parts

    def row(t, info):
        return jnp.where(t == 0, info[3], 1 - info[3])

    return call(
        shrink_first_kernel,
        "shrink_first",
        (2,),
        [
            pl.BlockSpec((tile, rows), lambda t, info: (row(t, info), 0)),
            whole((rows, ff)),
            pl.BlockSpec((tile, ff // 2), lambda t, info: (row(t, info), 0)),
        ]
        + [whole(first.shape)] * 4,
        [
            pl.BlockSpec((tile, rows), lambda t, info: (row(t, info), 0)),
            pl.BlockSpec((tile, ff), lambda t, info: (row(t, info), 0)),
        ],
        [shaped((width, rows), F32), shaped((width, ff), BF16)],
    )(info, middle, hidden, own, first, third, second, fourth)


def ffn_back_kernel(
    info,
    grad,
    middle,
    gain,
    silu,
    slope,
    down,
    gate,
    up,
    out_weight,
    gate_grad,
    up_grad,
    branch,
    grad_middle,
    attn_grad,
    mixed_grad,
    gain_grad,
    branch_rows,
    total,
):
    step = pl.program_id(0)
    steps = pl.num_programs(0)

    @pl.when(step == 0)
    def _():
        branch[...] = grad[...].astype(BF16)
        branch_rows[...] = branch[...].T
        total[...] = jnp.zeros_like(total)

    incoming = dot(branch_rows[...], down[...], 1, 0)
    gate_grad[...] = (incoming * slope[...].astype(F32)).astype(BF16)
    up_grad[...] = (incoming * silu[...].astype(F32)).astype(BF16)
    total[...] += dot(gate[...], gate_grad[...], 1, 1) + dot(up[...], up_grad[...], 1, 1)

    @pl.when(step == steps - 1)
    def _():
        back, gain_sum = norm_back(middle[...], gain[...], total[...])
        gain_grad[...] = gain_sum
        result = grad[...].astype(F32) + back
        grad_middle[...] = result
        attn_grad[...] = result.astype(BF16)
        mixed_grad[...] = dot(out_weight[...], attn_grad[...], 1, 0).astype(BF16)


def ffn_back(info, grad, middle, gain, silu, slope, down, gate, up, out_weight):
    width, rows = middle.shape
    ff = silu.shape[1]
    tile = ff // 5
    heads = out_weight.shape[0]
    token = pl.BlockSpec((rows, tile), lambda t, info: (0, t))
    weight = pl.BlockSpec((width, tile), lambda t, info: (0, t))
    return call(
        ffn_back_kernel,
        "ffn_back",
        (ff // tile,),
        [
            whole((width, rows)),
            whole((width, rows)),
            whole((width, 1)),
            token,
            token,
            weight,
            weight,
            weight,
            whole((heads, width)),
        ],
        [
            token,
            token,
            whole((width, rows)),
            whole((width, rows)),
            whole((width, rows)),
            whole((heads, rows)),
            whole((width, 1)),
        ],
        [
            shaped((rows, ff), BF16),
            shaped((rows, ff), BF16),
            shaped((width, rows), BF16),
            shaped((width, rows), F32),
            shaped((width, rows), BF16),
            shaped((heads, rows), BF16),
            shaped((width, 1), F32),
        ],
        [pltpu.VMEM((rows, width), BF16), pltpu.VMEM((width, rows), F32)],
    )(info, grad, middle, gain, silu, slope, down, gate, up, out_weight)


def attend_back_kernel(
    info,
    q,
    k_own,
    v_own,
    k_past,
    v_past,
    mixed_grad,
    mixed,
    lse,
    cosine,
    sine,
    q_grad,
    own_grad,
    past_grad,
    keys_own,
    values_own,
    keys_past,
    values_past,
    inner,
    q_sum,
):
    rows = q.shape[1]
    block = min(256, rows)
    hd = HEAD_DIM
    groups = [(group, slice(group * hd, (group + 1) * hd)) for group in range(GROUP)]
    keys_own[...] = k_own[...].T
    values_own[...] = v_own[...].T

    @pl.loop(0, info[1])
    def _(device):
        keys_past[device] = k_past[device].T
        values_past[device] = v_past[device].T

    @pl.loop(info[1], past_grad.shape[0])
    def _(device):
        past_grad[device] = jnp.zeros_like(past_grad[device])

    for group, head in groups:
        product = mixed_grad[head, :].astype(F32) * mixed[head, :].astype(F32)
        inner[group : group + 1, :] = jnp.sum(product, 0, keepdims=True)

    def step(keys, key_rows, value_rows, start, masked, first):
        key_sum = value_sum = None
        for group, head in groups:
            query, incoming = q[head, start:], mixed_grad[head, start:]
            one = slice(group, group + 1)
            probs = jnp.exp(scores_of(key_rows, query, masked) - lse[0, one, start:])
            slopes = dot(value_rows, incoming, 1, 0)
            low = (probs * (slopes - inner[one, start:])).astype(BF16)
            value_part = dot(incoming, probs.astype(BF16), 1, 1)
            key_part = dot(query, low, 1, 1)
            key_sum = key_part if key_sum is None else key_sum + key_part
            value_sum = value_part if value_sum is None else value_sum + value_part
            query_part = dot(keys, low, 1, 0)
            if first:
                q_sum[head, :] = query_part
            else:
                q_sum[head, start:] += query_part
        return key_sum, value_sum

    for start in range(0, rows, block):
        part = slice(start, start + block)
        key_sum, value_sum = step(
            k_own[:, part], keys_own[part, :], values_own[part, :], start, True, start == 0
        )
        own_grad[0, :hd, part] = key_sum
        own_grad[0, hd:, part] = value_sum

    @pl.loop(0, info[1])
    def _(device):
        key_sum, value_sum = step(
            k_past[device], keys_past[device], values_past[device], 0, False, False
        )
        past_grad[device, 0, :hd, :] = key_sum.astype(past_grad.dtype)
        past_grad[device, 0, hd:, :] = value_sum.astype(past_grad.dtype)

    cos, sin = cosine[...], -sine[...]
    for group, head in groups:
        first, second = rotate(q_sum[head, :], cos, sin)
        at = group * hd
        q_grad[at : at + hd // 2, :] = (first * hd**-0.5).astype(BF16)
        q_grad[at + hd // 2 : at + hd, :] = (second * hd**-0.5).astype(BF16)


def attend_back(info, qkv, past, mixed_grad, mixed, lse, tables, base, heads):
    rows = qkv.shape[1]
    count = past.shape[0]
    hd = HEAD_DIM
    group = pl.BlockSpec((GROUP * hd, rows), lambda h, info: (base + h, 0))
    return call(
        attend_back_kernel,
        "attend_back",
        (heads,),
        attention_specs(rows, count, base)
        + [
            group,
            group,
            pl.BlockSpec((1, 8, rows), lambda h, info: (base + h, 0, 0)),
            whole(tables[0].shape),
            whole(tables[1].shape),
        ],
        [
            pl.BlockSpec((GROUP * hd, rows), lambda h, info: (h, 0)),
            pl.BlockSpec((1, 2 * hd, rows), lambda h, info: (h, 0, 0)),
            pl.BlockSpec((count, 1, 2 * hd, rows), lambda h, info: (0, h, 0, 0)),
        ],
        [
            shaped((heads * GROUP * hd, rows), BF16),
            shaped((heads, 2 * hd, rows), F32),
            shaped((count, heads, 2 * hd, rows), BF16 if count == 1 else F32),
        ],
        [
            pltpu.VMEM((rows, hd), BF16),
            pltpu.VMEM((rows, hd), BF16),
            pltpu.VMEM((count, rows, hd), BF16),
            pltpu.VMEM((count, rows, hd), BF16),
            pltpu.VMEM((8, rows), F32),
            pltpu.VMEM((GROUP * hd, rows), F32),
        ],
    )(info, qkv, qkv, qkv, past, past, mixed_grad, mixed, lse, *tables)


def project_back_kernel(parts, info, x, gain, grad_middle, *refs):
    q_grads, own_grads, arrived = refs[:parts], refs[parts : 2 * parts], refs[2 * parts : 3 * parts]
    (
        q_weight,
        k_own,
        k_oth,
        v_own,
        v_oth,
        cosine,
        sine,
        q_grad,
        kv_grad,
        out,
        branch,
        gain_grad,
        total,
    ) = refs[3 * parts :]
    half = x.shape[0] // 2
    hd = HEAD_DIM
    kv = KEY_HEADS * hd
    cos, sin = cosine[...], -sine[...]
    head = 0
    for piece, own, far in zip(q_grads, own_grads, arrived):
        q_grad[head * GROUP * hd : head * GROUP * hd + piece.shape[0], :] = piece[...]
        for item in range(own.shape[0]):
            both = own[item] + far[item].astype(F32)
            first, second = rotate(both[:hd], cos, sin)
            at = head * hd
            kv_grad[at : at + hd // 2, :] = first.astype(BF16)
            kv_grad[at + hd // 2 : at + hd, :] = second.astype(BF16)
            kv_grad[kv + at : kv + at + hd, :] = both[hd:].astype(BF16)
            head += 1
    total[...] = dot(q_weight[...], q_grad[...], 1, 0)
    for mine, k, v in ((info[0], k_own, v_own), (1 - info[0], k_oth, v_oth)):
        total[pl.ds(pl.multiple_of(mine * half, half), half), :] += dot(
            k[...], kv_grad[:kv, :], 0, 0
        ) + dot(v[...], kv_grad[kv:, :], 0, 0)
    back, gain_sum = norm_back(x[...].astype(F32), gain[...], total[...])
    gain_grad[...] = gain_sum
    result = grad_middle[...] + back
    out[...] = result
    branch[...] = result.astype(BF16)


def project_back(info, x, gain, grad_middle, q_grads, own_grads, arrived, weights, tables):
    width, rows = x.shape
    q, k, v = weights
    heads = q.shape[1]
    kv = 2 * KEY_HEADS * HEAD_DIM
    operands = (x, gain, grad_middle, *q_grads, *own_grads, *arrived, q, *k, *v, *tables)
    shapes = [
        shaped((heads, rows), BF16),
        shaped((kv, rows), BF16),
        shaped((width, rows), F32),
        shaped((width, rows), BF16),
        shaped((width, 1), F32),
    ]
    return call(
        functools.partial(project_back_kernel, len(q_grads)),
        "project_back",
        (1,),
        [whole(item.shape) for item in operands],
        [whole(item.shape) for item in shapes],
        shapes,
        [pltpu.VMEM((width, rows), F32)],
    )(info, *operands)


def order_rows(info, target, sources):
    rows = sources[0].shape[1]
    size = target.shape[0] // 4
    at = 0
    for core in (1 - info[2], info[2]):
        for half in (1 - info[0], info[0]):
            start = pl.multiple_of((2 * half + core) * size, size)
            for index, source in enumerate(sources):
                target[at : at + size, index * rows : (index + 1) * rows] = source[
                    pl.ds(start, size), :
                ]
            at += size


def order_halves(info, target, sources):
    rows = sources[0].shape[1]
    size = target.shape[0] // 2
    for at, core in ((0, 1 - info[2]), (size, info[2])):
        start = pl.multiple_of(core * size, size)
        for index, source in enumerate(sources):
            target[at : at + size, index * rows : (index + 1) * rows] = source[pl.ds(start, size), :]


def outer_kernel(split_columns, info, left_a, right_a, left_b, right_b, sent, kept, left, right):
    rows = left_a.shape[1]

    @pl.when(pl.program_id(0) == 0)
    def _():
        order = order_halves if split_columns else order_rows
        order(info, left, (left_a, left_b))

    right[:rows, :] = right_a[...]
    right[rows:, :] = right_b[...]
    count, size = sent.shape[0], sent.shape[1]
    for at, out in ((0, sent), (count * size, kept)):
        product = dot(left[at : at + count * size, :], right[...], 1, 0).astype(BF16)
        for index in range(count):
            out[index] = product[index * size : (index + 1) * size]


def outer(info, parts, split_columns):
    left_a, right_a, left_b, right_b = parts
    width, rows = left_a.shape
    columns = right_a.shape[1]
    if split_columns:
        tile = columns // 4

        def column(t, info):
            return jnp.where(t < 2, (1 - info[0]) * 2 + t, info[0] * 2 + t - 2)

        right = pl.BlockSpec((rows, tile), lambda t, info: (0, column(t, info)))
        result = pl.BlockSpec((1, width // 2, tile), lambda t, info: (t // 2, 0, t % 2))
        shape = shaped((2, width // 2, columns // 2), BF16)
    else:
        tile = columns // 5
        right = pl.BlockSpec((rows, tile), lambda t, info: (0, t))
        result = pl.BlockSpec((2, width // 4, tile), lambda t, info: (0, 0, t))
        shape = shaped((2, width // 4, columns), BF16)
    return call(
        functools.partial(outer_kernel, split_columns),
        "outer",
        (columns // tile,),
        [whole((width, rows)), right, whole((width, rows)), right],
        [result, result],
        [shape, shape],
        [pltpu.VMEM((width, 2 * rows), BF16), pltpu.VMEM((2 * rows, tile), BF16)],
    )(info, *parts)


def pack_kernel(info, left_a, *refs):
    sent, kept, left, right = refs[-4:]
    left_b, rights_a, rights_b = refs[0], refs[1:-4:2], refs[2:-4:2]
    rows = left_a.shape[1]
    order_rows(info, left, (left_a, left_b))
    at = 0
    for right_a, right_b in zip(rights_a, rights_b):
        right[at : at + right_a.shape[0], :rows] = right_a[...]
        right[at : at + right_a.shape[0], rows:] = right_b[...]
        at += right_a.shape[0]
    count, size = sent.shape[0], sent.shape[1]
    for base, out in ((0, sent), (count * size, kept)):
        for start, span in spans(right.shape[0], 512):
            product = dot(left[base : base + count * size, :], right[start : start + span, :], 1, 1)
            for index in range(count):
                out[index, :, start : start + span] = product[
                    index * size : (index + 1) * size
                ].astype(BF16)


def pack(info, left_a, left_b, rights):
    width, rows = left_a.shape
    columns = sum(item.shape[0] for item in rights[::2])
    operands = (left_a, left_b, *rights)
    shape = shaped((2, width // 4, columns), BF16)
    return call(
        pack_kernel,
        "pack",
        (1,),
        [whole(item.shape) for item in operands],
        [whole(shape.shape)] * 2,
        [shape, shape],
        [pltpu.VMEM((width, 2 * rows), BF16), pltpu.VMEM((columns, 2 * rows), BF16)],
    )(info, *operands)


def swap(values, axis, bit):
    size = lax.axis_size(axis)
    return lax.ppermute(values, axis, [(i, i ^ bit) for i in range(size)])


def bits_of(axis):
    size = lax.axis_size(axis)
    assert size & (size - 1) == 0
    return [1 << i for i in range(size.bit_length() - 1)]


def high(axis, bit):
    return (lax.axis_index(axis) // bit) % 2


def halves(values, dim, which):
    half = values.shape[dim] // 2
    return lax.dynamic_slice_in_dim(values, which * half, half, dim)


def joined(mine, other, dim, which):
    return jnp.where(
        which == 0,
        jnp.concatenate([mine, other], dim),
        jnp.concatenate([other, mine], dim),
    )


def tied(values, others):
    return lax.optimization_barrier((values, others))[0]


def from_pieces(own, pieces, mine, core, low_batch):
    near = joined(pieces[0], pieces[2], 0, core)
    far = joined(pieces[1], pieces[3], 0, core)
    return joined(own, joined(near, far, 0, low_batch), 0, mine)


def split_dim(shape):
    if shape[0] % 16 == 0:
        return 0
    if shape[1] % 256 == 0:
        return 1
    return 0 if shape[0] % 2 == 0 else 1


def over_fsdp(values):
    return swap(values, "fsdp", 1)


class Chain:
    def __init__(self, sent, kept):
        self.sent, self.held, self.stages = sent, kept, []
        self.todo = [("fsdp", 1)]
        self.todo += [("seq", bit) for bit in bits_of("seq")[1:]]
        self.todo += [("batch", bit) for bit in bits_of("batch")]
        self.back = None

    def step(self, wait=()):
        if self.todo:
            axis, bit = self.todo.pop(0)
            if axis == "fsdp":
                arrived = swap(tied(self.sent, wait), axis, bit)
                self.held = self.held.astype(F32) + arrived.astype(F32)
                return arrived
            which = high(axis, bit)
            dim = split_dim(self.held.shape)
            low = self.held.astype(BF16)
            arrived = swap(tied(halves(low, dim, 1 - which), wait), axis, bit)
            self.held = halves(self.held, dim, which) + arrived.astype(F32)
            self.stages.append((axis, bit, dim, which))
            return arrived
        if self.back is None:
            self.held = self.held.astype(BF16)
            self.back = [("seq", 1, 0, high("seq", 1))] + self.stages
        axis, bit, dim, which = self.back.pop()
        arrived = swap(tied(self.held, wait), axis, bit)
        self.held = joined(self.held, arrived, dim, which)
        return arrived

    def finish(self):
        while self.back is None or self.back:
            self.step()
        return self.held.astype(F32)


def per_device(
    tokens,
    attn_gain,
    w_query,
    key_weight,
    value_weight,
    w_out,
    ffn_gain,
    w_gate,
    w_up,
    w_down,
    cotangent,
):
    assert tokens.shape[0] == 1 and lax.axis_size("fsdp") == 2
    mine, spot, core = lax.axis_index("fsdp"), lax.axis_index("seq"), high("seq", 1)
    low_batch = high("batch", 1)
    devices = lax.axis_size("seq")
    info = jnp.stack([mine, spot, core, low_batch]).astype(jnp.int32)
    start_in = tokens[0].T
    incoming = cotangent[0].T
    width, rows = start_in.shape

    gains = jnp.stack([attn_gain, ffn_gain])
    gains = joined(gains, swap(gains, "fsdp", 1), 1, mine).astype(F32)[..., None]
    key_weight, value_weight, w_down = key_weight.T, value_weight.T, w_down.T
    def fsdp(values):
        return swap(values, "fsdp", 1)

    def pair(values):
        return swap(values, "batch", 1)

    def cores(values):
        return swap(values, "seq", 1)

    q_piece = halves(halves(w_query, 0, low_batch), 0, core)
    kv_piece = halves(jnp.where(core == 0, key_weight, value_weight), 0, low_batch)
    q_0, kv_0 = fsdp(q_piece), fsdp(kv_piece)
    out_0 = fsdp(tied(halves(halves(w_out, 0, low_batch), 0, core), (q_0, kv_0)))
    q_1, kv_1, q_2, kv_2 = pair(q_0), pair(kv_0), cores(q_0), cores(kv_0)
    gate_0 = fsdp(tied(halves(halves(w_gate, 0, low_batch), 1, core), out_0))
    q_3, kv_3 = cores(q_1), cores(kv_1)
    q_weight = from_pieces(w_query, (q_0, q_1, q_2, q_3), mine, core, low_batch)
    held = joined(kv_0, kv_1, 0, low_batch)
    other = joined(kv_2, kv_3, 0, low_batch)
    k_oth, v_oth = jnp.where(core == 0, held, other), jnp.where(core == 0, other, held)
    qkv_weights = (q_weight, (key_weight, k_oth), (value_weight, v_oth))

    positions = (spot * rows + jnp.arange(rows, dtype=jnp.int32)).astype(F32)
    frequency = jnp.exp(
        jnp.arange(HEAD_DIM // 2, dtype=F32) * (-2.0 * math.log(10000.0) / HEAD_DIM)
    )
    angles = frequency[:, None] * positions[None, :]
    tables = (jnp.cos(angles), jnp.sin(angles))

    def to_attention(x):
        normed, qkv = project(info, x, gains[0], qkv_weights, tables)
        kv = qkv[QUERY_HEADS * HEAD_DIM :]
        if devices == 2:
            past = cores(kv)[None]
        else:
            past = lax.all_gather(kv, "seq")
        return normed, qkv, past

    low_normed, low_qkv, low_past = to_attention(start_in)
    ready = (low_qkv, gate_0)
    up_0 = fsdp(tied(halves(halves(w_up, 0, low_batch), 1, core), ready))
    down_0 = fsdp(tied(halves(halves(w_down, 0, low_batch), 0, core), ready))
    out_1, out_2 = pair(tied(out_0, (q_1, kv_1))), cores(out_0)
    gate_1, gate_2 = pair(tied(gate_0, (low_qkv, out_1))), cores(gate_0)
    out_3 = cores(out_1)
    out_weight = from_pieces(w_out, (out_0, out_1, out_2, out_3), mine, core, low_batch)
    low_mixed, low_lse = attend(info, low_qkv, tied(low_past, out_weight))
    low_mixed = tied(low_mixed, (up_0, down_0, gate_1))
    gate_3, up_1, up_2 = cores(gate_1), pair(tied(up_0, low_mixed)), cores(up_0)
    low_middle, low_normed_ffn = mix(info, start_in, low_mixed, out_weight, gains[1])
    up_3 = cores(tied(up_1, low_middle))
    down_1, down_2 = pair(tied(down_0, (up_1, low_middle))), cores(tied(down_0, low_middle))
    low_hidden, low_silu, low_slope, gate, up = expand_first(
        info,
        low_normed_ffn,
        (w_gate, gate_0, gate_1, gate_2, gate_3),
        (w_up, up_0, up_1, up_2, up_3),
    )
    down_3 = cores(tied(down_1, low_hidden))
    middle_in, down = shrink_first(
        info, low_middle, low_hidden, (w_down, down_0, down_1, down_2, down_3)
    )

    high_normed, high_qkv, high_past = to_attention(middle_in)
    high_mixed, high_lse = attend(info, high_qkv, high_past)
    high_middle, high_normed_ffn = mix(info, middle_in, high_mixed, out_weight, gains[1])
    high_hidden, high_silu, high_slope = expand(info, high_normed_ffn, gate, up)

    def attention_back(qkv, past, mixed_grad, mixed, lse, base, heads):
        q_grad, own_grad, past_grad = attend_back(
            info, qkv, past, mixed_grad, mixed, lse, tables, base, heads
        )
        if devices == 2:
            return q_grad, own_grad, cores(past_grad[0])
        return q_grad, own_grad, lax.psum_scatter(past_grad, "seq", scatter_dimension=0)

    def to_input(x, grad_middle, parts):
        return project_back(
            info, x, gains[0], grad_middle, *zip(*parts), qkv_weights, tables
        )

    high_gate, high_up, high_branch, grad_middle, high_attn, mixed_grad, high_ffn_gain = ffn_back(
        info, incoming, high_middle, gains[1], high_silu, high_slope, down, gate, up, out_weight
    )
    parts = [
        attention_back(high_qkv, high_past, mixed_grad, high_mixed, high_lse, base, heads)
        for base, heads in ((0, 3), (3, 2))
    ]
    high_q, high_kv, grad_between, low_branch, high_attn_gain = to_input(
        middle_in, grad_middle, parts
    )

    def with_core(kept, arrived):
        both = kept.astype(F32) + arrived.astype(F32)
        return both[0].astype(BF16), both[1]

    down_away, down_kept = outer(info, (high_branch, high_hidden, low_branch, low_hidden), True)
    down_core = cores(down_away)
    final_out = shrink(info, tied(high_middle, down_away), high_hidden, down, BF16)
    grad_between, down_core = tied((grad_between, down_core), final_out)
    down_chain = Chain(*with_core(down_kept, down_core))
    grad_between, down_chain.sent = tied((grad_between, down_chain.sent), ())
    grad_between = tied(grad_between, down_chain.sent)
    low_gate, low_up, _, grad_middle, low_attn, mixed_grad, low_ffn_gain = ffn_back(
        info, grad_between, low_middle, gains[1], low_silu, low_slope, down, gate, up, out_weight
    )
    gate_away, gate_kept = outer(info, (high_normed_ffn, high_gate, low_normed_ffn, low_gate), False)
    gate_core = cores(gate_away)
    down_y = down_chain.step()
    low_up = tied(low_up, (down_y, gate_away))
    up_away, up_kept = outer(info, (high_normed_ffn, high_up, low_normed_ffn, low_up), False)
    down_x = down_chain.step()
    up_core = cores(up_away)
    low_attn, gate_core = tied((low_attn, gate_core), (up_away, gate_core))
    gate_chain = Chain(*with_core(gate_kept, gate_core))
    low_attn = tied(low_attn, gate_chain.sent)
    out_away, out_kept = pack(info, high_mixed, low_mixed, (high_attn, low_attn))
    out_core = cores(out_away)
    mixed_grad = tied(mixed_grad, (out_away, down_x, up_core))
    up_chain = Chain(*with_core(up_kept, up_core))
    parts = []

    def low_part(base, heads):
        parts.append(
            attention_back(low_qkv, low_past, mixed_grad, low_mixed, low_lse, base, heads)
        )
        return parts[-1][0]

    gate_y = gate_chain.step()
    down_z = down_chain.step()
    grown = low_part(0, 2)
    mixed_grad = tied(mixed_grad, (grown, down_z, out_core))
    out_chain = Chain(*with_core(out_kept, out_core))
    down_z = down_chain.step((grown,))
    grown = low_part(2, 2)
    mixed_grad = tied(mixed_grad, (grown, down_z, gate_y))
    up_y = up_chain.step((gate_y,))
    gate_x = gate_chain.step()
    down_z = down_chain.step((grown,))
    grown = low_part(4, 1)
    grad_middle = tied(grad_middle, (grown, down_z))
    down_z = down_chain.step((grown,))
    low_q, low_kv, grad_start, _, low_attn_gain = to_input(start_in, grad_middle, parts)
    low_q = tied(low_q, (low_kv, gate_x, down_z, up_y))
    gate_z = gate_chain.step((low_kv,))
    down_x = down_chain.step((gate_x,))
    qkv_away, qkv_kept = pack(info, high_normed, low_normed, (high_q, low_q, high_kv, low_kv))
    qkv_core = cores(qkv_away)
    qkv_chain = Chain(*with_core(qkv_kept, qkv_core))
    out_y = out_chain.step((low_kv, up_y))
    qkv_y = qkv_chain.step((out_y,))
    up_x = up_chain.step((down_x,))
    gate_z = gate_chain.step((gate_z,))
    down_grad = down_chain.finish()
    gate_z = gate_chain.step()
    gate_z = gate_chain.step()
    up_z = up_chain.step((gate_z,))
    qkv_x = qkv_chain.step((up_x,))
    up_z = up_chain.step()
    qkv_z = qkv_chain.step()
    gate_x = gate_chain.step((qkv_x,))
    qkv_z = qkv_chain.step((up_z,))
    up_z = up_chain.step()
    qkv_z = qkv_chain.step()
    up_z = up_chain.step()
    qkv_z = qkv_chain.step()
    out_x = out_chain.step((gate_x,))
    up_x = up_chain.step((out_x,))
    out_chain.step()
    qkv_x = qkv_chain.step((up_x,))
    out_chain.step()
    out_chain.step()
    out_chain.step()
    out_chain.step((qkv_x,))
    gate_grad, up_grad = gate_chain.finish(), up_chain.finish()
    qkv_grad, out_grad = qkv_chain.finish(), out_chain.finish()
    gain_grads = jnp.stack(
        [(high_attn_gain + low_attn_gain)[:, 0], (high_ffn_gain + low_ffn_gain)[:, 0]]
    )
    for axis in ("seq", "fsdp", "batch"):
        for bit in bits_of(axis):
            gain_grads = gain_grads + swap(gain_grads, axis, bit)
    gain_grads = halves(gain_grads, 1, mine)
    narrow = KEY_HEADS * HEAD_DIM
    query_part, key_part, value_part = jnp.split(qkv_grad, [width, width + narrow], 1)
    return (
        final_out.T[None],
        grad_start.T[None],
        gain_grads[0],
        query_part,
        key_part,
        value_part,
        out_grad,
        gain_grads[1],
        gate_grad,
        up_grad,
        down_grad.T,
    )


def solution(mesh):
    return jax.shard_map(
        per_device,
        mesh=mesh,
        in_specs=(
            P(("batch", "fsdp"), "seq", None),
            P("fsdp"),
            P("fsdp", None),
            P("fsdp", None),
            P("fsdp", None),
            P("fsdp", None),
            P("fsdp"),
            P("fsdp", None),
            P("fsdp", None),
            P("fsdp", None),
            P(("batch", "fsdp"), "seq", None),
        ),
        out_specs=(
            P(("batch", "fsdp"), "seq", None),
            P(("batch", "fsdp"), "seq", None),
            P("fsdp"),
            P("fsdp", None),
            P("fsdp", None),
            P("fsdp", None),
            P("fsdp", None),
            P("fsdp"),
            P("fsdp", None),
            P("fsdp", None),
            P("fsdp", None),
        ),
        check_vma=False,
    )
```

```python
import functools
import math

import jax
import jax.numpy as jnp
from jax import lax
from jax.experimental import pallas as pl
from jax.experimental.pallas import tpu as pltpu
from jax.sharding import PartitionSpec as P

QUERY_HEADS = 15
KEY_HEADS = 5
HEAD_DIM = 64
GROUP = QUERY_HEADS // KEY_HEADS
EPSILON = 1e-05
F32 = jnp.float32
BF16 = jnp.bfloat16


def dot(left, right, left_dim, right_dim):
    return lax.dot_general(
        left, right, (((left_dim,), (right_dim,)), ((), ())), preferred_element_type=F32
    )


def spans(total, size):
    return [(start, min(size, total - start)) for start in range(0, total, size)]


COSTS = {
    "project": 6.0,
    "attend": 20.0,
    "mix": 5.5,
    "expand": 10.0,
    "expand_first": 14.0,
    "shrink": 6.5,
    "shrink_first": 8.0,
    "ffn_back": 18.0,
    "attend_back": 6.5,
    "project_back": 9.5,
    "outer": 10.0,
    "pack": 7.0,
}


LIMITS = {
    "project": 12,
    "attend": 14,
    "mix": 12,
    "expand": 24,
    "expand_first": 34,
    "shrink": 22,
    "shrink_first": 34,
    "ffn_back": 40,
    "attend_back": 16,
    "project_back": 16,
    "outer": 26,
    "pack": 20,
}


def call(kernel, name, grid, in_specs, out_specs, out_shape, scratch=()):
    cost = int(COSTS[name] * 0.45e9 * (grid[0] if name == "attend_back" else 1))
    options = dict(
        name=name,
        out_shape=out_shape,
        compiler_params=pltpu.CompilerParams(vmem_limit_bytes=LIMITS[name] * 1024 * 1024),
        cost_estimate=pl.CostEstimate(flops=cost, bytes_accessed=1, transcendentals=0),
    )
    if name in ("project", "mix", "project_back", "pack"):
        memory = pl.BlockSpec(memory_space=pltpu.VMEM)
        return pl.pallas_call(
            kernel,
            in_specs=[pl.BlockSpec(memory_space=pltpu.SMEM)] + [memory] * len(in_specs),
            out_specs=[memory] * len(out_specs),
            scratch_shapes=list(scratch),
            **options,
        )
    return pl.pallas_call(
        kernel,
        grid_spec=pltpu.PrefetchScalarGridSpec(
            num_scalar_prefetch=1,
            grid=grid,
            in_specs=in_specs,
            out_specs=out_specs,
            scratch_shapes=list(scratch),
        ),
        **options,
    )


def whole(shape):
    return pl.BlockSpec(shape, lambda *_: (0,) * len(shape))


def shaped(shape, dtype):
    return jax.ShapeDtypeStruct(shape, dtype)


def scale_of(values):
    return lax.rsqrt(jnp.mean(values * values, 0, keepdims=True) + EPSILON)


def norm_back(values, gain, incoming):
    scales = scale_of(values)
    weighted = gain * incoming
    inner = jnp.mean(values * weighted, 0, keepdims=True)
    grad = scales * weighted - values * (scales * scales * scales * inner)
    return grad, jnp.sum(incoming * values * scales, 1, keepdims=True)


def rotate(values, cosine, sine):
    half = HEAD_DIM // 2
    first, second = values[:half], values[half:]
    return first * cosine - second * sine, second * cosine + first * sine


def project_kernel(
    info, x, gain, q_weight, k_own, k_oth, v_own, v_oth, cosine, sine, normed, out
):
    width = x.shape[0]
    half = width // 2
    values = x[...].astype(F32)
    normed[...] = (values * scale_of(values) * gain[...]).astype(BF16)
    own = normed[pl.ds(pl.multiple_of(info[0] * half, half), half), :]
    oth = normed[pl.ds(pl.multiple_of((1 - info[0]) * half, half), half), :]
    cos, sin = cosine[...], sine[...]
    hd = HEAD_DIM

    def turned(rows, base, factor):
        for head in range(rows.shape[0] // hd):
            first, second = rotate(rows[head * hd : (head + 1) * hd], cos, sin)
            at = base + head * hd
            out[at : at + hd // 2, :] = (first * factor).astype(BF16)
            out[at + hd // 2 : at + hd, :] = (second * factor).astype(BF16)

    q_width = q_weight.shape[1]
    turned(dot(q_weight[...], normed[...], 0, 0), 0, hd**-0.5)
    kv = k_own.shape[0]
    turned(dot(k_own[...], own, 1, 0) + dot(k_oth[...], oth, 1, 0), q_width, 1.0)
    rows = dot(v_own[...], own, 1, 0) + dot(v_oth[...], oth, 1, 0)
    out[q_width + kv : q_width + 2 * kv, :] = rows.astype(BF16)


def project(info, x, gain, weights, tables):
    width, rows = x.shape
    q, k, v = weights
    total = q.shape[1] + 2 * k[0].shape[0]
    operands = (x, gain, q, *k, *v, *tables)
    return call(
        project_kernel,
        "project",
        (1,),
        [whole(item.shape) for item in operands],
        [whole((width, rows)), whole((total, rows))],
        [shaped((width, rows), BF16), shaped((total, rows), BF16)],
    )(info, *operands)


def scores_of(keys, queries, masked):
    scores = dot(keys, queries, 1, 0)
    if not masked:
        return scores
    key_row = lax.broadcasted_iota(jnp.int32, scores.shape, 0)
    query_row = lax.broadcasted_iota(jnp.int32, scores.shape, 1)
    return jnp.where(key_row <= query_row, scores, -1e30)


def attend_kernel(
    info, q, k_own, v_own, k_past, v_past, out, lse, keys_own, keys_past, peak, total, mixed
):
    rows = q.shape[1]
    block = min(256, rows)
    hd = HEAD_DIM
    groups = [(group, slice(group * hd, (group + 1) * hd)) for group in range(GROUP)]
    keys_own[...] = k_own[...].T

    @pl.loop(0, info[1])
    def _(device):
        keys_past[device] = k_past[device].T

    for start in range(0, rows, block):
        for group, head in groups:
            scores = scores_of(keys_own[start : start + block, :], q[head, start:], True)
            fresh = jnp.max(scores, 0, keepdims=True)
            if start > 0:
                fresh = jnp.maximum(fresh, peak[group : group + 1, start:])
            peak[group : group + 1, start:] = fresh

    @pl.loop(0, info[1])
    def _(device):
        for group, head in groups:
            scores = scores_of(keys_past[device], q[head, :], False)
            peak[group : group + 1, :] = jnp.maximum(
                peak[group : group + 1, :], jnp.max(scores, 0, keepdims=True)
            )

    def add(group, head, keys, values, start, masked, first):
        scores = scores_of(keys, q[head, start:], masked)
        exponent = jnp.exp(scores - peak[group : group + 1, start:])
        sums = jnp.sum(exponent, 0, keepdims=True)
        product = dot(values, exponent.astype(BF16), 1, 0)
        if first:
            total[group : group + 1, :] = sums
            mixed[head, :] = product
        else:
            total[group : group + 1, start:] += sums
            mixed[head, start:] += product

    for start in range(0, rows, block):
        part = slice(start, start + block)
        for group, head in groups:
            add(group, head, keys_own[part, :], v_own[:, part], start, True, start == 0)

    @pl.loop(0, info[1])
    def _(device):
        for group, head in groups:
            add(group, head, keys_past[device], v_past[device], 0, False, False)

    for group, head in groups:
        sums = total[group : group + 1, :]
        out[head, :] = (mixed[head, :] / sums).astype(BF16)
        lse[0, group : group + 1, :] = peak[group : group + 1, :] + jnp.log(sums)


def attention_specs(rows, past, base):
    hd = HEAD_DIM
    return [
        pl.BlockSpec((GROUP * hd, rows), lambda h, info: (base + h, 0)),
        pl.BlockSpec((hd, rows), lambda h, info: (QUERY_HEADS + base + h, 0)),
        pl.BlockSpec((hd, rows), lambda h, info: (QUERY_HEADS + KEY_HEADS + base + h, 0)),
        pl.BlockSpec((past, hd, rows), lambda h, info: (0, base + h, 0)),
        pl.BlockSpec((past, hd, rows), lambda h, info: (0, KEY_HEADS + base + h, 0)),
    ]


def attend(info, qkv, past):
    rows = qkv.shape[1]
    count = past.shape[0]
    return call(
        attend_kernel,
        "attend",
        (KEY_HEADS,),
        attention_specs(rows, count, 0),
        [
            pl.BlockSpec((GROUP * HEAD_DIM, rows), lambda h, info: (h, 0)),
            pl.BlockSpec((1, 8, rows), lambda h, info: (h, 0, 0)),
        ],
        [shaped((QUERY_HEADS * HEAD_DIM, rows), BF16), shaped((KEY_HEADS, 8, rows), F32)],
        [
            pltpu.VMEM((rows, HEAD_DIM), BF16),
            pltpu.VMEM((count, rows, HEAD_DIM), BF16),
            pltpu.VMEM((8, rows), F32),
            pltpu.VMEM((8, rows), F32),
            pltpu.VMEM((GROUP * HEAD_DIM, rows), F32),
        ],
    )(info, qkv, qkv, qkv, past, past)


def mix_kernel(info, x, mixed, weight, gain, middle, normed):
    middle[...] = x[...].astype(F32) + dot(weight[...], mixed[...], 0, 0)
    values = middle[...]
    normed[...] = (values * scale_of(values) * gain[...]).astype(BF16)


def mix(info, x, mixed, weight, gain):
    width, rows = x.shape
    operands = (x, mixed, weight, gain)
    return call(
        mix_kernel,
        "mix",
        (1,),
        [whole(item.shape) for item in operands],
        [whole((width, rows)), whole((width, rows))],
        [shaped((width, rows), F32), shaped((width, rows), BF16)],
    )(info, *operands)


def activate(token_rows, gate_weight, up_weight, hidden, silu, slope):
    gate = dot(token_rows[...], gate_weight[...], 1, 0)
    up = dot(token_rows[...], up_weight[...], 1, 0)
    sigmoid = 0.5 * jnp.tanh(0.5 * gate) + 0.5
    active = gate * sigmoid
    hidden[...] = (active * up).astype(BF16)
    silu[...] = active.astype(BF16)
    slope[...] = (up * (sigmoid + active * (1.0 - sigmoid))).astype(BF16)


def expand_kernel(info, normed, gate_weight, up_weight, hidden, silu, slope, token_rows):
    @pl.when(pl.program_id(0) == 0)
    def _():
        token_rows[...] = normed[...].T

    activate(token_rows, gate_weight, up_weight, hidden, silu, slope)


def expand(info, normed, gate, up):
    width, rows = normed.shape
    ff = gate.shape[1]
    tile = ff // 5
    weight = pl.BlockSpec((width, tile), lambda t, info: (0, t))
    result = pl.BlockSpec((rows, tile), lambda t, info: (0, t))
    return call(
        expand_kernel,
        "expand",
        (ff // tile,),
        [whole((width, rows)), weight, weight],
        [result] * 3,
        [shaped((rows, ff), BF16)] * 3,
        [pltpu.VMEM((rows, width), BF16)],
    )(info, normed, gate, up)


def expand_first_kernel(info, normed, *refs):
    gate_parts, up_parts = refs[:5], refs[5:10]
    hidden, silu, slope, gate_weight, up_weight, token_rows = refs[10:]
    step = pl.program_id(0)
    steps = pl.num_programs(0)

    @pl.when(step == 0)
    def _():
        token_rows[...] = normed[...].T

    for (own, *pieces), target in ((gate_parts, gate_weight), (up_parts, up_weight)):
        half, quarter = own.shape[0], pieces[0].shape[0]
        target[pl.ds(pl.multiple_of(info[0] * half, half), half), :] = own[...]
        other = (1 - info[0]) * half
        near = pl.ds(pl.multiple_of(other + info[3] * quarter, quarter), quarter)
        far = pl.ds(pl.multiple_of(other + (1 - info[3]) * quarter, quarter), quarter)

        @pl.when(step < steps // 2)
        def _():
            target[near, :] = pieces[0][...]
            target[far, :] = pieces[1][...]

        @pl.when(step >= steps // 2)
        def _():
            target[near, :] = pieces[2][...]
            target[far, :] = pieces[3][...]

    activate(token_rows, gate_weight, up_weight, hidden, silu, slope)


def expand_first(info, normed, gate, up):
    width, rows = normed.shape
    half, ff = gate[0].shape
    steps = 4
    tile = ff // steps
    quarter = half // 2

    def column(t, info):
        own = info[2] * (steps // 2) + t
        return jnp.where(t < steps // 2, own, (1 - info[2]) * (steps // 2) + t - steps // 2)

    early = pl.BlockSpec((quarter, tile), lambda t, info: (0, jnp.minimum(t, steps // 2 - 1)))
    late = pl.BlockSpec((quarter, tile), lambda t, info: (0, jnp.maximum(t - steps // 2, 0)))
    parts = [pl.BlockSpec((half, tile), lambda t, info: (0, column(t, info)))]
    parts += [early, early, late, late]
    result = pl.BlockSpec((rows, tile), lambda t, info: (0, column(t, info)))
    weight = pl.BlockSpec((width, tile), lambda t, info: (0, column(t, info)))
    return call(
        expand_first_kernel,
        "expand_first",
        (steps,),
        [whole((width, rows))] + parts * 2,
        [result] * 3 + [weight] * 2,
        [shaped((rows, ff), BF16)] * 3 + [shaped((width, ff), BF16)] * 2,
        [pltpu.VMEM((rows, width), BF16)],
    )(info, normed, *gate, *up)


def shrink_kernel(info, middle, hidden, weight, out):
    out[...] = (middle[...] + dot(weight[...], hidden[...], 1, 1)).astype(out.dtype)


def shrink(info, middle, hidden, down, dtype):
    width, rows = middle.shape
    ff = hidden.shape[1]
    tile = width // 2
    return call(
        shrink_kernel,
        "shrink",
        (width // tile,),
        [
            pl.BlockSpec((tile, rows), lambda t, info: (t, 0)),
            whole((rows, ff)),
            pl.BlockSpec((tile, ff), lambda t, info: (t, 0)),
        ],
        [pl.BlockSpec((tile, rows), lambda t, info: (t, 0))],
        [shaped((width, rows), dtype)],
    )(info, middle, hidden, down)[0]


def shrink_first_kernel(info, middle, hidden, own, near_0, far_0, near_1, far_1, out, weight):
    half, quarter = own.shape[1], near_0.shape[0]
    weight[:, pl.ds(pl.multiple_of(info[0] * half, half), half)] = own[...]
    other = pl.ds(pl.multiple_of((1 - info[0]) * half, half), half)
    at_near = pl.ds(pl.multiple_of(info[2] * quarter, quarter), quarter)
    at_far = pl.ds(pl.multiple_of((1 - info[2]) * quarter, quarter), quarter)
    for step, near, far in ((0, near_0, far_0), (1, near_1, far_1)):

        @pl.when(pl.program_id(0) == step)
        def _():
            weight[at_near, other] = near[...]
            weight[at_far, other] = far[...]

    out[...] = middle[...] + dot(weight[...], hidden[...], 1, 1)


def shrink_first(info, middle, hidden, parts):
    width, rows = middle.shape
    ff = hidden.shape[1]
    tile = width // 2
    own, first, second, third, fourth = parts

    def row(t, info):
        return jnp.where(t == 0, info[3], 1 - info[3])

    return call(
        shrink_first_kernel,
        "shrink_first",
        (2,),
        [
            pl.BlockSpec((tile, rows), lambda t, info: (row(t, info), 0)),
            whole((rows, ff)),
            pl.BlockSpec((tile, ff // 2), lambda t, info: (row(t, info), 0)),
        ]
        + [whole(first.shape)] * 4,
        [
            pl.BlockSpec((tile, rows), lambda t, info: (row(t, info), 0)),
            pl.BlockSpec((tile, ff), lambda t, info: (row(t, info), 0)),
        ],
        [shaped((width, rows), F32), shaped((width, ff), BF16)],
    )(info, middle, hidden, own, first, third, second, fourth)


def ffn_back_kernel(
    info,
    grad,
    middle,
    gain,
    silu,
    slope,
    down,
    gate,
    up,
    out_weight,
    gate_grad,
    up_grad,
    branch,
    grad_middle,
    attn_grad,
    mixed_grad,
    gain_grad,
    branch_rows,
    total,
):
    step = pl.program_id(0)
    steps = pl.num_programs(0)

    @pl.when(step == 0)
    def _():
        branch[...] = grad[...].astype(BF16)
        branch_rows[...] = branch[...].T
        total[...] = jnp.zeros_like(total)

    incoming = dot(branch_rows[...], down[...], 1, 0)
    gate_grad[...] = (incoming * slope[...].astype(F32)).astype(BF16)
    up_grad[...] = (incoming * silu[...].astype(F32)).astype(BF16)
    total[...] += dot(gate[...], gate_grad[...], 1, 1) + dot(up[...], up_grad[...], 1, 1)

    @pl.when(step == steps - 1)
    def _():
        back, gain_sum = norm_back(middle[...], gain[...], total[...])
        gain_grad[...] = gain_sum
        result = grad[...].astype(F32) + back
        grad_middle[...] = result
        attn_grad[...] = result.astype(BF16)
        mixed_grad[...] = dot(out_weight[...], attn_grad[...], 1, 0).astype(BF16)


def ffn_back(info, grad, middle, gain, silu, slope, down, gate, up, out_weight):
    width, rows = middle.shape
    ff = silu.shape[1]
    tile = ff // 5
    heads = out_weight.shape[0]
    token = pl.BlockSpec((rows, tile), lambda t, info: (0, t))
    weight = pl.BlockSpec((width, tile), lambda t, info: (0, t))
    return call(
        ffn_back_kernel,
        "ffn_back",
        (ff // tile,),
        [
            whole((width, rows)),
            whole((width, rows)),
            whole((width, 1)),
            token,
            token,
            weight,
            weight,
            weight,
            whole((heads, width)),
        ],
        [
            token,
            token,
            whole((width, rows)),
            whole((width, rows)),
            whole((width, rows)),
            whole((heads, rows)),
            whole((width, 1)),
        ],
        [
            shaped((rows, ff), BF16),
            shaped((rows, ff), BF16),
            shaped((width, rows), BF16),
            shaped((width, rows), F32),
            shaped((width, rows), BF16),
            shaped((heads, rows), BF16),
            shaped((width, 1), F32),
        ],
        [pltpu.VMEM((rows, width), BF16), pltpu.VMEM((width, rows), F32)],
    )(info, grad, middle, gain, silu, slope, down, gate, up, out_weight)


def attend_back_kernel(
    info,
    q,
    k_own,
    v_own,
    k_past,
    v_past,
    mixed_grad,
    mixed,
    lse,
    cosine,
    sine,
    q_grad,
    own_grad,
    past_grad,
    keys_own,
    values_own,
    keys_past,
    values_past,
    inner,
    q_sum,
):
    rows = q.shape[1]
    block = min(256, rows)
    hd = HEAD_DIM
    groups = [(group, slice(group * hd, (group + 1) * hd)) for group in range(GROUP)]
    keys_own[...] = k_own[...].T
    values_own[...] = v_own[...].T

    @pl.loop(0, info[1])
    def _(device):
        keys_past[device] = k_past[device].T
        values_past[device] = v_past[device].T

    @pl.loop(info[1], past_grad.shape[0])
    def _(device):
        past_grad[device] = jnp.zeros_like(past_grad[device])

    for group, head in groups:
        product = mixed_grad[head, :].astype(F32) * mixed[head, :].astype(F32)
        inner[group : group + 1, :] = jnp.sum(product, 0, keepdims=True)

    def step(keys, key_rows, value_rows, start, masked, first):
        key_sum = value_sum = None
        for group, head in groups:
            query, incoming = q[head, start:], mixed_grad[head, start:]
            one = slice(group, group + 1)
            probs = jnp.exp(scores_of(key_rows, query, masked) - lse[0, one, start:])
            slopes = dot(value_rows, incoming, 1, 0)
            low = (probs * (slopes - inner[one, start:])).astype(BF16)
            value_part = dot(incoming, probs.astype(BF16), 1, 1)
            key_part = dot(query, low, 1, 1)
            key_sum = key_part if key_sum is None else key_sum + key_part
            value_sum = value_part if value_sum is None else value_sum + value_part
            query_part = dot(keys, low, 1, 0)
            if first:
                q_sum[head, :] = query_part
            else:
                q_sum[head, start:] += query_part
        return key_sum, value_sum

    for start in range(0, rows, block):
        part = slice(start, start + block)
        key_sum, value_sum = step(
            k_own[:, part], keys_own[part, :], values_own[part, :], start, True, start == 0
        )
        own_grad[0, :hd, part] = key_sum
        own_grad[0, hd:, part] = value_sum

    @pl.loop(0, info[1])
    def _(device):
        key_sum, value_sum = step(
            k_past[device], keys_past[device], values_past[device], 0, False, False
        )
        past_grad[device, 0, :hd, :] = key_sum.astype(past_grad.dtype)
        past_grad[device, 0, hd:, :] = value_sum.astype(past_grad.dtype)

    cos, sin = cosine[...], -sine[...]
    for group, head in groups:
        first, second = rotate(q_sum[head, :], cos, sin)
        at = group * hd
        q_grad[at : at + hd // 2, :] = (first * hd**-0.5).astype(BF16)
        q_grad[at + hd // 2 : at + hd, :] = (second * hd**-0.5).astype(BF16)


def attend_back(info, qkv, past, mixed_grad, mixed, lse, tables, base, heads):
    rows = qkv.shape[1]
    count = past.shape[0]
    hd = HEAD_DIM
    group = pl.BlockSpec((GROUP * hd, rows), lambda h, info: (base + h, 0))
    return call(
        attend_back_kernel,
        "attend_back",
        (heads,),
        attention_specs(rows, count, base)
        + [
            group,
            group,
            pl.BlockSpec((1, 8, rows), lambda h, info: (base + h, 0, 0)),
            whole(tables[0].shape),
            whole(tables[1].shape),
        ],
        [
            pl.BlockSpec((GROUP * hd, rows), lambda h, info: (h, 0)),
            pl.BlockSpec((1, 2 * hd, rows), lambda h, info: (h, 0, 0)),
            pl.BlockSpec((count, 1, 2 * hd, rows), lambda h, info: (0, h, 0, 0)),
        ],
        [
            shaped((heads * GROUP * hd, rows), BF16),
            shaped((heads, 2 * hd, rows), F32),
            shaped((count, heads, 2 * hd, rows), BF16 if count == 1 else F32),
        ],
        [
            pltpu.VMEM((rows, hd), BF16),
            pltpu.VMEM((rows, hd), BF16),
            pltpu.VMEM((count, rows, hd), BF16),
            pltpu.VMEM((count, rows, hd), BF16),
            pltpu.VMEM((8, rows), F32),
            pltpu.VMEM((GROUP * hd, rows), F32),
        ],
    )(info, qkv, qkv, qkv, past, past, mixed_grad, mixed, lse, *tables)


def project_back_kernel(parts, info, x, gain, grad_middle, *refs):
    q_grads, own_grads, arrived = refs[:parts], refs[parts : 2 * parts], refs[2 * parts : 3 * parts]
    (
        q_weight,
        k_own,
        k_oth,
        v_own,
        v_oth,
        cosine,
        sine,
        q_grad,
        kv_grad,
        out,
        branch,
        gain_grad,
        total,
    ) = refs[3 * parts :]
    half = x.shape[0] // 2
    hd = HEAD_DIM
    kv = KEY_HEADS * hd
    cos, sin = cosine[...], -sine[...]
    head = 0
    for piece, own, far in zip(q_grads, own_grads, arrived):
        q_grad[head * GROUP * hd : head * GROUP * hd + piece.shape[0], :] = piece[...]
        for item in range(own.shape[0]):
            both = own[item] + far[item].astype(F32)
            first, second = rotate(both[:hd], cos, sin)
            at = head * hd
            kv_grad[at : at + hd // 2, :] = first.astype(BF16)
            kv_grad[at + hd // 2 : at + hd, :] = second.astype(BF16)
            kv_grad[kv + at : kv + at + hd, :] = both[hd:].astype(BF16)
            head += 1
    total[...] = dot(q_weight[...], q_grad[...], 1, 0)
    for mine, k, v in ((info[0], k_own, v_own), (1 - info[0], k_oth, v_oth)):
        total[pl.ds(pl.multiple_of(mine * half, half), half), :] += dot(
            k[...], kv_grad[:kv, :], 0, 0
        ) + dot(v[...], kv_grad[kv:, :], 0, 0)
    back, gain_sum = norm_back(x[...].astype(F32), gain[...], total[...])
    gain_grad[...] = gain_sum
    result = grad_middle[...] + back
    out[...] = result
    branch[...] = result.astype(BF16)


def project_back(info, x, gain, grad_middle, q_grads, own_grads, arrived, weights, tables):
    width, rows = x.shape
    q, k, v = weights
    heads = q.shape[1]
    kv = 2 * KEY_HEADS * HEAD_DIM
    operands = (x, gain, grad_middle, *q_grads, *own_grads, *arrived, q, *k, *v, *tables)
    shapes = [
        shaped((heads, rows), BF16),
        shaped((kv, rows), BF16),
        shaped((width, rows), F32),
        shaped((width, rows), BF16),
        shaped((width, 1), F32),
    ]
    return call(
        functools.partial(project_back_kernel, len(q_grads)),
        "project_back",
        (1,),
        [whole(item.shape) for item in operands],
        [whole(item.shape) for item in shapes],
        shapes,
        [pltpu.VMEM((width, rows), F32)],
    )(info, *operands)


def order_rows(info, target, sources):
    rows = sources[0].shape[1]
    size = target.shape[0] // 4
    at = 0
    for core in (1 - info[2], info[2]):
        for half in (1 - info[0], info[0]):
            start = pl.multiple_of((2 * half + core) * size, size)
            for index, source in enumerate(sources):
                target[at : at + size, index * rows : (index + 1) * rows] = source[
                    pl.ds(start, size), :
                ]
            at += size


def order_halves(info, target, sources):
    rows = sources[0].shape[1]
    size = target.shape[0] // 2
    for at, core in ((0, 1 - info[2]), (size, info[2])):
        start = pl.multiple_of(core * size, size)
        for index, source in enumerate(sources):
            target[at : at + size, index * rows : (index + 1) * rows] = source[pl.ds(start, size), :]


def outer_kernel(split_columns, info, left_a, right_a, left_b, right_b, sent, kept, left, right):
    rows = left_a.shape[1]

    @pl.when(pl.program_id(0) == 0)
    def _():
        order = order_halves if split_columns else order_rows
        order(info, left, (left_a, left_b))

    right[:rows, :] = right_a[...]
    right[rows:, :] = right_b[...]
    count, size = sent.shape[0], sent.shape[1]
    for at, out in ((0, sent), (count * size, kept)):
        product = dot(left[at : at + count * size, :], right[...], 1, 0).astype(BF16)
        for index in range(count):
            out[index] = product[index * size : (index + 1) * size]


def outer(info, parts, split_columns):
    left_a, right_a, left_b, right_b = parts
    width, rows = left_a.shape
    columns = right_a.shape[1]
    if split_columns:
        tile = columns // 4

        def column(t, info):
            return jnp.where(t < 2, (1 - info[0]) * 2 + t, info[0] * 2 + t - 2)

        right = pl.BlockSpec((rows, tile), lambda t, info: (0, column(t, info)))
        result = pl.BlockSpec((1, width // 2, tile), lambda t, info: (t // 2, 0, t % 2))
        shape = shaped((2, width // 2, columns // 2), BF16)
    else:
        tile = columns // 5
        right = pl.BlockSpec((rows, tile), lambda t, info: (0, t))
        result = pl.BlockSpec((2, width // 4, tile), lambda t, info: (0, 0, t))
        shape = shaped((2, width // 4, columns), BF16)
    return call(
        functools.partial(outer_kernel, split_columns),
        "outer",
        (columns // tile,),
        [whole((width, rows)), right, whole((width, rows)), right],
        [result, result],
        [shape, shape],
        [pltpu.VMEM((width, 2 * rows), BF16), pltpu.VMEM((2 * rows, tile), BF16)],
    )(info, *parts)


def pack_kernel(info, left_a, *refs):
    sent, kept, left, right = refs[-4:]
    left_b, rights_a, rights_b = refs[0], refs[1:-4:2], refs[2:-4:2]
    rows = left_a.shape[1]
    order_rows(info, left, (left_a, left_b))
    at = 0
    for right_a, right_b in zip(rights_a, rights_b):
        right[at : at + right_a.shape[0], :rows] = right_a[...]
        right[at : at + right_a.shape[0], rows:] = right_b[...]
        at += right_a.shape[0]
    count, size = sent.shape[0], sent.shape[1]
    for base, out in ((0, sent), (count * size, kept)):
        for start, span in spans(right.shape[0], 512):
            product = dot(left[base : base + count * size, :], right[start : start + span, :], 1, 1)
            for index in range(count):
                out[index, :, start : start + span] = product[
                    index * size : (index + 1) * size
                ].astype(BF16)


def pack(info, left_a, left_b, rights):
    width, rows = left_a.shape
    columns = sum(item.shape[0] for item in rights[::2])
    operands = (left_a, left_b, *rights)
    shape = shaped((2, width // 4, columns), BF16)
    return call(
        pack_kernel,
        "pack",
        (1,),
        [whole(item.shape) for item in operands],
        [whole(shape.shape)] * 2,
        [shape, shape],
        [pltpu.VMEM((width, 2 * rows), BF16), pltpu.VMEM((columns, 2 * rows), BF16)],
    )(info, *operands)


def swap(values, axis, bit):
    size = lax.axis_size(axis)
    return lax.ppermute(values, axis, [(i, i ^ bit) for i in range(size)])


def bits_of(axis):
    size = lax.axis_size(axis)
    assert size & (size - 1) == 0
    return [1 << i for i in range(size.bit_length() - 1)]


def high(axis, bit):
    return (lax.axis_index(axis) // bit) % 2


def halves(values, dim, which):
    half = values.shape[dim] // 2
    return lax.dynamic_slice_in_dim(values, which * half, half, dim)


def joined(mine, other, dim, which):
    return jnp.where(
        which == 0,
        jnp.concatenate([mine, other], dim),
        jnp.concatenate([other, mine], dim),
    )


def tied(values, others):
    return lax.optimization_barrier((values, others))[0]


def from_pieces(own, pieces, mine, core, low_batch):
    near = joined(pieces[0], pieces[2], 0, core)
    far = joined(pieces[1], pieces[3], 0, core)
    return joined(own, joined(near, far, 0, low_batch), 0, mine)


def split_dim(shape):
    if shape[0] % 16 == 0:
        return 0
    if shape[1] % 256 == 0:
        return 1
    return 0 if shape[0] % 2 == 0 else 1


def over_fsdp(values):
    return swap(values, "fsdp", 1)


class Chain:
    def __init__(self, sent, kept):
        self.sent, self.held, self.stages = sent, kept, []
        self.todo = [("fsdp", 1)]
        self.todo += [("seq", bit) for bit in bits_of("seq")[1:]]
        self.todo += [("batch", bit) for bit in bits_of("batch")]
        self.back = None

    def step(self, wait=()):
        if self.todo:
            axis, bit = self.todo.pop(0)
            if axis == "fsdp":
                arrived = swap(tied(self.sent, wait), axis, bit)
                self.held = self.held.astype(F32) + arrived.astype(F32)
                return arrived
            which = high(axis, bit)
            dim = split_dim(self.held.shape)
            low = self.held.astype(BF16)
            arrived = swap(tied(halves(low, dim, 1 - which), wait), axis, bit)
            self.held = halves(self.held, dim, which) + arrived.astype(F32)
            self.stages.append((axis, bit, dim, which))
            return arrived
        if self.back is None:
            self.held = self.held.astype(BF16)
            self.back = [("seq", 1, 0, high("seq", 1))] + self.stages
        axis, bit, dim, which = self.back.pop()
        arrived = swap(tied(self.held, wait), axis, bit)
        self.held = joined(self.held, arrived, dim, which)
        return arrived

    def finish(self):
        while self.back is None or self.back:
            self.step()
        return self.held.astype(F32)


def per_device(
    tokens,
    attn_gain,
    w_query,
    key_weight,
    value_weight,
    w_out,
    ffn_gain,
    w_gate,
    w_up,
    w_down,
    cotangent,
):
    assert tokens.shape[0] == 1 and lax.axis_size("fsdp") == 2
    mine, spot, core = lax.axis_index("fsdp"), lax.axis_index("seq"), high("seq", 1)
    low_batch = high("batch", 1)
    devices = lax.axis_size("seq")
    info = jnp.stack([mine, spot, core, low_batch]).astype(jnp.int32)
    start_in = tokens[0].T
    incoming = cotangent[0].T
    width, rows = start_in.shape

    gains = jnp.stack([attn_gain, ffn_gain])
    gains = joined(gains, swap(gains, "fsdp", 1), 1, mine).astype(F32)[..., None]
    key_weight, value_weight, w_down = key_weight.T, value_weight.T, w_down.T
    def fsdp(values):
        return swap(values, "fsdp", 1)

    def pair(values):
        return swap(values, "batch", 1)

    def cores(values):
        return swap(values, "seq", 1)

    q_piece = halves(halves(w_query, 0, low_batch), 0, core)
    kv_piece = halves(jnp.where(core == 0, key_weight, value_weight), 0, low_batch)
    q_0, kv_0 = fsdp(q_piece), fsdp(kv_piece)
    out_0 = fsdp(tied(halves(halves(w_out, 0, low_batch), 0, core), (q_0, kv_0)))
    q_1, kv_1, q_2, kv_2 = pair(q_0), pair(kv_0), cores(q_0), cores(kv_0)
    gate_0 = fsdp(tied(halves(halves(w_gate, 0, low_batch), 1, core), out_0))
    q_3, kv_3 = cores(q_1), cores(kv_1)
    q_weight = from_pieces(w_query, (q_0, q_1, q_2, q_3), mine, core, low_batch)
    held = joined(kv_0, kv_1, 0, low_batch)
    other = joined(kv_2, kv_3, 0, low_batch)
    k_oth, v_oth = jnp.where(core == 0, held, other), jnp.where(core == 0, other, held)
    qkv_weights = (q_weight, (key_weight, k_oth), (value_weight, v_oth))

    positions = (spot * rows + jnp.arange(rows, dtype=jnp.int32)).astype(F32)
    frequency = jnp.exp(
        jnp.arange(HEAD_DIM // 2, dtype=F32) * (-2.0 * math.log(10000.0) / HEAD_DIM)
    )
    angles = frequency[:, None] * positions[None, :]
    tables = (jnp.cos(angles), jnp.sin(angles))

    def to_attention(x):
        normed, qkv = project(info, x, gains[0], qkv_weights, tables)
        kv = qkv[QUERY_HEADS * HEAD_DIM :]
        if devices == 2:
            past = cores(kv)[None]
        else:
            past = lax.all_gather(kv, "seq")
        return normed, qkv, past

    low_normed, low_qkv, low_past = to_attention(start_in)
    ready = (low_qkv, gate_0)
    up_0 = fsdp(tied(halves(halves(w_up, 0, low_batch), 1, core), ready))
    down_0 = fsdp(tied(halves(halves(w_down, 0, low_batch), 0, core), ready))
    out_1, out_2 = pair(tied(out_0, (q_1, kv_1))), cores(out_0)
    gate_1, gate_2 = pair(tied(gate_0, (low_qkv, out_1))), cores(gate_0)
    out_3 = cores(out_1)
    out_weight = from_pieces(w_out, (out_0, out_1, out_2, out_3), mine, core, low_batch)
    low_mixed, low_lse = attend(info, low_qkv, tied(low_past, out_weight))
    low_mixed = tied(low_mixed, (up_0, down_0, gate_1))
    gate_3, up_1, up_2 = cores(gate_1), pair(tied(up_0, low_mixed)), cores(up_0)
    low_middle, low_normed_ffn = mix(info, start_in, low_mixed, out_weight, gains[1])
    up_3 = cores(tied(up_1, low_middle))
    down_1, down_2 = pair(tied(down_0, (up_1, low_middle))), cores(tied(down_0, low_middle))
    low_hidden, low_silu, low_slope, gate, up = expand_first(
        info,
        low_normed_ffn,
        (w_gate, gate_0, gate_1, gate_2, gate_3),
        (w_up, up_0, up_1, up_2, up_3),
    )
    down_3 = cores(tied(down_1, low_hidden))
    middle_in, down = shrink_first(
        info, low_middle, low_hidden, (w_down, down_0, down_1, down_2, down_3)
    )

    high_normed, high_qkv, high_past = to_attention(middle_in)
    high_mixed, high_lse = attend(info, high_qkv, high_past)
    high_middle, high_normed_ffn = mix(info, middle_in, high_mixed, out_weight, gains[1])
    high_hidden, high_silu, high_slope = expand(info, high_normed_ffn, gate, up)

    def attention_back(qkv, past, mixed_grad, mixed, lse, base, heads):
        q_grad, own_grad, past_grad = attend_back(
            info, qkv, past, mixed_grad, mixed, lse, tables, base, heads
        )
        if devices == 2:
            return q_grad, own_grad, cores(past_grad[0])
        return q_grad, own_grad, lax.psum_scatter(past_grad, "seq", scatter_dimension=0)

    def to_input(x, grad_middle, parts):
        return project_back(
            info, x, gains[0], grad_middle, *zip(*parts), qkv_weights, tables
        )

    high_gate, high_up, high_branch, grad_middle, high_attn, mixed_grad, high_ffn_gain = ffn_back(
        info, incoming, high_middle, gains[1], high_silu, high_slope, down, gate, up, out_weight
    )
    parts = [
        attention_back(high_qkv, high_past, mixed_grad, high_mixed, high_lse, base, heads)
        for base, heads in ((0, 3), (3, 2))
    ]
    high_q, high_kv, grad_between, low_branch, high_attn_gain = to_input(
        middle_in, grad_middle, parts
    )

    def with_core(kept, arrived):
        both = kept.astype(F32) + arrived.astype(F32)
        return both[0].astype(BF16), both[1]

    down_away, down_kept = outer(info, (high_branch, high_hidden, low_branch, low_hidden), True)
    down_core = cores(down_away)
    final_out = shrink(info, tied(high_middle, down_away), high_hidden, down, BF16)
    grad_between, down_core = tied((grad_between, down_core), final_out)
    down_chain = Chain(*with_core(down_kept, down_core))
    grad_between, down_chain.sent = tied((grad_between, down_chain.sent), ())
    grad_between = tied(grad_between, down_chain.sent)
    low_gate, low_up, _, grad_middle, low_attn, mixed_grad, low_ffn_gain = ffn_back(
        info, grad_between, low_middle, gains[1], low_silu, low_slope, down, gate, up, out_weight
    )
    gate_away, gate_kept = outer(info, (high_normed_ffn, high_gate, low_normed_ffn, low_gate), False)
    gate_core = cores(gate_away)
    down_y = down_chain.step()
    low_up = tied(low_up, (down_y, gate_away))
    up_away, up_kept = outer(info, (high_normed_ffn, high_up, low_normed_ffn, low_up), False)
    down_x = down_chain.step()
    up_core = cores(up_away)
    low_attn, gate_core = tied((low_attn, gate_core), (up_away, gate_core))
    gate_chain = Chain(*with_core(gate_kept, gate_core))
    low_attn = tied(low_attn, gate_chain.sent)
    out_away, out_kept = pack(info, high_mixed, low_mixed, (high_attn, low_attn))
    out_core = cores(out_away)
    mixed_grad = tied(mixed_grad, (out_away, down_x, up_core))
    up_chain = Chain(*with_core(up_kept, up_core))
    parts = []

    def low_part(base, heads):
        parts.append(
            attention_back(low_qkv, low_past, mixed_grad, low_mixed, low_lse, base, heads)
        )
        return parts[-1][0]

    gate_y = gate_chain.step()
    down_z = down_chain.step()
    grown = low_part(0, 2)
    mixed_grad = tied(mixed_grad, (grown, down_z, out_core))
    out_chain = Chain(*with_core(out_kept, out_core))
    down_z = down_chain.step((grown,))
    grown = low_part(2, 2)
    mixed_grad = tied(mixed_grad, (grown, down_z, gate_y))
    up_y = up_chain.step((gate_y,))
    gate_x = gate_chain.step()
    down_z = down_chain.step((grown,))
    grown = low_part(4, 1)
    grad_middle = tied(grad_middle, (grown, down_z))
    down_z = down_chain.step((grown,))
    low_q, low_kv, grad_start, _, low_attn_gain = to_input(start_in, grad_middle, parts)
    low_q = tied(low_q, (low_kv, gate_x, down_z, up_y))
    gate_z = gate_chain.step((low_kv,))
    down_x = down_chain.step((gate_x,))
    qkv_away, qkv_kept = pack(info, high_normed, low_normed, (high_q, low_q, high_kv, low_kv))
    qkv_core = cores(qkv_away)
    qkv_chain = Chain(*with_core(qkv_kept, qkv_core))
    out_y = out_chain.step((low_kv, up_y))
    qkv_y = qkv_chain.step((out_y,))
    up_x = up_chain.step((down_x,))
    gate_z = gate_chain.step((gate_z,))
    down_grad = down_chain.finish()
    gate_z = gate_chain.step()
    gate_z = gate_chain.step()
    up_z = up_chain.step((gate_z,))
    qkv_x = qkv_chain.step((up_x,))
    up_z = up_chain.step()
    qkv_z = qkv_chain.step()
    gate_x = gate_chain.step((qkv_x,))
    qkv_z = qkv_chain.step((up_z,))
    up_z = up_chain.step()
    qkv_z = qkv_chain.step()
    up_z = up_chain.step()
    qkv_z = qkv_chain.step()
    out_x = out_chain.step((gate_x,))
    up_x = up_chain.step((out_x,))
    out_chain.step()
    qkv_x = qkv_chain.step((up_x,))
    out_chain.step()
    out_chain.step()
    out_chain.step()
    out_chain.step((qkv_x,))
    gate_grad, up_grad = gate_chain.finish(), up_chain.finish()
    qkv_grad, out_grad = qkv_chain.finish(), out_chain.finish()
    gain_grads = jnp.stack(
        [(high_attn_gain + low_attn_gain)[:, 0], (high_ffn_gain + low_ffn_gain)[:, 0]]
    )
    for axis in ("seq", "fsdp", "batch"):
        for bit in bits_of(axis):
            gain_grads = gain_grads + swap(gain_grads, axis, bit)
    gain_grads = halves(gain_grads, 1, mine)
    narrow = KEY_HEADS * HEAD_DIM
    query_part, key_part, value_part = jnp.split(qkv_grad, [width, width + narrow], 1)
    return (
        final_out.T[None],
        grad_start.T[None],
        gain_grads[0],
        query_part,
        key_part,
        value_part,
        out_grad,
        gain_grads[1],
        gate_grad,
        up_grad,
        down_grad.T,
    )


def solution(mesh):
    return jax.shard_map(
        per_device,
        mesh=mesh,
        in_specs=(
            P(("batch", "fsdp"), "seq", None),
            P("fsdp"),
            P("fsdp", None),
            P("fsdp", None),
            P("fsdp", None),
            P("fsdp", None),
            P("fsdp"),
            P("fsdp", None),
            P("fsdp", None),
            P("fsdp", None),
            P(("batch", "fsdp"), "seq", None),
        ),
        out_specs=(
            P(("batch", "fsdp"), "seq", None),
            P(("batch", "fsdp"), "seq", None),
            P("fsdp"),
            P("fsdp", None),
            P("fsdp", None),
            P("fsdp", None),
            P("fsdp", None),
            P("fsdp"),
            P("fsdp", None),
            P("fsdp", None),
            P("fsdp", None),
        ),
        check_vma=False,
    )
```

```python
import functools
import math

import jax
import jax.numpy as jnp
from jax import lax
from jax.experimental import pallas as pl
from jax.experimental.pallas import tpu as pltpu
from jax.sharding import PartitionSpec as P

QUERY_HEADS = 15
KEY_HEADS = 5
HEAD_DIM = 64
GROUP = QUERY_HEADS // KEY_HEADS
EPSILON = 1e-05
F32 = jnp.float32
BF16 = jnp.bfloat16


def dot(left, right, left_dim, right_dim):
    return lax.dot_general(
        left, right, (((left_dim,), (right_dim,)), ((), ())), preferred_element_type=F32
    )


def spans(total, size):
    return [(start, min(size, total - start)) for start in range(0, total, size)]


COSTS = {
    "project": 3.0,
    "attend": 4.0,
    "mix": 2.4,
    "expand": 10.0,
    "expand_first": 14.0,
    "shrink": 6.5,
    "shrink_first": 8.0,
    "ffn_back": 18.0,
    "attend_back": 5.0,
    "project_back": 5.0,
    "outer": 8.0,
    "pack": 3.5,
}


LIMITS = {
    "project": 12,
    "attend": 14,
    "mix": 12,
    "expand": 24,
    "expand_first": 34,
    "shrink": 22,
    "shrink_first": 34,
    "ffn_back": 40,
    "attend_back": 16,
    "project_back": 16,
    "outer": 26,
    "pack": 20,
    "both_cores": 8,
}


def call(kernel, name, grid, in_specs, out_specs, out_shape, scratch=(), cost=None):
    if cost is None:
        cost = COSTS[name] * 0.45 * (grid[0] if name.startswith("attend") else 1)
    cost = int(cost * 1e9) + 1
    options = dict(
        name=name,
        out_shape=out_shape,
        compiler_params=pltpu.CompilerParams(vmem_limit_bytes=LIMITS[name] * 1024 * 1024),
        cost_estimate=pl.CostEstimate(flops=cost, bytes_accessed=1, transcendentals=0),
    )
    if name in ("project", "mix", "project_back", "pack", "both_cores"):
        memory = pl.BlockSpec(memory_space=pltpu.VMEM)
        return pl.pallas_call(
            kernel,
            in_specs=[pl.BlockSpec(memory_space=pltpu.SMEM)] + [memory] * len(in_specs),
            out_specs=[memory] * len(out_specs),
            scratch_shapes=list(scratch),
            **options,
        )
    return pl.pallas_call(
        kernel,
        grid_spec=pltpu.PrefetchScalarGridSpec(
            num_scalar_prefetch=1,
            grid=grid,
            in_specs=in_specs,
            out_specs=out_specs,
            scratch_shapes=list(scratch),
        ),
        **options,
    )


def whole(shape):
    return pl.BlockSpec(shape, lambda *_: (0,) * len(shape))


def shaped(shape, dtype):
    return jax.ShapeDtypeStruct(shape, dtype)


def scale_of(values):
    return lax.rsqrt(jnp.mean(values * values, 0, keepdims=True) + EPSILON)


def norm_back(values, gain, incoming):
    scales = scale_of(values)
    weighted = gain * incoming
    inner = jnp.mean(values * weighted, 0, keepdims=True)
    grad = scales * weighted - values * (scales * scales * scales * inner)
    return grad, jnp.sum(incoming * values * scales, 1, keepdims=True)


def rotate(values, cosine, sine):
    half = HEAD_DIM // 2
    first, second = values[:half], values[half:]
    return first * cosine - second * sine, second * cosine + first * sine


def project_kernel(
    info, x, gain, q_weight, k_own, k_oth, v_own, v_oth, cosine, sine, normed, out
):
    width = x.shape[0]
    half = width // 2
    values = x[...].astype(F32)
    normed[...] = (values * scale_of(values) * gain[...]).astype(BF16)
    own = normed[pl.ds(pl.multiple_of(info[0] * half, half), half), :]
    oth = normed[pl.ds(pl.multiple_of((1 - info[0]) * half, half), half), :]
    cos, sin = cosine[...], sine[...]
    hd = HEAD_DIM

    def turned(rows, base, factor):
        for head in range(rows.shape[0] // hd):
            first, second = rotate(rows[head * hd : (head + 1) * hd], cos, sin)
            at = base + head * hd
            out[at : at + hd // 2, :] = (first * factor).astype(BF16)
            out[at + hd // 2 : at + hd, :] = (second * factor).astype(BF16)

    q_width = q_weight.shape[1]
    turned(dot(q_weight[...], normed[...], 0, 0), 0, hd**-0.5)
    kv = k_own.shape[0]
    turned(dot(k_own[...], own, 1, 0) + dot(k_oth[...], oth, 1, 0), q_width, 1.0)
    rows = dot(v_own[...], own, 1, 0) + dot(v_oth[...], oth, 1, 0)
    out[q_width + kv : q_width + 2 * kv, :] = rows.astype(BF16)


def project(info, x, gain, weights, tables):
    width, rows = x.shape
    q, k, v = weights
    total = q.shape[1] + 2 * k[0].shape[0]
    operands = (x, gain, q, *k, *v, *tables)
    return call(
        project_kernel,
        "project",
        (1,),
        [whole(item.shape) for item in operands],
        [whole((width, rows)), whole((total, rows))],
        [shaped((width, rows), BF16), shaped((total, rows), BF16)],
    )(info, *operands)


def scores_of(keys, queries, masked):
    scores = dot(keys, queries, 1, 0)
    if not masked:
        return scores
    key_row = lax.broadcasted_iota(jnp.int32, scores.shape, 0)
    query_row = lax.broadcasted_iota(jnp.int32, scores.shape, 1)
    return jnp.where(key_row <= query_row, scores, -1e30)


def attend_kernel(
    info, q, k_own, v_own, k_past, v_past, out, lse, keys_own, keys_past, peak, total, mixed
):
    rows = q.shape[1]
    block = min(256, rows)
    hd = HEAD_DIM
    groups = [(group, slice(group * hd, (group + 1) * hd)) for group in range(GROUP)]
    keys_own[...] = k_own[...].T

    @pl.loop(0, info[1])
    def _(device):
        keys_past[device] = k_past[device].T

    for start in range(0, rows, block):
        for group, head in groups:
            scores = scores_of(keys_own[start : start + block, :], q[head, start:], True)
            fresh = jnp.max(scores, 0, keepdims=True)
            if start > 0:
                fresh = jnp.maximum(fresh, peak[group : group + 1, start:])
            peak[group : group + 1, start:] = fresh

    @pl.loop(0, info[1])
    def _(device):
        for group, head in groups:
            scores = scores_of(keys_past[device], q[head, :], False)
            peak[group : group + 1, :] = jnp.maximum(
                peak[group : group + 1, :], jnp.max(scores, 0, keepdims=True)
            )

    def add(group, head, keys, values, start, masked, first):
        scores = scores_of(keys, q[head, start:], masked)
        exponent = jnp.exp(scores - peak[group : group + 1, start:])
        sums = jnp.sum(exponent, 0, keepdims=True)
        product = dot(values, exponent.astype(BF16), 1, 0)
        if first:
            total[group : group + 1, :] = sums
            mixed[head, :] = product
        else:
            total[group : group + 1, start:] += sums
            mixed[head, start:] += product

    for start in range(0, rows, block):
        part = slice(start, start + block)
        for group, head in groups:
            add(group, head, keys_own[part, :], v_own[:, part], start, True, start == 0)

    @pl.loop(0, info[1])
    def _(device):
        for group, head in groups:
            add(group, head, keys_past[device], v_past[device], 0, False, False)

    for group, head in groups:
        sums = total[group : group + 1, :]
        out[head, :] = (mixed[head, :] / sums).astype(BF16)
        lse[0, group : group + 1, :] = peak[group : group + 1, :] + jnp.log(sums)


def attention_specs(rows, past, base):
    hd = HEAD_DIM
    return [
        pl.BlockSpec((GROUP * hd, rows), lambda h, info: (base + h, 0)),
        pl.BlockSpec((hd, rows), lambda h, info: (QUERY_HEADS + base + h, 0)),
        pl.BlockSpec((hd, rows), lambda h, info: (QUERY_HEADS + KEY_HEADS + base + h, 0)),
        pl.BlockSpec((past, hd, rows), lambda h, info: (0, base + h, 0)),
        pl.BlockSpec((past, hd, rows), lambda h, info: (0, KEY_HEADS + base + h, 0)),
    ]


def attend(info, qkv, past, base, heads):
    rows = qkv.shape[1]
    count = past.shape[0]
    group = GROUP * HEAD_DIM
    return call(
        attend_kernel,
        "attend",
        (heads,),
        attention_specs(rows, count, base),
        [
            pl.BlockSpec((group, rows), lambda h, info: (h, 0)),
            pl.BlockSpec((1, 8, rows), lambda h, info: (h, 0, 0)),
        ],
        [shaped((heads * group, rows), BF16), shaped((heads, 8, rows), F32)],
        [
            pltpu.VMEM((rows, HEAD_DIM), BF16),
            pltpu.VMEM((count, rows, HEAD_DIM), BF16),
            pltpu.VMEM((8, rows), F32),
            pltpu.VMEM((8, rows), F32),
            pltpu.VMEM((GROUP * HEAD_DIM, rows), F32),
        ],
    )(info, qkv, qkv, qkv, past, past)


def mix_kernel(info, x, mixed, weight, gain, middle, normed):
    middle[...] = x[...].astype(F32) + dot(weight[...], mixed[...], 0, 0)
    values = middle[...]
    normed[...] = (values * scale_of(values) * gain[...]).astype(BF16)


def mix(info, x, mixed, weight, gain):
    width, rows = x.shape
    operands = (x, mixed, weight, gain)
    return call(
        mix_kernel,
        "mix",
        (1,),
        [whole(item.shape) for item in operands],
        [whole((width, rows)), whole((width, rows))],
        [shaped((width, rows), F32), shaped((width, rows), BF16)],
    )(info, *operands)


def activate(token_rows, gate_weight, up_weight, hidden, silu, slope):
    gate = dot(token_rows[...], gate_weight[...], 1, 0)
    up = dot(token_rows[...], up_weight[...], 1, 0)
    sigmoid = 0.5 * jnp.tanh(0.5 * gate) + 0.5
    active = gate * sigmoid
    hidden[...] = (active * up).astype(BF16)
    silu[...] = active.astype(BF16)
    slope[...] = (up * (sigmoid + active * (1.0 - sigmoid))).astype(BF16)


def expand_kernel(info, normed, gate_weight, up_weight, hidden, silu, slope, token_rows):
    @pl.when(pl.program_id(0) == 0)
    def _():
        token_rows[...] = normed[...].T

    activate(token_rows, gate_weight, up_weight, hidden, silu, slope)


def expand(info, normed, gate, up):
    width, rows = normed.shape
    ff = gate.shape[1]
    tile = ff // 5
    weight = pl.BlockSpec((width, tile), lambda t, info: (0, t))
    result = pl.BlockSpec((rows, tile), lambda t, info: (0, t))
    return call(
        expand_kernel,
        "expand",
        (ff // tile,),
        [whole((width, rows)), weight, weight],
        [result] * 3,
        [shaped((rows, ff), BF16)] * 3,
        [pltpu.VMEM((rows, width), BF16)],
    )(info, normed, gate, up)


def expand_first_kernel(info, normed, *refs):
    gate_parts, up_parts = refs[:5], refs[5:10]
    hidden, silu, slope, gate_weight, up_weight, token_rows = refs[10:]
    step = pl.program_id(0)
    steps = pl.num_programs(0)

    @pl.when(step == 0)
    def _():
        token_rows[...] = normed[...].T

    for (own, *pieces), target in ((gate_parts, gate_weight), (up_parts, up_weight)):
        half, quarter = own.shape[0], pieces[0].shape[0]
        target[pl.ds(pl.multiple_of(info[0] * half, half), half), :] = own[...]
        other = (1 - info[0]) * half
        near = pl.ds(pl.multiple_of(other + info[3] * quarter, quarter), quarter)
        far = pl.ds(pl.multiple_of(other + (1 - info[3]) * quarter, quarter), quarter)

        @pl.when(step < steps // 2)
        def _():
            target[near, :] = pieces[0][...]
            target[far, :] = pieces[1][...]

        @pl.when(step >= steps // 2)
        def _():
            target[near, :] = pieces[2][...]
            target[far, :] = pieces[3][...]

    activate(token_rows, gate_weight, up_weight, hidden, silu, slope)


def expand_first(info, normed, gate, up):
    width, rows = normed.shape
    half, ff = gate[0].shape
    steps = 4
    tile = ff // steps
    quarter = half // 2

    def column(t, info):
        own = info[2] * (steps // 2) + t
        return jnp.where(t < steps // 2, own, (1 - info[2]) * (steps // 2) + t - steps // 2)

    early = pl.BlockSpec((quarter, tile), lambda t, info: (0, jnp.minimum(t, steps // 2 - 1)))
    late = pl.BlockSpec((quarter, tile), lambda t, info: (0, jnp.maximum(t - steps // 2, 0)))
    parts = [pl.BlockSpec((half, tile), lambda t, info: (0, column(t, info)))]
    parts += [early, early, late, late]
    result = pl.BlockSpec((rows, tile), lambda t, info: (0, column(t, info)))
    weight = pl.BlockSpec((width, tile), lambda t, info: (0, column(t, info)))
    return call(
        expand_first_kernel,
        "expand_first",
        (steps,),
        [whole((width, rows))] + parts * 2,
        [result] * 3 + [weight] * 2,
        [shaped((rows, ff), BF16)] * 3 + [shaped((width, ff), BF16)] * 2,
        [pltpu.VMEM((rows, width), BF16)],
    )(info, normed, *gate, *up)


def shrink_kernel(info, middle, hidden, weight, out):
    out[...] = (middle[...] + dot(weight[...], hidden[...], 1, 1)).astype(out.dtype)


def shrink(info, middle, hidden, down, dtype, cost=None):
    width, rows = middle.shape
    ff = hidden.shape[1]
    tile = width // 2
    return call(
        shrink_kernel,
        "shrink",
        (width // tile,),
        [
            pl.BlockSpec((tile, rows), lambda t, info: (t, 0)),
            whole((rows, ff)),
            pl.BlockSpec((tile, ff), lambda t, info: (t, 0)),
        ],
        [pl.BlockSpec((tile, rows), lambda t, info: (t, 0))],
        [shaped((width, rows), dtype)],
        cost=cost,
    )(info, middle, hidden, down)[0]


def shrink_first_kernel(info, middle, hidden, own, near_0, far_0, near_1, far_1, out, weight):
    half, quarter = own.shape[1], near_0.shape[0]
    weight[:, pl.ds(pl.multiple_of(info[0] * half, half), half)] = own[...]
    other = pl.ds(pl.multiple_of((1 - info[0]) * half, half), half)
    at_near = pl.ds(pl.multiple_of(info[2] * quarter, quarter), quarter)
    at_far = pl.ds(pl.multiple_of((1 - info[2]) * quarter, quarter), quarter)
    for step, near, far in ((0, near_0, far_0), (1, near_1, far_1)):

        @pl.when(pl.program_id(0) == step)
        def _():
            weight[at_near, other] = near[...]
            weight[at_far, other] = far[...]

    out[...] = middle[...] + dot(weight[...], hidden[...], 1, 1)


def shrink_first(info, middle, hidden, parts):
    width, rows = middle.shape
    ff = hidden.shape[1]
    tile = width // 2
    own, first, second, third, fourth = parts

    def row(t, info):
        return jnp.where(t == 0, info[3], 1 - info[3])

    return call(
        shrink_first_kernel,
        "shrink_first",
        (2,),
        [
            pl.BlockSpec((tile, rows), lambda t, info: (row(t, info), 0)),
            whole((rows, ff)),
            pl.BlockSpec((tile, ff // 2), lambda t, info: (row(t, info), 0)),
        ]
        + [whole(first.shape)] * 4,
        [
            pl.BlockSpec((tile, rows), lambda t, info: (row(t, info), 0)),
            pl.BlockSpec((tile, ff), lambda t, info: (row(t, info), 0)),
        ],
        [shaped((width, rows), F32), shaped((width, ff), BF16)],
    )(info, middle, hidden, own, first, third, second, fourth)


def ffn_back_kernel(
    info,
    grad,
    middle,
    gain,
    silu,
    slope,
    down,
    gate,
    up,
    out_weight,
    gate_grad,
    up_grad,
    branch,
    grad_middle,
    attn_grad,
    mixed_grad,
    gain_grad,
    branch_rows,
    total,
):
    step = pl.program_id(0)
    steps = pl.num_programs(0)

    @pl.when(step == 0)
    def _():
        branch[...] = grad[...].astype(BF16)
        branch_rows[...] = branch[...].T
        total[...] = jnp.zeros_like(total)

    incoming = dot(branch_rows[...], down[...], 1, 0)
    gate_grad[...] = (incoming * slope[...].astype(F32)).astype(BF16)
    up_grad[...] = (incoming * silu[...].astype(F32)).astype(BF16)
    total[...] += dot(gate[...], gate_grad[...], 1, 1) + dot(up[...], up_grad[...], 1, 1)

    @pl.when(step == steps - 1)
    def _():
        back, gain_sum = norm_back(middle[...], gain[...], total[...])
        gain_grad[...] = gain_sum
        result = grad[...].astype(F32) + back
        grad_middle[...] = result
        attn_grad[...] = result.astype(BF16)
        mixed_grad[...] = dot(out_weight[...], attn_grad[...], 1, 0).astype(BF16)


def ffn_back(info, grad, middle, gain, silu, slope, down, gate, up, out_weight, cost=None):
    width, rows = middle.shape
    ff = silu.shape[1]
    tile = ff // 5
    heads = out_weight.shape[0]
    token = pl.BlockSpec((rows, tile), lambda t, info: (0, t))
    weight = pl.BlockSpec((width, tile), lambda t, info: (0, t))
    return call(
        ffn_back_kernel,
        "ffn_back",
        (ff // tile,),
        [
            whole((width, rows)),
            whole((width, rows)),
            whole((width, 1)),
            token,
            token,
            weight,
            weight,
            weight,
            whole((heads, width)),
        ],
        [
            token,
            token,
            whole((width, rows)),
            whole((width, rows)),
            whole((width, rows)),
            whole((heads, rows)),
            whole((width, 1)),
        ],
        [
            shaped((rows, ff), BF16),
            shaped((rows, ff), BF16),
            shaped((width, rows), BF16),
            shaped((width, rows), F32),
            shaped((width, rows), BF16),
            shaped((heads, rows), BF16),
            shaped((width, 1), F32),
        ],
        [pltpu.VMEM((rows, width), BF16), pltpu.VMEM((width, rows), F32)],
        cost=cost,
    )(info, grad, middle, gain, silu, slope, down, gate, up, out_weight)


def attend_back_kernel(
    info,
    q,
    k_own,
    v_own,
    k_past,
    v_past,
    mixed_grad,
    mixed,
    lse,
    cosine,
    sine,
    q_grad,
    own_grad,
    past_grad,
    keys_own,
    values_own,
    keys_past,
    values_past,
    inner,
    q_sum,
):
    rows = q.shape[1]
    block = min(256, rows)
    hd = HEAD_DIM
    groups = [(group, slice(group * hd, (group + 1) * hd)) for group in range(GROUP)]
    keys_own[...] = k_own[...].T
    values_own[...] = v_own[...].T

    @pl.loop(0, info[1])
    def _(device):
        keys_past[device] = k_past[device].T
        values_past[device] = v_past[device].T

    @pl.loop(info[1], past_grad.shape[0])
    def _(device):
        past_grad[device] = jnp.zeros_like(past_grad[device])

    for group, head in groups:
        product = mixed_grad[head, :].astype(F32) * mixed[head, :].astype(F32)
        inner[group : group + 1, :] = jnp.sum(product, 0, keepdims=True)

    def step(keys, key_rows, value_rows, start, masked, first):
        key_sum = value_sum = None
        for group, head in groups:
            query, incoming = q[head, start:], mixed_grad[head, start:]
            one = slice(group, group + 1)
            probs = jnp.exp(scores_of(key_rows, query, masked) - lse[0, one, start:])
            slopes = dot(value_rows, incoming, 1, 0)
            low = (probs * (slopes - inner[one, start:])).astype(BF16)
            value_part = dot(incoming, probs.astype(BF16), 1, 1)
            key_part = dot(query, low, 1, 1)
            key_sum = key_part if key_sum is None else key_sum + key_part
            value_sum = value_part if value_sum is None else value_sum + value_part
            query_part = dot(keys, low, 1, 0)
            if first:
                q_sum[head, :] = query_part
            else:
                q_sum[head, start:] += query_part
        return key_sum, value_sum

    for start in range(0, rows, block):
        part = slice(start, start + block)
        key_sum, value_sum = step(
            k_own[:, part], keys_own[part, :], values_own[part, :], start, True, start == 0
        )
        own_grad[0, :hd, part] = key_sum
        own_grad[0, hd:, part] = value_sum

    @pl.loop(0, info[1])
    def _(device):
        key_sum, value_sum = step(
            k_past[device], keys_past[device], values_past[device], 0, False, False
        )
        past_grad[device, 0, :hd, :] = key_sum.astype(past_grad.dtype)
        past_grad[device, 0, hd:, :] = value_sum.astype(past_grad.dtype)

    cos, sin = cosine[...], -sine[...]
    for group, head in groups:
        first, second = rotate(q_sum[head, :], cos, sin)
        at = group * hd
        q_grad[at : at + hd // 2, :] = (first * hd**-0.5).astype(BF16)
        q_grad[at + hd // 2 : at + hd, :] = (second * hd**-0.5).astype(BF16)


def attend_back(info, qkv, past, mixed_grad, mixed, lse, tables, base, heads, cost=None):
    rows = qkv.shape[1]
    count = past.shape[0]
    hd = HEAD_DIM
    group = pl.BlockSpec((GROUP * hd, rows), lambda h, info: (base + h, 0))
    return call(
        attend_back_kernel,
        "attend_back",
        (heads,),
        attention_specs(rows, count, base)
        + [
            group,
            group,
            pl.BlockSpec((1, 8, rows), lambda h, info: (base + h, 0, 0)),
            whole(tables[0].shape),
            whole(tables[1].shape),
        ],
        [
            pl.BlockSpec((GROUP * hd, rows), lambda h, info: (h, 0)),
            pl.BlockSpec((1, 2 * hd, rows), lambda h, info: (h, 0, 0)),
            pl.BlockSpec((count, 1, 2 * hd, rows), lambda h, info: (0, h, 0, 0)),
        ],
        [
            shaped((heads * GROUP * hd, rows), BF16),
            shaped((heads, 2 * hd, rows), F32),
            shaped((count, heads, 2 * hd, rows), BF16 if count == 1 else F32),
        ],
        [
            pltpu.VMEM((rows, hd), BF16),
            pltpu.VMEM((rows, hd), BF16),
            pltpu.VMEM((count, rows, hd), BF16),
            pltpu.VMEM((count, rows, hd), BF16),
            pltpu.VMEM((8, rows), F32),
            pltpu.VMEM((GROUP * hd, rows), F32),
        ],
        cost=cost,
    )(info, qkv, qkv, qkv, past, past, mixed_grad, mixed, lse, *tables)


def project_back_kernel(parts, info, x, gain, grad_middle, *refs):
    q_grads, own_grads, arrived = refs[:parts], refs[parts : 2 * parts], refs[2 * parts : 3 * parts]
    (
        q_weight,
        k_own,
        k_oth,
        v_own,
        v_oth,
        cosine,
        sine,
        q_grad,
        kv_grad,
        out,
        branch,
        gain_grad,
        total,
    ) = refs[3 * parts :]
    half = x.shape[0] // 2
    hd = HEAD_DIM
    kv = KEY_HEADS * hd
    cos, sin = cosine[...], -sine[...]
    head = 0
    for piece, own, far in zip(q_grads, own_grads, arrived):
        q_grad[head * GROUP * hd : head * GROUP * hd + piece.shape[0], :] = piece[...]
        for item in range(own.shape[0]):
            both = own[item] + far[item].astype(F32)
            first, second = rotate(both[:hd], cos, sin)
            at = head * hd
            kv_grad[at : at + hd // 2, :] = first.astype(BF16)
            kv_grad[at + hd // 2 : at + hd, :] = second.astype(BF16)
            kv_grad[kv + at : kv + at + hd, :] = both[hd:].astype(BF16)
            head += 1
    total[...] = dot(q_weight[...], q_grad[...], 1, 0)
    for mine, k, v in ((info[0], k_own, v_own), (1 - info[0], k_oth, v_oth)):
        total[pl.ds(pl.multiple_of(mine * half, half), half), :] += dot(
            k[...], kv_grad[:kv, :], 0, 0
        ) + dot(v[...], kv_grad[kv:, :], 0, 0)
    back, gain_sum = norm_back(x[...].astype(F32), gain[...], total[...])
    gain_grad[...] = gain_sum
    result = grad_middle[...] + back
    out[...] = result
    branch[...] = result.astype(BF16)


def project_back(info, x, gain, grad_middle, q_grads, own_grads, arrived, weights, tables, cost=None):
    width, rows = x.shape
    q, k, v = weights
    heads = q.shape[1]
    kv = 2 * KEY_HEADS * HEAD_DIM
    operands = (x, gain, grad_middle, *q_grads, *own_grads, *arrived, q, *k, *v, *tables)
    shapes = [
        shaped((heads, rows), BF16),
        shaped((kv, rows), BF16),
        shaped((width, rows), F32),
        shaped((width, rows), BF16),
        shaped((width, 1), F32),
    ]
    return call(
        functools.partial(project_back_kernel, len(q_grads)),
        "project_back",
        (1,),
        [whole(item.shape) for item in operands],
        [whole(item.shape) for item in shapes],
        shapes,
        [pltpu.VMEM((width, rows), F32)],
        cost=cost,
    )(info, *operands)


def order_rows(info, target, sources):
    rows = sources[0].shape[1]
    size = target.shape[0] // 4
    at = 0
    for core in (1 - info[2], info[2]):
        for half in (1 - info[0], info[0]):
            start = pl.multiple_of((2 * half + core) * size, size)
            for index, source in enumerate(sources):
                target[at : at + size, index * rows : (index + 1) * rows] = source[
                    pl.ds(start, size), :
                ]
            at += size


def order_halves(info, target, sources):
    rows = sources[0].shape[1]
    size = target.shape[0] // 2
    for at, core in ((0, 1 - info[2]), (size, info[2])):
        start = pl.multiple_of(core * size, size)
        for index, source in enumerate(sources):
            target[at : at + size, index * rows : (index + 1) * rows] = source[pl.ds(start, size), :]


def outer_kernel(split_columns, info, left_a, right_a, left_b, right_b, sent, kept, left, right):
    rows = left_a.shape[1]

    @pl.when(pl.program_id(0) == 0)
    def _():
        order = order_halves if split_columns else order_rows
        order(info, left, (left_a, left_b))

    right[:rows, :] = right_a[...]
    right[rows:, :] = right_b[...]
    count, size = sent.shape[0], sent.shape[1]
    for at, out in ((0, sent), (count * size, kept)):
        product = dot(left[at : at + count * size, :], right[...], 1, 0).astype(BF16)
        for index in range(count):
            out[index] = product[index * size : (index + 1) * size]


def outer(info, parts, split_columns, cost=None):
    left_a, right_a, left_b, right_b = parts
    width, rows = left_a.shape
    columns = right_a.shape[1]
    if split_columns:
        tile = columns // 4

        def column(t, info):
            return jnp.where(t < 2, (1 - info[0]) * 2 + t, info[0] * 2 + t - 2)

        right = pl.BlockSpec((rows, tile), lambda t, info: (0, column(t, info)))
        result = pl.BlockSpec((1, width // 2, tile), lambda t, info: (t // 2, 0, t % 2))
        shape = shaped((2, width // 2, columns // 2), BF16)
    else:
        tile = columns // 5
        right = pl.BlockSpec((rows, tile), lambda t, info: (0, t))
        result = pl.BlockSpec((2, width // 4, tile), lambda t, info: (0, 0, t))
        shape = shaped((2, width // 4, columns), BF16)
    return call(
        functools.partial(outer_kernel, split_columns),
        "outer",
        (columns // tile,),
        [whole((width, rows)), right, whole((width, rows)), right],
        [result, result],
        [shape, shape],
        [pltpu.VMEM((width, 2 * rows), BF16), pltpu.VMEM((2 * rows, tile), BF16)],
        cost=cost,
    )(info, *parts)


def pack_kernel(extra, info, left_a, *refs):
    sent, kept, left, right = refs[-4:]
    refs = refs[:-4]
    gains, refs = refs[len(refs) - extra :], refs[: len(refs) - extra]
    left_b, rights_a, rights_b = refs[0], refs[1::2], refs[2::2]
    rows = left_a.shape[1]
    order_rows(info, left, (left_a, left_b))
    at = 0
    for right_a, right_b in zip(rights_a, rights_b):
        right[at : at + right_a.shape[0], :rows] = right_a[...]
        right[at : at + right_a.shape[0], rows:] = right_b[...]
        at += right_a.shape[0]
    count, size = sent.shape[0], sent.shape[1]
    for base, core, out in ((0, 1 - info[2], sent), (count * size, info[2], kept)):
        for start, span in spans(right.shape[0], 512):
            product = dot(left[base : base + count * size, :], right[start : start + span, :], 1, 1)
            for index in range(count):
                out[index, :, start : start + span] = product[
                    index * size : (index + 1) * size
                ].astype(BF16)
        for index, half in enumerate((1 - info[0], info[0])):
            part = pl.ds(pl.multiple_of((2 * half + core) * size, size), size)
            for number in range(extra // 2):
                term = gains[2 * number][part, :] + gains[2 * number + 1][part, :]
                out[index, :, at + number : at + number + 1] = term.astype(BF16)
            if extra:
                out[index, :, at + extra // 2 :] = jnp.zeros((size, extra // 2), BF16)


def pack(info, left_a, left_b, rights, gains=(), cost=None):
    width, rows = left_a.shape
    columns = sum(item.shape[0] for item in rights[::2])
    operands = (left_a, left_b, *rights, *gains)
    shape = shaped((2, width // 4, columns + len(gains)), BF16)
    return call(
        functools.partial(pack_kernel, len(gains)),
        "pack",
        (1,),
        [whole(item.shape) for item in operands],
        [whole(shape.shape)] * 2,
        [shape, shape],
        [pltpu.VMEM((width, 2 * rows), BF16), pltpu.VMEM((columns, 2 * rows), BF16)],
        cost=cost,
    )(info, *operands)


def both_cores_kernel(info, kept, arrived, sent, held):
    for index, out in ((0, sent), (1, held)):
        out[...] = (kept[index].astype(F32) + arrived[index].astype(F32)).astype(BF16)


def both_cores(info, kept, arrived):
    shape = shaped(kept.shape[1:], BF16)
    return call(
        both_cores_kernel,
        "both_cores",
        (1,),
        [None] * 2,
        [None] * 2,
        [shape, shape],
        cost=0,
    )(info, kept, arrived)


def swap(values, axis, bit):
    size = lax.axis_size(axis)
    return lax.ppermute(values, axis, [(i, i ^ bit) for i in range(size)])


def bits_of(axis):
    size = lax.axis_size(axis)
    assert size & (size - 1) == 0
    return [1 << i for i in range(size.bit_length() - 1)]


def high(axis, bit):
    return (lax.axis_index(axis) // bit) % 2


def halves(values, dim, which):
    half = values.shape[dim] // 2
    return lax.dynamic_slice_in_dim(values, which * half, half, dim)


def joined(mine, other, dim, which):
    return jnp.where(
        which == 0,
        jnp.concatenate([mine, other], dim),
        jnp.concatenate([other, mine], dim),
    )


def tied(values, others):
    return lax.optimization_barrier((values, others))[0]


def from_pieces(own, pieces, mine, core, low_batch):
    near = joined(pieces[0], pieces[2], 0, core)
    far = joined(pieces[1], pieces[3], 0, core)
    return joined(own, joined(near, far, 0, low_batch), 0, mine)


def split_dim(shape, parts):
    if shape[0] % (8 * parts) == 0:
        return 0
    if shape[1] % (128 * parts) == 0:
        return 1
    return 0 if shape[0] % parts == 0 else 1


class Order:
    def __init__(self, token):
        self.token = token

    def __call__(self, *values):
        self.token, *values = lax.optimization_barrier((self.token, *values))
        return values[0] if len(values) == 1 else values


def quarters(values, dim, number):
    quarter = values.shape[dim] // 4
    return lax.dynamic_slice_in_dim(values, number * quarter, quarter, dim)


class Chain:
    def __init__(self, order, away, kept):
        self.order, self.kept = order, kept
        self.away = away
        self.steps = [self.core, self.fsdp]
        self.shares = [("seq", (1,), 0)]
        exchanges = [("seq", (bit,)) for bit in bits_of("seq")[1:]]
        bits = bits_of("batch")
        exchanges += [("batch", bits[:1])] if bits else []
        bits = bits[1:]
        while bits:
            exchanges.append(("batch", bits[:2]))
            bits = bits[2:]
        self.steps += [functools.partial(self.add, *item) for item in exchanges]
        self.steps += [self.share] * (1 + len(exchanges))
        self.waiting = None

    def send(self):
        self.waiting = self.steps.pop(0)()

    def core(self):
        def finish(arrived):
            self.sent, self.held = both_cores(self.order.token, self.kept, arrived)

        return [swap(self.order(self.away), "seq", 1)], finish

    def fsdp(self):
        def finish(arrived):
            self.held = (self.held.astype(F32) + arrived.astype(F32)).astype(BF16)

        return [swap(self.order(self.sent), "fsdp", 1)], finish

    def add(self, axis, bits):
        held = self.held
        dim = split_dim(held.shape, 2 * len(bits))
        take = halves if len(bits) == 1 else quarters
        number = sum(high(axis, bit) << index for index, bit in enumerate(bits))
        masks = range(1, 1 << len(bits))
        parts = self.order(*[take(held, dim, number ^ mask) for mask in masks])
        parts = parts if len(bits) > 1 else [parts]
        arrived = [
            swap(part, axis, sum(bit for index, bit in enumerate(bits) if mask >> index & 1))
            for mask, part in zip(masks, parts)
        ]
        self.shares.append((axis, bits, dim))

        def finish(*values):
            total = take(held, dim, number).astype(F32)
            for item in values:
                total = total + item.astype(F32)
            self.held = total.astype(BF16)

        return arrived, finish

    def share(self):
        axis, bits, dim = self.shares.pop()
        held = self.order(self.held)
        masks = range(1, 1 << len(bits))
        arrived = [
            swap(held, axis, sum(bit for index, bit in enumerate(bits) if mask >> index & 1))
            for mask in masks
        ]

        def finish(*values):
            low = high(axis, bits[0])
            if len(bits) == 1:
                self.held = joined(held, values[0], dim, low)
                return
            near, far = joined(held, values[0], dim, low), joined(values[1], values[2], dim, low)
            self.held = joined(near, far, dim, high(axis, bits[1]))

        return arrived, finish

    def result(self):
        while self.waiting or self.steps:
            if self.waiting:
                take(self)
            else:
                self.send()
        return self.order(self.held.astype(F32))


def take(*chains):
    flat = [item for chain in chains for item in chain.waiting[0]]
    values = chains[0].order(*flat)
    values = list(values) if len(flat) > 1 else [values]
    for chain in chains:
        arrived, finish = chain.waiting
        chain.waiting = None
        finish(*values[: len(arrived)])
        values = values[len(arrived) :]


def per_device(
    tokens,
    attn_gain,
    w_query,
    key_weight,
    value_weight,
    w_out,
    ffn_gain,
    w_gate,
    w_up,
    w_down,
    cotangent,
):
    assert tokens.shape[0] == 1 and lax.axis_size("fsdp") == 2
    mine, spot, core = lax.axis_index("fsdp"), lax.axis_index("seq"), high("seq", 1)
    low_batch = high("batch", 1)
    devices = lax.axis_size("seq")
    info = jnp.stack([mine, spot, core, low_batch]).astype(jnp.int32)
    start_in = tokens[0].T
    incoming = cotangent[0].T
    width, rows = start_in.shape

    gains = jnp.stack([attn_gain, ffn_gain])
    gains = joined(gains, swap(gains, "fsdp", 1), 1, mine).astype(F32)[..., None]
    key_weight, value_weight, w_down = key_weight.T, value_weight.T, w_down.T
    def fsdp(values):
        return swap(values, "fsdp", 1)

    def pair(values):
        return swap(values, "batch", 1)

    def cores(values):
        return swap(values, "seq", 1)

    q_piece = halves(halves(w_query, 0, low_batch), 0, core)
    kv_piece = halves(jnp.where(core == 0, key_weight, value_weight), 0, low_batch)
    q_0, kv_0 = fsdp(q_piece), fsdp(kv_piece)
    out_0 = fsdp(tied(halves(halves(w_out, 0, low_batch), 0, core), (q_0, kv_0)))
    q_1, kv_1, q_2, kv_2 = pair(q_0), pair(kv_0), cores(q_0), cores(kv_0)
    gate_0 = fsdp(tied(halves(halves(w_gate, 0, low_batch), 1, core), out_0))
    q_3, kv_3 = cores(q_1), cores(kv_1)
    q_weight = from_pieces(w_query, (q_0, q_1, q_2, q_3), mine, core, low_batch)
    held = joined(kv_0, kv_1, 0, low_batch)
    other = joined(kv_2, kv_3, 0, low_batch)
    k_oth, v_oth = jnp.where(core == 0, held, other), jnp.where(core == 0, other, held)
    qkv_weights = (q_weight, (key_weight, k_oth), (value_weight, v_oth))

    positions = (spot * rows + jnp.arange(rows, dtype=jnp.int32)).astype(F32)
    frequency = jnp.exp(
        jnp.arange(HEAD_DIM // 2, dtype=F32) * (-2.0 * math.log(10000.0) / HEAD_DIM)
    )
    angles = frequency[:, None] * positions[None, :]
    tables = (jnp.cos(angles), jnp.sin(angles))

    def to_attention(x):
        normed, qkv = project(info, x, gains[0], qkv_weights, tables)
        kv = qkv[QUERY_HEADS * HEAD_DIM :]
        if devices == 2:
            past = cores(kv)[None]
        else:
            past = lax.all_gather(kv, "seq")
        return normed, qkv, past

    low_normed, low_qkv, low_past = to_attention(start_in)
    order = Order(tied(info, low_qkv))

    def column_piece(weight):
        return halves(halves(weight, 0, low_batch), 1, core)

    up_0 = fsdp(order(column_piece(w_up)))
    out_1, out_2 = pair(order(tied(out_0, (q_1, kv_1)))), cores(out_0)
    gate_0 = order(gate_0)
    down_0 = fsdp(order(halves(halves(w_down, 0, low_batch), 0, core)))
    gate_1, gate_2 = pair(order(gate_0)), cores(gate_0)
    near_mixed, near_lse = attend(info, low_qkv, order(low_past), 0, 3)
    near_mixed, up_0 = order(near_mixed, up_0)
    up_1, up_2 = pair(up_0), cores(up_0)
    out_1, out_2, gate_1 = order(out_1, out_2, gate_1)
    out_3, gate_3 = cores(out_1), cores(gate_1)
    far_mixed, far_lse = attend(info, low_qkv, order(low_past), 3, 2)
    far_mixed = order(far_mixed)
    low_mixed = jnp.concatenate([near_mixed, far_mixed], 0)
    low_lse = jnp.concatenate([near_lse, far_lse], 0)
    out_weight = from_pieces(w_out, (out_0, out_1, out_2, out_3), mine, core, low_batch)
    low_middle, low_normed_ffn = mix(info, start_in, low_mixed, out_weight, gains[1])
    low_normed_ffn, down_0, up_1 = order(low_normed_ffn, down_0, up_1)
    up_3 = cores(up_1)
    down_1, down_2 = pair(down_0), cores(down_0)
    low_hidden, low_silu, low_slope, gate, up = expand_first(
        info,
        low_normed_ffn,
        (w_gate, gate_0, gate_1, gate_2, gate_3),
        (w_up, up_0, up_1, up_2, up_3),
    )
    down_3 = cores(tied(down_1, low_hidden))
    middle_in, down = shrink_first(
        info, low_middle, low_hidden, (w_down, down_0, down_1, down_2, down_3)
    )

    high_normed, high_qkv, high_past = to_attention(middle_in)
    high_mixed, high_lse = attend(info, high_qkv, high_past, 0, KEY_HEADS)
    high_middle, high_normed_ffn = mix(info, middle_in, high_mixed, out_weight, gains[1])
    high_hidden, high_silu, high_slope = expand(info, high_normed_ffn, gate, up)

    def attention_back(qkv, past, mixed_grad, mixed, lse, base, heads, cost=None):
        q_grad, own_grad, past_grad = attend_back(
            info, qkv, past, mixed_grad, mixed, lse, tables, base, heads, cost
        )
        if devices == 2:
            return q_grad, own_grad, cores(past_grad[0])
        return q_grad, own_grad, lax.psum_scatter(past_grad, "seq", scatter_dimension=0)

    def to_input(x, grad_middle, parts, cost=None):
        return project_back(
            info, x, gains[0], grad_middle, *zip(*parts), qkv_weights, tables, cost
        )

    high_gate, high_up, high_branch, grad_middle, high_attn, mixed_grad, high_ffn_gain = ffn_back(
        info, incoming, high_middle, gains[1], high_silu, high_slope, down, gate, up, out_weight
    )
    parts = [
        attention_back(high_qkv, high_past, mixed_grad, high_mixed, high_lse, base, heads)
        for base, heads in ((0, 3), (3, 2))
    ]
    high_q, high_kv, grad_between, low_branch, high_attn_gain = to_input(
        middle_in, grad_middle, parts
    )

    order = Order(tied(order.token, low_branch))
    down_terms = (high_branch, high_hidden, low_branch, low_hidden)
    down_g = Chain(order, *outer(info, down_terms, True, 0))
    down_g.send()
    final_out = order(shrink(info, order(high_middle), high_hidden, down, BF16, 0))
    take(down_g)
    down_g.send()
    low_gate, low_up, _, grad_middle, low_attn, mixed_grad, low_ffn_gain = ffn_back(
        info, order(grad_between), low_middle, gains[1], low_silu, low_slope,
        down, gate, up, out_weight, 0,
    )
    out_terms = (high_attn, order(low_attn))
    out_g = Chain(order, *pack(info, high_mixed, low_mixed, out_terms, cost=0))
    out_g.send()
    gate_terms = (high_normed_ffn, high_gate, low_normed_ffn, order(low_gate))
    gate_g = Chain(order, *outer(info, gate_terms, False, 0))
    gate_g.send()
    take(down_g, out_g)
    down_g.send()
    out_g.send()
    up_terms = (high_normed_ffn, high_up, low_normed_ffn, order(low_up))
    up_g = Chain(order, *outer(info, up_terms, False, 0))
    up_g.send()
    take(gate_g, out_g, down_g)
    gate_g.send()
    down_g.send()
    parts = []

    def low_part(base, heads, cost):
        mixed_now = order(mixed_grad)
        part = attention_back(low_qkv, low_past, mixed_now, low_mixed, low_lse, base, heads, cost)
        parts.append((order(part[0]), *part[1:]))

    low_part(0, 3, 20)
    take(up_g, down_g)
    down_g.send()
    out_g.send()
    low_part(3, 2, 0)
    take(gate_g, down_g, out_g)
    up_g.send()
    gate_g.send()
    down_g.send()
    out_g.send()
    low_q, low_kv, grad_start, _, low_attn_gain = to_input(
        start_in, order(grad_middle), parts, 0
    )
    qkv_terms = (high_q, order(low_q), high_kv, low_kv)
    gain_terms = (high_attn_gain, low_attn_gain, high_ffn_gain, low_ffn_gain)
    qkv_g = Chain(order, *pack(info, high_normed, low_normed, qkv_terms, gain_terms, 0))
    qkv_g.send()
    take(out_g, gate_g, down_g, up_g)
    gate_g.send()
    up_g.send()
    out_g.send()
    take(qkv_g)
    qkv_g.send()
    down_g.send()
    take(up_g, gate_g)
    up_g.send()
    gate_g.send()
    take(out_g)
    out_g.send()
    down_grad = down_g.result()
    take(qkv_g)
    qkv_g.send()
    take(out_g)
    out_g.send()
    take(qkv_g, up_g)
    qkv_g.send()
    take(gate_g)
    up_g.send()
    gate_g.send()
    out_grad = out_g.result()
    take(qkv_g)
    qkv_g.send()
    take(up_g, gate_g)
    up_g.send()
    gate_g.send()
    take(qkv_g)
    qkv_g.send()
    gate_grad = gate_g.result()
    take(up_g)
    up_g.send()
    take(qkv_g)
    qkv_g.send()
    up_grad, qkv_grad = up_g.result(), qkv_g.result()
    narrow = KEY_HEADS * HEAD_DIM
    query_part, key_part, value_part, gain_grads = jnp.split(
        qkv_grad, [width, width + narrow, width + 2 * narrow], 1
    )
    return (
        final_out.T[None],
        grad_start.T[None],
        gain_grads[:, 0],
        query_part,
        key_part,
        value_part,
        out_grad,
        gain_grads[:, 1],
        gate_grad,
        up_grad,
        down_grad.T,
    )


def solution(mesh):
    return jax.shard_map(
        per_device,
        mesh=mesh,
        in_specs=(
            P(("batch", "fsdp"), "seq", None),
            P("fsdp"),
            P("fsdp", None),
            P("fsdp", None),
            P("fsdp", None),
            P("fsdp", None),
            P("fsdp"),
            P("fsdp", None),
            P("fsdp", None),
            P("fsdp", None),
            P(("batch", "fsdp"), "seq", None),
        ),
        out_specs=(
            P(("batch", "fsdp"), "seq", None),
            P(("batch", "fsdp"), "seq", None),
            P("fsdp"),
            P("fsdp", None),
            P("fsdp", None),
            P("fsdp", None),
            P("fsdp", None),
            P("fsdp"),
            P("fsdp", None),
            P("fsdp", None),
            P("fsdp", None),
        ),
        check_vma=False,
    )
```

```python
import functools
import math

import jax
import jax.numpy as jnp
from jax import lax
from jax.experimental import pallas as pl
from jax.experimental.pallas import tpu as pltpu
from jax.sharding import PartitionSpec as P

QUERY_HEADS = 15
KEY_HEADS = 5
HEAD_DIM = 64
GROUP = QUERY_HEADS // KEY_HEADS
EPSILON = 1e-05
F32 = jnp.float32
BF16 = jnp.bfloat16


def dot(left, right, left_dim, right_dim):
    return lax.dot_general(
        left, right, (((left_dim,), (right_dim,)), ((), ())), preferred_element_type=F32
    )


def spans(total, size):
    return [(start, min(size, total - start)) for start in range(0, total, size)]


COSTS = {
    "project": 3.0,
    "attend": 4.0,
    "mix": 2.4,
    "expand": 10.0,
    "expand_first": 14.0,
    "shrink": 6.5,
    "shrink_first": 8.0,
    "ffn_back": 18.0,
    "attend_back": 5.0,
    "project_back": 5.0,
    "outer": 8.0,
    "pack": 3.5,
}


LIMITS = {
    "project": 12,
    "attend": 14,
    "mix": 12,
    "expand": 24,
    "expand_first": 60,
    "shrink": 22,
    "shrink_first": 60,
    "ffn_back": 40,
    "attend_back": 16,
    "project_back": 16,
    "outer": 26,
    "pack": 20,
    "both_cores": 12,
    "cross": 10,
    "last": 12,
}


def call(kernel, name, grid, in_specs, out_specs, out_shape, scratch=(), cost=None):
    if cost is None:
        cost = COSTS[name] * 0.45 * (grid[0] if name.startswith("attend") else 1)
    cost = int(cost * 1e9) + 1
    options = dict(
        name=name,
        out_shape=out_shape,
        compiler_params=pltpu.CompilerParams(vmem_limit_bytes=LIMITS[name] * 1024 * 1024),
        cost_estimate=pl.CostEstimate(flops=cost, bytes_accessed=1, transcendentals=0),
    )
    if name in ("project", "mix", "project_back", "pack", "both_cores", "cross", "last"):
        memory = pl.BlockSpec(memory_space=pltpu.VMEM)
        return pl.pallas_call(
            kernel,
            in_specs=[pl.BlockSpec(memory_space=pltpu.SMEM)] + [memory] * len(in_specs),
            out_specs=[memory] * len(out_specs),
            scratch_shapes=list(scratch),
            **options,
        )
    return pl.pallas_call(
        kernel,
        grid_spec=pltpu.PrefetchScalarGridSpec(
            num_scalar_prefetch=1,
            grid=grid,
            in_specs=in_specs,
            out_specs=out_specs,
            scratch_shapes=list(scratch),
        ),
        **options,
    )


def whole(shape):
    return pl.BlockSpec(shape, lambda *_: (0,) * len(shape))


def shaped(shape, dtype):
    return jax.ShapeDtypeStruct(shape, dtype)


def scale_of(values):
    return lax.rsqrt(jnp.mean(values * values, 0, keepdims=True) + EPSILON)


def norm_back(values, gain, incoming):
    scales = scale_of(values)
    weighted = gain * incoming
    inner = jnp.mean(values * weighted, 0, keepdims=True)
    grad = scales * weighted - values * (scales * scales * scales * inner)
    return grad, jnp.sum(incoming * values * scales, 1, keepdims=True)


def rotate(values, cosine, sine):
    half = HEAD_DIM // 2
    first, second = values[:half], values[half:]
    return first * cosine - second * sine, second * cosine + first * sine


def project_kernel(
    info, x, gain, q_weight, k_own, k_oth, v_own, v_oth, cosine, sine, normed, out
):
    width = x.shape[0]
    half = width // 2
    values = x[...].astype(F32)
    normed[...] = (values * scale_of(values) * gain[...]).astype(BF16)
    own = normed[pl.ds(pl.multiple_of(info[0] * half, half), half), :]
    oth = normed[pl.ds(pl.multiple_of((1 - info[0]) * half, half), half), :]
    cos, sin = cosine[...], sine[...]
    hd = HEAD_DIM

    def turned(rows, base, factor):
        for head in range(rows.shape[0] // hd):
            first, second = rotate(rows[head * hd : (head + 1) * hd], cos, sin)
            at = base + head * hd
            out[at : at + hd // 2, :] = (first * factor).astype(BF16)
            out[at + hd // 2 : at + hd, :] = (second * factor).astype(BF16)

    q_width = q_weight.shape[1]
    turned(dot(q_weight[...], normed[...], 0, 0), 0, hd**-0.5)
    kv = k_own.shape[0]
    turned(dot(k_own[...], own, 1, 0) + dot(k_oth[...], oth, 1, 0), q_width, 1.0)
    rows = dot(v_own[...], own, 1, 0) + dot(v_oth[...], oth, 1, 0)
    out[q_width + kv : q_width + 2 * kv, :] = rows.astype(BF16)


def project(info, x, gain, weights, tables, cost=None):
    width, rows = x.shape
    q, k, v = weights
    total = q.shape[1] + 2 * k[0].shape[0]
    operands = (x, gain, q, *k, *v, *tables)
    return call(
        project_kernel,
        "project",
        (1,),
        [whole(item.shape) for item in operands],
        [whole((width, rows)), whole((total, rows))],
        [shaped((width, rows), BF16), shaped((total, rows), BF16)],
        cost=cost,
    )(info, *operands)


def scores_of(keys, queries, masked):
    scores = dot(keys, queries, 1, 0)
    if not masked:
        return scores
    key_row = lax.broadcasted_iota(jnp.int32, scores.shape, 0)
    query_row = lax.broadcasted_iota(jnp.int32, scores.shape, 1)
    return jnp.where(key_row <= query_row, scores, -1e30)


def attend_kernel(
    info, q, k_own, v_own, k_past, v_past, out, lse, keys_own, keys_past, peak, total, mixed
):
    rows = q.shape[1]
    block = min(256, rows)
    hd = HEAD_DIM
    groups = [(group, slice(group * hd, (group + 1) * hd)) for group in range(GROUP)]
    keys_own[...] = k_own[...].T

    @pl.loop(0, info[1])
    def _(device):
        keys_past[device] = k_past[device].T

    for start in range(0, rows, block):
        for group, head in groups:
            scores = scores_of(keys_own[start : start + block, :], q[head, start:], True)
            fresh = jnp.max(scores, 0, keepdims=True)
            if start > 0:
                fresh = jnp.maximum(fresh, peak[group : group + 1, start:])
            peak[group : group + 1, start:] = fresh

    @pl.loop(0, info[1])
    def _(device):
        for group, head in groups:
            scores = scores_of(keys_past[device], q[head, :], False)
            peak[group : group + 1, :] = jnp.maximum(
                peak[group : group + 1, :], jnp.max(scores, 0, keepdims=True)
            )

    def add(group, head, keys, values, start, masked, first):
        scores = scores_of(keys, q[head, start:], masked)
        exponent = jnp.exp(scores - peak[group : group + 1, start:])
        sums = jnp.sum(exponent, 0, keepdims=True)
        product = dot(values, exponent.astype(BF16), 1, 0)
        if first:
            total[group : group + 1, :] = sums
            mixed[head, :] = product
        else:
            total[group : group + 1, start:] += sums
            mixed[head, start:] += product

    for start in range(0, rows, block):
        part = slice(start, start + block)
        for group, head in groups:
            add(group, head, keys_own[part, :], v_own[:, part], start, True, start == 0)

    @pl.loop(0, info[1])
    def _(device):
        for group, head in groups:
            add(group, head, keys_past[device], v_past[device], 0, False, False)

    for group, head in groups:
        sums = total[group : group + 1, :]
        out[head, :] = (mixed[head, :] / sums).astype(BF16)
        lse[0, group : group + 1, :] = peak[group : group + 1, :] + jnp.log(sums)


def attention_specs(rows, past, base):
    hd = HEAD_DIM
    return [
        pl.BlockSpec((GROUP * hd, rows), lambda h, info: (base + h, 0)),
        pl.BlockSpec((hd, rows), lambda h, info: (QUERY_HEADS + base + h, 0)),
        pl.BlockSpec((hd, rows), lambda h, info: (QUERY_HEADS + KEY_HEADS + base + h, 0)),
        pl.BlockSpec((past, hd, rows), lambda h, info: (0, base + h, 0)),
        pl.BlockSpec((past, hd, rows), lambda h, info: (0, KEY_HEADS + base + h, 0)),
    ]


def attend(info, qkv, past, base, heads):
    rows = qkv.shape[1]
    count = past.shape[0]
    group = GROUP * HEAD_DIM
    return call(
        attend_kernel,
        "attend",
        (heads,),
        attention_specs(rows, count, base),
        [
            pl.BlockSpec((group, rows), lambda h, info: (h, 0)),
            pl.BlockSpec((1, 8, rows), lambda h, info: (h, 0, 0)),
        ],
        [shaped((heads * group, rows), BF16), shaped((heads, 8, rows), F32)],
        [
            pltpu.VMEM((rows, HEAD_DIM), BF16),
            pltpu.VMEM((count, rows, HEAD_DIM), BF16),
            pltpu.VMEM((8, rows), F32),
            pltpu.VMEM((8, rows), F32),
            pltpu.VMEM((GROUP * HEAD_DIM, rows), F32),
        ],
    )(info, qkv, qkv, qkv, past, past)


def mix_kernel(info, x, mixed, weight, gain, middle, normed):
    middle[...] = x[...].astype(F32) + dot(weight[...], mixed[...], 0, 0)
    values = middle[...]
    normed[...] = (values * scale_of(values) * gain[...]).astype(BF16)


def mix(info, x, mixed, weight, gain):
    width, rows = x.shape
    operands = (x, mixed, weight, gain)
    return call(
        mix_kernel,
        "mix",
        (1,),
        [whole(item.shape) for item in operands],
        [whole((width, rows)), whole((width, rows))],
        [shaped((width, rows), F32), shaped((width, rows), BF16)],
    )(info, *operands)


def activate(token_rows, gate_weight, up_weight, hidden, silu, slope):
    gate = dot(token_rows[...], gate_weight[...], 1, 0)
    up = dot(token_rows[...], up_weight[...], 1, 0)
    sigmoid = 0.5 * jnp.tanh(0.5 * gate) + 0.5
    active = gate * sigmoid
    hidden[...] = (active * up).astype(BF16)
    silu[...] = active.astype(BF16)
    slope[...] = (up * (sigmoid + active * (1.0 - sigmoid))).astype(BF16)


def expand_kernel(info, normed, gate_weight, up_weight, hidden, silu, slope, token_rows):
    @pl.when(pl.program_id(0) == 0)
    def _():
        token_rows[...] = normed[...].T

    activate(token_rows, gate_weight, up_weight, hidden, silu, slope)


def expand(info, normed, gate, up):
    width, rows = normed.shape
    ff = gate.shape[1]
    tile = ff // 5
    weight = pl.BlockSpec((width, tile), lambda t, info: (0, t))
    result = pl.BlockSpec((rows, tile), lambda t, info: (0, t))
    return call(
        expand_kernel,
        "expand",
        (ff // tile,),
        [whole((width, rows)), weight, weight],
        [result] * 3,
        [shaped((rows, ff), BF16)] * 3,
        [pltpu.VMEM((rows, width), BF16)],
    )(info, normed, gate, up)


def expand_first_kernel(info, normed, *refs):
    gate_parts, up_parts = refs[:5], refs[5:10]
    hidden, silu, slope, gate_weight, up_weight, token_rows = refs[10:]
    step = pl.program_id(0)
    steps = pl.num_programs(0)

    @pl.when(step == 0)
    def _():
        token_rows[...] = normed[...].T

    for (own, *pieces), target in ((gate_parts, gate_weight), (up_parts, up_weight)):
        half, quarter = own.shape[0], pieces[0].shape[0]
        target[pl.ds(pl.multiple_of(info[0] * half, half), half), :] = own[...]
        other = (1 - info[0]) * half
        near = pl.ds(pl.multiple_of(other + info[3] * quarter, quarter), quarter)
        far = pl.ds(pl.multiple_of(other + (1 - info[3]) * quarter, quarter), quarter)

        @pl.when(step < steps // 2)
        def _():
            target[near, :] = pieces[0][...]
            target[far, :] = pieces[1][...]

        @pl.when(step >= steps // 2)
        def _():
            target[near, :] = pieces[2][...]
            target[far, :] = pieces[3][...]

    activate(token_rows, gate_weight, up_weight, hidden, silu, slope)


def expand_first(info, normed, gate, up):
    width, rows = normed.shape
    half, ff = gate[0].shape
    steps = 4
    tile = ff // steps
    quarter = half // 2

    def column(t, info):
        own = info[2] * (steps // 2) + t
        return jnp.where(t < steps // 2, own, (1 - info[2]) * (steps // 2) + t - steps // 2)

    early = pl.BlockSpec((quarter, tile), lambda t, info: (0, jnp.minimum(t, steps // 2 - 1)))
    late = pl.BlockSpec((quarter, tile), lambda t, info: (0, jnp.maximum(t - steps // 2, 0)))
    parts = [pl.BlockSpec((half, tile), lambda t, info: (0, column(t, info)))]
    parts += [early, early, late, late]
    result = pl.BlockSpec((rows, tile), lambda t, info: (0, column(t, info)))
    weight = pl.BlockSpec((width, tile), lambda t, info: (0, column(t, info)))
    return call(
        expand_first_kernel,
        "expand_first",
        (steps,),
        [whole((width, rows))] + parts * 2,
        [result] * 3 + [weight] * 2,
        [shaped((rows, ff), BF16)] * 3 + [shaped((width, ff), BF16)] * 2,
        [pltpu.VMEM((rows, width), BF16)],
    )(info, normed, *gate, *up)


def shrink_kernel(info, middle, hidden, weight, out):
    out[...] = (middle[...] + dot(weight[...], hidden[...], 1, 1)).astype(out.dtype)


def shrink(info, middle, hidden, down, dtype, cost=None):
    width, rows = middle.shape
    ff = hidden.shape[1]
    tile = width // 2
    return call(
        shrink_kernel,
        "shrink",
        (width // tile,),
        [
            pl.BlockSpec((tile, rows), lambda t, info: (t, 0)),
            whole((rows, ff)),
            pl.BlockSpec((tile, ff), lambda t, info: (t, 0)),
        ],
        [pl.BlockSpec((tile, rows), lambda t, info: (t, 0))],
        [shaped((width, rows), dtype)],
        cost=cost,
    )(info, middle, hidden, down)[0]


def shrink_first_kernel(info, middle, hidden, own, near_0, far_0, near_1, far_1, out, weight):
    half, quarter = own.shape[1], near_0.shape[0]
    weight[:, pl.ds(pl.multiple_of(info[0] * half, half), half)] = own[...]
    other = pl.ds(pl.multiple_of((1 - info[0]) * half, half), half)
    at_near = pl.ds(pl.multiple_of(info[2] * quarter, quarter), quarter)
    at_far = pl.ds(pl.multiple_of((1 - info[2]) * quarter, quarter), quarter)
    for step, near, far in ((0, near_0, far_0), (1, near_1, far_1)):

        @pl.when(pl.program_id(0) == step)
        def _():
            weight[at_near, other] = near[...]
            weight[at_far, other] = far[...]

    out[...] = middle[...] + dot(weight[...], hidden[...], 1, 1)


def shrink_first(info, middle, hidden, parts):
    width, rows = middle.shape
    ff = hidden.shape[1]
    tile = width // 2
    own, first, second, third, fourth = parts

    def row(t, info):
        return jnp.where(t == 0, info[3], 1 - info[3])

    return call(
        shrink_first_kernel,
        "shrink_first",
        (2,),
        [
            pl.BlockSpec((tile, rows), lambda t, info: (row(t, info), 0)),
            whole((rows, ff)),
            pl.BlockSpec((tile, ff // 2), lambda t, info: (row(t, info), 0)),
        ]
        + [whole(first.shape)] * 4,
        [
            pl.BlockSpec((tile, rows), lambda t, info: (row(t, info), 0)),
            pl.BlockSpec((tile, ff), lambda t, info: (row(t, info), 0)),
        ],
        [shaped((width, rows), F32), shaped((width, ff), BF16)],
    )(info, middle, hidden, own, first, third, second, fourth)


def ffn_back_kernel(
    info,
    grad,
    middle,
    gain,
    silu,
    slope,
    down,
    gate,
    up,
    out_weight,
    gate_grad,
    up_grad,
    branch,
    grad_middle,
    attn_grad,
    mixed_grad,
    gain_grad,
    branch_rows,
    total,
):
    step = pl.program_id(0)
    steps = pl.num_programs(0)

    @pl.when(step == 0)
    def _():
        branch[...] = grad[...].astype(BF16)
        branch_rows[...] = branch[...].T
        total[...] = jnp.zeros_like(total)

    incoming = dot(branch_rows[...], down[...], 1, 0)
    gate_grad[...] = (incoming * slope[...].astype(F32)).astype(BF16)
    up_grad[...] = (incoming * silu[...].astype(F32)).astype(BF16)
    total[...] += dot(gate[...], gate_grad[...], 1, 1) + dot(up[...], up_grad[...], 1, 1)

    @pl.when(step == steps - 1)
    def _():
        back, gain_sum = norm_back(middle[...], gain[...], total[...])
        gain_grad[...] = gain_sum
        result = grad[...].astype(F32) + back
        grad_middle[...] = result
        attn_grad[...] = result.astype(BF16)
        mixed_grad[...] = dot(out_weight[...], attn_grad[...], 1, 0).astype(BF16)


def ffn_back(info, grad, middle, gain, silu, slope, down, gate, up, out_weight, cost=None):
    width, rows = middle.shape
    ff = silu.shape[1]
    tile = ff // 5
    heads = out_weight.shape[0]
    token = pl.BlockSpec((rows, tile), lambda t, info: (0, t))
    weight = pl.BlockSpec((width, tile), lambda t, info: (0, t))
    return call(
        ffn_back_kernel,
        "ffn_back",
        (ff // tile,),
        [
            whole((width, rows)),
            whole((width, rows)),
            whole((width, 1)),
            token,
            token,
            weight,
            weight,
            weight,
            whole((heads, width)),
        ],
        [
            token,
            token,
            whole((width, rows)),
            whole((width, rows)),
            whole((width, rows)),
            whole((heads, rows)),
            whole((width, 1)),
        ],
        [
            shaped((rows, ff), BF16),
            shaped((rows, ff), BF16),
            shaped((width, rows), BF16),
            shaped((width, rows), F32),
            shaped((width, rows), BF16),
            shaped((heads, rows), BF16),
            shaped((width, 1), F32),
        ],
        [pltpu.VMEM((rows, width), BF16), pltpu.VMEM((width, rows), F32)],
        cost=cost,
    )(info, grad, middle, gain, silu, slope, down, gate, up, out_weight)


def attend_back_kernel(
    info,
    q,
    k_own,
    v_own,
    k_past,
    v_past,
    mixed_grad,
    mixed,
    lse,
    cosine,
    sine,
    q_grad,
    own_grad,
    past_grad,
    keys_own,
    values_own,
    keys_past,
    values_past,
    inner,
    q_sum,
):
    rows = q.shape[1]
    block = min(256, rows)
    hd = HEAD_DIM
    groups = [(group, slice(group * hd, (group + 1) * hd)) for group in range(GROUP)]
    keys_own[...] = k_own[...].T
    values_own[...] = v_own[...].T

    @pl.loop(0, info[1])
    def _(device):
        keys_past[device] = k_past[device].T
        values_past[device] = v_past[device].T

    @pl.loop(info[1], past_grad.shape[0])
    def _(device):
        past_grad[device] = jnp.zeros_like(past_grad[device])

    for group, head in groups:
        product = mixed_grad[head, :].astype(F32) * mixed[head, :].astype(F32)
        inner[group : group + 1, :] = jnp.sum(product, 0, keepdims=True)

    def step(keys, key_rows, value_rows, start, masked, first):
        key_sum = value_sum = None
        for group, head in groups:
            query, incoming = q[head, start:], mixed_grad[head, start:]
            one = slice(group, group + 1)
            probs = jnp.exp(scores_of(key_rows, query, masked) - lse[0, one, start:])
            slopes = dot(value_rows, incoming, 1, 0)
            low = (probs * (slopes - inner[one, start:])).astype(BF16)
            value_part = dot(incoming, probs.astype(BF16), 1, 1)
            key_part = dot(query, low, 1, 1)
            key_sum = key_part if key_sum is None else key_sum + key_part
            value_sum = value_part if value_sum is None else value_sum + value_part
            query_part = dot(keys, low, 1, 0)
            if first:
                q_sum[head, :] = query_part
            else:
                q_sum[head, start:] += query_part
        return key_sum, value_sum

    for start in range(0, rows, block):
        part = slice(start, start + block)
        key_sum, value_sum = step(
            k_own[:, part], keys_own[part, :], values_own[part, :], start, True, start == 0
        )
        own_grad[0, :hd, part] = key_sum
        own_grad[0, hd:, part] = value_sum

    @pl.loop(0, info[1])
    def _(device):
        key_sum, value_sum = step(
            k_past[device], keys_past[device], values_past[device], 0, False, False
        )
        past_grad[device, 0, :hd, :] = key_sum.astype(past_grad.dtype)
        past_grad[device, 0, hd:, :] = value_sum.astype(past_grad.dtype)

    cos, sin = cosine[...], -sine[...]
    for group, head in groups:
        first, second = rotate(q_sum[head, :], cos, sin)
        at = group * hd
        q_grad[at : at + hd // 2, :] = (first * hd**-0.5).astype(BF16)
        q_grad[at + hd // 2 : at + hd, :] = (second * hd**-0.5).astype(BF16)


def attend_back(info, qkv, past, mixed_grad, mixed, lse, tables, base, heads, cost=None):
    rows = qkv.shape[1]
    count = past.shape[0]
    hd = HEAD_DIM
    group = pl.BlockSpec((GROUP * hd, rows), lambda h, info: (base + h, 0))
    return call(
        attend_back_kernel,
        "attend_back",
        (heads,),
        attention_specs(rows, count, base)
        + [
            group,
            group,
            pl.BlockSpec((1, 8, rows), lambda h, info: (base + h, 0, 0)),
            whole(tables[0].shape),
            whole(tables[1].shape),
        ],
        [
            pl.BlockSpec((GROUP * hd, rows), lambda h, info: (h, 0)),
            pl.BlockSpec((1, 2 * hd, rows), lambda h, info: (h, 0, 0)),
            pl.BlockSpec((count, 1, 2 * hd, rows), lambda h, info: (0, h, 0, 0)),
        ],
        [
            shaped((heads * GROUP * hd, rows), BF16),
            shaped((heads, 2 * hd, rows), F32),
            shaped((count, heads, 2 * hd, rows), BF16 if count == 1 else F32),
        ],
        [
            pltpu.VMEM((rows, hd), BF16),
            pltpu.VMEM((rows, hd), BF16),
            pltpu.VMEM((count, rows, hd), BF16),
            pltpu.VMEM((count, rows, hd), BF16),
            pltpu.VMEM((8, rows), F32),
            pltpu.VMEM((GROUP * hd, rows), F32),
        ],
        cost=cost,
    )(info, qkv, qkv, qkv, past, past, mixed_grad, mixed, lse, *tables)


def project_back_kernel(parts, info, x, gain, grad_middle, *refs):
    q_grads, own_grads, arrived = refs[:parts], refs[parts : 2 * parts], refs[2 * parts : 3 * parts]
    (
        q_weight,
        k_own,
        k_oth,
        v_own,
        v_oth,
        cosine,
        sine,
        q_grad,
        kv_grad,
        out,
        branch,
        gain_grad,
        total,
    ) = refs[3 * parts :]
    half = x.shape[0] // 2
    hd = HEAD_DIM
    kv = KEY_HEADS * hd
    cos, sin = cosine[...], -sine[...]
    head = 0
    for piece, own, far in zip(q_grads, own_grads, arrived):
        q_grad[head * GROUP * hd : head * GROUP * hd + piece.shape[0], :] = piece[...]
        for item in range(own.shape[0]):
            both = own[item] + far[item].astype(F32)
            first, second = rotate(both[:hd], cos, sin)
            at = head * hd
            kv_grad[at : at + hd // 2, :] = first.astype(BF16)
            kv_grad[at + hd // 2 : at + hd, :] = second.astype(BF16)
            kv_grad[kv + at : kv + at + hd, :] = both[hd:].astype(BF16)
            head += 1
    total[...] = dot(q_weight[...], q_grad[...], 1, 0)
    for mine, k, v in ((info[0], k_own, v_own), (1 - info[0], k_oth, v_oth)):
        total[pl.ds(pl.multiple_of(mine * half, half), half), :] += dot(
            k[...], kv_grad[:kv, :], 0, 0
        ) + dot(v[...], kv_grad[kv:, :], 0, 0)
    back, gain_sum = norm_back(x[...].astype(F32), gain[...], total[...])
    gain_grad[...] = gain_sum
    result = grad_middle[...] + back
    out[...] = result
    branch[...] = result.astype(BF16)


def project_back(info, x, gain, grad_middle, q_grads, own_grads, arrived, weights, tables, cost=None):
    width, rows = x.shape
    q, k, v = weights
    heads = q.shape[1]
    kv = 2 * KEY_HEADS * HEAD_DIM
    operands = (x, gain, grad_middle, *q_grads, *own_grads, *arrived, q, *k, *v, *tables)
    shapes = [
        shaped((heads, rows), BF16),
        shaped((kv, rows), BF16),
        shaped((width, rows), F32),
        shaped((width, rows), BF16),
        shaped((width, 1), F32),
    ]
    return call(
        functools.partial(project_back_kernel, len(q_grads)),
        "project_back",
        (1,),
        [whole(item.shape) for item in operands],
        [whole(item.shape) for item in shapes],
        shapes,
        [pltpu.VMEM((width, rows), F32)],
        cost=cost,
    )(info, *operands)


def order_rows(info, target, sources):
    rows = sources[0].shape[1]
    size = target.shape[0] // 4
    at = 0
    for core in (1 - info[2], info[2]):
        for half in (1 - info[0], info[0]):
            start = pl.multiple_of((2 * half + core) * size, size)
            for index, source in enumerate(sources):
                target[at : at + size, index * rows : (index + 1) * rows] = source[
                    pl.ds(start, size), :
                ]
            at += size


def order_halves(info, target, sources):
    rows = sources[0].shape[1]
    size = target.shape[0] // 2
    for at, core in ((0, 1 - info[2]), (size, info[2])):
        start = pl.multiple_of(core * size, size)
        for index, source in enumerate(sources):
            target[at : at + size, index * rows : (index + 1) * rows] = source[pl.ds(start, size), :]


def outer_kernel(split_columns, info, left_a, right_a, left_b, right_b, sent, kept, left, right):
    rows = left_a.shape[1]

    @pl.when(pl.program_id(0) == 0)
    def _():
        order = order_halves if split_columns else order_rows
        order(info, left, (left_a, left_b))

    right[:rows, :] = right_a[...]
    right[rows:, :] = right_b[...]
    count, size = sent.shape[0], sent.shape[1]
    for at, out in ((0, sent), (count * size, kept)):
        product = dot(left[at : at + count * size, :], right[...], 1, 0).astype(BF16)
        for index in range(count):
            out[index] = product[index * size : (index + 1) * size]


def outer(info, parts, split_columns, cost=None):
    left_a, right_a, left_b, right_b = parts
    width, rows = left_a.shape
    columns = right_a.shape[1]
    if split_columns:
        tile = columns // 4

        def column(t, info):
            return jnp.where(t < 2, (1 - info[0]) * 2 + t, info[0] * 2 + t - 2)

        right = pl.BlockSpec((rows, tile), lambda t, info: (0, column(t, info)))
        result = pl.BlockSpec((1, width // 2, tile), lambda t, info: (t // 2, 0, t % 2))
        shape = shaped((2, width // 2, columns // 2), BF16)
    else:
        tile = columns // 5
        right = pl.BlockSpec((rows, tile), lambda t, info: (0, t))
        result = pl.BlockSpec((2, width // 4, tile), lambda t, info: (0, 0, t))
        shape = shaped((2, width // 4, columns), BF16)
    return call(
        functools.partial(outer_kernel, split_columns),
        "outer",
        (columns // tile,),
        [whole((width, rows)), right, whole((width, rows)), right],
        [result, result],
        [shape, shape],
        [pltpu.VMEM((width, 2 * rows), BF16), pltpu.VMEM((2 * rows, tile), BF16)],
        cost=cost,
    )(info, *parts)


def pack_kernel(extra, info, left_a, *refs):
    sent, kept, left, right = refs[-4:]
    refs = refs[:-4]
    gains, refs = refs[len(refs) - extra :], refs[: len(refs) - extra]
    left_b, rights_a, rights_b = refs[0], refs[1::2], refs[2::2]
    rows = left_a.shape[1]
    order_rows(info, left, (left_a, left_b))
    at = 0
    for right_a, right_b in zip(rights_a, rights_b):
        right[at : at + right_a.shape[0], :rows] = right_a[...]
        right[at : at + right_a.shape[0], rows:] = right_b[...]
        at += right_a.shape[0]
    count, size = sent.shape[0], sent.shape[1]
    for base, core, out in ((0, 1 - info[2], sent), (count * size, info[2], kept)):
        for start, span in spans(right.shape[0], 512):
            product = dot(left[base : base + count * size, :], right[start : start + span, :], 1, 1)
            for index in range(count):
                out[index, :, start : start + span] = product[
                    index * size : (index + 1) * size
                ].astype(BF16)
        for index, half in enumerate((1 - info[0], info[0])):
            part = pl.ds(pl.multiple_of((2 * half + core) * size, size), size)
            for number in range(extra // 2):
                term = gains[2 * number][part, :] + gains[2 * number + 1][part, :]
                out[index, :, at + number : at + number + 1] = term.astype(BF16)
            if extra:
                out[index, :, at + extra // 2 :] = jnp.zeros((size, extra // 2), BF16)


def pack(info, left_a, left_b, rights, gains=(), cost=None):
    width, rows = left_a.shape
    columns = sum(item.shape[0] for item in rights[::2])
    operands = (left_a, left_b, *rights, *gains)
    shape = shaped((2, width // 4, columns + len(gains)), BF16)
    return call(
        functools.partial(pack_kernel, len(gains)),
        "pack",
        (1,),
        [whole(item.shape) for item in operands],
        [whole(shape.shape)] * 2,
        [shape, shape],
        [pltpu.VMEM((width, 2 * rows), BF16), pltpu.VMEM((columns, 2 * rows), BF16)],
        cost=cost,
    )(info, *operands)


def last_kernel(info, held, query, key, value, gains):
    width, narrow = query.shape[1], key.shape[0]
    values = held[...].astype(F32)
    query[...] = values[:, :width]
    key[...] = values[:, width : width + narrow].T
    value[...] = values[:, width + narrow : width + 2 * narrow].T
    gains[...] = values[:, width + 2 * narrow :]


def last(info, held, width, narrow):
    rows, columns = held.shape
    shapes = [
        shaped((rows, width), F32),
        shaped((narrow, rows), F32),
        shaped((narrow, rows), F32),
        shaped((rows, columns - width - 2 * narrow), F32),
    ]
    return call(last_kernel, "last", (1,), [None], [None] * 4, shapes, cost=0)(info, held)


def column_split(columns):
    return columns // 2 // 128 * 128


def both_cores_kernel(info, kept, arrived, over_y, keep_y, over_x, keep_x):
    split = over_y.shape[1]
    half = over_x.shape[1]
    for index, out in ((0, over_y), (1, keep_y)):
        total = kept[index].astype(F32) + arrived[index].astype(F32)
        out[...] = total[:, :split].astype(BF16)
        low, top = total[:half, split:], total[half:, split:]
        keep_x[index] = jnp.where(info[3] == 0, low, top).astype(BF16)
        over_x[index] = jnp.where(info[3] == 0, top, low).astype(BF16)


def both_cores(info, kept, arrived):
    _, rows, columns = kept.shape
    split = column_split(columns)
    first = shaped((rows, split), BF16)
    second = shaped((2, rows // 2, columns - split), BF16)
    shapes = [first, first, second, second]
    return call(
        both_cores_kernel, "both_cores", (1,), [None] * 2, [None] * 4, shapes, cost=0
    )(info, kept, arrived)


def cross_kernel(info, keep_y, from_y, keep_x, from_x, over_x, over_y, kept):
    split, half = over_x.shape[1], over_x.shape[0]
    total = keep_y[...].astype(F32) + from_y[...].astype(F32)
    low, top = total[:half], total[half:]
    over_x[...] = jnp.where(info[3] == 0, top, low).astype(BF16)
    kept[:, :split] = jnp.where(info[3] == 0, low, top).astype(BF16)
    over_y[...] = (keep_x[0].astype(F32) + from_x[0].astype(F32)).astype(BF16)
    kept[:, split:] = (keep_x[1].astype(F32) + from_x[1].astype(F32)).astype(BF16)


def cross(info, keep_y, from_y, keep_x, from_x):
    rows, split = keep_y.shape
    rest = keep_x.shape[2]
    shapes = [
        shaped((rows // 2, split), BF16),
        shaped((rows // 2, rest), BF16),
        shaped((rows // 2, split + rest), BF16),
    ]
    return call(cross_kernel, "cross", (1,), [None] * 4, [None] * 3, shapes, cost=0)(
        info, keep_y, from_y, keep_x, from_x
    )


def swap(values, axis, bit):
    size = lax.axis_size(axis)
    return lax.ppermute(values, axis, [(i, i ^ bit) for i in range(size)])


def bits_of(axis):
    size = lax.axis_size(axis)
    assert size & (size - 1) == 0
    return [1 << i for i in range(size.bit_length() - 1)]


def high(axis, bit):
    return (lax.axis_index(axis) // bit) % 2


def halves(values, dim, which):
    half = values.shape[dim] // 2
    return lax.dynamic_slice_in_dim(values, which * half, half, dim)


def joined(mine, other, dim, which):
    return jnp.where(
        which == 0,
        jnp.concatenate([mine, other], dim),
        jnp.concatenate([other, mine], dim),
    )


def tied(values, others):
    return lax.optimization_barrier((values, others))[0]


def from_pieces(own, pieces, mine, core, low_batch):
    near = joined(pieces[0], pieces[2], 0, core)
    far = joined(pieces[1], pieces[3], 0, core)
    return joined(own, joined(near, far, 0, low_batch), 0, mine)


def split_dim(shape, parts):
    if shape[0] % (8 * parts) == 0:
        return 0
    if shape[1] % (128 * parts) == 0:
        return 1
    return 0 if shape[0] % parts == 0 else 1


class Order:
    def __init__(self, token):
        self.token = token

    def __call__(self, *values):
        self.token, *values = lax.optimization_barrier((self.token, *values))
        return values[0] if len(values) == 1 else values


def quarters(values, dim, number):
    quarter = values.shape[dim] // 4
    return lax.dynamic_slice_in_dim(values, number * quarter, quarter, dim)


class Chain:
    def __init__(self, order, away, kept):
        self.order, self.kept = order, kept
        self.away = away
        self.steps = [self.core, self.first, self.second]
        self.shares = [("seq", (1,), 0), ("batch", (1,), 0)]
        exchanges = [("seq", (bit,)) for bit in bits_of("seq")[1:]]
        bits = bits_of("batch")[1:]
        while bits:
            exchanges.append(("batch", bits[:2]))
            bits = bits[2:]
        self.steps += [functools.partial(self.add, *item) for item in exchanges]
        self.steps += [self.share] * (2 + len(exchanges))
        self.waiting = None

    def send(self):
        self.waiting = self.steps.pop(0)()

    def core(self):
        def finish(arrived):
            self.parts = both_cores(self.order.token, self.kept, arrived)

        return [swap(self.order(self.away), "seq", 1)], finish

    def first(self):
        over_y, keep_y, over_x, keep_x = self.parts
        over_y, over_x = self.order(over_y, over_x)

        def finish(from_y, from_x):
            self.parts = cross(self.order.token, keep_y, from_y, keep_x, from_x)

        return [swap(over_y, "fsdp", 1), swap(over_x, "batch", 1)], finish

    def second(self):
        over_x, over_y, kept = self.parts
        over_x, over_y = self.order(over_x, over_y)

        def finish(from_x, from_y):
            arrived = jnp.concatenate([from_x, from_y], 1)
            self.held = (kept.astype(F32) + arrived.astype(F32)).astype(BF16)

        return [swap(over_x, "batch", 1), swap(over_y, "fsdp", 1)], finish

    def add(self, axis, bits):
        held = self.held
        dim = split_dim(held.shape, 2 * len(bits))
        take = halves if len(bits) == 1 else quarters
        number = sum(high(axis, bit) << index for index, bit in enumerate(bits))
        masks = range(1, 1 << len(bits))
        parts = self.order(*[take(held, dim, number ^ mask) for mask in masks])
        parts = parts if len(bits) > 1 else [parts]
        arrived = [
            swap(part, axis, sum(bit for index, bit in enumerate(bits) if mask >> index & 1))
            for mask, part in zip(masks, parts)
        ]
        self.shares.append((axis, bits, dim))

        def finish(*values):
            total = take(held, dim, number).astype(F32)
            for item in values:
                total = total + item.astype(F32)
            self.held = total.astype(BF16)

        return arrived, finish

    def share(self):
        axis, bits, dim = self.shares.pop()
        held = self.order(self.held)
        masks = range(1, 1 << len(bits))
        arrived = [
            swap(held, axis, sum(bit for index, bit in enumerate(bits) if mask >> index & 1))
            for mask in masks
        ]

        def finish(*values):
            low = high(axis, bits[0])
            if len(bits) == 1:
                self.held = joined(held, values[0], dim, low)
                return
            near, far = joined(held, values[0], dim, low), joined(values[1], values[2], dim, low)
            self.held = joined(near, far, dim, high(axis, bits[1]))

        return arrived, finish

    def result(self):
        while self.waiting or self.steps:
            if self.waiting:
                take(self)
            else:
                self.send()
        return self.held


def take(*chains):
    flat = [item for chain in chains for item in chain.waiting[0]]
    values = chains[0].order(*flat)
    values = list(values) if len(flat) > 1 else [values]
    for chain in chains:
        arrived, finish = chain.waiting
        chain.waiting = None
        finish(*values[: len(arrived)])
        values = values[len(arrived) :]


def per_device(
    tokens,
    attn_gain,
    w_query,
    key_weight,
    value_weight,
    w_out,
    ffn_gain,
    w_gate,
    w_up,
    w_down,
    cotangent,
):
    assert tokens.shape[0] == 1 and lax.axis_size("fsdp") == 2
    mine, spot, core = lax.axis_index("fsdp"), lax.axis_index("seq"), high("seq", 1)
    low_batch = high("batch", 1)
    devices = lax.axis_size("seq")
    info = jnp.stack([mine, spot, core, low_batch]).astype(jnp.int32)
    start_in = tokens[0].T
    incoming = cotangent[0].T
    width, rows = start_in.shape

    gains = jnp.stack([attn_gain, ffn_gain])
    gains = joined(gains, swap(gains, "fsdp", 1), 1, mine).astype(F32)[..., None]
    key_weight, value_weight, w_down = key_weight.T, value_weight.T, w_down.T
    def fsdp(values):
        return swap(values, "fsdp", 1)

    def pair(values):
        return swap(values, "batch", 1)

    def cores(values):
        return swap(values, "seq", 1)

    positions = (spot * rows + jnp.arange(rows, dtype=jnp.int32)).astype(F32)
    frequency = jnp.exp(
        jnp.arange(HEAD_DIM // 2, dtype=F32) * (-2.0 * math.log(10000.0) / HEAD_DIM)
    )
    angles = frequency[:, None] * positions[None, :]
    tables = (jnp.cos(angles), jnp.sin(angles))

    def gathered(qkv):
        kv = qkv[QUERY_HEADS * HEAD_DIM :]
        if devices == 2:
            return cores(kv)[None]
        return lax.all_gather(kv, "seq")

    order = Order(info)

    def column_piece(weight):
        return halves(halves(weight, 0, low_batch), 1, core)

    def row_piece(weight):
        return halves(halves(weight, 0, low_batch), 0, core)

    kv_piece = halves(jnp.where(core == 0, key_weight, value_weight), 0, low_batch)
    q_piece, kv_piece = order(row_piece(w_query), kv_piece)
    q_0, kv_0 = fsdp(q_piece), fsdp(kv_piece)
    out_piece, gate_piece = row_piece(w_out), column_piece(w_gate)
    q_0, kv_0, out_piece, gate_piece = order(q_0, kv_0, out_piece, gate_piece)
    q_1, kv_1, q_2, kv_2 = pair(q_0), pair(kv_0), cores(q_0), cores(kv_0)
    out_0, gate_0 = fsdp(out_piece), fsdp(gate_piece)
    q_1, kv_1, q_2, kv_2 = order(q_1, kv_1, q_2, kv_2)
    q_3, kv_3 = order(cores(q_1), cores(kv_1))
    q_weight = from_pieces(w_query, (q_0, q_1, q_2, q_3), mine, core, low_batch)
    held = joined(kv_0, kv_1, 0, low_batch)
    other = joined(kv_2, kv_3, 0, low_batch)
    k_oth, v_oth = jnp.where(core == 0, held, other), jnp.where(core == 0, other, held)
    qkv_weights = (q_weight, (key_weight, k_oth), (value_weight, v_oth))
    low_normed, low_qkv = project(info, start_in, gains[0], qkv_weights, tables, 0)
    low_qkv, out_0, gate_0, up_piece = order(low_qkv, out_0, gate_0, column_piece(w_up))
    low_past, up_0 = gathered(low_qkv), fsdp(up_piece)
    out_1, out_2, gate_1, gate_2 = pair(out_0), cores(out_0), pair(gate_0), cores(gate_0)
    near_mixed, near_lse = attend(info, low_qkv, order(low_past), 0, 3)
    near_mixed, up_0, out_1, out_2, gate_1, gate_2, down_piece = order(
        near_mixed, up_0, out_1, out_2, gate_1, gate_2, row_piece(w_down)
    )
    down_0, up_1, up_2 = fsdp(down_piece), pair(up_0), cores(up_0)
    out_3, gate_3 = cores(out_1), cores(gate_1)
    far_mixed, far_lse = attend(info, low_qkv, order(low_past), 3, 2)
    far_mixed, out_3, gate_3, up_2 = order(far_mixed, out_3, gate_3, up_2)
    low_mixed = jnp.concatenate([near_mixed, far_mixed], 0)
    low_lse = jnp.concatenate([near_lse, far_lse], 0)
    out_weight = from_pieces(w_out, (out_0, out_1, out_2, out_3), mine, core, low_batch)
    low_middle, low_normed_ffn = mix(info, start_in, low_mixed, out_weight, gains[1])
    low_normed_ffn, down_0, up_1 = order(low_normed_ffn, down_0, up_1)
    up_3, down_1, down_2 = cores(up_1), pair(down_0), cores(down_0)
    low_normed_ffn, up_3 = order(low_normed_ffn, up_3)
    low_hidden, low_silu, low_slope, gate, up = expand_first(
        info,
        low_normed_ffn,
        (w_gate, gate_0, gate_1, gate_2, gate_3),
        (w_up, up_0, up_1, up_2, up_3),
    )
    low_hidden, down_1, down_2 = order(low_hidden, down_1, down_2)
    down_3 = order(cores(down_1))
    middle_in, down = shrink_first(
        info, low_middle, low_hidden, (w_down, down_0, down_1, down_2, down_3)
    )

    high_normed, high_qkv = project(info, middle_in, gains[0], qkv_weights, tables)
    high_past = gathered(high_qkv)
    high_mixed, high_lse = attend(info, high_qkv, high_past, 0, KEY_HEADS)
    high_middle, high_normed_ffn = mix(info, middle_in, high_mixed, out_weight, gains[1])
    high_hidden, high_silu, high_slope = expand(info, high_normed_ffn, gate, up)

    def attention_back(qkv, past, mixed_grad, mixed, lse, base, heads, cost=None):
        return attend_back(
            info, qkv, past, mixed_grad, mixed, lse, tables, base, heads, cost
        )

    def returned(past_grad):
        if devices == 2:
            return cores(past_grad[0])
        return lax.psum_scatter(past_grad, "seq", scatter_dimension=0)

    def to_input(x, grad_middle, parts, cost=None):
        return project_back(
            info, x, gains[0], grad_middle, *zip(*parts), qkv_weights, tables, cost
        )

    high_gate, high_up, high_branch, grad_middle, high_attn, mixed_grad, high_ffn_gain = ffn_back(
        info, incoming, high_middle, gains[1], high_silu, high_slope, down, gate, up, out_weight
    )
    parts = [
        attention_back(high_qkv, high_past, mixed_grad, high_mixed, high_lse, base, heads)
        for base, heads in ((0, 3), (3, 2))
    ]
    parts = [(*part[:2], returned(part[2])) for part in parts]
    high_q, high_kv, grad_between, low_branch, high_attn_gain = to_input(
        middle_in, grad_middle, parts
    )

    order = Order(tied(order.token, low_branch))
    down_terms = (high_branch, high_hidden, low_branch, low_hidden)
    down_g = Chain(order, *outer(info, down_terms, True, 0))
    down_g.send()
    final_out = order(shrink(info, order(high_middle), high_hidden, down, BF16, 20))
    take(down_g)
    down_g.send()
    low_gate, low_up, _, grad_middle, low_attn, mixed_grad, low_ffn_gain = ffn_back(
        info, order(grad_between), low_middle, gains[1], low_silu, low_slope,
        down, gate, up, out_weight, 20,
    )
    low_attn = order(low_attn)
    take(down_g)
    down_g.send()
    out_terms = (high_attn, order(low_attn))
    out_g = Chain(order, *pack(info, high_mixed, low_mixed, out_terms, cost=0))
    out_g.send()
    gate_terms = (high_normed_ffn, high_gate, low_normed_ffn, order(low_gate))
    gate_g = Chain(order, *outer(info, gate_terms, False, 0))
    gate_g.send()
    take(down_g, out_g)
    down_g.send()
    out_g.send()
    up_terms = (high_normed_ffn, high_up, low_normed_ffn, order(low_up))
    up_g = Chain(order, *outer(info, up_terms, False, 20))
    up_g.send()
    take(gate_g)
    gate_g.send()
    parts = []

    def low_part(base, heads, cost):
        mixed_now = order(mixed_grad)
        part = attention_back(low_qkv, low_past, mixed_now, low_mixed, low_lse, base, heads, cost)
        parts.append((order(part[0]), *part[1:]))

    low_part(0, 2, 20)
    take(gate_g, down_g, up_g, out_g)
    gate_g.send()
    up_g.send()
    down_g.send()
    out_g.send()
    low_part(2, 2, 20)
    take(gate_g, down_g, out_g)
    gate_g.send()
    down_g.send()
    out_g.send()
    low_part(4, 1, 0)
    parts = [(*part[:2], returned(order(part[2]))) for part in parts]
    take(up_g)
    up_g.send()
    low_q, low_kv, grad_start, _, low_attn_gain = to_input(
        start_in, order(grad_middle), parts, 20
    )
    low_q = order(low_q)
    take(gate_g, up_g, out_g)
    gate_g.send()
    up_g.send()
    out_g.send()
    qkv_terms = (high_q, order(low_q), high_kv, low_kv)
    gain_terms = (high_attn_gain, low_attn_gain, high_ffn_gain, low_ffn_gain)
    qkv_g = Chain(order, *pack(info, high_normed, low_normed, qkv_terms, gain_terms, 20))
    qkv_g.send()
    take(qkv_g, out_g, down_g)
    qkv_g.send()
    out_g.send()
    down_g.send()
    take(qkv_g)
    qkv_g.send()
    take(qkv_g, gate_g, up_g, down_g, out_g)
    qkv_g.send()
    up_g.send()
    gate_g.send()
    down_grad = order(down_g.result().astype(F32))
    out_grad = order(out_g.result().astype(F32))
    take(qkv_g, gate_g, up_g)
    qkv_g.send()
    up_g.send()
    gate_g.send()
    take(qkv_g, gate_g, up_g)
    qkv_g.send()
    up_g.send()
    gate_grad = order(gate_g.result().astype(F32))
    take(qkv_g, up_g)
    qkv_g.send()
    up_grad = order(up_g.result().astype(F32))
    held = order(qkv_g.result())
    narrow = KEY_HEADS * HEAD_DIM
    query_part, key_part, value_part, gain_grads = last(order.token, held, width, narrow)
    return (
        final_out.T[None],
        grad_start.T[None],
        gain_grads[:, 0],
        query_part,
        key_part.T,
        value_part.T,
        out_grad,
        gain_grads[:, 1],
        gate_grad,
        up_grad,
        down_grad.T,
    )


def solution(mesh):
    return jax.shard_map(
        per_device,
        mesh=mesh,
        in_specs=(
            P(("batch", "fsdp"), "seq", None),
            P("fsdp"),
            P("fsdp", None),
            P("fsdp", None),
            P("fsdp", None),
            P("fsdp", None),
            P("fsdp"),
            P("fsdp", None),
            P("fsdp", None),
            P("fsdp", None),
            P(("batch", "fsdp"), "seq", None),
        ),
        out_specs=(
            P(("batch", "fsdp"), "seq", None),
            P(("batch", "fsdp"), "seq", None),
            P("fsdp"),
            P("fsdp", None),
            P("fsdp", None),
            P("fsdp", None),
            P("fsdp", None),
            P("fsdp"),
            P("fsdp", None),
            P("fsdp", None),
            P("fsdp", None),
        ),
        check_vma=False,
    )
```

```python
import functools
import math

import jax
import jax.numpy as jnp
from jax import lax
from jax.experimental import pallas as pl
from jax.experimental.pallas import tpu as pltpu
from jax.sharding import PartitionSpec as P

QUERY_HEADS = 15
KEY_HEADS = 5
HEAD_DIM = 64
GROUP = QUERY_HEADS // KEY_HEADS
EPSILON = 1e-05
F32 = jnp.float32
BF16 = jnp.bfloat16


def dot(left, right, left_dim, right_dim):
    return lax.dot_general(
        left, right, (((left_dim,), (right_dim,)), ((), ())), preferred_element_type=F32
    )


def spans(total, size):
    return [(start, min(size, total - start)) for start in range(0, total, size)]


COSTS = {
    "project": 6.0,
    "attend": 4.0,
    "mix": 5.5,
    "expand": 10.0,
    "expand_first": 14.0,
    "shrink": 6.5,
    "shrink_first": 8.0,
    "ffn_back": 18.0,
    "attend_back": 6.5,
    "project_back": 6.0,
    "outer": 10.0,
    "pack": 4.0,
    "both_cores": 0.0,
    "cross": 0.0,
    "last": 0.0,
    "divide": 0.0,
    "sum": 0.0,
    "unite": 0.0,
}


LIMITS = {
    "project": 12,
    "attend": 14,
    "mix": 12,
    "expand": 24,
    "expand_first": 34,
    "shrink": 22,
    "shrink_first": 34,
    "ffn_back": 40,
    "attend_back": 16,
    "project_back": 16,
    "outer": 26,
    "pack": 20,
    "both_cores": 12,
    "cross": 10,
    "last": 12,
    "divide": 10,
    "sum": 6,
    "unite": 14,
}


def call(kernel, name, grid, in_specs, out_specs, out_shape, scratch=(), cost=None):
    if cost is None:
        cost = COSTS[name] * 0.45 * (grid[0] if name.startswith("attend") else 1)
    cost = int(cost * 1e9) + 1
    options = dict(
        name=name,
        out_shape=out_shape,
        compiler_params=pltpu.CompilerParams(vmem_limit_bytes=LIMITS[name] * 1024 * 1024),
        cost_estimate=pl.CostEstimate(flops=cost, bytes_accessed=1, transcendentals=0),
    )
    if name in ("project", "mix", "project_back", "pack", "both_cores", "cross", "last", "divide", "sum", "unite"):
        memory = pl.BlockSpec(memory_space=pltpu.VMEM)
        return pl.pallas_call(
            kernel,
            in_specs=[pl.BlockSpec(memory_space=pltpu.SMEM)] + [memory] * len(in_specs),
            out_specs=[memory] * len(out_specs),
            scratch_shapes=list(scratch),
            **options,
        )
    return pl.pallas_call(
        kernel,
        grid_spec=pltpu.PrefetchScalarGridSpec(
            num_scalar_prefetch=1,
            grid=grid,
            in_specs=in_specs,
            out_specs=out_specs,
            scratch_shapes=list(scratch),
        ),
        **options,
    )


def whole(shape):
    return pl.BlockSpec(shape, lambda *_: (0,) * len(shape))


def shaped(shape, dtype):
    return jax.ShapeDtypeStruct(shape, dtype)


def scale_of(values):
    return lax.rsqrt(jnp.mean(values * values, 0, keepdims=True) + EPSILON)


def norm_back(values, gain, incoming):
    scales = scale_of(values)
    weighted = gain * incoming
    inner = jnp.mean(values * weighted, 0, keepdims=True)
    grad = scales * weighted - values * (scales * scales * scales * inner)
    return grad, jnp.sum(incoming * values * scales, 1, keepdims=True)


def rotate(values, cosine, sine):
    half = HEAD_DIM // 2
    first, second = values[:half], values[half:]
    return first * cosine - second * sine, second * cosine + first * sine


def project_kernel(
    info, x, gain, q_weight, k_own, k_oth, v_own, v_oth, cosine, sine, normed, out
):
    width = x.shape[0]
    half = width // 2
    values = x[...].astype(F32)
    normed[...] = (values * scale_of(values) * gain[...]).astype(BF16)
    own = normed[pl.ds(pl.multiple_of(info[0] * half, half), half), :]
    oth = normed[pl.ds(pl.multiple_of((1 - info[0]) * half, half), half), :]
    cos, sin = cosine[...], sine[...]
    hd = HEAD_DIM

    def turned(rows, base, factor):
        for head in range(rows.shape[0] // hd):
            first, second = rotate(rows[head * hd : (head + 1) * hd], cos, sin)
            at = base + head * hd
            out[at : at + hd // 2, :] = (first * factor).astype(BF16)
            out[at + hd // 2 : at + hd, :] = (second * factor).astype(BF16)

    q_width = q_weight.shape[1]
    turned(dot(q_weight[...], normed[...], 0, 0), 0, hd**-0.5)
    kv = k_own.shape[0]
    turned(dot(k_own[...], own, 1, 0) + dot(k_oth[...], oth, 1, 0), q_width, 1.0)
    rows = dot(v_own[...], own, 1, 0) + dot(v_oth[...], oth, 1, 0)
    out[q_width + kv : q_width + 2 * kv, :] = rows.astype(BF16)


def project(info, x, gain, weights, tables, cost=None):
    width, rows = x.shape
    q, k, v = weights
    total = q.shape[1] + 2 * k[0].shape[0]
    operands = (x, gain, q, *k, *v, *tables)
    return call(
        project_kernel,
        "project",
        (1,),
        [whole(item.shape) for item in operands],
        [whole((width, rows)), whole((total, rows))],
        [shaped((width, rows), BF16), shaped((total, rows), BF16)],
        cost=cost,
    )(info, *operands)


def scores_of(keys, queries, masked):
    scores = dot(keys, queries, 1, 0)
    if not masked:
        return scores
    key_row = lax.broadcasted_iota(jnp.int32, scores.shape, 0)
    query_row = lax.broadcasted_iota(jnp.int32, scores.shape, 1)
    return jnp.where(key_row <= query_row, scores, -1e30)


def attend_kernel(
    info, q, k_own, v_own, k_past, v_past, out, lse, keys_own, keys_past, peak, total, mixed
):
    rows = q.shape[1]
    block = min(256, rows)
    hd = HEAD_DIM
    groups = [(group, slice(group * hd, (group + 1) * hd)) for group in range(GROUP)]
    keys_own[...] = k_own[...].T

    @pl.loop(0, info[1])
    def _(device):
        keys_past[device] = k_past[device].T

    for start in range(0, rows, block):
        for group, head in groups:
            scores = scores_of(keys_own[start : start + block, :], q[head, start:], True)
            fresh = jnp.max(scores, 0, keepdims=True)
            if start > 0:
                fresh = jnp.maximum(fresh, peak[group : group + 1, start:])
            peak[group : group + 1, start:] = fresh

    @pl.loop(0, info[1])
    def _(device):
        for group, head in groups:
            scores = scores_of(keys_past[device], q[head, :], False)
            peak[group : group + 1, :] = jnp.maximum(
                peak[group : group + 1, :], jnp.max(scores, 0, keepdims=True)
            )

    def add(group, head, keys, values, start, masked, first):
        scores = scores_of(keys, q[head, start:], masked)
        exponent = jnp.exp(scores - peak[group : group + 1, start:])
        sums = jnp.sum(exponent, 0, keepdims=True)
        product = dot(values, exponent.astype(BF16), 1, 0)
        if first:
            total[group : group + 1, :] = sums
            mixed[head, :] = product
        else:
            total[group : group + 1, start:] += sums
            mixed[head, start:] += product

    for start in range(0, rows, block):
        part = slice(start, start + block)
        for group, head in groups:
            add(group, head, keys_own[part, :], v_own[:, part], start, True, start == 0)

    @pl.loop(0, info[1])
    def _(device):
        for group, head in groups:
            add(group, head, keys_past[device], v_past[device], 0, False, False)

    for group, head in groups:
        sums = total[group : group + 1, :]
        out[head, :] = (mixed[head, :] / sums).astype(BF16)
        lse[0, group : group + 1, :] = peak[group : group + 1, :] + jnp.log(sums)


def attention_specs(rows, past, base):
    hd = HEAD_DIM
    return [
        pl.BlockSpec((GROUP * hd, rows), lambda h, info: (base + h, 0)),
        pl.BlockSpec((hd, rows), lambda h, info: (QUERY_HEADS + base + h, 0)),
        pl.BlockSpec((hd, rows), lambda h, info: (QUERY_HEADS + KEY_HEADS + base + h, 0)),
        pl.BlockSpec((past, hd, rows), lambda h, info: (0, base + h, 0)),
        pl.BlockSpec((past, hd, rows), lambda h, info: (0, KEY_HEADS + base + h, 0)),
    ]


def attend(info, qkv, past, base, heads):
    rows = qkv.shape[1]
    count = past.shape[0]
    group = GROUP * HEAD_DIM
    return call(
        attend_kernel,
        "attend",
        (heads,),
        attention_specs(rows, count, base),
        [
            pl.BlockSpec((group, rows), lambda h, info: (h, 0)),
            pl.BlockSpec((1, 8, rows), lambda h, info: (h, 0, 0)),
        ],
        [shaped((heads * group, rows), BF16), shaped((heads, 8, rows), F32)],
        [
            pltpu.VMEM((rows, HEAD_DIM), BF16),
            pltpu.VMEM((count, rows, HEAD_DIM), BF16),
            pltpu.VMEM((8, rows), F32),
            pltpu.VMEM((8, rows), F32),
            pltpu.VMEM((GROUP * HEAD_DIM, rows), F32),
        ],
    )(info, qkv, qkv, qkv, past, past)


def mix_kernel(info, x, mixed, weight, gain, middle, normed):
    middle[...] = x[...].astype(F32) + dot(weight[...], mixed[...], 0, 0)
    values = middle[...]
    normed[...] = (values * scale_of(values) * gain[...]).astype(BF16)


def mix(info, x, mixed, weight, gain):
    width, rows = x.shape
    operands = (x, mixed, weight, gain)
    return call(
        mix_kernel,
        "mix",
        (1,),
        [whole(item.shape) for item in operands],
        [whole((width, rows)), whole((width, rows))],
        [shaped((width, rows), F32), shaped((width, rows), BF16)],
    )(info, *operands)


def activate(token_rows, gate_weight, up_weight, hidden, silu, slope):
    gate = dot(token_rows[...], gate_weight[...], 1, 0)
    up = dot(token_rows[...], up_weight[...], 1, 0)
    sigmoid = 0.5 * jnp.tanh(0.5 * gate) + 0.5
    active = gate * sigmoid
    hidden[...] = (active * up).astype(BF16)
    silu[...] = active.astype(BF16)
    slope[...] = (up * (sigmoid + active * (1.0 - sigmoid))).astype(BF16)


def expand_kernel(info, normed, gate_weight, up_weight, hidden, silu, slope, token_rows):
    @pl.when(pl.program_id(0) == 0)
    def _():
        token_rows[...] = normed[...].T

    activate(token_rows, gate_weight, up_weight, hidden, silu, slope)


def expand(info, normed, gate, up):
    width, rows = normed.shape
    ff = gate.shape[1]
    tile = ff // 5
    weight = pl.BlockSpec((width, tile), lambda t, info: (0, t))
    result = pl.BlockSpec((rows, tile), lambda t, info: (0, t))
    return call(
        expand_kernel,
        "expand",
        (ff // tile,),
        [whole((width, rows)), weight, weight],
        [result] * 3,
        [shaped((rows, ff), BF16)] * 3,
        [pltpu.VMEM((rows, width), BF16)],
    )(info, normed, gate, up)


def expand_first_kernel(info, normed, *refs):
    gate_parts, up_parts = refs[:5], refs[5:10]
    hidden, silu, slope, gate_weight, up_weight, token_rows = refs[10:]
    step = pl.program_id(0)
    steps = pl.num_programs(0)

    @pl.when(step == 0)
    def _():
        token_rows[...] = normed[...].T

    for (own, *pieces), target in ((gate_parts, gate_weight), (up_parts, up_weight)):
        half, quarter = own.shape[0], pieces[0].shape[0]
        target[pl.ds(pl.multiple_of(info[0] * half, half), half), :] = own[...]
        other = (1 - info[0]) * half
        near = pl.ds(pl.multiple_of(other + info[3] * quarter, quarter), quarter)
        far = pl.ds(pl.multiple_of(other + (1 - info[3]) * quarter, quarter), quarter)

        @pl.when(step < steps // 2)
        def _():
            target[near, :] = pieces[0][...]
            target[far, :] = pieces[1][...]

        @pl.when(step >= steps // 2)
        def _():
            target[near, :] = pieces[2][...]
            target[far, :] = pieces[3][...]

    activate(token_rows, gate_weight, up_weight, hidden, silu, slope)


def expand_first(info, normed, gate, up):
    width, rows = normed.shape
    half, ff = gate[0].shape
    steps = 4
    tile = ff // steps
    quarter = half // 2

    def column(t, info):
        own = info[2] * (steps // 2) + t
        return jnp.where(t < steps // 2, own, (1 - info[2]) * (steps // 2) + t - steps // 2)

    early = pl.BlockSpec((quarter, tile), lambda t, info: (0, jnp.minimum(t, steps // 2 - 1)))
    late = pl.BlockSpec((quarter, tile), lambda t, info: (0, jnp.maximum(t - steps // 2, 0)))
    parts = [pl.BlockSpec((half, tile), lambda t, info: (0, column(t, info)))]
    parts += [early, early, late, late]
    result = pl.BlockSpec((rows, tile), lambda t, info: (0, column(t, info)))
    weight = pl.BlockSpec((width, tile), lambda t, info: (0, column(t, info)))
    return call(
        expand_first_kernel,
        "expand_first",
        (steps,),
        [whole((width, rows))] + parts * 2,
        [result] * 3 + [weight] * 2,
        [shaped((rows, ff), BF16)] * 3 + [shaped((width, ff), BF16)] * 2,
        [pltpu.VMEM((rows, width), BF16)],
    )(info, normed, *gate, *up)


def shrink_kernel(info, middle, hidden, weight, out):
    out[...] = (middle[...] + dot(weight[...], hidden[...], 1, 1)).astype(out.dtype)


def shrink(info, middle, hidden, down, dtype, cost=None):
    width, rows = middle.shape
    ff = hidden.shape[1]
    tile = width // 2
    return call(
        shrink_kernel,
        "shrink",
        (width // tile,),
        [
            pl.BlockSpec((tile, rows), lambda t, info: (t, 0)),
            whole((rows, ff)),
            pl.BlockSpec((tile, ff), lambda t, info: (t, 0)),
        ],
        [pl.BlockSpec((tile, rows), lambda t, info: (t, 0))],
        [shaped((width, rows), dtype)],
        cost=cost,
    )(info, middle, hidden, down)[0]


def shrink_first_kernel(info, middle, hidden, own, near_0, far_0, near_1, far_1, out, weight):
    half, quarter = own.shape[1], near_0.shape[0]
    weight[:, pl.ds(pl.multiple_of(info[0] * half, half), half)] = own[...]
    other = pl.ds(pl.multiple_of((1 - info[0]) * half, half), half)
    at_near = pl.ds(pl.multiple_of(info[2] * quarter, quarter), quarter)
    at_far = pl.ds(pl.multiple_of((1 - info[2]) * quarter, quarter), quarter)
    for step, near, far in ((0, near_0, far_0), (1, near_1, far_1)):

        @pl.when(pl.program_id(0) == step)
        def _():
            weight[at_near, other] = near[...]
            weight[at_far, other] = far[...]

    out[...] = middle[...] + dot(weight[...], hidden[...], 1, 1)


def shrink_first(info, middle, hidden, parts):
    width, rows = middle.shape
    ff = hidden.shape[1]
    tile = width // 2
    own, first, second, third, fourth = parts

    def row(t, info):
        return jnp.where(t == 0, info[3], 1 - info[3])

    return call(
        shrink_first_kernel,
        "shrink_first",
        (2,),
        [
            pl.BlockSpec((tile, rows), lambda t, info: (row(t, info), 0)),
            whole((rows, ff)),
            pl.BlockSpec((tile, ff // 2), lambda t, info: (row(t, info), 0)),
        ]
        + [whole(first.shape)] * 4,
        [
            pl.BlockSpec((tile, rows), lambda t, info: (row(t, info), 0)),
            pl.BlockSpec((tile, ff), lambda t, info: (row(t, info), 0)),
        ],
        [shaped((width, rows), F32), shaped((width, ff), BF16)],
    )(info, middle, hidden, own, first, third, second, fourth)


def ffn_back_kernel(
    info,
    grad,
    middle,
    gain,
    silu,
    slope,
    down,
    gate,
    up,
    out_weight,
    gate_grad,
    up_grad,
    branch,
    grad_middle,
    attn_grad,
    mixed_grad,
    gain_grad,
    branch_rows,
    total,
):
    step = pl.program_id(0)
    steps = pl.num_programs(0)

    @pl.when(step == 0)
    def _():
        branch[...] = grad[...].astype(BF16)
        branch_rows[...] = branch[...].T
        total[...] = jnp.zeros_like(total)

    incoming = dot(branch_rows[...], down[...], 1, 0)
    gate_grad[...] = (incoming * slope[...].astype(F32)).astype(BF16)
    up_grad[...] = (incoming * silu[...].astype(F32)).astype(BF16)
    total[...] += dot(gate[...], gate_grad[...], 1, 1) + dot(up[...], up_grad[...], 1, 1)

    @pl.when(step == steps - 1)
    def _():
        back, gain_sum = norm_back(middle[...], gain[...], total[...])
        gain_grad[...] = gain_sum
        result = grad[...].astype(F32) + back
        grad_middle[...] = result
        attn_grad[...] = result.astype(BF16)
        mixed_grad[...] = dot(out_weight[...], attn_grad[...], 1, 0).astype(BF16)


def ffn_back(info, grad, middle, gain, silu, slope, down, gate, up, out_weight, cost=None):
    width, rows = middle.shape
    ff = silu.shape[1]
    tile = ff // 5
    heads = out_weight.shape[0]
    token = pl.BlockSpec((rows, tile), lambda t, info: (0, t))
    weight = pl.BlockSpec((width, tile), lambda t, info: (0, t))
    return call(
        ffn_back_kernel,
        "ffn_back",
        (ff // tile,),
        [
            whole((width, rows)),
            whole((width, rows)),
            whole((width, 1)),
            token,
            token,
            weight,
            weight,
            weight,
            whole((heads, width)),
        ],
        [
            token,
            token,
            whole((width, rows)),
            whole((width, rows)),
            whole((width, rows)),
            whole((heads, rows)),
            whole((width, 1)),
        ],
        [
            shaped((rows, ff), BF16),
            shaped((rows, ff), BF16),
            shaped((width, rows), BF16),
            shaped((width, rows), F32),
            shaped((width, rows), BF16),
            shaped((heads, rows), BF16),
            shaped((width, 1), F32),
        ],
        [pltpu.VMEM((rows, width), BF16), pltpu.VMEM((width, rows), F32)],
        cost=cost,
    )(info, grad, middle, gain, silu, slope, down, gate, up, out_weight)


def attend_back_kernel(
    info,
    q,
    k_own,
    v_own,
    k_past,
    v_past,
    mixed_grad,
    mixed,
    lse,
    cosine,
    sine,
    q_grad,
    own_grad,
    past_grad,
    keys_own,
    values_own,
    keys_past,
    values_past,
    inner,
    q_sum,
):
    rows = q.shape[1]
    block = min(256, rows)
    hd = HEAD_DIM
    groups = [(group, slice(group * hd, (group + 1) * hd)) for group in range(GROUP)]
    keys_own[...] = k_own[...].T
    values_own[...] = v_own[...].T

    @pl.loop(0, info[1])
    def _(device):
        keys_past[device] = k_past[device].T
        values_past[device] = v_past[device].T

    @pl.loop(info[1], past_grad.shape[0])
    def _(device):
        past_grad[device] = jnp.zeros_like(past_grad[device])

    for group, head in groups:
        product = mixed_grad[head, :].astype(F32) * mixed[head, :].astype(F32)
        inner[group : group + 1, :] = jnp.sum(product, 0, keepdims=True)

    def step(keys, key_rows, value_rows, start, masked, first):
        key_sum = value_sum = None
        for group, head in groups:
            query, incoming = q[head, start:], mixed_grad[head, start:]
            one = slice(group, group + 1)
            probs = jnp.exp(scores_of(key_rows, query, masked) - lse[0, one, start:])
            slopes = dot(value_rows, incoming, 1, 0)
            low = (probs * (slopes - inner[one, start:])).astype(BF16)
            value_part = dot(incoming, probs.astype(BF16), 1, 1)
            key_part = dot(query, low, 1, 1)
            key_sum = key_part if key_sum is None else key_sum + key_part
            value_sum = value_part if value_sum is None else value_sum + value_part
            query_part = dot(keys, low, 1, 0)
            if first:
                q_sum[head, :] = query_part
            else:
                q_sum[head, start:] += query_part
        return key_sum, value_sum

    for start in range(0, rows, block):
        part = slice(start, start + block)
        key_sum, value_sum = step(
            k_own[:, part], keys_own[part, :], values_own[part, :], start, True, start == 0
        )
        own_grad[0, :hd, part] = key_sum
        own_grad[0, hd:, part] = value_sum

    @pl.loop(0, info[1])
    def _(device):
        key_sum, value_sum = step(
            k_past[device], keys_past[device], values_past[device], 0, False, False
        )
        past_grad[device, 0, :hd, :] = key_sum.astype(past_grad.dtype)
        past_grad[device, 0, hd:, :] = value_sum.astype(past_grad.dtype)

    cos, sin = cosine[...], -sine[...]
    for group, head in groups:
        first, second = rotate(q_sum[head, :], cos, sin)
        at = group * hd
        q_grad[at : at + hd // 2, :] = (first * hd**-0.5).astype(BF16)
        q_grad[at + hd // 2 : at + hd, :] = (second * hd**-0.5).astype(BF16)


def attend_back(info, qkv, past, mixed_grad, mixed, lse, tables, base, heads, cost=None):
    rows = qkv.shape[1]
    count = past.shape[0]
    hd = HEAD_DIM
    group = pl.BlockSpec((GROUP * hd, rows), lambda h, info: (base + h, 0))
    return call(
        attend_back_kernel,
        "attend_back",
        (heads,),
        attention_specs(rows, count, base)
        + [
            group,
            group,
            pl.BlockSpec((1, 8, rows), lambda h, info: (base + h, 0, 0)),
            whole(tables[0].shape),
            whole(tables[1].shape),
        ],
        [
            pl.BlockSpec((GROUP * hd, rows), lambda h, info: (h, 0)),
            pl.BlockSpec((1, 2 * hd, rows), lambda h, info: (h, 0, 0)),
            pl.BlockSpec((count, 1, 2 * hd, rows), lambda h, info: (0, h, 0, 0)),
        ],
        [
            shaped((heads * GROUP * hd, rows), BF16),
            shaped((heads, 2 * hd, rows), F32),
            shaped((count, heads, 2 * hd, rows), BF16 if count == 1 else F32),
        ],
        [
            pltpu.VMEM((rows, hd), BF16),
            pltpu.VMEM((rows, hd), BF16),
            pltpu.VMEM((count, rows, hd), BF16),
            pltpu.VMEM((count, rows, hd), BF16),
            pltpu.VMEM((8, rows), F32),
            pltpu.VMEM((GROUP * hd, rows), F32),
        ],
        cost=cost,
    )(info, qkv, qkv, qkv, past, past, mixed_grad, mixed, lse, *tables)


def project_back_kernel(parts, info, x, gain, grad_middle, *refs):
    q_grads, own_grads, arrived = refs[:parts], refs[parts : 2 * parts], refs[2 * parts : 3 * parts]
    (
        q_weight,
        k_own,
        k_oth,
        v_own,
        v_oth,
        cosine,
        sine,
        q_grad,
        kv_grad,
        out,
        branch,
        gain_grad,
        total,
    ) = refs[3 * parts :]
    half = x.shape[0] // 2
    hd = HEAD_DIM
    kv = KEY_HEADS * hd
    cos, sin = cosine[...], -sine[...]
    head = 0
    for piece, own, far in zip(q_grads, own_grads, arrived):
        q_grad[head * GROUP * hd : head * GROUP * hd + piece.shape[0], :] = piece[...]
        for item in range(own.shape[0]):
            both = own[item] + far[item].astype(F32)
            first, second = rotate(both[:hd], cos, sin)
            at = head * hd
            kv_grad[at : at + hd // 2, :] = first.astype(BF16)
            kv_grad[at + hd // 2 : at + hd, :] = second.astype(BF16)
            kv_grad[kv + at : kv + at + hd, :] = both[hd:].astype(BF16)
            head += 1
    total[...] = dot(q_weight[...], q_grad[...], 1, 0)
    for mine, k, v in ((info[0], k_own, v_own), (1 - info[0], k_oth, v_oth)):
        total[pl.ds(pl.multiple_of(mine * half, half), half), :] += dot(
            k[...], kv_grad[:kv, :], 0, 0
        ) + dot(v[...], kv_grad[kv:, :], 0, 0)
    back, gain_sum = norm_back(x[...].astype(F32), gain[...], total[...])
    gain_grad[...] = gain_sum
    result = grad_middle[...] + back
    out[...] = result
    branch[...] = result.astype(BF16)


def project_back(info, x, gain, grad_middle, q_grads, own_grads, arrived, weights, tables, cost=None):
    width, rows = x.shape
    q, k, v = weights
    heads = q.shape[1]
    kv = 2 * KEY_HEADS * HEAD_DIM
    operands = (x, gain, grad_middle, *q_grads, *own_grads, *arrived, q, *k, *v, *tables)
    shapes = [
        shaped((heads, rows), BF16),
        shaped((kv, rows), BF16),
        shaped((width, rows), F32),
        shaped((width, rows), BF16),
        shaped((width, 1), F32),
    ]
    return call(
        functools.partial(project_back_kernel, len(q_grads)),
        "project_back",
        (1,),
        [whole(item.shape) for item in operands],
        [whole(item.shape) for item in shapes],
        shapes,
        [pltpu.VMEM((width, rows), F32)],
        cost=cost,
    )(info, *operands)


def order_rows(info, target, sources):
    rows = sources[0].shape[1]
    size = target.shape[0] // 4
    at = 0
    for core in (1 - info[2], info[2]):
        for half in (1 - info[0], info[0]):
            start = pl.multiple_of((2 * half + core) * size, size)
            for index, source in enumerate(sources):
                target[at : at + size, index * rows : (index + 1) * rows] = source[
                    pl.ds(start, size), :
                ]
            at += size


def order_halves(info, target, sources):
    rows = sources[0].shape[1]
    size = target.shape[0] // 2
    for at, core in ((0, 1 - info[2]), (size, info[2])):
        start = pl.multiple_of(core * size, size)
        for index, source in enumerate(sources):
            target[at : at + size, index * rows : (index + 1) * rows] = source[pl.ds(start, size), :]


def outer_kernel(split_columns, info, left_a, right_a, left_b, right_b, sent, kept, left, right):
    rows = left_a.shape[1]

    @pl.when(pl.program_id(0) == 0)
    def _():
        order = order_halves if split_columns else order_rows
        order(info, left, (left_a, left_b))

    right[:rows, :] = right_a[...]
    right[rows:, :] = right_b[...]
    count, size = sent.shape[0], sent.shape[1]
    for at, out in ((0, sent), (count * size, kept)):
        product = dot(left[at : at + count * size, :], right[...], 1, 0).astype(BF16)
        for index in range(count):
            out[index] = product[index * size : (index + 1) * size]


def outer(info, parts, split_columns, cost=None):
    left_a, right_a, left_b, right_b = parts
    width, rows = left_a.shape
    columns = right_a.shape[1]
    if split_columns:
        tile = columns // 4

        def column(t, info):
            return jnp.where(t < 2, (1 - info[0]) * 2 + t, info[0] * 2 + t - 2)

        right = pl.BlockSpec((rows, tile), lambda t, info: (0, column(t, info)))
        result = pl.BlockSpec((1, width // 2, tile), lambda t, info: (t // 2, 0, t % 2))
        shape = shaped((2, width // 2, columns // 2), BF16)
    else:
        tile = columns // 5
        right = pl.BlockSpec((rows, tile), lambda t, info: (0, t))
        result = pl.BlockSpec((2, width // 4, tile), lambda t, info: (0, 0, t))
        shape = shaped((2, width // 4, columns), BF16)
    return call(
        functools.partial(outer_kernel, split_columns),
        "outer",
        (columns // tile,),
        [whole((width, rows)), right, whole((width, rows)), right],
        [result, result],
        [shape, shape],
        [pltpu.VMEM((width, 2 * rows), BF16), pltpu.VMEM((2 * rows, tile), BF16)],
        cost=cost,
    )(info, *parts)


def pack_kernel(extra, info, left_a, *refs):
    sent, kept, left, right = refs[-4:]
    refs = refs[:-4]
    gains, refs = refs[len(refs) - extra :], refs[: len(refs) - extra]
    left_b, rights_a, rights_b = refs[0], refs[1::2], refs[2::2]
    rows = left_a.shape[1]
    order_rows(info, left, (left_a, left_b))
    at = 0
    for right_a, right_b in zip(rights_a, rights_b):
        right[at : at + right_a.shape[0], :rows] = right_a[...]
        right[at : at + right_a.shape[0], rows:] = right_b[...]
        at += right_a.shape[0]
    count, size = sent.shape[0], sent.shape[1]
    for base, core, out in ((0, 1 - info[2], sent), (count * size, info[2], kept)):
        for start, span in spans(right.shape[0], 512):
            product = dot(left[base : base + count * size, :], right[start : start + span, :], 1, 1)
            for index in range(count):
                out[index, :, start : start + span] = product[
                    index * size : (index + 1) * size
                ].astype(BF16)
        for index, half in enumerate((1 - info[0], info[0])):
            part = pl.ds(pl.multiple_of((2 * half + core) * size, size), size)
            for number in range(extra // 2):
                term = gains[2 * number][part, :] + gains[2 * number + 1][part, :]
                out[index, :, at + number : at + number + 1] = term.astype(BF16)
            if extra:
                out[index, :, at + extra // 2 :] = jnp.zeros((size, extra // 2), BF16)


def pack(info, left_a, left_b, rights, gains=(), cost=None):
    width, rows = left_a.shape
    columns = sum(item.shape[0] for item in rights[::2])
    operands = (left_a, left_b, *rights, *gains)
    shape = shaped((2, width // 4, columns + len(gains)), BF16)
    return call(
        functools.partial(pack_kernel, len(gains)),
        "pack",
        (1,),
        [whole(item.shape) for item in operands],
        [whole(shape.shape)] * 2,
        [shape, shape],
        [pltpu.VMEM((width, 2 * rows), BF16), pltpu.VMEM((columns, 2 * rows), BF16)],
        cost=cost,
    )(info, *operands)


def last_kernel(info, held, query, key, value, gains):
    width, narrow = query.shape[1], key.shape[0]
    values = held[...].astype(F32)
    query[...] = values[:, :width]
    key[...] = values[:, width : width + narrow].T
    value[...] = values[:, width + narrow : width + 2 * narrow].T
    gains[...] = values[:, width + 2 * narrow :]


def last(info, held, width, narrow):
    rows, columns = held.shape
    shapes = [
        shaped((rows, width), F32),
        shaped((narrow, rows), F32),
        shaped((narrow, rows), F32),
        shaped((rows, columns - width - 2 * narrow), F32),
    ]
    return call(last_kernel, "last", (1,), [None], [None] * 4, shapes)(info, held)


def column_split(columns):
    return columns // 2 // 128 * 128


def both_cores_kernel(info, kept, arrived, over_y, keep_y, over_x, keep_x):
    split = over_y.shape[1]
    half = over_x.shape[1]
    for index, out in ((0, over_y), (1, keep_y)):
        total = kept[index].astype(F32) + arrived[index].astype(F32)
        out[...] = total[:, :split].astype(BF16)
        low, top = total[:half, split:], total[half:, split:]
        keep_x[index] = jnp.where(info[3] == 0, low, top).astype(BF16)
        over_x[index] = jnp.where(info[3] == 0, top, low).astype(BF16)


def both_cores(info, kept, arrived):
    _, rows, columns = kept.shape
    split = column_split(columns)
    first = shaped((rows, split), BF16)
    second = shaped((2, rows // 2, columns - split), BF16)
    shapes = [first, first, second, second]
    return call(
        both_cores_kernel, "both_cores", (1,), [None] * 2, [None] * 4, shapes
    )(info, kept, arrived)


def cross_kernel(info, keep_y, from_y, keep_x, from_x, over_x, over_y, kept):
    split, half = over_x.shape[1], over_x.shape[0]
    total = keep_y[...].astype(F32) + from_y[...].astype(F32)
    low, top = total[:half], total[half:]
    over_x[...] = jnp.where(info[3] == 0, top, low).astype(BF16)
    kept[:, :split] = jnp.where(info[3] == 0, low, top).astype(BF16)
    over_y[...] = (keep_x[0].astype(F32) + from_x[0].astype(F32)).astype(BF16)
    kept[:, split:] = (keep_x[1].astype(F32) + from_x[1].astype(F32)).astype(BF16)


def cross(info, keep_y, from_y, keep_x, from_x):
    rows, split = keep_y.shape
    rest = keep_x.shape[2]
    shapes = [
        shaped((rows // 2, split), BF16),
        shaped((rows // 2, rest), BF16),
        shaped((rows // 2, split + rest), BF16),
    ]
    return call(cross_kernel, "cross", (1,), [None] * 4, [None] * 3, shapes)(
        info, keep_y, from_y, keep_x, from_x
    )


def chosen(values, number):
    result = values[0]
    for index in range(1, len(values)):
        result = jnp.where(number == index, values[index], result)
    return result


def cut_up(values, dim, count):
    size = values.shape[dim] // count
    if dim == 0:
        return [values[index * size : (index + 1) * size] for index in range(count)]
    return [values[:, index * size : (index + 1) * size] for index in range(count)]


def divide_kernel(dim, info, kept, from_x, from_y, *outs):
    split = from_x.shape[1]
    total = kept[...].astype(F32)
    total = jnp.concatenate(
        [total[:, :split] + from_x[...].astype(F32), total[:, split:] + from_y[...].astype(F32)], 1
    )
    parts = cut_up(total, dim, 4)
    for mask, out in enumerate(outs):
        order = [parts[index ^ mask] for index in range(4)]
        out[...] = chosen(order, info[4]).astype(BF16)


def divide(info, kept, from_x, from_y, dim):
    rows, columns = kept.shape
    shape = (rows // 4, columns) if dim == 0 else (rows, columns // 4)
    return call(
        functools.partial(divide_kernel, dim),
        "divide",
        (1,),
        [None] * 3,
        [None] * 4,
        [shaped(shape, BF16)] * 4,
    )(info, kept, from_x, from_y)


def sum_kernel(info, *refs):
    total = refs[0][...].astype(F32)
    for item in refs[1:-1]:
        total = total + item[...].astype(F32)
    refs[-1][...] = total.astype(BF16)


def sum_all(info, *parts):
    shape = shaped(parts[0].shape, BF16)
    return call(sum_kernel, "sum", (1,), [None] * len(parts), [None], [shape])(info, *parts)[0]


def unite_kernel(dim, place, info, *refs):
    values, out = [item[...].astype(F32) for item in refs[:-1]], refs[-1]
    number = info[place]
    ordered = [
        chosen([values[index ^ other] for other in range(len(values))], number)
        for index in range(len(values))
    ]
    out[...] = jnp.concatenate(ordered, dim).astype(out.dtype)


def unite(info, parts, dim, place, dtype):
    shape = list(parts[0].shape)
    shape[dim] *= len(parts)
    return call(
        functools.partial(unite_kernel, dim, place),
        "unite",
        (1,),
        [None] * len(parts),
        [None],
        [shaped(tuple(shape), dtype)],
    )(info, *parts)[0]


def swap(values, axis, bit):
    size = lax.axis_size(axis)
    return lax.ppermute(values, axis, [(i, i ^ bit) for i in range(size)])


def bits_of(axis):
    size = lax.axis_size(axis)
    assert size & (size - 1) == 0
    return [1 << i for i in range(size.bit_length() - 1)]


def high(axis, bit):
    return (lax.axis_index(axis) // bit) % 2


def halves(values, dim, which):
    half = values.shape[dim] // 2
    return lax.dynamic_slice_in_dim(values, which * half, half, dim)


def joined(mine, other, dim, which):
    return jnp.where(
        which == 0,
        jnp.concatenate([mine, other], dim),
        jnp.concatenate([other, mine], dim),
    )


def tied(values, others):
    return lax.optimization_barrier((values, others))[0]


def from_pieces(own, pieces, mine, core, low_batch):
    near = joined(pieces[0], pieces[2], 0, core)
    far = joined(pieces[1], pieces[3], 0, core)
    return joined(own, joined(near, far, 0, low_batch), 0, mine)


def split_dim(shape, parts):
    if shape[0] % (8 * parts) == 0:
        return 0
    if shape[1] % (128 * parts) == 0:
        return 1
    return 0 if shape[0] % parts == 0 else 1


class Order:
    def __init__(self, token):
        self.token = token

    def __call__(self, *values):
        self.token, *values = lax.optimization_barrier((self.token, *values))
        return values[0] if len(values) == 1 else values


def quarters(values, dim, number):
    quarter = values.shape[dim] // 4
    return lax.dynamic_slice_in_dim(values, number * quarter, quarter, dim)


class Chain:
    def __init__(self, order, away, kept):
        self.order, self.kept = order, kept
        self.away = away
        self.steps = [self.core, self.first, self.second]
        self.shares = [("seq", (1,), 0), ("batch", (1,), 0)]
        exchanges = [("seq", (bit,)) for bit in bits_of("seq")[1:]]
        bits = bits_of("batch")[1:]
        self.plain = not exchanges and len(bits) == 2
        while bits:
            exchanges.append(("batch", bits[:2]))
            bits = bits[2:]
        self.steps += [functools.partial(self.add, *item) for item in exchanges]
        self.steps += [self.share] * (2 + len(exchanges))
        self.waiting = None

    result_type = F32

    def send(self):
        self.waiting = self.steps.pop(0)()

    def core(self):
        def finish(arrived):
            self.parts = both_cores(self.order.token, self.kept, arrived)

        return [swap(self.order(self.away), "seq", 1)], finish

    def first(self):
        over_y, keep_y, over_x, keep_x = self.parts
        over_y, over_x = self.order(over_y, over_x)

        def finish(from_y, from_x):
            self.parts = cross(self.order.token, keep_y, from_y, keep_x, from_x)

        return [swap(over_y, "fsdp", 1), swap(over_x, "batch", 1)], finish

    def second(self):
        over_x, over_y, kept = self.parts
        over_x, over_y = self.order(over_x, over_y)

        def finish(from_x, from_y):
            if self.plain:
                self.dim = split_dim(kept.shape, 4)
                self.held = divide(self.order.token, kept, from_x, from_y, self.dim)
                return
            arrived = jnp.concatenate([from_x, from_y], 1)
            self.held = (kept.astype(F32) + arrived.astype(F32)).astype(BF16)

        return [swap(over_x, "batch", 1), swap(over_y, "fsdp", 1)], finish

    def add(self, axis, bits):
        held = self.held
        if self.plain:
            own, *parts = held
            parts = self.order(*parts)
            arrived = [
                swap(part, axis, bits[0] * (mask & 1) + bits[1] * (mask >> 1))
                for mask, part in zip((1, 2, 3), parts)
            ]
            self.shares.append((axis, bits, self.dim))

            def finish(*values):
                self.held = sum_all(self.order.token, own, *values)

            return arrived, finish
        dim = split_dim(held.shape, 2 * len(bits))
        take = halves if len(bits) == 1 else quarters
        number = sum(high(axis, bit) << index for index, bit in enumerate(bits))
        masks = range(1, 1 << len(bits))
        parts = self.order(*[take(held, dim, number ^ mask) for mask in masks])
        parts = parts if len(bits) > 1 else [parts]
        arrived = [
            swap(part, axis, sum(bit for index, bit in enumerate(bits) if mask >> index & 1))
            for mask, part in zip(masks, parts)
        ]
        self.shares.append((axis, bits, dim))

        def finish(*values):
            total = take(held, dim, number).astype(F32)
            for item in values:
                total = total + item.astype(F32)
            self.held = total.astype(BF16)

        return arrived, finish

    def share(self):
        axis, bits, dim = self.shares.pop()
        held = self.order(self.held)
        masks = range(1, 1 << len(bits))
        arrived = [
            swap(held, axis, sum(bit for index, bit in enumerate(bits) if mask >> index & 1))
            for mask in masks
        ]

        def finish(*values):
            low = high(axis, bits[0])
            if self.plain:
                place = 4 if len(bits) == 2 else 3 if axis == "batch" else 2
                dtype = BF16 if self.shares else self.result_type
                self.held = unite(self.order.token, (held, *values), dim, place, dtype)
                return
            if len(bits) == 1:
                self.held = joined(held, values[0], dim, low)
                return
            near, far = joined(held, values[0], dim, low), joined(values[1], values[2], dim, low)
            self.held = joined(near, far, dim, high(axis, bits[1]))

        return arrived, finish

    def result(self):
        while self.waiting or self.steps:
            if self.waiting:
                take(self)
            else:
                self.send()
        return self.held.astype(self.result_type)


def take(*chains):
    flat = [item for chain in chains for item in chain.waiting[0]]
    values = chains[0].order(*flat)
    values = list(values) if len(flat) > 1 else [values]
    for chain in chains:
        arrived, finish = chain.waiting
        chain.waiting = None
        finish(*values[: len(arrived)])
        values = values[len(arrived) :]


def per_device(
    tokens,
    attn_gain,
    w_query,
    key_weight,
    value_weight,
    w_out,
    ffn_gain,
    w_gate,
    w_up,
    w_down,
    cotangent,
):
    assert tokens.shape[0] == 1 and lax.axis_size("fsdp") == 2
    mine, spot, core = lax.axis_index("fsdp"), lax.axis_index("seq"), high("seq", 1)
    low_batch = high("batch", 1)
    devices = lax.axis_size("seq")
    deep = lax.axis_index("batch") // 2 % 4
    info = jnp.stack([mine, spot, core, low_batch, deep]).astype(jnp.int32)
    start_in = tokens[0].T
    incoming = cotangent[0].T
    width, rows = start_in.shape

    gains = jnp.stack([attn_gain, ffn_gain])
    gains = joined(gains, swap(gains, "fsdp", 1), 1, mine).astype(F32)[..., None]
    key_weight, value_weight, w_down = key_weight.T, value_weight.T, w_down.T
    def fsdp(values):
        return swap(values, "fsdp", 1)

    def pair(values):
        return swap(values, "batch", 1)

    def cores(values):
        return swap(values, "seq", 1)

    q_piece = halves(halves(w_query, 0, low_batch), 0, core)
    kv_piece = halves(jnp.where(core == 0, key_weight, value_weight), 0, low_batch)
    q_0, kv_0 = fsdp(q_piece), fsdp(kv_piece)
    out_0 = fsdp(tied(halves(halves(w_out, 0, low_batch), 0, core), (q_0, kv_0)))
    q_1, kv_1, q_2, kv_2 = pair(q_0), pair(kv_0), cores(q_0), cores(kv_0)
    gate_0 = fsdp(tied(halves(halves(w_gate, 0, low_batch), 1, core), out_0))
    q_3, kv_3 = cores(q_1), cores(kv_1)
    q_weight = from_pieces(w_query, (q_0, q_1, q_2, q_3), mine, core, low_batch)
    held = joined(kv_0, kv_1, 0, low_batch)
    other = joined(kv_2, kv_3, 0, low_batch)
    k_oth, v_oth = jnp.where(core == 0, held, other), jnp.where(core == 0, other, held)
    qkv_weights = (q_weight, (key_weight, k_oth), (value_weight, v_oth))

    positions = (spot * rows + jnp.arange(rows, dtype=jnp.int32)).astype(F32)
    frequency = jnp.exp(
        jnp.arange(HEAD_DIM // 2, dtype=F32) * (-2.0 * math.log(10000.0) / HEAD_DIM)
    )
    angles = frequency[:, None] * positions[None, :]
    tables = (jnp.cos(angles), jnp.sin(angles))

    def gathered(qkv):
        kv = qkv[QUERY_HEADS * HEAD_DIM :]
        if devices == 2:
            return cores(kv)[None]
        return lax.all_gather(kv, "seq")

    low_normed, low_qkv = project(info, start_in, gains[0], qkv_weights, tables)
    low_past = gathered(low_qkv)
    ready = (low_qkv, gate_0)
    up_0 = fsdp(tied(halves(halves(w_up, 0, low_batch), 1, core), ready))
    down_0 = fsdp(tied(halves(halves(w_down, 0, low_batch), 0, core), ready))
    out_1, out_2 = pair(tied(out_0, (q_1, kv_1))), cores(out_0)
    gate_1, gate_2 = pair(tied(gate_0, (low_qkv, out_1))), cores(gate_0)
    out_3 = cores(out_1)
    out_weight = from_pieces(w_out, (out_0, out_1, out_2, out_3), mine, core, low_batch)
    low_mixed, low_lse = attend(info, low_qkv, tied(low_past, out_weight), 0, KEY_HEADS)
    low_mixed = tied(low_mixed, (up_0, down_0, gate_1))
    gate_3, up_1, up_2 = cores(gate_1), pair(tied(up_0, low_mixed)), cores(up_0)
    low_middle, low_normed_ffn = mix(info, start_in, low_mixed, out_weight, gains[1])
    up_3 = cores(tied(up_1, low_middle))
    down_1, down_2 = pair(tied(down_0, (up_1, low_middle))), cores(tied(down_0, low_middle))
    low_hidden, low_silu, low_slope, gate, up = expand_first(
        info,
        low_normed_ffn,
        (w_gate, gate_0, gate_1, gate_2, gate_3),
        (w_up, up_0, up_1, up_2, up_3),
    )
    down_3 = cores(tied(down_1, low_hidden))
    middle_in, down = shrink_first(
        info, low_middle, low_hidden, (w_down, down_0, down_1, down_2, down_3)
    )

    high_normed, high_qkv = project(info, middle_in, gains[0], qkv_weights, tables)
    high_past = gathered(high_qkv)
    high_mixed, high_lse = attend(info, high_qkv, high_past, 0, KEY_HEADS)
    high_middle, high_normed_ffn = mix(info, middle_in, high_mixed, out_weight, gains[1])
    high_hidden, high_silu, high_slope = expand(info, high_normed_ffn, gate, up)

    def attention_back(qkv, past, mixed_grad, mixed, lse, base, heads, cost=None):
        return attend_back(
            info, qkv, past, mixed_grad, mixed, lse, tables, base, heads, cost
        )

    def returned(past_grad):
        if devices == 2:
            return cores(past_grad[0])
        return lax.psum_scatter(past_grad, "seq", scatter_dimension=0)

    def to_input(x, grad_middle, parts, cost=None):
        return project_back(
            info, x, gains[0], grad_middle, *zip(*parts), qkv_weights, tables, cost
        )

    high_gate, high_up, high_branch, grad_middle, high_attn, mixed_grad, high_ffn_gain = ffn_back(
        info, incoming, high_middle, gains[1], high_silu, high_slope, down, gate, up, out_weight
    )
    parts = [
        attention_back(high_qkv, high_past, mixed_grad, high_mixed, high_lse, base, heads)
        for base, heads in ((0, 3), (3, 2))
    ]
    parts = [(*part[:2], returned(part[2])) for part in parts]
    high_q, high_kv, grad_between, low_branch, high_attn_gain = to_input(
        middle_in, grad_middle, parts
    )

    order = Order(tied(info, low_branch))
    down_terms = (high_branch, high_hidden, low_branch, low_hidden)
    down_g = Chain(order, *outer(info, down_terms, True))
    down_g.send()
    final_out = order(shrink(info, order(high_middle), high_hidden, down, BF16))
    take(down_g)
    down_g.send()
    low_gate, low_up, _, grad_middle, low_attn, mixed_grad, low_ffn_gain = ffn_back(
        info, order(grad_between), low_middle, gains[1], low_silu, low_slope,
        down, gate, up, out_weight,
    )
    low_attn = order(low_attn)
    take(down_g)
    down_g.send()
    out_terms = (high_attn, order(low_attn))
    out_g = Chain(order, *pack(info, high_mixed, low_mixed, out_terms))
    out_g.send()
    gate_terms = (high_normed_ffn, high_gate, low_normed_ffn, order(low_gate))
    gate_g = Chain(order, *outer(info, gate_terms, False))
    gate_g.send()
    take(down_g, out_g)
    down_g.send()
    out_g.send()
    up_terms = (high_normed_ffn, high_up, low_normed_ffn, order(low_up))
    up_g = Chain(order, *outer(info, up_terms, False))
    up_g.send()
    take(gate_g, out_g)
    gate_g.send()
    out_g.send()
    parts = []

    def low_part(base, heads):
        mixed_now = order(mixed_grad)
        part = attention_back(low_qkv, low_past, mixed_now, low_mixed, low_lse, base, heads)
        parts.append((order(part[0]), *part[1:]))

    low_part(0, 2)
    take(gate_g, down_g, up_g, out_g)
    gate_g.send()
    up_g.send()
    down_g.send()
    out_g.send()
    low_part(2, 3)
    parts = [(*part[:2], returned(order(part[2]))) for part in parts]
    take(gate_g, up_g, down_g, out_g)
    up_g.send()
    gate_g.send()
    out_g.send()
    low_q, low_kv, grad_start, _, low_attn_gain = to_input(
        start_in, order(grad_middle), parts, 0
    )
    low_q = order(low_q)
    take(up_g, gate_g, out_g)
    gate_g.send()
    down_g.send()
    qkv_terms = (high_q, order(low_q), high_kv, low_kv)
    gain_terms = (high_attn_gain, low_attn_gain, high_ffn_gain, low_ffn_gain)
    qkv_g = Chain(order, *pack(info, high_normed, low_normed, qkv_terms, gain_terms, 0))
    qkv_g.result_type = BF16
    qkv_g.send()
    take(qkv_g, gate_g, down_g)
    qkv_g.send()
    up_g.send()
    out_g.send()
    down_g.send()
    take(qkv_g, up_g, out_g, down_g)
    qkv_g.send()
    out_g.send()
    take(qkv_g, out_g)
    qkv_g.send()
    up_g.send()
    gate_g.send()
    take(qkv_g, up_g, gate_g)
    qkv_g.send()
    up_g.send()
    gate_g.send()
    take(qkv_g, up_g, gate_g)
    qkv_g.send()
    up_g.send()
    take(qkv_g, up_g)
    qkv_g.send()
    down_grad, out_grad = order(down_g.result(), out_g.result())
    gate_grad, up_grad = order(gate_g.result(), up_g.result())
    held = order(qkv_g.result())
    narrow = KEY_HEADS * HEAD_DIM
    query_part, key_part, value_part, gain_grads = last(order.token, held, width, narrow)
    return (
        final_out.T[None],
        grad_start.T[None],
        gain_grads[:, 0],
        query_part,
        key_part.T,
        value_part.T,
        out_grad,
        gain_grads[:, 1],
        gate_grad,
        up_grad,
        down_grad.T,
    )


def solution(mesh):
    return jax.shard_map(
        per_device,
        mesh=mesh,
        in_specs=(
            P(("batch", "fsdp"), "seq", None),
            P("fsdp"),
            P("fsdp", None),
            P("fsdp", None),
            P("fsdp", None),
            P("fsdp", None),
            P("fsdp"),
            P("fsdp", None),
            P("fsdp", None),
            P("fsdp", None),
            P(("batch", "fsdp"), "seq", None),
        ),
        out_specs=(
            P(("batch", "fsdp"), "seq", None),
            P(("batch", "fsdp"), "seq", None),
            P("fsdp"),
            P("fsdp", None),
            P("fsdp", None),
            P("fsdp", None),
            P("fsdp", None),
            P("fsdp"),
            P("fsdp", None),
            P("fsdp", None),
            P("fsdp", None),
        ),
        check_vma=False,
    )
```

```python
import functools
import math

import jax
import jax.numpy as jnp
from jax import lax
from jax.experimental import pallas as pl
from jax.experimental.pallas import tpu as pltpu
from jax.sharding import PartitionSpec as P

QUERY_HEADS = 15
KEY_HEADS = 5
HEAD_DIM = 64
GROUP = QUERY_HEADS // KEY_HEADS
EPSILON = 1e-05
F32 = jnp.float32
BF16 = jnp.bfloat16


def dot(left, right, left_dim, right_dim):
    return lax.dot_general(
        left, right, (((left_dim,), (right_dim,)), ((), ())), preferred_element_type=F32
    )


def spans(total, size):
    return [(start, min(size, total - start)) for start in range(0, total, size)]


COSTS = {
    "project": 6.0,
    "attend": 4.0,
    "mix": 5.5,
    "expand": 10.0,
    "expand_first": 14.0,
    "shrink": 6.5,
    "shrink_first": 8.0,
    "ffn_back": 18.0,
    "attend_back": 6.5,
    "project_back": 6.0,
    "outer": 10.0,
    "pack": 4.0,
    "both_cores": 0.0,
    "cross": 0.0,
    "last": 0.0,
    "divide": 0.0,
    "split_pair": 0.0,
    "sum": 0.0,
    "unite": 0.0,
}


LIMITS = {
    "project": 12,
    "attend": 14,
    "mix": 12,
    "expand": 24,
    "expand_first": 34,
    "shrink": 22,
    "shrink_first": 34,
    "ffn_back": 40,
    "attend_back": 16,
    "project_back": 16,
    "outer": 26,
    "pack": 20,
    "both_cores": 12,
    "cross": 10,
    "last": 12,
    "divide": 10,
    "split_pair": 16,
    "sum": 6,
    "unite": 14,
}


def call(kernel, name, grid, in_specs, out_specs, out_shape, scratch=(), cost=None):
    if cost is None:
        cost = COSTS[name] * 0.45 * (grid[0] if name.startswith("attend") else 1)
    cost = int(cost * 1e9) + 1
    options = dict(
        name=name,
        out_shape=out_shape,
        compiler_params=pltpu.CompilerParams(vmem_limit_bytes=LIMITS[name] * 1024 * 1024),
        cost_estimate=pl.CostEstimate(flops=cost, bytes_accessed=1, transcendentals=0),
    )
    if name in ("project", "mix", "project_back", "pack", "both_cores", "cross", "last", "divide", "sum", "unite", "split_pair"):
        memory = pl.BlockSpec(memory_space=pltpu.VMEM)
        return pl.pallas_call(
            kernel,
            in_specs=[pl.BlockSpec(memory_space=pltpu.SMEM)] + [memory] * len(in_specs),
            out_specs=[memory] * len(out_specs),
            scratch_shapes=list(scratch),
            **options,
        )
    return pl.pallas_call(
        kernel,
        grid_spec=pltpu.PrefetchScalarGridSpec(
            num_scalar_prefetch=1,
            grid=grid,
            in_specs=in_specs,
            out_specs=out_specs,
            scratch_shapes=list(scratch),
        ),
        **options,
    )


def whole(shape):
    return pl.BlockSpec(shape, lambda *_: (0,) * len(shape))


def shaped(shape, dtype):
    return jax.ShapeDtypeStruct(shape, dtype)


def scale_of(values):
    return lax.rsqrt(jnp.mean(values * values, 0, keepdims=True) + EPSILON)


def norm_back(values, gain, incoming):
    scales = scale_of(values)
    weighted = gain * incoming
    inner = jnp.mean(values * weighted, 0, keepdims=True)
    grad = scales * weighted - values * (scales * scales * scales * inner)
    return grad, jnp.sum(incoming * values * scales, 1, keepdims=True)


def rotate(values, cosine, sine):
    half = HEAD_DIM // 2
    first, second = values[:half], values[half:]
    return first * cosine - second * sine, second * cosine + first * sine


def project_kernel(
    info, x, gain, q_weight, k_own, k_oth, v_own, v_oth, cosine, sine, normed, out
):
    width = x.shape[0]
    half = width // 2
    values = x[...].astype(F32)
    normed[...] = (values * scale_of(values) * gain[...]).astype(BF16)
    own = normed[pl.ds(pl.multiple_of(info[0] * half, half), half), :]
    oth = normed[pl.ds(pl.multiple_of((1 - info[0]) * half, half), half), :]
    cos, sin = cosine[...], sine[...]
    hd = HEAD_DIM

    def turned(rows, base, factor):
        for head in range(rows.shape[0] // hd):
            first, second = rotate(rows[head * hd : (head + 1) * hd], cos, sin)
            at = base + head * hd
            out[at : at + hd // 2, :] = (first * factor).astype(BF16)
            out[at + hd // 2 : at + hd, :] = (second * factor).astype(BF16)

    q_width = q_weight.shape[1]
    turned(dot(q_weight[...], normed[...], 0, 0), 0, hd**-0.5)
    kv = k_own.shape[0]
    turned(dot(k_own[...], own, 1, 0) + dot(k_oth[...], oth, 1, 0), q_width, 1.0)
    rows = dot(v_own[...], own, 1, 0) + dot(v_oth[...], oth, 1, 0)
    out[q_width + kv : q_width + 2 * kv, :] = rows.astype(BF16)


def project(info, x, gain, weights, tables, cost=None):
    width, rows = x.shape
    q, k, v = weights
    total = q.shape[1] + 2 * k[0].shape[0]
    operands = (x, gain, q, *k, *v, *tables)
    return call(
        project_kernel,
        "project",
        (1,),
        [whole(item.shape) for item in operands],
        [whole((width, rows)), whole((total, rows))],
        [shaped((width, rows), BF16), shaped((total, rows), BF16)],
        cost=cost,
    )(info, *operands)


def scores_of(keys, queries, masked):
    scores = dot(keys, queries, 1, 0)
    if not masked:
        return scores
    key_row = lax.broadcasted_iota(jnp.int32, scores.shape, 0)
    query_row = lax.broadcasted_iota(jnp.int32, scores.shape, 1)
    return jnp.where(key_row <= query_row, scores, -1e30)


def attend_kernel(
    info, q, k_own, v_own, k_past, v_past, out, lse, keys_own, keys_past, peak, total, mixed
):
    rows = q.shape[1]
    block = min(256, rows)
    hd = HEAD_DIM
    groups = [(group, slice(group * hd, (group + 1) * hd)) for group in range(GROUP)]
    keys_own[...] = k_own[...].T

    @pl.loop(0, info[1])
    def _(device):
        keys_past[device] = k_past[device].T

    for start in range(0, rows, block):
        for group, head in groups:
            scores = scores_of(keys_own[start : start + block, :], q[head, start:], True)
            fresh = jnp.max(scores, 0, keepdims=True)
            if start > 0:
                fresh = jnp.maximum(fresh, peak[group : group + 1, start:])
            peak[group : group + 1, start:] = fresh

    @pl.loop(0, info[1])
    def _(device):
        for group, head in groups:
            scores = scores_of(keys_past[device], q[head, :], False)
            peak[group : group + 1, :] = jnp.maximum(
                peak[group : group + 1, :], jnp.max(scores, 0, keepdims=True)
            )

    def add(group, head, keys, values, start, masked, first):
        scores = scores_of(keys, q[head, start:], masked)
        exponent = jnp.exp(scores - peak[group : group + 1, start:])
        sums = jnp.sum(exponent, 0, keepdims=True)
        product = dot(values, exponent.astype(BF16), 1, 0)
        if first:
            total[group : group + 1, :] = sums
            mixed[head, :] = product
        else:
            total[group : group + 1, start:] += sums
            mixed[head, start:] += product

    for start in range(0, rows, block):
        part = slice(start, start + block)
        for group, head in groups:
            add(group, head, keys_own[part, :], v_own[:, part], start, True, start == 0)

    @pl.loop(0, info[1])
    def _(device):
        for group, head in groups:
            add(group, head, keys_past[device], v_past[device], 0, False, False)

    for group, head in groups:
        sums = total[group : group + 1, :]
        out[head, :] = (mixed[head, :] / sums).astype(BF16)
        lse[0, group : group + 1, :] = peak[group : group + 1, :] + jnp.log(sums)


def attention_specs(rows, past, base):
    hd = HEAD_DIM
    return [
        pl.BlockSpec((GROUP * hd, rows), lambda h, info: (base + h, 0)),
        pl.BlockSpec((hd, rows), lambda h, info: (QUERY_HEADS + base + h, 0)),
        pl.BlockSpec((hd, rows), lambda h, info: (QUERY_HEADS + KEY_HEADS + base + h, 0)),
        pl.BlockSpec((past, hd, rows), lambda h, info: (0, base + h, 0)),
        pl.BlockSpec((past, hd, rows), lambda h, info: (0, KEY_HEADS + base + h, 0)),
    ]


def attend(info, qkv, past, base, heads):
    rows = qkv.shape[1]
    count = past.shape[0]
    group = GROUP * HEAD_DIM
    return call(
        attend_kernel,
        "attend",
        (heads,),
        attention_specs(rows, count, base),
        [
            pl.BlockSpec((group, rows), lambda h, info: (h, 0)),
            pl.BlockSpec((1, 8, rows), lambda h, info: (h, 0, 0)),
        ],
        [shaped((heads * group, rows), BF16), shaped((heads, 8, rows), F32)],
        [
            pltpu.VMEM((rows, HEAD_DIM), BF16),
            pltpu.VMEM((count, rows, HEAD_DIM), BF16),
            pltpu.VMEM((8, rows), F32),
            pltpu.VMEM((8, rows), F32),
            pltpu.VMEM((GROUP * HEAD_DIM, rows), F32),
        ],
    )(info, qkv, qkv, qkv, past, past)


def mix_kernel(info, x, mixed, weight, gain, middle, normed):
    middle[...] = x[...].astype(F32) + dot(weight[...], mixed[...], 0, 0)
    values = middle[...]
    normed[...] = (values * scale_of(values) * gain[...]).astype(BF16)


def mix(info, x, mixed, weight, gain):
    width, rows = x.shape
    operands = (x, mixed, weight, gain)
    return call(
        mix_kernel,
        "mix",
        (1,),
        [whole(item.shape) for item in operands],
        [whole((width, rows)), whole((width, rows))],
        [shaped((width, rows), F32), shaped((width, rows), BF16)],
    )(info, *operands)


def activate(token_rows, gate_weight, up_weight, hidden, silu, slope):
    gate = dot(token_rows[...], gate_weight[...], 1, 0)
    up = dot(token_rows[...], up_weight[...], 1, 0)
    sigmoid = 0.5 * jnp.tanh(0.5 * gate) + 0.5
    active = gate * sigmoid
    hidden[...] = (active * up).astype(BF16)
    silu[...] = active.astype(BF16)
    slope[...] = (up * (sigmoid + active * (1.0 - sigmoid))).astype(BF16)


def expand_kernel(info, normed, gate_weight, up_weight, hidden, silu, slope, token_rows):
    @pl.when(pl.program_id(0) == 0)
    def _():
        token_rows[...] = normed[...].T

    activate(token_rows, gate_weight, up_weight, hidden, silu, slope)


def expand(info, normed, gate, up):
    width, rows = normed.shape
    ff = gate.shape[1]
    tile = ff // 5
    weight = pl.BlockSpec((width, tile), lambda t, info: (0, t))
    result = pl.BlockSpec((rows, tile), lambda t, info: (0, t))
    return call(
        expand_kernel,
        "expand",
        (ff // tile,),
        [whole((width, rows)), weight, weight],
        [result] * 3,
        [shaped((rows, ff), BF16)] * 3,
        [pltpu.VMEM((rows, width), BF16)],
    )(info, normed, gate, up)


def expand_first_kernel(info, normed, *refs):
    gate_parts, up_parts = refs[:5], refs[5:10]
    hidden, silu, slope, gate_weight, up_weight, token_rows = refs[10:]
    step = pl.program_id(0)
    steps = pl.num_programs(0)

    @pl.when(step == 0)
    def _():
        token_rows[...] = normed[...].T

    for (own, *pieces), target in ((gate_parts, gate_weight), (up_parts, up_weight)):
        half, quarter = own.shape[0], pieces[0].shape[0]
        target[pl.ds(pl.multiple_of(info[0] * half, half), half), :] = own[...]
        other = (1 - info[0]) * half
        near = pl.ds(pl.multiple_of(other + info[3] * quarter, quarter), quarter)
        far = pl.ds(pl.multiple_of(other + (1 - info[3]) * quarter, quarter), quarter)

        @pl.when(step < steps // 2)
        def _():
            target[near, :] = pieces[0][...]
            target[far, :] = pieces[1][...]

        @pl.when(step >= steps // 2)
        def _():
            target[near, :] = pieces[2][...]
            target[far, :] = pieces[3][...]

    activate(token_rows, gate_weight, up_weight, hidden, silu, slope)


def expand_first(info, normed, gate, up):
    width, rows = normed.shape
    half, ff = gate[0].shape
    steps = 4
    tile = ff // steps
    quarter = half // 2

    def column(t, info):
        own = info[2] * (steps // 2) + t
        return jnp.where(t < steps // 2, own, (1 - info[2]) * (steps // 2) + t - steps // 2)

    early = pl.BlockSpec((quarter, tile), lambda t, info: (0, jnp.minimum(t, steps // 2 - 1)))
    late = pl.BlockSpec((quarter, tile), lambda t, info: (0, jnp.maximum(t - steps // 2, 0)))
    parts = [pl.BlockSpec((half, tile), lambda t, info: (0, column(t, info)))]
    parts += [early, early, late, late]
    result = pl.BlockSpec((rows, tile), lambda t, info: (0, column(t, info)))
    weight = pl.BlockSpec((width, tile), lambda t, info: (0, column(t, info)))
    return call(
        expand_first_kernel,
        "expand_first",
        (steps,),
        [whole((width, rows))] + parts * 2,
        [result] * 3 + [weight] * 2,
        [shaped((rows, ff), BF16)] * 3 + [shaped((width, ff), BF16)] * 2,
        [pltpu.VMEM((rows, width), BF16)],
    )(info, normed, *gate, *up)


def shrink_kernel(info, middle, hidden, weight, out):
    out[...] = (middle[...] + dot(weight[...], hidden[...], 1, 1)).astype(out.dtype)


def shrink(info, middle, hidden, down, dtype, cost=None):
    width, rows = middle.shape
    ff = hidden.shape[1]
    tile = width // 2
    return call(
        shrink_kernel,
        "shrink",
        (width // tile,),
        [
            pl.BlockSpec((tile, rows), lambda t, info: (t, 0)),
            whole((rows, ff)),
            pl.BlockSpec((tile, ff), lambda t, info: (t, 0)),
        ],
        [pl.BlockSpec((tile, rows), lambda t, info: (t, 0))],
        [shaped((width, rows), dtype)],
        cost=cost,
    )(info, middle, hidden, down)[0]


def shrink_first_kernel(info, middle, hidden, own, near_0, far_0, near_1, far_1, out, weight):
    half, quarter = own.shape[1], near_0.shape[0]
    weight[:, pl.ds(pl.multiple_of(info[0] * half, half), half)] = own[...]
    other = pl.ds(pl.multiple_of((1 - info[0]) * half, half), half)
    at_near = pl.ds(pl.multiple_of(info[2] * quarter, quarter), quarter)
    at_far = pl.ds(pl.multiple_of((1 - info[2]) * quarter, quarter), quarter)
    for step, near, far in ((0, near_0, far_0), (1, near_1, far_1)):

        @pl.when(pl.program_id(0) == step)
        def _():
            weight[at_near, other] = near[...]
            weight[at_far, other] = far[...]

    out[...] = middle[...] + dot(weight[...], hidden[...], 1, 1)


def shrink_first(info, middle, hidden, parts):
    width, rows = middle.shape
    ff = hidden.shape[1]
    tile = width // 2
    own, first, second, third, fourth = parts

    def row(t, info):
        return jnp.where(t == 0, info[3], 1 - info[3])

    return call(
        shrink_first_kernel,
        "shrink_first",
        (2,),
        [
            pl.BlockSpec((tile, rows), lambda t, info: (row(t, info), 0)),
            whole((rows, ff)),
            pl.BlockSpec((tile, ff // 2), lambda t, info: (row(t, info), 0)),
        ]
        + [whole(first.shape)] * 4,
        [
            pl.BlockSpec((tile, rows), lambda t, info: (row(t, info), 0)),
            pl.BlockSpec((tile, ff), lambda t, info: (row(t, info), 0)),
        ],
        [shaped((width, rows), F32), shaped((width, ff), BF16)],
    )(info, middle, hidden, own, first, third, second, fourth)


def ffn_back_kernel(
    info,
    grad,
    middle,
    gain,
    silu,
    slope,
    down,
    gate,
    up,
    out_weight,
    gate_grad,
    up_grad,
    branch,
    grad_middle,
    attn_grad,
    mixed_grad,
    gain_grad,
    branch_rows,
    total,
):
    step = pl.program_id(0)
    steps = pl.num_programs(0)

    @pl.when(step == 0)
    def _():
        branch[...] = grad[...].astype(BF16)
        branch_rows[...] = branch[...].T
        total[...] = jnp.zeros_like(total)

    incoming = dot(branch_rows[...], down[...], 1, 0)
    gate_grad[...] = (incoming * slope[...].astype(F32)).astype(BF16)
    up_grad[...] = (incoming * silu[...].astype(F32)).astype(BF16)
    total[...] += dot(gate[...], gate_grad[...], 1, 1) + dot(up[...], up_grad[...], 1, 1)

    @pl.when(step == steps - 1)
    def _():
        back, gain_sum = norm_back(middle[...], gain[...], total[...])
        gain_grad[...] = gain_sum
        result = grad[...].astype(F32) + back
        grad_middle[...] = result
        attn_grad[...] = result.astype(BF16)
        mixed_grad[...] = dot(out_weight[...], attn_grad[...], 1, 0).astype(BF16)


def ffn_back(info, grad, middle, gain, silu, slope, down, gate, up, out_weight, cost=None):
    width, rows = middle.shape
    ff = silu.shape[1]
    tile = ff // 5
    heads = out_weight.shape[0]
    token = pl.BlockSpec((rows, tile), lambda t, info: (0, t))
    weight = pl.BlockSpec((width, tile), lambda t, info: (0, t))
    return call(
        ffn_back_kernel,
        "ffn_back",
        (ff // tile,),
        [
            whole((width, rows)),
            whole((width, rows)),
            whole((width, 1)),
            token,
            token,
            weight,
            weight,
            weight,
            whole((heads, width)),
        ],
        [
            token,
            token,
            whole((width, rows)),
            whole((width, rows)),
            whole((width, rows)),
            whole((heads, rows)),
            whole((width, 1)),
        ],
        [
            shaped((rows, ff), BF16),
            shaped((rows, ff), BF16),
            shaped((width, rows), BF16),
            shaped((width, rows), F32),
            shaped((width, rows), BF16),
            shaped((heads, rows), BF16),
            shaped((width, 1), F32),
        ],
        [pltpu.VMEM((rows, width), BF16), pltpu.VMEM((width, rows), F32)],
        cost=cost,
    )(info, grad, middle, gain, silu, slope, down, gate, up, out_weight)


def attend_back_kernel(
    info,
    q,
    k_own,
    v_own,
    k_past,
    v_past,
    mixed_grad,
    mixed,
    lse,
    cosine,
    sine,
    q_grad,
    own_grad,
    past_grad,
    keys_own,
    values_own,
    keys_past,
    values_past,
    inner,
    q_sum,
):
    rows = q.shape[1]
    block = min(256, rows)
    hd = HEAD_DIM
    groups = [(group, slice(group * hd, (group + 1) * hd)) for group in range(GROUP)]
    keys_own[...] = k_own[...].T
    values_own[...] = v_own[...].T

    @pl.loop(0, info[1])
    def _(device):
        keys_past[device] = k_past[device].T
        values_past[device] = v_past[device].T

    @pl.loop(info[1], past_grad.shape[0])
    def _(device):
        past_grad[device] = jnp.zeros_like(past_grad[device])

    for group, head in groups:
        product = mixed_grad[head, :].astype(F32) * mixed[head, :].astype(F32)
        inner[group : group + 1, :] = jnp.sum(product, 0, keepdims=True)

    def step(keys, key_rows, value_rows, start, masked, first):
        key_sum = value_sum = None
        for group, head in groups:
            query, incoming = q[head, start:], mixed_grad[head, start:]
            one = slice(group, group + 1)
            probs = jnp.exp(scores_of(key_rows, query, masked) - lse[0, one, start:])
            slopes = dot(value_rows, incoming, 1, 0)
            low = (probs * (slopes - inner[one, start:])).astype(BF16)
            value_part = dot(incoming, probs.astype(BF16), 1, 1)
            key_part = dot(query, low, 1, 1)
            key_sum = key_part if key_sum is None else key_sum + key_part
            value_sum = value_part if value_sum is None else value_sum + value_part
            query_part = dot(keys, low, 1, 0)
            if first:
                q_sum[head, :] = query_part
            else:
                q_sum[head, start:] += query_part
        return key_sum, value_sum

    for start in range(0, rows, block):
        part = slice(start, start + block)
        key_sum, value_sum = step(
            k_own[:, part], keys_own[part, :], values_own[part, :], start, True, start == 0
        )
        own_grad[0, :hd, part] = key_sum
        own_grad[0, hd:, part] = value_sum

    @pl.loop(0, info[1])
    def _(device):
        key_sum, value_sum = step(
            k_past[device], keys_past[device], values_past[device], 0, False, False
        )
        past_grad[device, 0, :hd, :] = key_sum.astype(past_grad.dtype)
        past_grad[device, 0, hd:, :] = value_sum.astype(past_grad.dtype)

    cos, sin = cosine[...], -sine[...]
    for group, head in groups:
        first, second = rotate(q_sum[head, :], cos, sin)
        at = group * hd
        q_grad[at : at + hd // 2, :] = (first * hd**-0.5).astype(BF16)
        q_grad[at + hd // 2 : at + hd, :] = (second * hd**-0.5).astype(BF16)


def attend_back(info, qkv, past, mixed_grad, mixed, lse, tables, base, heads, cost=None):
    rows = qkv.shape[1]
    count = past.shape[0]
    hd = HEAD_DIM
    group = pl.BlockSpec((GROUP * hd, rows), lambda h, info: (base + h, 0))
    return call(
        attend_back_kernel,
        "attend_back",
        (heads,),
        attention_specs(rows, count, base)
        + [
            group,
            group,
            pl.BlockSpec((1, 8, rows), lambda h, info: (base + h, 0, 0)),
            whole(tables[0].shape),
            whole(tables[1].shape),
        ],
        [
            pl.BlockSpec((GROUP * hd, rows), lambda h, info: (h, 0)),
            pl.BlockSpec((1, 2 * hd, rows), lambda h, info: (h, 0, 0)),
            pl.BlockSpec((count, 1, 2 * hd, rows), lambda h, info: (0, h, 0, 0)),
        ],
        [
            shaped((heads * GROUP * hd, rows), BF16),
            shaped((heads, 2 * hd, rows), F32),
            shaped((count, heads, 2 * hd, rows), BF16 if count == 1 else F32),
        ],
        [
            pltpu.VMEM((rows, hd), BF16),
            pltpu.VMEM((rows, hd), BF16),
            pltpu.VMEM((count, rows, hd), BF16),
            pltpu.VMEM((count, rows, hd), BF16),
            pltpu.VMEM((8, rows), F32),
            pltpu.VMEM((GROUP * hd, rows), F32),
        ],
        cost=cost,
    )(info, qkv, qkv, qkv, past, past, mixed_grad, mixed, lse, *tables)


def project_back_kernel(parts, info, x, gain, grad_middle, *refs):
    q_grads, own_grads, arrived = refs[:parts], refs[parts : 2 * parts], refs[2 * parts : 3 * parts]
    (
        q_weight,
        k_own,
        k_oth,
        v_own,
        v_oth,
        cosine,
        sine,
        q_grad,
        kv_grad,
        out,
        branch,
        gain_grad,
        total,
    ) = refs[3 * parts :]
    half = x.shape[0] // 2
    hd = HEAD_DIM
    kv = KEY_HEADS * hd
    cos, sin = cosine[...], -sine[...]
    head = 0
    for piece, own, far in zip(q_grads, own_grads, arrived):
        q_grad[head * GROUP * hd : head * GROUP * hd + piece.shape[0], :] = piece[...]
        for item in range(own.shape[0]):
            both = own[item] + far[item].astype(F32)
            first, second = rotate(both[:hd], cos, sin)
            at = head * hd
            kv_grad[at : at + hd // 2, :] = first.astype(BF16)
            kv_grad[at + hd // 2 : at + hd, :] = second.astype(BF16)
            kv_grad[kv + at : kv + at + hd, :] = both[hd:].astype(BF16)
            head += 1
    total[...] = dot(q_weight[...], q_grad[...], 1, 0)
    for mine, k, v in ((info[0], k_own, v_own), (1 - info[0], k_oth, v_oth)):
        total[pl.ds(pl.multiple_of(mine * half, half), half), :] += dot(
            k[...], kv_grad[:kv, :], 0, 0
        ) + dot(v[...], kv_grad[kv:, :], 0, 0)
    back, gain_sum = norm_back(x[...].astype(F32), gain[...], total[...])
    gain_grad[...] = gain_sum
    result = grad_middle[...] + back
    out[...] = result
    branch[...] = result.astype(BF16)


def project_back(info, x, gain, grad_middle, q_grads, own_grads, arrived, weights, tables, cost=None):
    width, rows = x.shape
    q, k, v = weights
    heads = q.shape[1]
    kv = 2 * KEY_HEADS * HEAD_DIM
    operands = (x, gain, grad_middle, *q_grads, *own_grads, *arrived, q, *k, *v, *tables)
    shapes = [
        shaped((heads, rows), BF16),
        shaped((kv, rows), BF16),
        shaped((width, rows), F32),
        shaped((width, rows), BF16),
        shaped((width, 1), F32),
    ]
    return call(
        functools.partial(project_back_kernel, len(q_grads)),
        "project_back",
        (1,),
        [whole(item.shape) for item in operands],
        [whole(item.shape) for item in shapes],
        shapes,
        [pltpu.VMEM((width, rows), F32)],
        cost=cost,
    )(info, *operands)


def order_rows(info, target, sources):
    rows = sources[0].shape[1]
    size = target.shape[0] // 4
    at = 0
    for core in (1 - info[2], info[2]):
        for half in (1 - info[0], info[0]):
            start = pl.multiple_of((2 * half + core) * size, size)
            for index, source in enumerate(sources):
                target[at : at + size, index * rows : (index + 1) * rows] = source[
                    pl.ds(start, size), :
                ]
            at += size


def order_halves(info, target, sources):
    rows = sources[0].shape[1]
    size = target.shape[0] // 2
    for at, core in ((0, 1 - info[2]), (size, info[2])):
        start = pl.multiple_of(core * size, size)
        for index, source in enumerate(sources):
            target[at : at + size, index * rows : (index + 1) * rows] = source[pl.ds(start, size), :]


def outer_kernel(split_columns, info, left_a, right_a, left_b, right_b, sent, kept, left, right):
    rows = left_a.shape[1]

    @pl.when(pl.program_id(0) == 0)
    def _():
        order = order_halves if split_columns else order_rows
        order(info, left, (left_a, left_b))

    right[:rows, :] = right_a[...]
    right[rows:, :] = right_b[...]
    count, size = sent.shape[0], sent.shape[1]
    for at, out in ((0, sent), (count * size, kept)):
        product = dot(left[at : at + count * size, :], right[...], 1, 0).astype(BF16)
        for index in range(count):
            out[index] = product[index * size : (index + 1) * size]


def outer(info, parts, split_columns, cost=None):
    left_a, right_a, left_b, right_b = parts
    width, rows = left_a.shape
    columns = right_a.shape[1]
    if split_columns:
        tile = columns // 4

        def column(t, info):
            return jnp.where(t < 2, (1 - info[0]) * 2 + t, info[0] * 2 + t - 2)

        right = pl.BlockSpec((rows, tile), lambda t, info: (0, column(t, info)))
        result = pl.BlockSpec((1, width // 2, tile), lambda t, info: (t // 2, 0, t % 2))
        shape = shaped((2, width // 2, columns // 2), BF16)
    else:
        tile = columns // 5
        right = pl.BlockSpec((rows, tile), lambda t, info: (0, t))
        result = pl.BlockSpec((2, width // 4, tile), lambda t, info: (0, 0, t))
        shape = shaped((2, width // 4, columns), BF16)
    return call(
        functools.partial(outer_kernel, split_columns),
        "outer",
        (columns // tile,),
        [whole((width, rows)), right, whole((width, rows)), right],
        [result, result],
        [shape, shape],
        [pltpu.VMEM((width, 2 * rows), BF16), pltpu.VMEM((2 * rows, tile), BF16)],
        cost=cost,
    )(info, *parts)


def pack_kernel(extra, info, left_a, *refs):
    sent, kept, left, right = refs[-4:]
    refs = refs[:-4]
    gains, refs = refs[len(refs) - extra :], refs[: len(refs) - extra]
    left_b, rights_a, rights_b = refs[0], refs[1::2], refs[2::2]
    rows = left_a.shape[1]
    order_rows(info, left, (left_a, left_b))
    at = 0
    for right_a, right_b in zip(rights_a, rights_b):
        right[at : at + right_a.shape[0], :rows] = right_a[...]
        right[at : at + right_a.shape[0], rows:] = right_b[...]
        at += right_a.shape[0]
    count, size = sent.shape[0], sent.shape[1]
    for base, core, out in ((0, 1 - info[2], sent), (count * size, info[2], kept)):
        for start, span in spans(right.shape[0], 512):
            product = dot(left[base : base + count * size, :], right[start : start + span, :], 1, 1)
            for index in range(count):
                out[index, :, start : start + span] = product[
                    index * size : (index + 1) * size
                ].astype(BF16)
        for index, half in enumerate((1 - info[0], info[0])):
            part = pl.ds(pl.multiple_of((2 * half + core) * size, size), size)
            for number in range(extra // 2):
                term = gains[2 * number][part, :] + gains[2 * number + 1][part, :]
                out[index, :, at + number : at + number + 1] = term.astype(BF16)
            if extra:
                out[index, :, at + extra // 2 :] = jnp.zeros((size, extra // 2), BF16)


def pack(info, left_a, left_b, rights, gains=(), cost=None):
    width, rows = left_a.shape
    columns = sum(item.shape[0] for item in rights[::2])
    operands = (left_a, left_b, *rights, *gains)
    shape = shaped((2, width // 4, columns + len(gains)), BF16)
    return call(
        functools.partial(pack_kernel, len(gains)),
        "pack",
        (1,),
        [whole(item.shape) for item in operands],
        [whole(shape.shape)] * 2,
        [shape, shape],
        [pltpu.VMEM((width, 2 * rows), BF16), pltpu.VMEM((columns, 2 * rows), BF16)],
        cost=cost,
    )(info, *operands)


def last_kernel(info, held, query, key, value, gains):
    width, narrow = query.shape[1], key.shape[0]
    values = held[...].astype(F32)
    query[...] = values[:, :width]
    key[...] = values[:, width : width + narrow].T
    value[...] = values[:, width + narrow : width + 2 * narrow].T
    gains[...] = values[:, width + 2 * narrow :]


def last(info, held, width, narrow):
    rows, columns = held.shape
    shapes = [
        shaped((rows, width), F32),
        shaped((narrow, rows), F32),
        shaped((narrow, rows), F32),
        shaped((rows, columns - width - 2 * narrow), F32),
    ]
    return call(last_kernel, "last", (1,), [None], [None] * 4, shapes)(info, held)


def column_split(columns):
    return columns // 2 // 128 * 128


def both_cores_kernel(info, *refs):
    pairs = list(zip(refs[:-4:2], refs[1:-4:2]))
    over_y, keep_y, over_x, keep_x = refs[-4:]
    half = over_x.shape[1]
    for index, out in ((0, over_y), (1, keep_y)):
        at_y = at_x = 0
        for kept, arrived in pairs:
            total = kept[index].astype(F32) + arrived[index].astype(F32)
            split = column_split(total.shape[1])
            out[:, at_y : at_y + split] = total[:, :split].astype(BF16)
            low, top = total[:half, split:], total[half:, split:]
            end = at_x + total.shape[1] - split
            keep_x[index, :, at_x:end] = jnp.where(info[3] == 0, low, top).astype(BF16)
            over_x[index, :, at_x:end] = jnp.where(info[3] == 0, top, low).astype(BF16)
            at_y, at_x = at_y + split, end
        if at_x < keep_x.shape[2]:
            rest = jnp.zeros((half, keep_x.shape[2] - at_x), BF16)
            keep_x[index, :, at_x:] = rest
            over_x[index, :, at_x:] = rest


def both_cores(info, pairs):
    rows = pairs[0][0].shape[1]
    columns = [kept.shape[2] for kept, _ in pairs]
    split = sum(column_split(item) for item in columns)
    rest = sum(columns) - split
    if len(pairs) > 1:
        rest = -(-(split + rest) // 512) * 512 - split
    first = shaped((rows, split), BF16)
    second = shaped((2, rows // 2, rest), BF16)
    shapes = [first, first, second, second]
    operands = [item for pair in pairs for item in pair]
    return call(both_cores_kernel, "both_cores", (1,), [None] * len(operands), [None] * 4, shapes)(
        info, *operands
    )


def split_pair_kernel(info, held, first, second):
    a, b = column_split(first.shape[1]), column_split(second.shape[1])
    values = held[...]
    first[:, :a] = values[:, :a].astype(F32)
    second[:, :b] = values[:, a : a + b].astype(F32)
    rest = a + b + first.shape[1] - a
    first[:, a:] = values[:, a + b : rest].astype(F32)
    second[:, b:] = values[:, rest : rest + second.shape[1] - b].astype(F32)


def split_pair(info, held, first, second):
    shapes = [shaped((held.shape[0], first), F32), shaped((held.shape[0], second), F32)]
    return call(split_pair_kernel, "split_pair", (1,), [None], [None] * 2, shapes)(info, held)


def cross_kernel(info, keep_y, from_y, keep_x, from_x, over_x, over_y, kept):
    split, half = over_x.shape[1], over_x.shape[0]
    total = keep_y[...].astype(F32) + from_y[...].astype(F32)
    low, top = total[:half], total[half:]
    over_x[...] = jnp.where(info[3] == 0, top, low).astype(BF16)
    kept[:, :split] = jnp.where(info[3] == 0, low, top).astype(BF16)
    over_y[...] = (keep_x[0].astype(F32) + from_x[0].astype(F32)).astype(BF16)
    kept[:, split:] = (keep_x[1].astype(F32) + from_x[1].astype(F32)).astype(BF16)


def cross(info, keep_y, from_y, keep_x, from_x):
    rows, split = keep_y.shape
    rest = keep_x.shape[2]
    shapes = [
        shaped((rows // 2, split), BF16),
        shaped((rows // 2, rest), BF16),
        shaped((rows // 2, split + rest), BF16),
    ]
    return call(cross_kernel, "cross", (1,), [None] * 4, [None] * 3, shapes)(
        info, keep_y, from_y, keep_x, from_x
    )


def chosen(values, number):
    result = values[0]
    for index in range(1, len(values)):
        result = jnp.where(number == index, values[index], result)
    return result


def cut_up(values, dim, count):
    size = values.shape[dim] // count
    if dim == 0:
        return [values[index * size : (index + 1) * size] for index in range(count)]
    return [values[:, index * size : (index + 1) * size] for index in range(count)]


def divide_kernel(dim, info, kept, from_x, from_y, *outs):
    split = from_x.shape[1]
    total = kept[...].astype(F32)
    total = jnp.concatenate(
        [total[:, :split] + from_x[...].astype(F32), total[:, split:] + from_y[...].astype(F32)], 1
    )
    parts = cut_up(total, dim, 4)
    for mask, out in enumerate(outs):
        order = [parts[index ^ mask] for index in range(4)]
        out[...] = chosen(order, info[4]).astype(BF16)


def divide(info, kept, from_x, from_y, dim):
    rows, columns = kept.shape
    shape = (rows // 4, columns) if dim == 0 else (rows, columns // 4)
    return call(
        functools.partial(divide_kernel, dim),
        "divide",
        (1,),
        [None] * 3,
        [None] * 4,
        [shaped(shape, BF16)] * 4,
    )(info, kept, from_x, from_y)


def sum_kernel(info, *refs):
    total = refs[0][...].astype(F32)
    for item in refs[1:-1]:
        total = total + item[...].astype(F32)
    refs[-1][...] = total.astype(BF16)


def sum_all(info, *parts):
    shape = shaped(parts[0].shape, BF16)
    return call(sum_kernel, "sum", (1,), [None] * len(parts), [None], [shape])(info, *parts)[0]


def unite_kernel(dim, place, info, *refs):
    values, out = [item[...].astype(F32) for item in refs[:-1]], refs[-1]
    number = info[place]
    ordered = [
        chosen([values[index ^ other] for other in range(len(values))], number)
        for index in range(len(values))
    ]
    out[...] = jnp.concatenate(ordered, dim).astype(out.dtype)


def unite(info, parts, dim, place, dtype):
    shape = list(parts[0].shape)
    shape[dim] *= len(parts)
    return call(
        functools.partial(unite_kernel, dim, place),
        "unite",
        (1,),
        [None] * len(parts),
        [None],
        [shaped(tuple(shape), dtype)],
    )(info, *parts)[0]


def swap(values, axis, bit):
    size = lax.axis_size(axis)
    return lax.ppermute(values, axis, [(i, i ^ bit) for i in range(size)])


def bits_of(axis):
    size = lax.axis_size(axis)
    assert size & (size - 1) == 0
    return [1 << i for i in range(size.bit_length() - 1)]


def high(axis, bit):
    return (lax.axis_index(axis) // bit) % 2


def halves(values, dim, which):
    half = values.shape[dim] // 2
    return lax.dynamic_slice_in_dim(values, which * half, half, dim)


def joined(mine, other, dim, which):
    return jnp.where(
        which == 0,
        jnp.concatenate([mine, other], dim),
        jnp.concatenate([other, mine], dim),
    )


def tied(values, others):
    return lax.optimization_barrier((values, others))[0]


def from_pieces(own, pieces, mine, core, low_batch):
    near = joined(pieces[0], pieces[2], 0, core)
    far = joined(pieces[1], pieces[3], 0, core)
    return joined(own, joined(near, far, 0, low_batch), 0, mine)


def split_dim(shape, parts):
    if shape[0] % (8 * parts) == 0:
        return 0
    if shape[1] % (128 * parts) == 0:
        return 1
    return 0 if shape[0] % parts == 0 else 1


class Order:
    def __init__(self, token):
        self.token = token

    def __call__(self, *values):
        self.token, *values = lax.optimization_barrier((self.token, *values))
        return values[0] if len(values) == 1 else values


def quarters(values, dim, number):
    quarter = values.shape[dim] // 4
    return lax.dynamic_slice_in_dim(values, number * quarter, quarter, dim)


class Chain:
    def __init__(self, order, *pairs):
        self.order, self.pairs = order, pairs
        self.steps = [self.core, self.first, self.second]
        self.shares = [("seq", (1,), 0), ("batch", (1,), 0)]
        exchanges = [("seq", (bit,)) for bit in bits_of("seq")[1:]]
        bits = bits_of("batch")[1:]
        self.plain = not exchanges and len(bits) == 2
        while bits:
            exchanges.append(("batch", bits[:2]))
            bits = bits[2:]
        self.steps += [functools.partial(self.add, *item) for item in exchanges]
        self.steps += [self.share] * (2 + len(exchanges))
        self.waiting = None

    result_type = F32

    def send(self):
        self.waiting = self.steps.pop(0)()

    def core(self):
        def finish(*arrived):
            pairs = [(kept, far) for (_, kept), far in zip(self.pairs, arrived)]
            self.parts = both_cores(self.order.token, pairs)

        return [swap(self.order(away), "seq", 1) for away, _ in self.pairs], finish

    def first(self):
        over_y, keep_y, over_x, keep_x = self.parts
        over_y, over_x = self.order(over_y, over_x)

        def finish(from_y, from_x):
            self.parts = cross(self.order.token, keep_y, from_y, keep_x, from_x)

        return [swap(over_y, "fsdp", 1), swap(over_x, "batch", 1)], finish

    def second(self):
        over_x, over_y, kept = self.parts
        over_x, over_y = self.order(over_x, over_y)

        def finish(from_x, from_y):
            if self.plain:
                self.dim = split_dim(kept.shape, 4)
                self.held = divide(self.order.token, kept, from_x, from_y, self.dim)
                return
            arrived = jnp.concatenate([from_x, from_y], 1)
            self.held = (kept.astype(F32) + arrived.astype(F32)).astype(BF16)

        return [swap(over_x, "batch", 1), swap(over_y, "fsdp", 1)], finish

    def add(self, axis, bits):
        held = self.held
        if self.plain:
            own, *parts = held
            parts = self.order(*parts)
            arrived = [
                swap(part, axis, bits[0] * (mask & 1) + bits[1] * (mask >> 1))
                for mask, part in zip((1, 2, 3), parts)
            ]
            self.shares.append((axis, bits, self.dim))

            def finish(*values):
                self.held = sum_all(self.order.token, own, *values)

            return arrived, finish
        dim = split_dim(held.shape, 2 * len(bits))
        take = halves if len(bits) == 1 else quarters
        number = sum(high(axis, bit) << index for index, bit in enumerate(bits))
        masks = range(1, 1 << len(bits))
        parts = self.order(*[take(held, dim, number ^ mask) for mask in masks])
        parts = parts if len(bits) > 1 else [parts]
        arrived = [
            swap(part, axis, sum(bit for index, bit in enumerate(bits) if mask >> index & 1))
            for mask, part in zip(masks, parts)
        ]
        self.shares.append((axis, bits, dim))

        def finish(*values):
            total = take(held, dim, number).astype(F32)
            for item in values:
                total = total + item.astype(F32)
            self.held = total.astype(BF16)

        return arrived, finish

    def share(self):
        axis, bits, dim = self.shares.pop()
        held = self.order(self.held)
        masks = range(1, 1 << len(bits))
        arrived = [
            swap(held, axis, sum(bit for index, bit in enumerate(bits) if mask >> index & 1))
            for mask in masks
        ]

        def finish(*values):
            low = high(axis, bits[0])
            if self.plain:
                place = 4 if len(bits) == 2 else 3 if axis == "batch" else 2
                dtype = BF16 if self.shares else self.result_type
                self.held = unite(self.order.token, (held, *values), dim, place, dtype)
                return
            if len(bits) == 1:
                self.held = joined(held, values[0], dim, low)
                return
            near, far = joined(held, values[0], dim, low), joined(values[1], values[2], dim, low)
            self.held = joined(near, far, dim, high(axis, bits[1]))

        return arrived, finish

    def result(self):
        while self.waiting or self.steps:
            if self.waiting:
                take(self)
            else:
                self.send()
        return self.held.astype(self.result_type)


def take(*chains):
    flat = [item for chain in chains for item in chain.waiting[0]]
    values = chains[0].order(*flat)
    values = list(values) if len(flat) > 1 else [values]
    for chain in chains:
        arrived, finish = chain.waiting
        chain.waiting = None
        finish(*values[: len(arrived)])
        values = values[len(arrived) :]


def per_device(
    tokens,
    attn_gain,
    w_query,
    key_weight,
    value_weight,
    w_out,
    ffn_gain,
    w_gate,
    w_up,
    w_down,
    cotangent,
):
    assert tokens.shape[0] == 1 and lax.axis_size("fsdp") == 2
    mine, spot, core = lax.axis_index("fsdp"), lax.axis_index("seq"), high("seq", 1)
    low_batch = high("batch", 1)
    devices = lax.axis_size("seq")
    deep = lax.axis_index("batch") // 2 % 4
    info = jnp.stack([mine, spot, core, low_batch, deep]).astype(jnp.int32)
    start_in = tokens[0].T
    incoming = cotangent[0].T
    width, rows = start_in.shape

    gains = jnp.stack([attn_gain, ffn_gain])
    gains = joined(gains, swap(gains, "fsdp", 1), 1, mine).astype(F32)[..., None]
    key_weight, value_weight, w_down = key_weight.T, value_weight.T, w_down.T
    def fsdp(values):
        return swap(values, "fsdp", 1)

    def pair(values):
        return swap(values, "batch", 1)

    def cores(values):
        return swap(values, "seq", 1)

    q_piece = halves(halves(w_query, 0, low_batch), 0, core)
    kv_piece = halves(jnp.where(core == 0, key_weight, value_weight), 0, low_batch)
    q_0, kv_0 = fsdp(q_piece), fsdp(kv_piece)
    out_0 = fsdp(tied(halves(halves(w_out, 0, low_batch), 0, core), (q_0, kv_0)))
    q_1, kv_1, q_2, kv_2 = pair(q_0), pair(kv_0), cores(q_0), cores(kv_0)
    gate_0 = fsdp(tied(halves(halves(w_gate, 0, low_batch), 1, core), out_0))
    q_3, kv_3 = cores(q_1), cores(kv_1)
    q_weight = from_pieces(w_query, (q_0, q_1, q_2, q_3), mine, core, low_batch)
    held = joined(kv_0, kv_1, 0, low_batch)
    other = joined(kv_2, kv_3, 0, low_batch)
    k_oth, v_oth = jnp.where(core == 0, held, other), jnp.where(core == 0, other, held)
    qkv_weights = (q_weight, (key_weight, k_oth), (value_weight, v_oth))

    positions = (spot * rows + jnp.arange(rows, dtype=jnp.int32)).astype(F32)
    frequency = jnp.exp(
        jnp.arange(HEAD_DIM // 2, dtype=F32) * (-2.0 * math.log(10000.0) / HEAD_DIM)
    )
    angles = frequency[:, None] * positions[None, :]
    tables = (jnp.cos(angles), jnp.sin(angles))

    def gathered(qkv):
        kv = qkv[QUERY_HEADS * HEAD_DIM :]
        if devices == 2:
            return cores(kv)[None]
        return lax.all_gather(kv, "seq")

    low_normed, low_qkv = project(info, start_in, gains[0], qkv_weights, tables)
    low_past = gathered(low_qkv)
    ready = (low_qkv, gate_0)
    up_0 = fsdp(tied(halves(halves(w_up, 0, low_batch), 1, core), ready))
    down_0 = fsdp(tied(halves(halves(w_down, 0, low_batch), 0, core), ready))
    out_1, out_2 = pair(tied(out_0, (q_1, kv_1))), cores(out_0)
    gate_1, gate_2 = pair(tied(gate_0, (low_qkv, out_1))), cores(gate_0)
    out_3 = cores(out_1)
    out_weight = from_pieces(w_out, (out_0, out_1, out_2, out_3), mine, core, low_batch)
    low_mixed, low_lse = attend(info, low_qkv, tied(low_past, out_weight), 0, KEY_HEADS)
    low_mixed = tied(low_mixed, (up_0, down_0, gate_1))
    gate_3, up_1, up_2 = cores(gate_1), pair(tied(up_0, low_mixed)), cores(up_0)
    low_middle, low_normed_ffn = mix(info, start_in, low_mixed, out_weight, gains[1])
    up_3 = cores(tied(up_1, low_middle))
    down_1, down_2 = pair(tied(down_0, (up_1, low_middle))), cores(tied(down_0, low_middle))
    low_hidden, low_silu, low_slope, gate, up = expand_first(
        info,
        low_normed_ffn,
        (w_gate, gate_0, gate_1, gate_2, gate_3),
        (w_up, up_0, up_1, up_2, up_3),
    )
    down_3 = cores(tied(down_1, low_hidden))
    middle_in, down = shrink_first(
        info, low_middle, low_hidden, (w_down, down_0, down_1, down_2, down_3)
    )

    high_normed, high_qkv = project(info, middle_in, gains[0], qkv_weights, tables)
    high_past = gathered(high_qkv)
    high_mixed, high_lse = attend(info, high_qkv, high_past, 0, KEY_HEADS)
    high_middle, high_normed_ffn = mix(info, middle_in, high_mixed, out_weight, gains[1])
    high_hidden, high_silu, high_slope = expand(info, high_normed_ffn, gate, up)

    def attention_back(qkv, past, mixed_grad, mixed, lse, base, heads, cost=None):
        return attend_back(
            info, qkv, past, mixed_grad, mixed, lse, tables, base, heads, cost
        )

    def returned(past_grad):
        if devices == 2:
            return cores(past_grad[0])
        return lax.psum_scatter(past_grad, "seq", scatter_dimension=0)

    def to_input(x, grad_middle, parts, cost=None):
        return project_back(
            info, x, gains[0], grad_middle, *zip(*parts), qkv_weights, tables, cost
        )

    high_gate, high_up, high_branch, grad_middle, high_attn, mixed_grad, high_ffn_gain = ffn_back(
        info, incoming, high_middle, gains[1], high_silu, high_slope, down, gate, up, out_weight
    )
    parts = [
        attention_back(high_qkv, high_past, mixed_grad, high_mixed, high_lse, base, heads)
        for base, heads in ((0, 3), (3, 2))
    ]
    parts = [(*part[:2], returned(part[2])) for part in parts]
    high_q, high_kv, grad_between, low_branch, high_attn_gain = to_input(
        middle_in, grad_middle, parts
    )

    order = Order(tied(info, low_branch))
    down_terms = (high_branch, high_hidden, low_branch, low_hidden)
    down_g = Chain(order, outer(info, down_terms, True))
    down_g.send()
    final_out = order(shrink(info, order(high_middle), high_hidden, down, BF16))
    take(down_g)
    down_g.send()
    low_gate, low_up, _, grad_middle, low_attn, mixed_grad, low_ffn_gain = ffn_back(
        info, order(grad_between), low_middle, gains[1], low_silu, low_slope,
        down, gate, up, out_weight,
    )
    low_attn = order(low_attn)
    take(down_g)
    down_g.send()
    out_pair = pack(info, high_mixed, low_mixed, (high_attn, order(low_attn)))
    gate_terms = (high_normed_ffn, high_gate, low_normed_ffn, order(low_gate))
    gate_g = Chain(order, outer(info, gate_terms, False), out_pair)
    gate_g.result_type = BF16
    gate_g.send()
    take(down_g)
    down_g.send()
    up_terms = (high_normed_ffn, high_up, low_normed_ffn, order(low_up))
    up_g = Chain(order, outer(info, up_terms, False))
    up_g.send()
    take(gate_g)
    gate_g.send()
    parts = []

    def low_part(base, heads):
        mixed_now = order(mixed_grad)
        part = attention_back(low_qkv, low_past, mixed_now, low_mixed, low_lse, base, heads)
        parts.append((order(part[0]), *part[1:]))

    low_part(0, 2)
    take(gate_g, up_g, down_g)
    gate_g.send()
    up_g.send()
    down_g.send()
    low_part(2, 3)
    parts = [(*part[:2], returned(order(part[2]))) for part in parts]
    take(gate_g, up_g, down_g)
    up_g.send()
    gate_g.send()
    low_q, low_kv, grad_start, _, low_attn_gain = to_input(
        start_in, order(grad_middle), parts, 0
    )
    low_q = order(low_q)
    take(up_g, gate_g)
    gate_g.send()
    down_g.send()
    qkv_terms = (high_q, order(low_q), high_kv, low_kv)
    gain_terms = (high_attn_gain, low_attn_gain, high_ffn_gain, low_ffn_gain)
    qkv_g = Chain(order, pack(info, high_normed, low_normed, qkv_terms, gain_terms, 0))
    qkv_g.result_type = BF16
    qkv_g.send()
    take(qkv_g, gate_g, down_g)
    qkv_g.send()
    up_g.send()
    down_g.send()
    take(qkv_g, up_g, down_g)
    down_grad = down_g.result()
    qkv_g.send()
    take(qkv_g)
    qkv_g.send()
    up_g.send()
    gate_g.send()
    down_grad = order(down_grad)
    take(qkv_g, up_g, gate_g)
    qkv_g.send()
    up_g.send()
    gate_g.send()
    take(qkv_g, up_g, gate_g)
    qkv_g.send()
    up_g.send()
    take(qkv_g, up_g)
    qkv_g.send()
    gate_grad, out_grad = split_pair(
        order.token, order(gate_g.result()), w_gate.shape[1], w_out.shape[1]
    )
    up_grad = order(up_g.result())
    held = order(qkv_g.result())
    narrow = KEY_HEADS * HEAD_DIM
    query_part, key_part, value_part, gain_grads = last(order.token, held, width, narrow)
    return (
        final_out.T[None],
        grad_start.T[None],
        gain_grads[:, 0],
        query_part,
        key_part.T,
        value_part.T,
        out_grad,
        gain_grads[:, 1],
        gate_grad,
        up_grad,
        down_grad.T,
    )


def solution(mesh):
    return jax.shard_map(
        per_device,
        mesh=mesh,
        in_specs=(
            P(("batch", "fsdp"), "seq", None),
            P("fsdp"),
            P("fsdp", None),
            P("fsdp", None),
            P("fsdp", None),
            P("fsdp", None),
            P("fsdp"),
            P("fsdp", None),
            P("fsdp", None),
            P("fsdp", None),
            P(("batch", "fsdp"), "seq", None),
        ),
        out_specs=(
            P(("batch", "fsdp"), "seq", None),
            P(("batch", "fsdp"), "seq", None),
            P("fsdp"),
            P("fsdp", None),
            P("fsdp", None),
            P("fsdp", None),
            P("fsdp", None),
            P("fsdp"),
            P("fsdp", None),
            P("fsdp", None),
            P("fsdp", None),
        ),
        check_vma=False,
    )
```

```python
import functools
import math

import jax
import jax.numpy as jnp
from jax import lax
from jax.experimental import pallas as pl
from jax.experimental.pallas import tpu as pltpu
from jax.sharding import PartitionSpec as P

QUERY_HEADS = 15
KEY_HEADS = 5
HEAD_DIM = 64
GROUP = QUERY_HEADS // KEY_HEADS
EPSILON = 1e-05
F32 = jnp.float32
BF16 = jnp.bfloat16


def dot(left, right, left_dim, right_dim):
    return lax.dot_general(
        left, right, (((left_dim,), (right_dim,)), ((), ())), preferred_element_type=F32
    )


def spans(total, size):
    return [(start, min(size, total - start)) for start in range(0, total, size)]


COSTS = {
    "project": 6.0,
    "attend": 4.0,
    "mix": 5.5,
    "expand": 10.0,
    "expand_first": 14.0,
    "shrink": 6.5,
    "shrink_first": 8.0,
    "ffn_back": 18.0,
    "attend_back": 6.5,
    "project_back": 6.0,
    "outer": 10.0,
    "pack": 4.0,
    "both_cores": 0.0,
    "cross": 0.0,
    "last": 0.0,
    "divide": 0.0,
    "split_pair": 0.0,
    "sum": 0.0,
    "unite": 0.0,
}


LIMITS = {
    "project": 12,
    "attend": 14,
    "mix": 12,
    "expand": 24,
    "expand_first": 34,
    "shrink": 22,
    "shrink_first": 34,
    "ffn_back": 40,
    "attend_back": 16,
    "project_back": 16,
    "outer": 26,
    "pack": 20,
    "both_cores": 12,
    "cross": 10,
    "last": 12,
    "divide": 10,
    "split_pair": 16,
    "sum": 6,
    "unite": 14,
}


def call(kernel, name, grid, in_specs, out_specs, out_shape, scratch=(), cost=None):
    if cost is None:
        cost = COSTS[name] * 0.45 * (grid[0] if name.startswith("attend") else 1)
    cost = int(cost * 1e9) + 1
    options = dict(
        name=name,
        out_shape=out_shape,
        compiler_params=pltpu.CompilerParams(vmem_limit_bytes=LIMITS[name] * 1024 * 1024),
        cost_estimate=pl.CostEstimate(flops=cost, bytes_accessed=1, transcendentals=0),
    )
    if name in ("project", "mix", "project_back", "pack", "both_cores", "cross", "last", "divide", "sum", "unite", "split_pair"):
        memory = pl.BlockSpec(memory_space=pltpu.VMEM)
        return pl.pallas_call(
            kernel,
            in_specs=[pl.BlockSpec(memory_space=pltpu.SMEM)] + [memory] * len(in_specs),
            out_specs=[memory] * len(out_specs),
            scratch_shapes=list(scratch),
            **options,
        )
    return pl.pallas_call(
        kernel,
        grid_spec=pltpu.PrefetchScalarGridSpec(
            num_scalar_prefetch=1,
            grid=grid,
            in_specs=in_specs,
            out_specs=out_specs,
            scratch_shapes=list(scratch),
        ),
        **options,
    )


def whole(shape):
    return pl.BlockSpec(shape, lambda *_: (0,) * len(shape))


def shaped(shape, dtype):
    return jax.ShapeDtypeStruct(shape, dtype)


def scale_of(values):
    return lax.rsqrt(jnp.mean(values * values, 0, keepdims=True) + EPSILON)


def norm_back(values, gain, incoming):
    scales = scale_of(values)
    weighted = gain * incoming
    inner = jnp.mean(values * weighted, 0, keepdims=True)
    grad = scales * weighted - values * (scales * scales * scales * inner)
    return grad, jnp.sum(incoming * values * scales, 1, keepdims=True)


def rotate(values, cosine, sine):
    half = HEAD_DIM // 2
    first, second = values[:half], values[half:]
    return first * cosine - second * sine, second * cosine + first * sine


def project_kernel(
    info, x, gain, q_weight, k_own, k_oth, v_own, v_oth, cosine, sine, normed, out
):
    width = x.shape[0]
    half = width // 2
    values = x[...].astype(F32)
    normed[...] = (values * scale_of(values) * gain[...]).astype(BF16)
    own = normed[pl.ds(pl.multiple_of(info[0] * half, half), half), :]
    oth = normed[pl.ds(pl.multiple_of((1 - info[0]) * half, half), half), :]
    cos, sin = cosine[...], sine[...]
    hd = HEAD_DIM

    def turned(rows, base, factor):
        for head in range(rows.shape[0] // hd):
            first, second = rotate(rows[head * hd : (head + 1) * hd], cos, sin)
            at = base + head * hd
            out[at : at + hd // 2, :] = (first * factor).astype(BF16)
            out[at + hd // 2 : at + hd, :] = (second * factor).astype(BF16)

    q_width = q_weight.shape[1]
    turned(dot(q_weight[...], normed[...], 0, 0), 0, hd**-0.5)
    kv = k_own.shape[0]
    turned(dot(k_own[...], own, 1, 0) + dot(k_oth[...], oth, 1, 0), q_width, 1.0)
    rows = dot(v_own[...], own, 1, 0) + dot(v_oth[...], oth, 1, 0)
    out[q_width + kv : q_width + 2 * kv, :] = rows.astype(BF16)


def project(info, x, gain, weights, tables, cost=None):
    width, rows = x.shape
    q, k, v = weights
    total = q.shape[1] + 2 * k[0].shape[0]
    operands = (x, gain, q, *k, *v, *tables)
    return call(
        project_kernel,
        "project",
        (1,),
        [whole(item.shape) for item in operands],
        [whole((width, rows)), whole((total, rows))],
        [shaped((width, rows), BF16), shaped((total, rows), BF16)],
        cost=cost,
    )(info, *operands)


def scores_of(keys, queries, masked):
    scores = dot(keys, queries, 1, 0)
    if not masked:
        return scores
    key_row = lax.broadcasted_iota(jnp.int32, scores.shape, 0)
    query_row = lax.broadcasted_iota(jnp.int32, scores.shape, 1)
    return jnp.where(key_row <= query_row, scores, -1e30)


def attend_kernel(
    info, q, k_own, v_own, k_past, v_past, out, lse, keys_own, keys_past, peak, total, mixed
):
    rows = q.shape[1]
    block = min(256, rows)
    hd = HEAD_DIM
    groups = [(group, slice(group * hd, (group + 1) * hd)) for group in range(GROUP)]
    keys_own[...] = k_own[...].T

    @pl.loop(0, info[1])
    def _(device):
        keys_past[device] = k_past[device].T

    for start in range(0, rows, block):
        for group, head in groups:
            scores = scores_of(keys_own[start : start + block, :], q[head, start:], True)
            fresh = jnp.max(scores, 0, keepdims=True)
            if start > 0:
                fresh = jnp.maximum(fresh, peak[group : group + 1, start:])
            peak[group : group + 1, start:] = fresh

    @pl.loop(0, info[1])
    def _(device):
        for group, head in groups:
            scores = scores_of(keys_past[device], q[head, :], False)
            peak[group : group + 1, :] = jnp.maximum(
                peak[group : group + 1, :], jnp.max(scores, 0, keepdims=True)
            )

    def add(group, head, keys, values, start, masked, first):
        scores = scores_of(keys, q[head, start:], masked)
        exponent = jnp.exp(scores - peak[group : group + 1, start:])
        sums = jnp.sum(exponent, 0, keepdims=True)
        product = dot(values, exponent.astype(BF16), 1, 0)
        if first:
            total[group : group + 1, :] = sums
            mixed[head, :] = product
        else:
            total[group : group + 1, start:] += sums
            mixed[head, start:] += product

    for start in range(0, rows, block):
        part = slice(start, start + block)
        for group, head in groups:
            add(group, head, keys_own[part, :], v_own[:, part], start, True, start == 0)

    @pl.loop(0, info[1])
    def _(device):
        for group, head in groups:
            add(group, head, keys_past[device], v_past[device], 0, False, False)

    for group, head in groups:
        sums = total[group : group + 1, :]
        out[head, :] = (mixed[head, :] / sums).astype(BF16)
        lse[0, group : group + 1, :] = peak[group : group + 1, :] + jnp.log(sums)


def attention_specs(rows, past, base):
    hd = HEAD_DIM
    return [
        pl.BlockSpec((GROUP * hd, rows), lambda h, info: (base + h, 0)),
        pl.BlockSpec((hd, rows), lambda h, info: (QUERY_HEADS + base + h, 0)),
        pl.BlockSpec((hd, rows), lambda h, info: (QUERY_HEADS + KEY_HEADS + base + h, 0)),
        pl.BlockSpec((past, hd, rows), lambda h, info: (0, base + h, 0)),
        pl.BlockSpec((past, hd, rows), lambda h, info: (0, KEY_HEADS + base + h, 0)),
    ]


def attend(info, qkv, past, base, heads):
    rows = qkv.shape[1]
    count = past.shape[0]
    group = GROUP * HEAD_DIM
    return call(
        attend_kernel,
        "attend",
        (heads,),
        attention_specs(rows, count, base),
        [
            pl.BlockSpec((group, rows), lambda h, info: (h, 0)),
            pl.BlockSpec((1, 8, rows), lambda h, info: (h, 0, 0)),
        ],
        [shaped((heads * group, rows), BF16), shaped((heads, 8, rows), F32)],
        [
            pltpu.VMEM((rows, HEAD_DIM), BF16),
            pltpu.VMEM((count, rows, HEAD_DIM), BF16),
            pltpu.VMEM((8, rows), F32),
            pltpu.VMEM((8, rows), F32),
            pltpu.VMEM((GROUP * HEAD_DIM, rows), F32),
        ],
    )(info, qkv, qkv, qkv, past, past)


def mix_kernel(info, x, mixed, weight, gain, middle, normed):
    middle[...] = x[...].astype(F32) + dot(weight[...], mixed[...], 0, 0)
    values = middle[...]
    normed[...] = (values * scale_of(values) * gain[...]).astype(BF16)


def mix(info, x, mixed, weight, gain):
    width, rows = x.shape
    operands = (x, mixed, weight, gain)
    return call(
        mix_kernel,
        "mix",
        (1,),
        [whole(item.shape) for item in operands],
        [whole((width, rows)), whole((width, rows))],
        [shaped((width, rows), F32), shaped((width, rows), BF16)],
    )(info, *operands)


def activate(token_rows, gate_weight, up_weight, hidden, silu, slope):
    gate = dot(token_rows[...], gate_weight[...], 1, 0)
    up = dot(token_rows[...], up_weight[...], 1, 0)
    sigmoid = 0.5 * jnp.tanh(0.5 * gate) + 0.5
    active = gate * sigmoid
    hidden[...] = (active * up).astype(BF16)
    silu[...] = active.astype(BF16)
    slope[...] = (up * (sigmoid + active * (1.0 - sigmoid))).astype(BF16)


def expand_kernel(info, normed, gate_weight, up_weight, hidden, silu, slope, token_rows):
    @pl.when(pl.program_id(0) == 0)
    def _():
        token_rows[...] = normed[...].T

    activate(token_rows, gate_weight, up_weight, hidden, silu, slope)


def expand(info, normed, gate, up):
    width, rows = normed.shape
    ff = gate.shape[1]
    tile = ff // 5
    weight = pl.BlockSpec((width, tile), lambda t, info: (0, t))
    result = pl.BlockSpec((rows, tile), lambda t, info: (0, t))
    return call(
        expand_kernel,
        "expand",
        (ff // tile,),
        [whole((width, rows)), weight, weight],
        [result] * 3,
        [shaped((rows, ff), BF16)] * 3,
        [pltpu.VMEM((rows, width), BF16)],
    )(info, normed, gate, up)


def expand_first_kernel(info, normed, *refs):
    gate_parts, up_parts = refs[:5], refs[5:10]
    hidden, silu, slope, gate_weight, up_weight, token_rows = refs[10:]
    step = pl.program_id(0)
    steps = pl.num_programs(0)

    @pl.when(step == 0)
    def _():
        token_rows[...] = normed[...].T

    for (own, *pieces), target in ((gate_parts, gate_weight), (up_parts, up_weight)):
        half, quarter = own.shape[0], pieces[0].shape[0]
        target[pl.ds(pl.multiple_of(info[0] * half, half), half), :] = own[...]
        other = (1 - info[0]) * half
        near = pl.ds(pl.multiple_of(other + info[3] * quarter, quarter), quarter)
        far = pl.ds(pl.multiple_of(other + (1 - info[3]) * quarter, quarter), quarter)

        @pl.when(step < steps // 2)
        def _():
            target[near, :] = pieces[0][...]
            target[far, :] = pieces[1][...]

        @pl.when(step >= steps // 2)
        def _():
            target[near, :] = pieces[2][...]
            target[far, :] = pieces[3][...]

    activate(token_rows, gate_weight, up_weight, hidden, silu, slope)


def expand_first(info, normed, gate, up):
    width, rows = normed.shape
    half, ff = gate[0].shape
    steps = 4
    tile = ff // steps
    quarter = half // 2

    def column(t, info):
        own = info[2] * (steps // 2) + t
        return jnp.where(t < steps // 2, own, (1 - info[2]) * (steps // 2) + t - steps // 2)

    early = pl.BlockSpec((quarter, tile), lambda t, info: (0, jnp.minimum(t, steps // 2 - 1)))
    late = pl.BlockSpec((quarter, tile), lambda t, info: (0, jnp.maximum(t - steps // 2, 0)))
    parts = [pl.BlockSpec((half, tile), lambda t, info: (0, column(t, info)))]
    parts += [early, early, late, late]
    result = pl.BlockSpec((rows, tile), lambda t, info: (0, column(t, info)))
    weight = pl.BlockSpec((width, tile), lambda t, info: (0, column(t, info)))
    return call(
        expand_first_kernel,
        "expand_first",
        (steps,),
        [whole((width, rows))] + parts * 2,
        [result] * 3 + [weight] * 2,
        [shaped((rows, ff), BF16)] * 3 + [shaped((width, ff), BF16)] * 2,
        [pltpu.VMEM((rows, width), BF16)],
    )(info, normed, *gate, *up)


def shrink_kernel(info, middle, hidden, weight, out):
    out[...] = (middle[...] + dot(weight[...], hidden[...], 1, 1)).astype(out.dtype)


def shrink(info, middle, hidden, down, dtype, cost=None):
    width, rows = middle.shape
    ff = hidden.shape[1]
    tile = width // 2
    return call(
        shrink_kernel,
        "shrink",
        (width // tile,),
        [
            pl.BlockSpec((tile, rows), lambda t, info: (t, 0)),
            whole((rows, ff)),
            pl.BlockSpec((tile, ff), lambda t, info: (t, 0)),
        ],
        [pl.BlockSpec((tile, rows), lambda t, info: (t, 0))],
        [shaped((width, rows), dtype)],
        cost=cost,
    )(info, middle, hidden, down)[0]


def shrink_first_kernel(info, middle, hidden, own, near_0, far_0, near_1, far_1, out, weight):
    half, quarter = own.shape[1], near_0.shape[0]
    weight[:, pl.ds(pl.multiple_of(info[0] * half, half), half)] = own[...]
    other = pl.ds(pl.multiple_of((1 - info[0]) * half, half), half)
    at_near = pl.ds(pl.multiple_of(info[2] * quarter, quarter), quarter)
    at_far = pl.ds(pl.multiple_of((1 - info[2]) * quarter, quarter), quarter)
    for step, near, far in ((0, near_0, far_0), (1, near_1, far_1)):

        @pl.when(pl.program_id(0) == step)
        def _():
            weight[at_near, other] = near[...]
            weight[at_far, other] = far[...]

    out[...] = middle[...] + dot(weight[...], hidden[...], 1, 1)


def shrink_first(info, middle, hidden, parts):
    width, rows = middle.shape
    ff = hidden.shape[1]
    tile = width // 2
    own, first, second, third, fourth = parts

    def row(t, info):
        return jnp.where(t == 0, info[3], 1 - info[3])

    return call(
        shrink_first_kernel,
        "shrink_first",
        (2,),
        [
            pl.BlockSpec((tile, rows), lambda t, info: (row(t, info), 0)),
            whole((rows, ff)),
            pl.BlockSpec((tile, ff // 2), lambda t, info: (row(t, info), 0)),
        ]
        + [whole(first.shape)] * 4,
        [
            pl.BlockSpec((tile, rows), lambda t, info: (row(t, info), 0)),
            pl.BlockSpec((tile, ff), lambda t, info: (row(t, info), 0)),
        ],
        [shaped((width, rows), F32), shaped((width, ff), BF16)],
    )(info, middle, hidden, own, first, third, second, fourth)


def ffn_back_kernel(
    info,
    grad,
    middle,
    gain,
    silu,
    slope,
    down,
    gate,
    up,
    out_weight,
    gate_grad,
    up_grad,
    branch,
    grad_middle,
    attn_grad,
    mixed_grad,
    gain_grad,
    branch_rows,
    total,
):
    step = pl.program_id(0)
    steps = pl.num_programs(0)

    @pl.when(step == 0)
    def _():
        branch[...] = grad[...].astype(BF16)
        branch_rows[...] = branch[...].T
        total[...] = jnp.zeros_like(total)

    incoming = dot(branch_rows[...], down[...], 1, 0)
    gate_grad[...] = (incoming * slope[...].astype(F32)).astype(BF16)
    up_grad[...] = (incoming * silu[...].astype(F32)).astype(BF16)
    total[...] += dot(gate[...], gate_grad[...], 1, 1) + dot(up[...], up_grad[...], 1, 1)

    @pl.when(step == steps - 1)
    def _():
        back, gain_sum = norm_back(middle[...], gain[...], total[...])
        gain_grad[...] = gain_sum
        result = grad[...].astype(F32) + back
        grad_middle[...] = result
        attn_grad[...] = result.astype(BF16)
        mixed_grad[...] = dot(out_weight[...], attn_grad[...], 1, 0).astype(BF16)


def ffn_back(info, grad, middle, gain, silu, slope, down, gate, up, out_weight, cost=None):
    width, rows = middle.shape
    ff = silu.shape[1]
    tile = ff // 5
    heads = out_weight.shape[0]
    token = pl.BlockSpec((rows, tile), lambda t, info: (0, t))
    weight = pl.BlockSpec((width, tile), lambda t, info: (0, t))
    return call(
        ffn_back_kernel,
        "ffn_back",
        (ff // tile,),
        [
            whole((width, rows)),
            whole((width, rows)),
            whole((width, 1)),
            token,
            token,
            weight,
            weight,
            weight,
            whole((heads, width)),
        ],
        [
            token,
            token,
            whole((width, rows)),
            whole((width, rows)),
            whole((width, rows)),
            whole((heads, rows)),
            whole((width, 1)),
        ],
        [
            shaped((rows, ff), BF16),
            shaped((rows, ff), BF16),
            shaped((width, rows), BF16),
            shaped((width, rows), F32),
            shaped((width, rows), BF16),
            shaped((heads, rows), BF16),
            shaped((width, 1), F32),
        ],
        [pltpu.VMEM((rows, width), BF16), pltpu.VMEM((width, rows), F32)],
        cost=cost,
    )(info, grad, middle, gain, silu, slope, down, gate, up, out_weight)


def attend_back_kernel(
    info,
    q,
    k_own,
    v_own,
    k_past,
    v_past,
    mixed_grad,
    mixed,
    lse,
    cosine,
    sine,
    q_grad,
    own_grad,
    past_grad,
    keys_own,
    values_own,
    keys_past,
    values_past,
    inner,
    q_sum,
):
    rows = q.shape[1]
    block = min(256, rows)
    hd = HEAD_DIM
    groups = [(group, slice(group * hd, (group + 1) * hd)) for group in range(GROUP)]
    keys_own[...] = k_own[...].T
    values_own[...] = v_own[...].T

    @pl.loop(0, info[1])
    def _(device):
        keys_past[device] = k_past[device].T
        values_past[device] = v_past[device].T

    @pl.loop(info[1], past_grad.shape[0])
    def _(device):
        past_grad[device] = jnp.zeros_like(past_grad[device])

    for group, head in groups:
        product = mixed_grad[head, :].astype(F32) * mixed[head, :].astype(F32)
        inner[group : group + 1, :] = jnp.sum(product, 0, keepdims=True)

    def step(keys, key_rows, value_rows, start, masked, first):
        key_sum = value_sum = None
        for group, head in groups:
            query, incoming = q[head, start:], mixed_grad[head, start:]
            one = slice(group, group + 1)
            probs = jnp.exp(scores_of(key_rows, query, masked) - lse[0, one, start:])
            slopes = dot(value_rows, incoming, 1, 0)
            low = (probs * (slopes - inner[one, start:])).astype(BF16)
            value_part = dot(incoming, probs.astype(BF16), 1, 1)
            key_part = dot(query, low, 1, 1)
            key_sum = key_part if key_sum is None else key_sum + key_part
            value_sum = value_part if value_sum is None else value_sum + value_part
            query_part = dot(keys, low, 1, 0)
            if first:
                q_sum[head, :] = query_part
            else:
                q_sum[head, start:] += query_part
        return key_sum, value_sum

    for start in range(0, rows, block):
        part = slice(start, start + block)
        key_sum, value_sum = step(
            k_own[:, part], keys_own[part, :], values_own[part, :], start, True, start == 0
        )
        own_grad[0, :hd, part] = key_sum
        own_grad[0, hd:, part] = value_sum

    @pl.loop(0, info[1])
    def _(device):
        key_sum, value_sum = step(
            k_past[device], keys_past[device], values_past[device], 0, False, False
        )
        past_grad[device, 0, :hd, :] = key_sum.astype(past_grad.dtype)
        past_grad[device, 0, hd:, :] = value_sum.astype(past_grad.dtype)

    cos, sin = cosine[...], -sine[...]
    for group, head in groups:
        first, second = rotate(q_sum[head, :], cos, sin)
        at = group * hd
        q_grad[at : at + hd // 2, :] = (first * hd**-0.5).astype(BF16)
        q_grad[at + hd // 2 : at + hd, :] = (second * hd**-0.5).astype(BF16)


def attend_back(info, qkv, past, mixed_grad, mixed, lse, tables, base, heads, cost=None):
    rows = qkv.shape[1]
    count = past.shape[0]
    hd = HEAD_DIM
    group = pl.BlockSpec((GROUP * hd, rows), lambda h, info: (base + h, 0))
    return call(
        attend_back_kernel,
        "attend_back",
        (heads,),
        attention_specs(rows, count, base)
        + [
            group,
            group,
            pl.BlockSpec((1, 8, rows), lambda h, info: (base + h, 0, 0)),
            whole(tables[0].shape),
            whole(tables[1].shape),
        ],
        [
            pl.BlockSpec((GROUP * hd, rows), lambda h, info: (h, 0)),
            pl.BlockSpec((1, 2 * hd, rows), lambda h, info: (h, 0, 0)),
            pl.BlockSpec((count, 1, 2 * hd, rows), lambda h, info: (0, h, 0, 0)),
        ],
        [
            shaped((heads * GROUP * hd, rows), BF16),
            shaped((heads, 2 * hd, rows), F32),
            shaped((count, heads, 2 * hd, rows), BF16 if count == 1 else F32),
        ],
        [
            pltpu.VMEM((rows, hd), BF16),
            pltpu.VMEM((rows, hd), BF16),
            pltpu.VMEM((count, rows, hd), BF16),
            pltpu.VMEM((count, rows, hd), BF16),
            pltpu.VMEM((8, rows), F32),
            pltpu.VMEM((GROUP * hd, rows), F32),
        ],
        cost=cost,
    )(info, qkv, qkv, qkv, past, past, mixed_grad, mixed, lse, *tables)


def project_back_kernel(parts, info, x, gain, grad_middle, *refs):
    q_grads, own_grads, arrived = refs[:parts], refs[parts : 2 * parts], refs[2 * parts : 3 * parts]
    (
        q_weight,
        k_own,
        k_oth,
        v_own,
        v_oth,
        cosine,
        sine,
        q_grad,
        kv_grad,
        out,
        branch,
        gain_grad,
        total,
    ) = refs[3 * parts :]
    half = x.shape[0] // 2
    hd = HEAD_DIM
    kv = KEY_HEADS * hd
    cos, sin = cosine[...], -sine[...]
    head = 0
    for piece, own, far in zip(q_grads, own_grads, arrived):
        q_grad[head * GROUP * hd : head * GROUP * hd + piece.shape[0], :] = piece[...]
        for item in range(own.shape[0]):
            both = own[item] + far[item].astype(F32)
            first, second = rotate(both[:hd], cos, sin)
            at = head * hd
            kv_grad[at : at + hd // 2, :] = first.astype(BF16)
            kv_grad[at + hd // 2 : at + hd, :] = second.astype(BF16)
            kv_grad[kv + at : kv + at + hd, :] = both[hd:].astype(BF16)
            head += 1
    total[...] = dot(q_weight[...], q_grad[...], 1, 0)
    for mine, k, v in ((info[0], k_own, v_own), (1 - info[0], k_oth, v_oth)):
        total[pl.ds(pl.multiple_of(mine * half, half), half), :] += dot(
            k[...], kv_grad[:kv, :], 0, 0
        ) + dot(v[...], kv_grad[kv:, :], 0, 0)
    back, gain_sum = norm_back(x[...].astype(F32), gain[...], total[...])
    gain_grad[...] = gain_sum
    result = grad_middle[...] + back
    out[...] = result
    branch[...] = result.astype(BF16)


def project_back(info, x, gain, grad_middle, q_grads, own_grads, arrived, weights, tables, cost=None):
    width, rows = x.shape
    q, k, v = weights
    heads = q.shape[1]
    kv = 2 * KEY_HEADS * HEAD_DIM
    operands = (x, gain, grad_middle, *q_grads, *own_grads, *arrived, q, *k, *v, *tables)
    shapes = [
        shaped((heads, rows), BF16),
        shaped((kv, rows), BF16),
        shaped((width, rows), F32),
        shaped((width, rows), BF16),
        shaped((width, 1), F32),
    ]
    return call(
        functools.partial(project_back_kernel, len(q_grads)),
        "project_back",
        (1,),
        [whole(item.shape) for item in operands],
        [whole(item.shape) for item in shapes],
        shapes,
        [pltpu.VMEM((width, rows), F32)],
        cost=cost,
    )(info, *operands)


def order_rows(info, target, sources):
    rows = sources[0].shape[1]
    size = target.shape[0] // 4
    at = 0
    for core in (1 - info[2], info[2]):
        for half in (1 - info[0], info[0]):
            start = pl.multiple_of((2 * half + core) * size, size)
            for index, source in enumerate(sources):
                target[at : at + size, index * rows : (index + 1) * rows] = source[
                    pl.ds(start, size), :
                ]
            at += size


def order_halves(info, target, sources):
    rows = sources[0].shape[1]
    size = target.shape[0] // 2
    for at, core in ((0, 1 - info[2]), (size, info[2])):
        start = pl.multiple_of(core * size, size)
        for index, source in enumerate(sources):
            target[at : at + size, index * rows : (index + 1) * rows] = source[pl.ds(start, size), :]


def outer_kernel(split_columns, info, left_a, right_a, left_b, right_b, sent, kept, left, right):
    rows = left_a.shape[1]

    @pl.when(pl.program_id(0) == 0)
    def _():
        order = order_halves if split_columns else order_rows
        order(info, left, (left_a, left_b))

    right[:rows, :] = right_a[...]
    right[rows:, :] = right_b[...]
    count, size = sent.shape[0], sent.shape[1]
    for at, out in ((0, sent), (count * size, kept)):
        product = dot(left[at : at + count * size, :], right[...], 1, 0).astype(BF16)
        for index in range(count):
            out[index] = product[index * size : (index + 1) * size]


def outer(info, parts, split_columns, cost=None):
    left_a, right_a, left_b, right_b = parts
    width, rows = left_a.shape
    columns = right_a.shape[1]
    if split_columns:
        tile = columns // 4

        def column(t, info):
            return jnp.where(t < 2, (1 - info[0]) * 2 + t, info[0] * 2 + t - 2)

        right = pl.BlockSpec((rows, tile), lambda t, info: (0, column(t, info)))
        result = pl.BlockSpec((1, width // 2, tile), lambda t, info: (t // 2, 0, t % 2))
        shape = shaped((2, width // 2, columns // 2), BF16)
    else:
        tile = columns // 5
        right = pl.BlockSpec((rows, tile), lambda t, info: (0, t))
        result = pl.BlockSpec((2, width // 4, tile), lambda t, info: (0, 0, t))
        shape = shaped((2, width // 4, columns), BF16)
    return call(
        functools.partial(outer_kernel, split_columns),
        "outer",
        (columns // tile,),
        [whole((width, rows)), right, whole((width, rows)), right],
        [result, result],
        [shape, shape],
        [pltpu.VMEM((width, 2 * rows), BF16), pltpu.VMEM((2 * rows, tile), BF16)],
        cost=cost,
    )(info, *parts)


def pack_kernel(extra, info, left_a, *refs):
    sent, kept, left, right = refs[-4:]
    refs = refs[:-4]
    gains, refs = refs[len(refs) - extra :], refs[: len(refs) - extra]
    left_b, rights_a, rights_b = refs[0], refs[1::2], refs[2::2]
    rows = left_a.shape[1]
    order_rows(info, left, (left_a, left_b))
    at = 0
    for right_a, right_b in zip(rights_a, rights_b):
        right[at : at + right_a.shape[0], :rows] = right_a[...]
        right[at : at + right_a.shape[0], rows:] = right_b[...]
        at += right_a.shape[0]
    count, size = sent.shape[0], sent.shape[1]
    for base, core, out in ((0, 1 - info[2], sent), (count * size, info[2], kept)):
        for start, span in spans(right.shape[0], 512):
            product = dot(left[base : base + count * size, :], right[start : start + span, :], 1, 1)
            for index in range(count):
                out[index, :, start : start + span] = product[
                    index * size : (index + 1) * size
                ].astype(BF16)
        for index, half in enumerate((1 - info[0], info[0])):
            part = pl.ds(pl.multiple_of((2 * half + core) * size, size), size)
            for number in range(extra // 2):
                term = gains[2 * number][part, :] + gains[2 * number + 1][part, :]
                out[index, :, at + number : at + number + 1] = term.astype(BF16)
            if extra:
                out[index, :, at + extra // 2 :] = jnp.zeros((size, extra // 2), BF16)


def pack(info, left_a, left_b, rights, gains=(), cost=None):
    width, rows = left_a.shape
    columns = sum(item.shape[0] for item in rights[::2])
    operands = (left_a, left_b, *rights, *gains)
    shape = shaped((2, width // 4, columns + len(gains)), BF16)
    return call(
        functools.partial(pack_kernel, len(gains)),
        "pack",
        (1,),
        [whole(item.shape) for item in operands],
        [whole(shape.shape)] * 2,
        [shape, shape],
        [pltpu.VMEM((width, 2 * rows), BF16), pltpu.VMEM((columns, 2 * rows), BF16)],
        cost=cost,
    )(info, *operands)


def last_kernel(info, held, query, key, value, gains):
    width, narrow = query.shape[1], key.shape[0]
    values = held[...].astype(F32)
    query[...] = values[:, :width]
    key[...] = values[:, width : width + narrow].T
    value[...] = values[:, width + narrow : width + 2 * narrow].T
    gains[...] = values[:, width + 2 * narrow :]


def last(info, held, width, narrow):
    rows, columns = held.shape
    shapes = [
        shaped((rows, width), F32),
        shaped((narrow, rows), F32),
        shaped((narrow, rows), F32),
        shaped((rows, columns - width - 2 * narrow), F32),
    ]
    return call(last_kernel, "last", (1,), [None], [None] * 4, shapes)(info, held)


def column_split(columns):
    return columns // 2 // 128 * 128


def both_cores_kernel(info, *refs):
    pairs = list(zip(refs[:-4:2], refs[1:-4:2]))
    over_y, keep_y, over_x, keep_x = refs[-4:]
    half = over_x.shape[1]
    for index, out in ((0, over_y), (1, keep_y)):
        at_y = at_x = 0
        for kept, arrived in pairs:
            total = kept[index].astype(F32) + arrived[index].astype(F32)
            split = column_split(total.shape[1])
            out[:, at_y : at_y + split] = total[:, :split].astype(BF16)
            low, top = total[:half, split:], total[half:, split:]
            end = at_x + total.shape[1] - split
            keep_x[index, :, at_x:end] = jnp.where(info[3] == 0, low, top).astype(BF16)
            over_x[index, :, at_x:end] = jnp.where(info[3] == 0, top, low).astype(BF16)
            at_y, at_x = at_y + split, end
        if at_x < keep_x.shape[2]:
            rest = jnp.zeros((half, keep_x.shape[2] - at_x), BF16)
            keep_x[index, :, at_x:] = rest
            over_x[index, :, at_x:] = rest


def both_cores(info, pairs):
    rows = pairs[0][0].shape[1]
    columns = [kept.shape[2] for kept, _ in pairs]
    split = sum(column_split(item) for item in columns)
    rest = sum(columns) - split
    if len(pairs) > 1:
        rest = -(-(split + rest) // 512) * 512 - split
    first = shaped((rows, split), BF16)
    second = shaped((2, rows // 2, rest), BF16)
    shapes = [first, first, second, second]
    operands = [item for pair in pairs for item in pair]
    return call(both_cores_kernel, "both_cores", (1,), [None] * len(operands), [None] * 4, shapes)(
        info, *operands
    )


def split_pair_kernel(info, held, first, second):
    a, b = column_split(first.shape[1]), column_split(second.shape[1])
    values = held[...]
    first[:, :a] = values[:, :a].astype(F32)
    second[:, :b] = values[:, a : a + b].astype(F32)
    rest = a + b + first.shape[1] - a
    first[:, a:] = values[:, a + b : rest].astype(F32)
    second[:, b:] = values[:, rest : rest + second.shape[1] - b].astype(F32)


def split_pair(info, held, first, second):
    shapes = [shaped((held.shape[0], first), F32), shaped((held.shape[0], second), F32)]
    return call(split_pair_kernel, "split_pair", (1,), [None], [None] * 2, shapes)(info, held)


def cross_kernel(info, keep_y, from_y, keep_x, from_x, over_x, over_y, kept):
    split, half = over_x.shape[1], over_x.shape[0]
    total = keep_y[...].astype(F32) + from_y[...].astype(F32)
    low, top = total[:half], total[half:]
    over_x[...] = jnp.where(info[3] == 0, top, low).astype(BF16)
    kept[:, :split] = jnp.where(info[3] == 0, low, top).astype(BF16)
    over_y[...] = (keep_x[0].astype(F32) + from_x[0].astype(F32)).astype(BF16)
    kept[:, split:] = (keep_x[1].astype(F32) + from_x[1].astype(F32)).astype(BF16)


def cross(info, keep_y, from_y, keep_x, from_x):
    rows, split = keep_y.shape
    rest = keep_x.shape[2]
    shapes = [
        shaped((rows // 2, split), BF16),
        shaped((rows // 2, rest), BF16),
        shaped((rows // 2, split + rest), BF16),
    ]
    return call(cross_kernel, "cross", (1,), [None] * 4, [None] * 3, shapes)(
        info, keep_y, from_y, keep_x, from_x
    )


def chosen(values, number):
    result = values[0]
    for index in range(1, len(values)):
        result = jnp.where(number == index, values[index], result)
    return result


def cut_up(values, dim, count):
    size = values.shape[dim] // count
    if dim == 0:
        return [values[index * size : (index + 1) * size] for index in range(count)]
    return [values[:, index * size : (index + 1) * size] for index in range(count)]


def divide_kernel(dim, info, kept, from_x, from_y, *outs):
    split = from_x.shape[1]
    total = kept[...].astype(F32)
    total = jnp.concatenate(
        [total[:, :split] + from_x[...].astype(F32), total[:, split:] + from_y[...].astype(F32)], 1
    )
    parts = cut_up(total, dim, 4)
    for mask, out in enumerate(outs):
        order = [parts[index ^ mask] for index in range(4)]
        out[...] = chosen(order, info[4]).astype(BF16)


def divide(info, kept, from_x, from_y, dim):
    rows, columns = kept.shape
    shape = (rows // 4, columns) if dim == 0 else (rows, columns // 4)
    return call(
        functools.partial(divide_kernel, dim),
        "divide",
        (1,),
        [None] * 3,
        [None] * 4,
        [shaped(shape, BF16)] * 4,
    )(info, kept, from_x, from_y)


def sum_kernel(info, *refs):
    total = refs[0][...].astype(F32)
    for item in refs[1:-1]:
        total = total + item[...].astype(F32)
    refs[-1][...] = total.astype(BF16)


def sum_all(info, *parts):
    shape = shaped(parts[0].shape, BF16)
    return call(sum_kernel, "sum", (1,), [None] * len(parts), [None], [shape])(info, *parts)[0]


def unite_kernel(dim, place, info, *refs):
    values, out = [item[...].astype(F32) for item in refs[:-1]], refs[-1]
    number = info[place]
    ordered = [
        chosen([values[index ^ other] for other in range(len(values))], number)
        for index in range(len(values))
    ]
    out[...] = jnp.concatenate(ordered, dim).astype(out.dtype)


def unite(info, parts, dim, place, dtype):
    shape = list(parts[0].shape)
    shape[dim] *= len(parts)
    return call(
        functools.partial(unite_kernel, dim, place),
        "unite",
        (1,),
        [None] * len(parts),
        [None],
        [shaped(tuple(shape), dtype)],
    )(info, *parts)[0]


def swap(values, axis, bit):
    size = lax.axis_size(axis)
    return lax.ppermute(values, axis, [(i, i ^ bit) for i in range(size)])


def bits_of(axis):
    size = lax.axis_size(axis)
    assert size & (size - 1) == 0
    return [1 << i for i in range(size.bit_length() - 1)]


def high(axis, bit):
    return (lax.axis_index(axis) // bit) % 2


def halves(values, dim, which):
    half = values.shape[dim] // 2
    return lax.dynamic_slice_in_dim(values, which * half, half, dim)


def joined(mine, other, dim, which):
    return jnp.where(
        which == 0,
        jnp.concatenate([mine, other], dim),
        jnp.concatenate([other, mine], dim),
    )


def tied(values, others):
    return lax.optimization_barrier((values, others))[0]


def from_pieces(own, pieces, mine, core, low_batch):
    near = joined(pieces[0], pieces[2], 0, core)
    far = joined(pieces[1], pieces[3], 0, core)
    return joined(own, joined(near, far, 0, low_batch), 0, mine)


def split_dim(shape, parts):
    if shape[0] % (8 * parts) == 0:
        return 0
    if shape[1] % (128 * parts) == 0:
        return 1
    return 0 if shape[0] % parts == 0 else 1


class Order:
    def __init__(self, token):
        self.token = token

    def __call__(self, *values):
        self.token, *values = lax.optimization_barrier((self.token, *values))
        return values[0] if len(values) == 1 else values


def quarters(values, dim, number):
    quarter = values.shape[dim] // 4
    return lax.dynamic_slice_in_dim(values, number * quarter, quarter, dim)


class Chain:
    def __init__(self, order, pair, beside=()):
        self.order, self.pair, self.beside = order, pair, beside
        self.steps = [self.core, self.first, self.second]
        self.shares = [("seq", (1,), 0), ("batch", (1,), 0)]
        exchanges = [("seq", (bit,)) for bit in bits_of("seq")[1:]]
        bits = bits_of("batch")[1:]
        self.plain = not exchanges and len(bits) == 2
        while bits:
            exchanges.append(("batch", bits[:2]))
            bits = bits[2:]
        self.steps += [functools.partial(self.add, *item) for item in exchanges]
        self.steps += [self.share] * (2 + len(exchanges))
        self.waiting = None

    result_type = F32

    def send(self):
        self.waiting = self.steps.pop(0)()

    def core(self):
        away, kept = self.pair

        def finish(arrived):
            self.parts = both_cores(self.order.token, [(kept, arrived), *self.beside])

        return [swap(self.order(away), "seq", 1)], finish

    def first(self):
        over_y, keep_y, over_x, keep_x = self.parts
        over_y, over_x = self.order(over_y, over_x)

        def finish(from_y, from_x):
            self.parts = cross(self.order.token, keep_y, from_y, keep_x, from_x)

        return [swap(over_y, "fsdp", 1), swap(over_x, "batch", 1)], finish

    def second(self):
        over_x, over_y, kept = self.parts
        over_x, over_y = self.order(over_x, over_y)

        def finish(from_x, from_y):
            if self.plain:
                self.dim = split_dim(kept.shape, 4)
                self.held = divide(self.order.token, kept, from_x, from_y, self.dim)
                return
            arrived = jnp.concatenate([from_x, from_y], 1)
            self.held = (kept.astype(F32) + arrived.astype(F32)).astype(BF16)

        return [swap(over_x, "batch", 1), swap(over_y, "fsdp", 1)], finish

    def add(self, axis, bits):
        held = self.held
        if self.plain:
            own, *parts = held
            parts = self.order(*parts)
            arrived = [
                swap(part, axis, bits[0] * (mask & 1) + bits[1] * (mask >> 1))
                for mask, part in zip((1, 2, 3), parts)
            ]
            self.shares.append((axis, bits, self.dim))

            def finish(*values):
                self.held = sum_all(self.order.token, own, *values)

            return arrived, finish
        dim = split_dim(held.shape, 2 * len(bits))
        take = halves if len(bits) == 1 else quarters
        number = sum(high(axis, bit) << index for index, bit in enumerate(bits))
        masks = range(1, 1 << len(bits))
        parts = self.order(*[take(held, dim, number ^ mask) for mask in masks])
        parts = parts if len(bits) > 1 else [parts]
        arrived = [
            swap(part, axis, sum(bit for index, bit in enumerate(bits) if mask >> index & 1))
            for mask, part in zip(masks, parts)
        ]
        self.shares.append((axis, bits, dim))

        def finish(*values):
            total = take(held, dim, number).astype(F32)
            for item in values:
                total = total + item.astype(F32)
            self.held = total.astype(BF16)

        return arrived, finish

    def share(self):
        axis, bits, dim = self.shares.pop()
        held = self.order(self.held)
        masks = range(1, 1 << len(bits))
        arrived = [
            swap(held, axis, sum(bit for index, bit in enumerate(bits) if mask >> index & 1))
            for mask in masks
        ]

        def finish(*values):
            low = high(axis, bits[0])
            if self.plain:
                place = 4 if len(bits) == 2 else 3 if axis == "batch" else 2
                dtype = BF16 if self.shares else self.result_type
                self.held = unite(self.order.token, (held, *values), dim, place, dtype)
                return
            if len(bits) == 1:
                self.held = joined(held, values[0], dim, low)
                return
            near, far = joined(held, values[0], dim, low), joined(values[1], values[2], dim, low)
            self.held = joined(near, far, dim, high(axis, bits[1]))

        return arrived, finish

    def result(self):
        while self.waiting or self.steps:
            if self.waiting:
                take(self)
            else:
                self.send()
        return self.held.astype(self.result_type)


def take(*chains):
    flat = [item for chain in chains for item in chain.waiting[0]]
    values = chains[0].order(*flat)
    values = list(values) if len(flat) > 1 else [values]
    for chain in chains:
        arrived, finish = chain.waiting
        chain.waiting = None
        finish(*values[: len(arrived)])
        values = values[len(arrived) :]


def per_device(
    tokens,
    attn_gain,
    w_query,
    key_weight,
    value_weight,
    w_out,
    ffn_gain,
    w_gate,
    w_up,
    w_down,
    cotangent,
):
    assert tokens.shape[0] == 1 and lax.axis_size("fsdp") == 2
    mine, spot, core = lax.axis_index("fsdp"), lax.axis_index("seq"), high("seq", 1)
    low_batch = high("batch", 1)
    devices = lax.axis_size("seq")
    deep = lax.axis_index("batch") // 2 % 4
    info = jnp.stack([mine, spot, core, low_batch, deep]).astype(jnp.int32)
    start_in = tokens[0].T
    incoming = cotangent[0].T
    width, rows = start_in.shape

    gains = jnp.stack([attn_gain, ffn_gain])
    gains = joined(gains, swap(gains, "fsdp", 1), 1, mine).astype(F32)[..., None]
    key_weight, value_weight, w_down = key_weight.T, value_weight.T, w_down.T
    def fsdp(values):
        return swap(values, "fsdp", 1)

    def pair(values):
        return swap(values, "batch", 1)

    def cores(values):
        return swap(values, "seq", 1)

    q_piece = halves(halves(w_query, 0, low_batch), 0, core)
    kv_piece = halves(jnp.where(core == 0, key_weight, value_weight), 0, low_batch)
    q_0, kv_0 = fsdp(q_piece), fsdp(kv_piece)
    out_0 = fsdp(tied(halves(halves(w_out, 0, low_batch), 0, core), (q_0, kv_0)))
    q_1, kv_1, q_2, kv_2 = pair(q_0), pair(kv_0), cores(q_0), cores(kv_0)
    gate_0 = fsdp(tied(halves(halves(w_gate, 0, low_batch), 1, core), out_0))
    q_3, kv_3 = cores(q_1), cores(kv_1)
    q_weight = from_pieces(w_query, (q_0, q_1, q_2, q_3), mine, core, low_batch)
    held = joined(kv_0, kv_1, 0, low_batch)
    other = joined(kv_2, kv_3, 0, low_batch)
    k_oth, v_oth = jnp.where(core == 0, held, other), jnp.where(core == 0, other, held)
    qkv_weights = (q_weight, (key_weight, k_oth), (value_weight, v_oth))

    positions = (spot * rows + jnp.arange(rows, dtype=jnp.int32)).astype(F32)
    frequency = jnp.exp(
        jnp.arange(HEAD_DIM // 2, dtype=F32) * (-2.0 * math.log(10000.0) / HEAD_DIM)
    )
    angles = frequency[:, None] * positions[None, :]
    tables = (jnp.cos(angles), jnp.sin(angles))

    def gathered(qkv):
        kv = qkv[QUERY_HEADS * HEAD_DIM :]
        if devices == 2:
            return cores(kv)[None]
        return lax.all_gather(kv, "seq")

    low_normed, low_qkv = project(info, start_in, gains[0], qkv_weights, tables)
    low_past = gathered(low_qkv)
    ready = (low_qkv, gate_0)
    up_0 = fsdp(tied(halves(halves(w_up, 0, low_batch), 1, core), ready))
    down_0 = fsdp(tied(halves(halves(w_down, 0, low_batch), 0, core), ready))
    out_1, out_2 = pair(tied(out_0, (q_1, kv_1))), cores(out_0)
    gate_1, gate_2 = pair(tied(gate_0, (low_qkv, out_1))), cores(gate_0)
    out_3 = cores(out_1)
    out_weight = from_pieces(w_out, (out_0, out_1, out_2, out_3), mine, core, low_batch)
    low_mixed, low_lse = attend(info, low_qkv, tied(low_past, out_weight), 0, KEY_HEADS)
    low_mixed = tied(low_mixed, (up_0, down_0, gate_1))
    gate_3, up_1, up_2 = cores(gate_1), pair(tied(up_0, low_mixed)), cores(up_0)
    low_middle, low_normed_ffn = mix(info, start_in, low_mixed, out_weight, gains[1])
    up_3 = cores(tied(up_1, low_middle))
    down_1, down_2 = pair(tied(down_0, (up_1, low_middle))), cores(tied(down_0, low_middle))
    low_hidden, low_silu, low_slope, gate, up = expand_first(
        info,
        low_normed_ffn,
        (w_gate, gate_0, gate_1, gate_2, gate_3),
        (w_up, up_0, up_1, up_2, up_3),
    )
    down_3 = cores(tied(down_1, low_hidden))
    middle_in, down = shrink_first(
        info, low_middle, low_hidden, (w_down, down_0, down_1, down_2, down_3)
    )

    high_normed, high_qkv = project(info, middle_in, gains[0], qkv_weights, tables)
    high_past = gathered(high_qkv)
    high_mixed, high_lse = attend(info, high_qkv, high_past, 0, KEY_HEADS)
    high_middle, high_normed_ffn = mix(info, middle_in, high_mixed, out_weight, gains[1])
    high_hidden, high_silu, high_slope = expand(info, high_normed_ffn, gate, up)

    def attention_back(qkv, past, mixed_grad, mixed, lse, base, heads, cost=None):
        return attend_back(
            info, qkv, past, mixed_grad, mixed, lse, tables, base, heads, cost
        )

    def returned(past_grad):
        if devices == 2:
            return cores(past_grad[0])
        return lax.psum_scatter(past_grad, "seq", scatter_dimension=0)

    def to_input(x, grad_middle, parts, cost=None):
        return project_back(
            info, x, gains[0], grad_middle, *zip(*parts), qkv_weights, tables, cost
        )

    high_gate, high_up, high_branch, grad_middle, high_attn, mixed_grad, high_ffn_gain = ffn_back(
        info, incoming, high_middle, gains[1], high_silu, high_slope, down, gate, up, out_weight
    )
    parts = [
        attention_back(high_qkv, high_past, mixed_grad, high_mixed, high_lse, base, heads)
        for base, heads in ((0, 3), (3, 2))
    ]
    parts = [(*part[:2], returned(part[2])) for part in parts]
    high_q, high_kv, grad_between, low_branch, high_attn_gain = to_input(
        middle_in, grad_middle, parts
    )

    order = Order(tied(info, low_branch))
    down_terms = (high_branch, high_hidden, low_branch, low_hidden)
    down_g = Chain(order, outer(info, down_terms, True))
    down_g.send()
    final_out = order(shrink(info, order(high_middle), high_hidden, down, BF16))
    take(down_g)
    down_g.send()
    low_gate, low_up, _, grad_middle, low_attn, mixed_grad, low_ffn_gain = ffn_back(
        info, order(grad_between), low_middle, gains[1], low_silu, low_slope,
        down, gate, up, out_weight,
    )
    low_attn = order(low_attn)
    take(down_g)
    down_g.send()
    out_away, out_kept = pack(info, high_mixed, low_mixed, (high_attn, order(low_attn)))
    out_far = cores(order(out_away))
    gate_terms = (high_normed_ffn, high_gate, low_normed_ffn, order(low_gate))
    gate_g = Chain(order, outer(info, gate_terms, False))
    gate_g.result_type = BF16
    gate_g.send()
    take(down_g)
    down_g.send()
    gate_g.beside = ((out_kept, order(out_far)),)
    up_terms = (high_normed_ffn, high_up, low_normed_ffn, order(low_up))
    up_g = Chain(order, outer(info, up_terms, False, 14))
    up_g.send()
    take(gate_g)
    gate_g.send()
    parts = []

    def low_part(base, heads):
        mixed_now = order(mixed_grad)
        part = attention_back(low_qkv, low_past, mixed_now, low_mixed, low_lse, base, heads)
        parts.append((order(part[0]), *part[1:]))

    low_part(0, 2)
    take(up_g, gate_g, down_g)
    gate_g.send()
    up_g.send()
    down_g.send()
    low_part(2, 3)
    parts = [(*part[:2], returned(order(part[2]))) for part in parts]
    take(gate_g, up_g, down_g)
    up_g.send()
    gate_g.send()
    low_q, low_kv, grad_start, _, low_attn_gain = to_input(
        start_in, order(grad_middle), parts, 0
    )
    low_q = order(low_q)
    take(up_g, gate_g)
    gate_g.send()
    down_g.send()
    qkv_terms = (high_q, order(low_q), high_kv, low_kv)
    gain_terms = (high_attn_gain, low_attn_gain, high_ffn_gain, low_ffn_gain)
    qkv_g = Chain(order, pack(info, high_normed, low_normed, qkv_terms, gain_terms, 0))
    qkv_g.result_type = BF16
    qkv_g.send()
    take(gate_g, down_g)
    take(qkv_g)
    qkv_g.send()
    up_g.send()
    take(qkv_g, up_g)
    qkv_g.send()
    up_g.send()
    take(qkv_g, up_g)
    qkv_g.send()
    gate_g.send()
    down_g.send()
    take(qkv_g, gate_g, down_g)
    down_grad = down_g.result()
    qkv_g.send()
    up_g.send()
    gate_g.send()
    down_grad = order(down_grad)
    take(qkv_g, up_g, gate_g)
    qkv_g.send()
    up_g.send()
    take(qkv_g, up_g)
    qkv_g.send()
    gate_grad, out_grad = split_pair(
        order.token, order(gate_g.result()), w_gate.shape[1], w_out.shape[1]
    )
    up_grad = order(up_g.result())
    held = order(qkv_g.result())
    narrow = KEY_HEADS * HEAD_DIM
    query_part, key_part, value_part, gain_grads = last(order.token, held, width, narrow)
    return (
        final_out.T[None],
        grad_start.T[None],
        gain_grads[:, 0],
        query_part,
        key_part.T,
        value_part.T,
        out_grad,
        gain_grads[:, 1],
        gate_grad,
        up_grad,
        down_grad.T,
    )


def solution(mesh):
    return jax.shard_map(
        per_device,
        mesh=mesh,
        in_specs=(
            P(("batch", "fsdp"), "seq", None),
            P("fsdp"),
            P("fsdp", None),
            P("fsdp", None),
            P("fsdp", None),
            P("fsdp", None),
            P("fsdp"),
            P("fsdp", None),
            P("fsdp", None),
            P("fsdp", None),
            P(("batch", "fsdp"), "seq", None),
        ),
        out_specs=(
            P(("batch", "fsdp"), "seq", None),
            P(("batch", "fsdp"), "seq", None),
            P("fsdp"),
            P("fsdp", None),
            P("fsdp", None),
            P("fsdp", None),
            P("fsdp", None),
            P("fsdp"),
            P("fsdp", None),
            P("fsdp", None),
            P("fsdp", None),
        ),
        check_vma=False,
    )
```

```python
import functools
import math

import jax
import jax.numpy as jnp
from jax import lax
from jax.experimental import pallas as pl
from jax.experimental.pallas import tpu as pltpu
from jax.sharding import PartitionSpec as P

QUERY_HEADS = 15
KEY_HEADS = 5
HEAD_DIM = 64
GROUP = QUERY_HEADS // KEY_HEADS
EPSILON = 1e-05
F32 = jnp.float32
BF16 = jnp.bfloat16


def dot(left, right, left_dim, right_dim):
    return lax.dot_general(
        left, right, (((left_dim,), (right_dim,)), ((), ())), preferred_element_type=F32
    )


def spans(total, size):
    return [(start, min(size, total - start)) for start in range(0, total, size)]


COSTS = {
    "project": 6.0,
    "attend": 4.0,
    "mix": 5.5,
    "expand": 10.0,
    "expand_first": 14.0,
    "shrink": 6.5,
    "shrink_first": 8.0,
    "ffn_back": 18.0,
    "attend_back": 6.5,
    "project_back": 6.0,
    "outer": 10.0,
    "pack": 4.0,
    "both_cores": 0.0,
    "cross": 0.0,
    "last": 0.0,
    "divide": 0.0,
    "split_pair": 0.0,
    "sum": 0.0,
    "unite": 0.0,
}


LIMITS = {
    "project": 12,
    "attend": 14,
    "mix": 12,
    "expand": 24,
    "expand_first": 34,
    "shrink": 22,
    "shrink_first": 34,
    "ffn_back": 40,
    "attend_back": 16,
    "project_back": 16,
    "outer": 26,
    "pack": 20,
    "both_cores": 12,
    "cross": 10,
    "last": 12,
    "divide": 10,
    "split_pair": 16,
    "sum": 6,
    "unite": 14,
}


def call(kernel, name, grid, in_specs, out_specs, out_shape, scratch=(), cost=None):
    if cost is None:
        cost = COSTS[name] * 0.45 * (grid[0] if name.startswith("attend") else 1)
    cost = int(cost * 1e9) + 1
    options = dict(
        name=name,
        out_shape=out_shape,
        compiler_params=pltpu.CompilerParams(vmem_limit_bytes=LIMITS[name] * 1024 * 1024),
        cost_estimate=pl.CostEstimate(flops=cost, bytes_accessed=1, transcendentals=0),
    )
    if name in ("project", "mix", "project_back", "pack", "both_cores", "cross", "last", "divide", "sum", "unite", "split_pair"):
        memory = pl.BlockSpec(memory_space=pltpu.VMEM)
        return pl.pallas_call(
            kernel,
            in_specs=[pl.BlockSpec(memory_space=pltpu.SMEM)] + [memory] * len(in_specs),
            out_specs=[memory] * len(out_specs),
            scratch_shapes=list(scratch),
            **options,
        )
    return pl.pallas_call(
        kernel,
        grid_spec=pltpu.PrefetchScalarGridSpec(
            num_scalar_prefetch=1,
            grid=grid,
            in_specs=in_specs,
            out_specs=out_specs,
            scratch_shapes=list(scratch),
        ),
        **options,
    )


def whole(shape):
    return pl.BlockSpec(shape, lambda *_: (0,) * len(shape))


def shaped(shape, dtype):
    return jax.ShapeDtypeStruct(shape, dtype)


def scale_of(values):
    return lax.rsqrt(jnp.mean(values * values, 0, keepdims=True) + EPSILON)


def norm_back(values, gain, incoming):
    scales = scale_of(values)
    weighted = gain * incoming
    inner = jnp.mean(values * weighted, 0, keepdims=True)
    grad = scales * weighted - values * (scales * scales * scales * inner)
    return grad, jnp.sum(incoming * values * scales, 1, keepdims=True)


def rotate(values, cosine, sine):
    half = HEAD_DIM // 2
    first, second = values[:half], values[half:]
    return first * cosine - second * sine, second * cosine + first * sine


def project_kernel(
    info, x, gain, q_weight, k_own, k_oth, v_own, v_oth, cosine, sine, normed, out
):
    width = x.shape[0]
    half = width // 2
    values = x[...].astype(F32)
    normed[...] = (values * scale_of(values) * gain[...]).astype(BF16)
    own = normed[pl.ds(pl.multiple_of(info[0] * half, half), half), :]
    oth = normed[pl.ds(pl.multiple_of((1 - info[0]) * half, half), half), :]
    cos, sin = cosine[...], sine[...]
    hd = HEAD_DIM

    def turned(rows, base, factor):
        for head in range(rows.shape[0] // hd):
            first, second = rotate(rows[head * hd : (head + 1) * hd], cos, sin)
            at = base + head * hd
            out[at : at + hd // 2, :] = (first * factor).astype(BF16)
            out[at + hd // 2 : at + hd, :] = (second * factor).astype(BF16)

    q_width = q_weight.shape[1]
    turned(dot(q_weight[...], normed[...], 0, 0), 0, hd**-0.5)
    kv = k_own.shape[0]
    turned(dot(k_own[...], own, 1, 0) + dot(k_oth[...], oth, 1, 0), q_width, 1.0)
    rows = dot(v_own[...], own, 1, 0) + dot(v_oth[...], oth, 1, 0)
    out[q_width + kv : q_width + 2 * kv, :] = rows.astype(BF16)


def project(info, x, gain, weights, tables, cost=None):
    width, rows = x.shape
    q, k, v = weights
    total = q.shape[1] + 2 * k[0].shape[0]
    operands = (x, gain, q, *k, *v, *tables)
    return call(
        project_kernel,
        "project",
        (1,),
        [whole(item.shape) for item in operands],
        [whole((width, rows)), whole((total, rows))],
        [shaped((width, rows), BF16), shaped((total, rows), BF16)],
        cost=cost,
    )(info, *operands)


def scores_of(keys, queries, masked):
    scores = dot(keys, queries, 1, 0)
    if not masked:
        return scores
    key_row = lax.broadcasted_iota(jnp.int32, scores.shape, 0)
    query_row = lax.broadcasted_iota(jnp.int32, scores.shape, 1)
    return jnp.where(key_row <= query_row, scores, -1e30)


def attend_kernel(
    info, q, k_own, v_own, k_past, v_past, out, lse, keys_own, keys_past, peak, total, mixed
):
    rows = q.shape[1]
    block = min(256, rows)
    hd = HEAD_DIM
    groups = [(group, slice(group * hd, (group + 1) * hd)) for group in range(GROUP)]
    keys_own[...] = k_own[...].T

    @pl.loop(0, info[1])
    def _(device):
        keys_past[device] = k_past[device].T

    for start in range(0, rows, block):
        for group, head in groups:
            scores = scores_of(keys_own[start : start + block, :], q[head, start:], True)
            fresh = jnp.max(scores, 0, keepdims=True)
            if start > 0:
                fresh = jnp.maximum(fresh, peak[group : group + 1, start:])
            peak[group : group + 1, start:] = fresh

    @pl.loop(0, info[1])
    def _(device):
        for group, head in groups:
            scores = scores_of(keys_past[device], q[head, :], False)
            peak[group : group + 1, :] = jnp.maximum(
                peak[group : group + 1, :], jnp.max(scores, 0, keepdims=True)
            )

    def add(group, head, keys, values, start, masked, first):
        scores = scores_of(keys, q[head, start:], masked)
        exponent = jnp.exp(scores - peak[group : group + 1, start:])
        sums = jnp.sum(exponent, 0, keepdims=True)
        product = dot(values, exponent.astype(BF16), 1, 0)
        if first:
            total[group : group + 1, :] = sums
            mixed[head, :] = product
        else:
            total[group : group + 1, start:] += sums
            mixed[head, start:] += product

    for start in range(0, rows, block):
        part = slice(start, start + block)
        for group, head in groups:
            add(group, head, keys_own[part, :], v_own[:, part], start, True, start == 0)

    @pl.loop(0, info[1])
    def _(device):
        for group, head in groups:
            add(group, head, keys_past[device], v_past[device], 0, False, False)

    for group, head in groups:
        sums = total[group : group + 1, :]
        out[head, :] = (mixed[head, :] / sums).astype(BF16)
        lse[0, group : group + 1, :] = peak[group : group + 1, :] + jnp.log(sums)


def attention_specs(rows, past, base):
    hd = HEAD_DIM
    return [
        pl.BlockSpec((GROUP * hd, rows), lambda h, info: (base + h, 0)),
        pl.BlockSpec((hd, rows), lambda h, info: (QUERY_HEADS + base + h, 0)),
        pl.BlockSpec((hd, rows), lambda h, info: (QUERY_HEADS + KEY_HEADS + base + h, 0)),
        pl.BlockSpec((past, hd, rows), lambda h, info: (0, base + h, 0)),
        pl.BlockSpec((past, hd, rows), lambda h, info: (0, KEY_HEADS + base + h, 0)),
    ]


def attend(info, qkv, past, base, heads):
    rows = qkv.shape[1]
    count = past.shape[0]
    group = GROUP * HEAD_DIM
    return call(
        attend_kernel,
        "attend",
        (heads,),
        attention_specs(rows, count, base),
        [
            pl.BlockSpec((group, rows), lambda h, info: (h, 0)),
            pl.BlockSpec((1, 8, rows), lambda h, info: (h, 0, 0)),
        ],
        [shaped((heads * group, rows), BF16), shaped((heads, 8, rows), F32)],
        [
            pltpu.VMEM((rows, HEAD_DIM), BF16),
            pltpu.VMEM((count, rows, HEAD_DIM), BF16),
            pltpu.VMEM((8, rows), F32),
            pltpu.VMEM((8, rows), F32),
            pltpu.VMEM((GROUP * HEAD_DIM, rows), F32),
        ],
    )(info, qkv, qkv, qkv, past, past)


def mix_kernel(info, x, mixed, weight, gain, middle, normed):
    middle[...] = x[...].astype(F32) + dot(weight[...], mixed[...], 0, 0)
    values = middle[...]
    normed[...] = (values * scale_of(values) * gain[...]).astype(BF16)


def mix(info, x, mixed, weight, gain):
    width, rows = x.shape
    operands = (x, mixed, weight, gain)
    return call(
        mix_kernel,
        "mix",
        (1,),
        [whole(item.shape) for item in operands],
        [whole((width, rows)), whole((width, rows))],
        [shaped((width, rows), F32), shaped((width, rows), BF16)],
    )(info, *operands)


def activate(token_rows, gate_weight, up_weight, hidden, silu, slope):
    gate = dot(token_rows[...], gate_weight[...], 1, 0)
    up = dot(token_rows[...], up_weight[...], 1, 0)
    sigmoid = 0.5 * jnp.tanh(0.5 * gate) + 0.5
    active = gate * sigmoid
    hidden[...] = (active * up).astype(BF16)
    silu[...] = active.astype(BF16)
    slope[...] = (up * (sigmoid + active * (1.0 - sigmoid))).astype(BF16)


def expand_kernel(info, normed, gate_weight, up_weight, hidden, silu, slope, token_rows):
    @pl.when(pl.program_id(0) == 0)
    def _():
        token_rows[...] = normed[...].T

    activate(token_rows, gate_weight, up_weight, hidden, silu, slope)


def expand(info, normed, gate, up):
    width, rows = normed.shape
    ff = gate.shape[1]
    tile = ff // 5
    weight = pl.BlockSpec((width, tile), lambda t, info: (0, t))
    result = pl.BlockSpec((rows, tile), lambda t, info: (0, t))
    return call(
        expand_kernel,
        "expand",
        (ff // tile,),
        [whole((width, rows)), weight, weight],
        [result] * 3,
        [shaped((rows, ff), BF16)] * 3,
        [pltpu.VMEM((rows, width), BF16)],
    )(info, normed, gate, up)


def expand_first_kernel(info, normed, *refs):
    gate_parts, up_parts = refs[:5], refs[5:10]
    hidden, silu, slope, gate_weight, up_weight, token_rows = refs[10:]
    step = pl.program_id(0)
    steps = pl.num_programs(0)

    @pl.when(step == 0)
    def _():
        token_rows[...] = normed[...].T

    for (own, *pieces), target in ((gate_parts, gate_weight), (up_parts, up_weight)):
        half, quarter = own.shape[0], pieces[0].shape[0]
        target[pl.ds(pl.multiple_of(info[0] * half, half), half), :] = own[...]
        other = (1 - info[0]) * half
        near = pl.ds(pl.multiple_of(other + info[3] * quarter, quarter), quarter)
        far = pl.ds(pl.multiple_of(other + (1 - info[3]) * quarter, quarter), quarter)

        @pl.when(step < steps // 2)
        def _():
            target[near, :] = pieces[0][...]
            target[far, :] = pieces[1][...]

        @pl.when(step >= steps // 2)
        def _():
            target[near, :] = pieces[2][...]
            target[far, :] = pieces[3][...]

    activate(token_rows, gate_weight, up_weight, hidden, silu, slope)


def expand_first(info, normed, gate, up):
    width, rows = normed.shape
    half, ff = gate[0].shape
    steps = 4
    tile = ff // steps
    quarter = half // 2

    def column(t, info):
        own = info[2] * (steps // 2) + t
        return jnp.where(t < steps // 2, own, (1 - info[2]) * (steps // 2) + t - steps // 2)

    early = pl.BlockSpec((quarter, tile), lambda t, info: (0, jnp.minimum(t, steps // 2 - 1)))
    late = pl.BlockSpec((quarter, tile), lambda t, info: (0, jnp.maximum(t - steps // 2, 0)))
    parts = [pl.BlockSpec((half, tile), lambda t, info: (0, column(t, info)))]
    parts += [early, early, late, late]
    result = pl.BlockSpec((rows, tile), lambda t, info: (0, column(t, info)))
    weight = pl.BlockSpec((width, tile), lambda t, info: (0, column(t, info)))
    return call(
        expand_first_kernel,
        "expand_first",
        (steps,),
        [whole((width, rows))] + parts * 2,
        [result] * 3 + [weight] * 2,
        [shaped((rows, ff), BF16)] * 3 + [shaped((width, ff), BF16)] * 2,
        [pltpu.VMEM((rows, width), BF16)],
    )(info, normed, *gate, *up)


def shrink_kernel(info, middle, hidden, weight, out):
    out[...] = (middle[...] + dot(weight[...], hidden[...], 1, 1)).astype(out.dtype)


def shrink(info, middle, hidden, down, dtype, cost=None):
    width, rows = middle.shape
    ff = hidden.shape[1]
    tile = width // 2
    return call(
        shrink_kernel,
        "shrink",
        (width // tile,),
        [
            pl.BlockSpec((tile, rows), lambda t, info: (t, 0)),
            whole((rows, ff)),
            pl.BlockSpec((tile, ff), lambda t, info: (t, 0)),
        ],
        [pl.BlockSpec((tile, rows), lambda t, info: (t, 0))],
        [shaped((width, rows), dtype)],
        cost=cost,
    )(info, middle, hidden, down)[0]


def shrink_first_kernel(info, middle, hidden, own, near_0, far_0, near_1, far_1, out, weight):
    half, quarter = own.shape[1], near_0.shape[0]
    weight[:, pl.ds(pl.multiple_of(info[0] * half, half), half)] = own[...]
    other = pl.ds(pl.multiple_of((1 - info[0]) * half, half), half)
    at_near = pl.ds(pl.multiple_of(info[2] * quarter, quarter), quarter)
    at_far = pl.ds(pl.multiple_of((1 - info[2]) * quarter, quarter), quarter)
    for step, near, far in ((0, near_0, far_0), (1, near_1, far_1)):

        @pl.when(pl.program_id(0) == step)
        def _():
            weight[at_near, other] = near[...]
            weight[at_far, other] = far[...]

    out[...] = middle[...] + dot(weight[...], hidden[...], 1, 1)


def shrink_first(info, middle, hidden, parts):
    width, rows = middle.shape
    ff = hidden.shape[1]
    tile = width // 2
    own, first, second, third, fourth = parts

    def row(t, info):
        return jnp.where(t == 0, info[3], 1 - info[3])

    return call(
        shrink_first_kernel,
        "shrink_first",
        (2,),
        [
            pl.BlockSpec((tile, rows), lambda t, info: (row(t, info), 0)),
            whole((rows, ff)),
            pl.BlockSpec((tile, ff // 2), lambda t, info: (row(t, info), 0)),
        ]
        + [whole(first.shape)] * 4,
        [
            pl.BlockSpec((tile, rows), lambda t, info: (row(t, info), 0)),
            pl.BlockSpec((tile, ff), lambda t, info: (row(t, info), 0)),
        ],
        [shaped((width, rows), F32), shaped((width, ff), BF16)],
    )(info, middle, hidden, own, first, third, second, fourth)


def ffn_back_kernel(
    info,
    grad,
    middle,
    gain,
    silu,
    slope,
    down,
    gate,
    up,
    out_weight,
    gate_grad,
    up_grad,
    branch,
    grad_middle,
    attn_grad,
    mixed_grad,
    gain_grad,
    branch_rows,
    total,
):
    step = pl.program_id(0)
    steps = pl.num_programs(0)

    @pl.when(step == 0)
    def _():
        branch[...] = grad[...].astype(BF16)
        branch_rows[...] = branch[...].T
        total[...] = jnp.zeros_like(total)

    incoming = dot(branch_rows[...], down[...], 1, 0)
    gate_grad[...] = (incoming * slope[...].astype(F32)).astype(BF16)
    up_grad[...] = (incoming * silu[...].astype(F32)).astype(BF16)
    total[...] += dot(gate[...], gate_grad[...], 1, 1) + dot(up[...], up_grad[...], 1, 1)

    @pl.when(step == steps - 1)
    def _():
        back, gain_sum = norm_back(middle[...], gain[...], total[...])
        gain_grad[...] = gain_sum
        result = grad[...].astype(F32) + back
        grad_middle[...] = result
        attn_grad[...] = result.astype(BF16)
        mixed_grad[...] = dot(out_weight[...], attn_grad[...], 1, 0).astype(BF16)


def ffn_back(info, grad, middle, gain, silu, slope, down, gate, up, out_weight, cost=None):
    width, rows = middle.shape
    ff = silu.shape[1]
    tile = ff // 5
    heads = out_weight.shape[0]
    token = pl.BlockSpec((rows, tile), lambda t, info: (0, t))
    weight = pl.BlockSpec((width, tile), lambda t, info: (0, t))
    return call(
        ffn_back_kernel,
        "ffn_back",
        (ff // tile,),
        [
            whole((width, rows)),
            whole((width, rows)),
            whole((width, 1)),
            token,
            token,
            weight,
            weight,
            weight,
            whole((heads, width)),
        ],
        [
            token,
            token,
            whole((width, rows)),
            whole((width, rows)),
            whole((width, rows)),
            whole((heads, rows)),
            whole((width, 1)),
        ],
        [
            shaped((rows, ff), BF16),
            shaped((rows, ff), BF16),
            shaped((width, rows), BF16),
            shaped((width, rows), F32),
            shaped((width, rows), BF16),
            shaped((heads, rows), BF16),
            shaped((width, 1), F32),
        ],
        [pltpu.VMEM((rows, width), BF16), pltpu.VMEM((width, rows), F32)],
        cost=cost,
    )(info, grad, middle, gain, silu, slope, down, gate, up, out_weight)


def attend_back_kernel(
    info,
    q,
    k_own,
    v_own,
    k_past,
    v_past,
    mixed_grad,
    mixed,
    lse,
    cosine,
    sine,
    q_grad,
    own_grad,
    past_grad,
    keys_own,
    values_own,
    keys_past,
    values_past,
    inner,
    q_sum,
):
    rows = q.shape[1]
    block = min(256, rows)
    hd = HEAD_DIM
    groups = [(group, slice(group * hd, (group + 1) * hd)) for group in range(GROUP)]
    keys_own[...] = k_own[...].T
    values_own[...] = v_own[...].T

    @pl.loop(0, info[1])
    def _(device):
        keys_past[device] = k_past[device].T
        values_past[device] = v_past[device].T

    @pl.loop(info[1], past_grad.shape[0])
    def _(device):
        past_grad[device] = jnp.zeros_like(past_grad[device])

    for group, head in groups:
        product = mixed_grad[head, :].astype(F32) * mixed[head, :].astype(F32)
        inner[group : group + 1, :] = jnp.sum(product, 0, keepdims=True)

    def step(keys, key_rows, value_rows, start, masked, first):
        key_sum = value_sum = None
        for group, head in groups:
            query, incoming = q[head, start:], mixed_grad[head, start:]
            one = slice(group, group + 1)
            probs = jnp.exp(scores_of(key_rows, query, masked) - lse[0, one, start:])
            slopes = dot(value_rows, incoming, 1, 0)
            low = (probs * (slopes - inner[one, start:])).astype(BF16)
            value_part = dot(incoming, probs.astype(BF16), 1, 1)
            key_part = dot(query, low, 1, 1)
            key_sum = key_part if key_sum is None else key_sum + key_part
            value_sum = value_part if value_sum is None else value_sum + value_part
            query_part = dot(keys, low, 1, 0)
            if first:
                q_sum[head, :] = query_part
            else:
                q_sum[head, start:] += query_part
        return key_sum, value_sum

    for start in range(0, rows, block):
        part = slice(start, start + block)
        key_sum, value_sum = step(
            k_own[:, part], keys_own[part, :], values_own[part, :], start, True, start == 0
        )
        own_grad[0, :hd, part] = key_sum
        own_grad[0, hd:, part] = value_sum

    @pl.loop(0, info[1])
    def _(device):
        key_sum, value_sum = step(
            k_past[device], keys_past[device], values_past[device], 0, False, False
        )
        past_grad[device, 0, :hd, :] = key_sum.astype(past_grad.dtype)
        past_grad[device, 0, hd:, :] = value_sum.astype(past_grad.dtype)

    cos, sin = cosine[...], -sine[...]
    for group, head in groups:
        first, second = rotate(q_sum[head, :], cos, sin)
        at = group * hd
        q_grad[at : at + hd // 2, :] = (first * hd**-0.5).astype(BF16)
        q_grad[at + hd // 2 : at + hd, :] = (second * hd**-0.5).astype(BF16)


def attend_back(info, qkv, past, mixed_grad, mixed, lse, tables, base, heads, cost=None):
    rows = qkv.shape[1]
    count = past.shape[0]
    hd = HEAD_DIM
    group = pl.BlockSpec((GROUP * hd, rows), lambda h, info: (base + h, 0))
    return call(
        attend_back_kernel,
        "attend_back",
        (heads,),
        attention_specs(rows, count, base)
        + [
            group,
            group,
            pl.BlockSpec((1, 8, rows), lambda h, info: (base + h, 0, 0)),
            whole(tables[0].shape),
            whole(tables[1].shape),
        ],
        [
            pl.BlockSpec((GROUP * hd, rows), lambda h, info: (h, 0)),
            pl.BlockSpec((1, 2 * hd, rows), lambda h, info: (h, 0, 0)),
            pl.BlockSpec((count, 1, 2 * hd, rows), lambda h, info: (0, h, 0, 0)),
        ],
        [
            shaped((heads * GROUP * hd, rows), BF16),
            shaped((heads, 2 * hd, rows), F32),
            shaped((count, heads, 2 * hd, rows), BF16 if count == 1 else F32),
        ],
        [
            pltpu.VMEM((rows, hd), BF16),
            pltpu.VMEM((rows, hd), BF16),
            pltpu.VMEM((count, rows, hd), BF16),
            pltpu.VMEM((count, rows, hd), BF16),
            pltpu.VMEM((8, rows), F32),
            pltpu.VMEM((GROUP * hd, rows), F32),
        ],
        cost=cost,
    )(info, qkv, qkv, qkv, past, past, mixed_grad, mixed, lse, *tables)


def project_back_kernel(parts, info, x, gain, grad_middle, *refs):
    q_grads, own_grads, arrived = refs[:parts], refs[parts : 2 * parts], refs[2 * parts : 3 * parts]
    (
        q_weight,
        k_own,
        k_oth,
        v_own,
        v_oth,
        cosine,
        sine,
        q_grad,
        kv_grad,
        out,
        branch,
        gain_grad,
        total,
    ) = refs[3 * parts :]
    half = x.shape[0] // 2
    hd = HEAD_DIM
    kv = KEY_HEADS * hd
    cos, sin = cosine[...], -sine[...]
    head = 0
    for piece, own, far in zip(q_grads, own_grads, arrived):
        q_grad[head * GROUP * hd : head * GROUP * hd + piece.shape[0], :] = piece[...]
        for item in range(own.shape[0]):
            both = own[item] + far[item].astype(F32)
            first, second = rotate(both[:hd], cos, sin)
            at = head * hd
            kv_grad[at : at + hd // 2, :] = first.astype(BF16)
            kv_grad[at + hd // 2 : at + hd, :] = second.astype(BF16)
            kv_grad[kv + at : kv + at + hd, :] = both[hd:].astype(BF16)
            head += 1
    total[...] = dot(q_weight[...], q_grad[...], 1, 0)
    for mine, k, v in ((info[0], k_own, v_own), (1 - info[0], k_oth, v_oth)):
        total[pl.ds(pl.multiple_of(mine * half, half), half), :] += dot(
            k[...], kv_grad[:kv, :], 0, 0
        ) + dot(v[...], kv_grad[kv:, :], 0, 0)
    back, gain_sum = norm_back(x[...].astype(F32), gain[...], total[...])
    gain_grad[...] = gain_sum
    result = grad_middle[...] + back
    out[...] = result
    branch[...] = result.astype(BF16)


def project_back(info, x, gain, grad_middle, q_grads, own_grads, arrived, weights, tables, cost=None):
    width, rows = x.shape
    q, k, v = weights
    heads = q.shape[1]
    kv = 2 * KEY_HEADS * HEAD_DIM
    operands = (x, gain, grad_middle, *q_grads, *own_grads, *arrived, q, *k, *v, *tables)
    shapes = [
        shaped((heads, rows), BF16),
        shaped((kv, rows), BF16),
        shaped((width, rows), F32),
        shaped((width, rows), BF16),
        shaped((width, 1), F32),
    ]
    return call(
        functools.partial(project_back_kernel, len(q_grads)),
        "project_back",
        (1,),
        [whole(item.shape) for item in operands],
        [whole(item.shape) for item in shapes],
        shapes,
        [pltpu.VMEM((width, rows), F32)],
        cost=cost,
    )(info, *operands)


def order_rows(info, target, sources):
    rows = sources[0].shape[1]
    size = target.shape[0] // 4
    at = 0
    for core in (1 - info[2], info[2]):
        for half in (1 - info[0], info[0]):
            start = pl.multiple_of((2 * half + core) * size, size)
            for index, source in enumerate(sources):
                target[at : at + size, index * rows : (index + 1) * rows] = source[
                    pl.ds(start, size), :
                ]
            at += size


def order_halves(info, target, sources):
    rows = sources[0].shape[1]
    size = target.shape[0] // 2
    for at, core in ((0, 1 - info[2]), (size, info[2])):
        start = pl.multiple_of(core * size, size)
        for index, source in enumerate(sources):
            target[at : at + size, index * rows : (index + 1) * rows] = source[pl.ds(start, size), :]


def outer_kernel(split_columns, info, left_a, right_a, left_b, right_b, sent, kept, left, right):
    rows = left_a.shape[1]

    @pl.when(pl.program_id(0) == 0)
    def _():
        order = order_halves if split_columns else order_rows
        order(info, left, (left_a, left_b))

    right[:rows, :] = right_a[...]
    right[rows:, :] = right_b[...]
    count, size = sent.shape[0], sent.shape[1]
    for at, out in ((0, sent), (count * size, kept)):
        product = dot(left[at : at + count * size, :], right[...], 1, 0).astype(BF16)
        for index in range(count):
            out[index] = product[index * size : (index + 1) * size]


def outer(info, parts, split_columns, cost=None):
    left_a, right_a, left_b, right_b = parts
    width, rows = left_a.shape
    columns = right_a.shape[1]
    if split_columns:
        tile = columns // 4

        def column(t, info):
            return jnp.where(t < 2, (1 - info[0]) * 2 + t, info[0] * 2 + t - 2)

        right = pl.BlockSpec((rows, tile), lambda t, info: (0, column(t, info)))
        result = pl.BlockSpec((1, width // 2, tile), lambda t, info: (t // 2, 0, t % 2))
        shape = shaped((2, width // 2, columns // 2), BF16)
    else:
        tile = columns // 5
        right = pl.BlockSpec((rows, tile), lambda t, info: (0, t))
        result = pl.BlockSpec((2, width // 4, tile), lambda t, info: (0, 0, t))
        shape = shaped((2, width // 4, columns), BF16)
    return call(
        functools.partial(outer_kernel, split_columns),
        "outer",
        (columns // tile,),
        [whole((width, rows)), right, whole((width, rows)), right],
        [result, result],
        [shape, shape],
        [pltpu.VMEM((width, 2 * rows), BF16), pltpu.VMEM((2 * rows, tile), BF16)],
        cost=cost,
    )(info, *parts)


def pack_kernel(extra, info, left_a, *refs):
    sent, kept, left, right = refs[-4:]
    refs = refs[:-4]
    gains, refs = refs[len(refs) - extra :], refs[: len(refs) - extra]
    left_b, rights_a, rights_b = refs[0], refs[1::2], refs[2::2]
    rows = left_a.shape[1]
    order_rows(info, left, (left_a, left_b))
    at = 0
    for right_a, right_b in zip(rights_a, rights_b):
        right[at : at + right_a.shape[0], :rows] = right_a[...]
        right[at : at + right_a.shape[0], rows:] = right_b[...]
        at += right_a.shape[0]
    count, size = sent.shape[0], sent.shape[1]
    for base, core, out in ((0, 1 - info[2], sent), (count * size, info[2], kept)):
        for start, span in spans(right.shape[0], 512):
            product = dot(left[base : base + count * size, :], right[start : start + span, :], 1, 1)
            for index in range(count):
                out[index, :, start : start + span] = product[
                    index * size : (index + 1) * size
                ].astype(BF16)
        for index, half in enumerate((1 - info[0], info[0])):
            part = pl.ds(pl.multiple_of((2 * half + core) * size, size), size)
            for number in range(extra // 2):
                term = gains[2 * number][part, :] + gains[2 * number + 1][part, :]
                out[index, :, at + number : at + number + 1] = term.astype(BF16)
            if extra:
                out[index, :, at + extra // 2 :] = jnp.zeros((size, extra // 2), BF16)


def pack(info, left_a, left_b, rights, gains=(), cost=None):
    width, rows = left_a.shape
    columns = sum(item.shape[0] for item in rights[::2])
    operands = (left_a, left_b, *rights, *gains)
    shape = shaped((2, width // 4, columns + len(gains)), BF16)
    return call(
        functools.partial(pack_kernel, len(gains)),
        "pack",
        (1,),
        [whole(item.shape) for item in operands],
        [whole(shape.shape)] * 2,
        [shape, shape],
        [pltpu.VMEM((width, 2 * rows), BF16), pltpu.VMEM((columns, 2 * rows), BF16)],
        cost=cost,
    )(info, *operands)


def last_kernel(info, held, query, key, value, gains):
    width, narrow = query.shape[1], key.shape[0]
    values = held[...].astype(F32)
    query[...] = values[:, :width]
    key[...] = values[:, width : width + narrow].T
    value[...] = values[:, width + narrow : width + 2 * narrow].T
    gains[...] = values[:, width + 2 * narrow :]


def last(info, held, width, narrow):
    rows, columns = held.shape
    shapes = [
        shaped((rows, width), F32),
        shaped((narrow, rows), F32),
        shaped((narrow, rows), F32),
        shaped((rows, columns - width - 2 * narrow), F32),
    ]
    return call(last_kernel, "last", (1,), [None], [None] * 4, shapes)(info, held)


def column_split(columns):
    return columns // 2 // 128 * 128


def both_cores_kernel(info, *refs):
    pairs = list(zip(refs[:-4:2], refs[1:-4:2]))
    over_y, keep_y, over_x, keep_x = refs[-4:]
    half = over_x.shape[1]
    for index, out in ((0, over_y), (1, keep_y)):
        at_y = at_x = 0
        for kept, arrived in pairs:
            total = kept[index].astype(F32) + arrived[index].astype(F32)
            split = column_split(total.shape[1])
            out[:, at_y : at_y + split] = total[:, :split].astype(BF16)
            low, top = total[:half, split:], total[half:, split:]
            end = at_x + total.shape[1] - split
            keep_x[index, :, at_x:end] = jnp.where(info[3] == 0, low, top).astype(BF16)
            over_x[index, :, at_x:end] = jnp.where(info[3] == 0, top, low).astype(BF16)
            at_y, at_x = at_y + split, end
        if at_x < keep_x.shape[2]:
            rest = jnp.zeros((half, keep_x.shape[2] - at_x), BF16)
            keep_x[index, :, at_x:] = rest
            over_x[index, :, at_x:] = rest


def both_cores(info, pairs):
    rows = pairs[0][0].shape[1]
    columns = [kept.shape[2] for kept, _ in pairs]
    split = sum(column_split(item) for item in columns)
    rest = sum(columns) - split
    if len(pairs) > 1:
        rest = -(-(split + rest) // 512) * 512 - split
    first = shaped((rows, split), BF16)
    second = shaped((2, rows // 2, rest), BF16)
    shapes = [first, first, second, second]
    operands = [item for pair in pairs for item in pair]
    return call(both_cores_kernel, "both_cores", (1,), [None] * len(operands), [None] * 4, shapes)(
        info, *operands
    )


def split_pair_kernel(info, held, first, second):
    a, b = column_split(first.shape[1]), column_split(second.shape[1])
    values = held[...]
    first[:, :a] = values[:, :a].astype(F32)
    second[:, :b] = values[:, a : a + b].astype(F32)
    rest = a + b + first.shape[1] - a
    first[:, a:] = values[:, a + b : rest].astype(F32)
    second[:, b:] = values[:, rest : rest + second.shape[1] - b].astype(F32)


def split_pair(info, held, first, second):
    shapes = [shaped((held.shape[0], first), F32), shaped((held.shape[0], second), F32)]
    return call(split_pair_kernel, "split_pair", (1,), [None], [None] * 2, shapes)(info, held)


def cross_kernel(info, keep_y, from_y, keep_x, from_x, over_x, over_y, kept):
    split, half = over_x.shape[1], over_x.shape[0]
    total = keep_y[...].astype(F32) + from_y[...].astype(F32)
    low, top = total[:half], total[half:]
    over_x[...] = jnp.where(info[3] == 0, top, low).astype(BF16)
    kept[:, :split] = jnp.where(info[3] == 0, low, top).astype(BF16)
    over_y[...] = (keep_x[0].astype(F32) + from_x[0].astype(F32)).astype(BF16)
    kept[:, split:] = (keep_x[1].astype(F32) + from_x[1].astype(F32)).astype(BF16)


def cross(info, keep_y, from_y, keep_x, from_x):
    rows, split = keep_y.shape
    rest = keep_x.shape[2]
    shapes = [
        shaped((rows // 2, split), BF16),
        shaped((rows // 2, rest), BF16),
        shaped((rows // 2, split + rest), BF16),
    ]
    return call(cross_kernel, "cross", (1,), [None] * 4, [None] * 3, shapes)(
        info, keep_y, from_y, keep_x, from_x
    )


def chosen(values, number):
    result = values[0]
    for index in range(1, len(values)):
        result = jnp.where(number == index, values[index], result)
    return result


def cut_up(values, dim, count):
    size = values.shape[dim] // count
    if dim == 0:
        return [values[index * size : (index + 1) * size] for index in range(count)]
    return [values[:, index * size : (index + 1) * size] for index in range(count)]


def divide_kernel(dim, info, kept, from_x, from_y, *outs):
    split = from_x.shape[1]
    total = kept[...].astype(F32)
    total = jnp.concatenate(
        [total[:, :split] + from_x[...].astype(F32), total[:, split:] + from_y[...].astype(F32)], 1
    )
    parts = cut_up(total, dim, 4)
    for mask, out in enumerate(outs):
        order = [parts[index ^ mask] for index in range(4)]
        out[...] = chosen(order, info[4]).astype(BF16)


def divide(info, kept, from_x, from_y, dim):
    rows, columns = kept.shape
    shape = (rows // 4, columns) if dim == 0 else (rows, columns // 4)
    return call(
        functools.partial(divide_kernel, dim),
        "divide",
        (1,),
        [None] * 3,
        [None] * 4,
        [shaped(shape, BF16)] * 4,
    )(info, kept, from_x, from_y)


def sum_kernel(info, *refs):
    total = refs[0][...].astype(F32)
    for item in refs[1:-1]:
        total = total + item[...].astype(F32)
    refs[-1][...] = total.astype(BF16)


def sum_all(info, *parts):
    shape = shaped(parts[0].shape, BF16)
    return call(sum_kernel, "sum", (1,), [None] * len(parts), [None], [shape])(info, *parts)[0]


def unite_kernel(dim, place, info, *refs):
    values, out = [item[...].astype(F32) for item in refs[:-1]], refs[-1]
    number = info[place]
    ordered = [
        chosen([values[index ^ other] for other in range(len(values))], number)
        for index in range(len(values))
    ]
    out[...] = jnp.concatenate(ordered, dim).astype(out.dtype)


def unite(info, parts, dim, place, dtype):
    shape = list(parts[0].shape)
    shape[dim] *= len(parts)
    return call(
        functools.partial(unite_kernel, dim, place),
        "unite",
        (1,),
        [None] * len(parts),
        [None],
        [shaped(tuple(shape), dtype)],
    )(info, *parts)[0]


def swap(values, axis, bit):
    size = lax.axis_size(axis)
    return lax.ppermute(values, axis, [(i, i ^ bit) for i in range(size)])


def bits_of(axis):
    size = lax.axis_size(axis)
    assert size & (size - 1) == 0
    return [1 << i for i in range(size.bit_length() - 1)]


def high(axis, bit):
    return (lax.axis_index(axis) // bit) % 2


def halves(values, dim, which):
    half = values.shape[dim] // 2
    return lax.dynamic_slice_in_dim(values, which * half, half, dim)


def joined(mine, other, dim, which):
    return jnp.where(
        which == 0,
        jnp.concatenate([mine, other], dim),
        jnp.concatenate([other, mine], dim),
    )


def tied(values, others):
    return lax.optimization_barrier((values, others))[0]


def from_pieces(own, pieces, mine, core, low_batch):
    near = joined(pieces[0], pieces[2], 0, core)
    far = joined(pieces[1], pieces[3], 0, core)
    return joined(own, joined(near, far, 0, low_batch), 0, mine)


def split_dim(shape, parts):
    if shape[0] % (8 * parts) == 0:
        return 0
    if shape[1] % (128 * parts) == 0:
        return 1
    return 0 if shape[0] % parts == 0 else 1


class Order:
    def __init__(self, token):
        self.token = token

    def __call__(self, *values):
        self.token, *values = lax.optimization_barrier((self.token, *values))
        return values[0] if len(values) == 1 else values


def quarters(values, dim, number):
    quarter = values.shape[dim] // 4
    return lax.dynamic_slice_in_dim(values, number * quarter, quarter, dim)


class Chain:
    def __init__(self, order, pair, beside=()):
        self.order, self.pair, self.beside = order, pair, beside
        self.steps = [self.core, self.first, self.second]
        self.shares = [("seq", (1,), 0), ("batch", (1,), 0)]
        exchanges = [("seq", (bit,)) for bit in bits_of("seq")[1:]]
        bits = bits_of("batch")[1:]
        self.plain = not exchanges and len(bits) == 2
        while bits:
            exchanges.append(("batch", bits[:2]))
            bits = bits[2:]
        self.steps += [functools.partial(self.add, *item) for item in exchanges]
        self.steps += [self.share] * (2 + len(exchanges))
        self.waiting = None

    result_type = F32

    def send(self):
        self.waiting = self.steps.pop(0)()

    def core(self):
        away, kept = self.pair

        def finish(arrived):
            self.parts = both_cores(self.order.token, [(kept, arrived), *self.beside])

        return [swap(self.order(away), "seq", 1)], finish

    def first(self):
        over_y, keep_y, over_x, keep_x = self.parts
        over_y, over_x = self.order(over_y, over_x)

        def finish(from_y, from_x):
            self.parts = cross(self.order.token, keep_y, from_y, keep_x, from_x)

        return [swap(over_y, "fsdp", 1), swap(over_x, "batch", 1)], finish

    def second(self):
        over_x, over_y, kept = self.parts
        over_x, over_y = self.order(over_x, over_y)

        def finish(from_x, from_y):
            if self.plain:
                self.dim = split_dim(kept.shape, 4)
                self.held = divide(self.order.token, kept, from_x, from_y, self.dim)
                return
            arrived = jnp.concatenate([from_x, from_y], 1)
            self.held = (kept.astype(F32) + arrived.astype(F32)).astype(BF16)

        return [swap(over_x, "batch", 1), swap(over_y, "fsdp", 1)], finish

    def add(self, axis, bits):
        held = self.held
        if self.plain:
            own, *parts = held
            parts = self.order(*parts)
            arrived = [
                swap(part, axis, bits[0] * (mask & 1) + bits[1] * (mask >> 1))
                for mask, part in zip((1, 2, 3), parts)
            ]
            self.shares.append((axis, bits, self.dim))

            def finish(*values):
                self.held = sum_all(self.order.token, own, *values)

            return arrived, finish
        dim = split_dim(held.shape, 2 * len(bits))
        take = halves if len(bits) == 1 else quarters
        number = sum(high(axis, bit) << index for index, bit in enumerate(bits))
        masks = range(1, 1 << len(bits))
        parts = self.order(*[take(held, dim, number ^ mask) for mask in masks])
        parts = parts if len(bits) > 1 else [parts]
        arrived = [
            swap(part, axis, sum(bit for index, bit in enumerate(bits) if mask >> index & 1))
            for mask, part in zip(masks, parts)
        ]
        self.shares.append((axis, bits, dim))

        def finish(*values):
            total = take(held, dim, number).astype(F32)
            for item in values:
                total = total + item.astype(F32)
            self.held = total.astype(BF16)

        return arrived, finish

    def share(self):
        axis, bits, dim = self.shares.pop()
        held = self.order(self.held)
        masks = range(1, 1 << len(bits))
        arrived = [
            swap(held, axis, sum(bit for index, bit in enumerate(bits) if mask >> index & 1))
            for mask in masks
        ]

        def finish(*values):
            low = high(axis, bits[0])
            if self.plain:
                place = 4 if len(bits) == 2 else 3 if axis == "batch" else 2
                dtype = BF16 if self.shares else self.result_type
                self.held = unite(self.order.token, (held, *values), dim, place, dtype)
                return
            if len(bits) == 1:
                self.held = joined(held, values[0], dim, low)
                return
            near, far = joined(held, values[0], dim, low), joined(values[1], values[2], dim, low)
            self.held = joined(near, far, dim, high(axis, bits[1]))

        return arrived, finish

    def result(self):
        while self.waiting or self.steps:
            if self.waiting:
                take(self)
            else:
                self.send()
        return self.held.astype(self.result_type)


def take(*chains):
    flat = [item for chain in chains for item in chain.waiting[0]]
    values = chains[0].order(*flat)
    values = list(values) if len(flat) > 1 else [values]
    for chain in chains:
        arrived, finish = chain.waiting
        chain.waiting = None
        finish(*values[: len(arrived)])
        values = values[len(arrived) :]


def per_device(
    tokens,
    attn_gain,
    w_query,
    key_weight,
    value_weight,
    w_out,
    ffn_gain,
    w_gate,
    w_up,
    w_down,
    cotangent,
):
    assert tokens.shape[0] == 1 and lax.axis_size("fsdp") == 2
    mine, spot, core = lax.axis_index("fsdp"), lax.axis_index("seq"), high("seq", 1)
    low_batch = high("batch", 1)
    devices = lax.axis_size("seq")
    deep = lax.axis_index("batch") // 2 % 4
    info = jnp.stack([mine, spot, core, low_batch, deep]).astype(jnp.int32)
    start_in = tokens[0].T
    incoming = cotangent[0].T
    width, rows = start_in.shape

    key_weight, value_weight, w_down = key_weight.T, value_weight.T, w_down.T
    def fsdp(values):
        return swap(values, "fsdp", 1)

    def pair(values):
        return swap(values, "batch", 1)

    def cores(values):
        return swap(values, "seq", 1)

    q_piece = halves(halves(w_query, 0, low_batch), 0, core)
    kv_piece = halves(jnp.where(core == 0, key_weight, value_weight), 0, low_batch)
    q_0, kv_0 = fsdp(q_piece), fsdp(kv_piece)
    gains = jnp.stack([attn_gain, ffn_gain])
    far_gains = fsdp(tied(gains, q_0))
    gains = joined(gains, far_gains, 1, mine).astype(F32)[..., None]
    out_0 = fsdp(tied(halves(halves(w_out, 0, low_batch), 0, core), (q_0, kv_0)))
    q_1, kv_1, q_2, kv_2 = pair(q_0), pair(kv_0), cores(q_0), cores(kv_0)
    gate_0 = fsdp(tied(halves(halves(w_gate, 0, low_batch), 1, core), out_0))
    q_3, kv_3 = cores(q_1), cores(kv_1)
    q_weight = from_pieces(w_query, (q_0, q_1, q_2, q_3), mine, core, low_batch)
    held = joined(kv_0, kv_1, 0, low_batch)
    other = joined(kv_2, kv_3, 0, low_batch)
    k_oth, v_oth = jnp.where(core == 0, held, other), jnp.where(core == 0, other, held)
    qkv_weights = (q_weight, (key_weight, k_oth), (value_weight, v_oth))

    positions = (spot * rows + jnp.arange(rows, dtype=jnp.int32)).astype(F32)
    frequency = jnp.exp(
        jnp.arange(HEAD_DIM // 2, dtype=F32) * (-2.0 * math.log(10000.0) / HEAD_DIM)
    )
    angles = frequency[:, None] * positions[None, :]
    tables = (jnp.cos(angles), jnp.sin(angles))

    def gathered(qkv):
        kv = qkv[QUERY_HEADS * HEAD_DIM :]
        if devices == 2:
            return cores(kv)[None]
        return lax.all_gather(kv, "seq")

    low_normed, low_qkv = project(info, start_in, gains[0], qkv_weights, tables)
    low_past = gathered(low_qkv)
    ready = (low_qkv, gate_0)
    up_0 = fsdp(tied(halves(halves(w_up, 0, low_batch), 1, core), ready))
    down_0 = fsdp(tied(halves(halves(w_down, 0, low_batch), 0, core), ready))
    out_1, out_2 = pair(tied(out_0, (q_1, kv_1))), cores(out_0)
    gate_1, gate_2 = pair(tied(gate_0, (low_qkv, out_1))), cores(gate_0)
    out_3 = cores(out_1)
    out_weight = from_pieces(w_out, (out_0, out_1, out_2, out_3), mine, core, low_batch)
    low_mixed, low_lse = attend(info, low_qkv, tied(low_past, out_weight), 0, KEY_HEADS)
    low_mixed = tied(low_mixed, (up_0, down_0, gate_1))
    gate_3, up_1, up_2 = cores(gate_1), pair(tied(up_0, low_mixed)), cores(up_0)
    low_middle, low_normed_ffn = mix(info, start_in, low_mixed, out_weight, gains[1])
    up_3 = cores(tied(up_1, low_middle))
    down_1, down_2 = pair(tied(down_0, (up_1, low_middle))), cores(tied(down_0, low_middle))
    low_hidden, low_silu, low_slope, gate, up = expand_first(
        info,
        low_normed_ffn,
        (w_gate, gate_0, gate_1, gate_2, gate_3),
        (w_up, up_0, up_1, up_2, up_3),
    )
    down_3 = cores(tied(down_1, low_hidden))
    middle_in, down = shrink_first(
        info, low_middle, low_hidden, (w_down, down_0, down_1, down_2, down_3)
    )

    high_normed, high_qkv = project(info, middle_in, gains[0], qkv_weights, tables)
    high_past = gathered(high_qkv)
    high_mixed, high_lse = attend(info, high_qkv, high_past, 0, KEY_HEADS)
    high_middle, high_normed_ffn = mix(info, middle_in, high_mixed, out_weight, gains[1])
    high_hidden, high_silu, high_slope = expand(info, high_normed_ffn, gate, up)

    def attention_back(qkv, past, mixed_grad, mixed, lse, base, heads, cost=None):
        return attend_back(
            info, qkv, past, mixed_grad, mixed, lse, tables, base, heads, cost
        )

    def returned(past_grad):
        if devices == 2:
            return cores(past_grad[0])
        return lax.psum_scatter(past_grad, "seq", scatter_dimension=0)

    def to_input(x, grad_middle, parts, cost=None):
        return project_back(
            info, x, gains[0], grad_middle, *zip(*parts), qkv_weights, tables, cost
        )

    high_gate, high_up, high_branch, grad_middle, high_attn, mixed_grad, high_ffn_gain = ffn_back(
        info, incoming, high_middle, gains[1], high_silu, high_slope, down, gate, up, out_weight
    )
    parts = [
        attention_back(high_qkv, high_past, mixed_grad, high_mixed, high_lse, base, heads)
        for base, heads in ((0, 3), (3, 2))
    ]
    parts = [(*part[:2], returned(part[2])) for part in parts]
    high_q, high_kv, grad_between, low_branch, high_attn_gain = to_input(
        middle_in, grad_middle, parts
    )

    order = Order(tied(info, low_branch))
    down_terms = (high_branch, high_hidden, low_branch, low_hidden)
    down_g = Chain(order, outer(info, down_terms, True))
    down_g.send()
    final_out = order(shrink(info, order(high_middle), high_hidden, down, BF16))
    take(down_g)
    down_g.send()
    low_gate, low_up, _, grad_middle, low_attn, mixed_grad, low_ffn_gain = ffn_back(
        info, order(grad_between), low_middle, gains[1], low_silu, low_slope,
        down, gate, up, out_weight,
    )
    low_attn = order(low_attn)
    take(down_g)
    down_g.send()
    out_away, out_kept = pack(info, high_mixed, low_mixed, (high_attn, order(low_attn)))
    out_far = cores(order(out_away))
    gate_terms = (high_normed_ffn, high_gate, low_normed_ffn, order(low_gate))
    gate_g = Chain(order, outer(info, gate_terms, False))
    gate_g.result_type = BF16
    gate_g.send()
    take(down_g)
    down_g.send()
    gate_g.beside = ((out_kept, order(out_far)),)
    up_terms = (high_normed_ffn, high_up, low_normed_ffn, order(low_up))
    up_g = Chain(order, outer(info, up_terms, False, 14))
    up_g.send()
    take(gate_g)
    gate_g.send()
    parts = []

    def low_part(base, heads):
        mixed_now = order(mixed_grad)
        part = attention_back(low_qkv, low_past, mixed_now, low_mixed, low_lse, base, heads)
        parts.append((order(part[0]), *part[1:]))

    low_part(0, 2)
    take(up_g, gate_g, down_g)
    gate_g.send()
    up_g.send()
    down_g.send()
    low_part(2, 3)
    parts = [(*part[:2], returned(order(part[2]))) for part in parts]
    take(gate_g, up_g, down_g)
    up_g.send()
    gate_g.send()
    low_q, low_kv, grad_start, _, low_attn_gain = to_input(
        start_in, order(grad_middle), parts, 0
    )
    low_q = order(low_q)
    take(up_g, gate_g)
    gate_g.send()
    down_g.send()
    qkv_terms = (high_q, order(low_q), high_kv, low_kv)
    gain_terms = (high_attn_gain, low_attn_gain, high_ffn_gain, low_ffn_gain)
    qkv_g = Chain(order, pack(info, high_normed, low_normed, qkv_terms, gain_terms, 0))
    qkv_g.result_type = BF16
    qkv_g.send()
    take(gate_g, down_g)
    take(qkv_g)
    qkv_g.send()
    up_g.send()
    take(qkv_g, up_g)
    qkv_g.send()
    up_g.send()
    take(qkv_g, up_g)
    qkv_g.send()
    gate_g.send()
    down_g.send()
    take(qkv_g, gate_g, down_g)
    down_grad = down_g.result()
    qkv_g.send()
    up_g.send()
    gate_g.send()
    down_grad = order(down_grad)
    take(qkv_g, up_g, gate_g)
    qkv_g.send()
    up_g.send()
    gate_grad, out_grad = order(
        *split_pair(order.token, gate_g.result(), w_gate.shape[1], w_out.shape[1])
    )
    take(qkv_g, up_g)
    qkv_g.send()
    up_grad = order(up_g.result())
    held = order(qkv_g.result())
    narrow = KEY_HEADS * HEAD_DIM
    query_part, key_part, value_part, gain_grads = last(order.token, held, width, narrow)
    return (
        final_out.T[None],
        grad_start.T[None],
        gain_grads[:, 0],
        query_part,
        key_part.T,
        value_part.T,
        out_grad,
        gain_grads[:, 1],
        gate_grad,
        up_grad,
        down_grad.T,
    )


def solution(mesh):
    return jax.shard_map(
        per_device,
        mesh=mesh,
        in_specs=(
            P(("batch", "fsdp"), "seq", None),
            P("fsdp"),
            P("fsdp", None),
            P("fsdp", None),
            P("fsdp", None),
            P("fsdp", None),
            P("fsdp"),
            P("fsdp", None),
            P("fsdp", None),
            P("fsdp", None),
            P(("batch", "fsdp"), "seq", None),
        ),
        out_specs=(
            P(("batch", "fsdp"), "seq", None),
            P(("batch", "fsdp"), "seq", None),
            P("fsdp"),
            P("fsdp", None),
            P("fsdp", None),
            P("fsdp", None),
            P("fsdp", None),
            P("fsdp"),
            P("fsdp", None),
            P("fsdp", None),
            P("fsdp", None),
        ),
        check_vma=False,
    )
```

```python
import functools
import math

import jax
import jax.numpy as jnp
from jax import lax
from jax.experimental import pallas as pl
from jax.experimental.pallas import tpu as pltpu
from jax.sharding import PartitionSpec as P

QUERY_HEADS = 15
KEY_HEADS = 5
HEAD_DIM = 64
GROUP = QUERY_HEADS // KEY_HEADS
EPSILON = 1e-05
F32 = jnp.float32
BF16 = jnp.bfloat16


def dot(left, right, left_dim, right_dim):
    return lax.dot_general(
        left, right, (((left_dim,), (right_dim,)), ((), ())), preferred_element_type=F32
    )


def spans(total, size):
    return [(start, min(size, total - start)) for start in range(0, total, size)]


COSTS = {
    "project": 6.0,
    "attend": 4.0,
    "mix": 5.5,
    "expand": 10.0,
    "expand_first": 14.0,
    "shrink": 6.5,
    "shrink_first": 8.0,
    "ffn_back": 18.0,
    "attend_back": 6.5,
    "project_back": 6.0,
    "outer": 10.0,
    "pack": 4.0,
    "both_cores": 0.0,
    "cross": 0.0,
    "last": 0.0,
    "divide": 0.0,
    "split_pair": 0.0,
    "sum": 0.0,
    "unite": 0.0,
}


LIMITS = {
    "project": 12,
    "attend": 14,
    "mix": 12,
    "expand": 24,
    "expand_first": 34,
    "shrink": 22,
    "shrink_first": 34,
    "ffn_back": 40,
    "attend_back": 16,
    "project_back": 16,
    "outer": 26,
    "pack": 20,
    "both_cores": 12,
    "cross": 10,
    "last": 12,
    "divide": 10,
    "split_pair": 16,
    "sum": 6,
    "unite": 14,
}


def call(kernel, name, grid, in_specs, out_specs, out_shape, scratch=(), cost=None):
    if cost is None:
        cost = COSTS[name] * 0.45 * (grid[0] if name.startswith("attend") else 1)
    cost = int(cost * 1e9) + 1
    options = dict(
        name=name,
        out_shape=out_shape,
        compiler_params=pltpu.CompilerParams(vmem_limit_bytes=LIMITS[name] * 1024 * 1024),
        cost_estimate=pl.CostEstimate(flops=cost, bytes_accessed=1, transcendentals=0),
    )
    if name in ("project", "mix", "project_back", "pack", "both_cores", "cross", "last", "divide", "sum", "unite", "split_pair"):
        memory = pl.BlockSpec(memory_space=pltpu.VMEM)
        return pl.pallas_call(
            kernel,
            in_specs=[pl.BlockSpec(memory_space=pltpu.SMEM)] + [memory] * len(in_specs),
            out_specs=[memory] * len(out_specs),
            scratch_shapes=list(scratch),
            **options,
        )
    return pl.pallas_call(
        kernel,
        grid_spec=pltpu.PrefetchScalarGridSpec(
            num_scalar_prefetch=1,
            grid=grid,
            in_specs=in_specs,
            out_specs=out_specs,
            scratch_shapes=list(scratch),
        ),
        **options,
    )


def whole(shape):
    return pl.BlockSpec(shape, lambda *_: (0,) * len(shape))


def shaped(shape, dtype):
    return jax.ShapeDtypeStruct(shape, dtype)


def scale_of(values):
    return lax.rsqrt(jnp.mean(values * values, 0, keepdims=True) + EPSILON)


def norm_back(values, gain, incoming):
    scales = scale_of(values)
    weighted = gain * incoming
    inner = jnp.mean(values * weighted, 0, keepdims=True)
    grad = scales * weighted - values * (scales * scales * scales * inner)
    return grad, jnp.sum(incoming * values * scales, 1, keepdims=True)


def rotate(values, cosine, sine):
    half = HEAD_DIM // 2
    first, second = values[:half], values[half:]
    return first * cosine - second * sine, second * cosine + first * sine


def project_kernel(
    info, x, gain, q_weight, k_own, k_oth, v_own, v_oth, cosine, sine, normed, out
):
    width = x.shape[0]
    half = width // 2
    values = x[...].astype(F32)
    normed[...] = (values * scale_of(values) * gain[...]).astype(BF16)
    own = normed[pl.ds(pl.multiple_of(info[0] * half, half), half), :]
    oth = normed[pl.ds(pl.multiple_of((1 - info[0]) * half, half), half), :]
    cos, sin = cosine[...], sine[...]
    hd = HEAD_DIM

    def turned(rows, base, factor):
        for head in range(rows.shape[0] // hd):
            first, second = rotate(rows[head * hd : (head + 1) * hd], cos, sin)
            at = base + head * hd
            out[at : at + hd // 2, :] = (first * factor).astype(BF16)
            out[at + hd // 2 : at + hd, :] = (second * factor).astype(BF16)

    q_width = q_weight.shape[1]
    turned(dot(q_weight[...], normed[...], 0, 0), 0, hd**-0.5)
    kv = k_own.shape[0]
    turned(dot(k_own[...], own, 1, 0) + dot(k_oth[...], oth, 1, 0), q_width, 1.0)
    rows = dot(v_own[...], own, 1, 0) + dot(v_oth[...], oth, 1, 0)
    out[q_width + kv : q_width + 2 * kv, :] = rows.astype(BF16)


def project(info, x, gain, weights, tables, cost=None):
    width, rows = x.shape
    q, k, v = weights
    total = q.shape[1] + 2 * k[0].shape[0]
    operands = (x, gain, q, *k, *v, *tables)
    return call(
        project_kernel,
        "project",
        (1,),
        [whole(item.shape) for item in operands],
        [whole((width, rows)), whole((total, rows))],
        [shaped((width, rows), BF16), shaped((total, rows), BF16)],
        cost=cost,
    )(info, *operands)


def scores_of(keys, queries, masked):
    scores = dot(keys, queries, 1, 0)
    if not masked:
        return scores
    key_row = lax.broadcasted_iota(jnp.int32, scores.shape, 0)
    query_row = lax.broadcasted_iota(jnp.int32, scores.shape, 1)
    return jnp.where(key_row <= query_row, scores, -1e30)


def attend_kernel(
    info, q, k_own, v_own, k_past, v_past, out, lse, keys_own, keys_past, peak, total, mixed
):
    rows = q.shape[1]
    block = min(256, rows)
    hd = HEAD_DIM
    groups = [(group, slice(group * hd, (group + 1) * hd)) for group in range(GROUP)]
    keys_own[...] = k_own[...].T

    @pl.loop(0, info[1])
    def _(device):
        keys_past[device] = k_past[device].T

    for start in range(0, rows, block):
        for group, head in groups:
            scores = scores_of(keys_own[start : start + block, :], q[head, start:], True)
            fresh = jnp.max(scores, 0, keepdims=True)
            if start > 0:
                fresh = jnp.maximum(fresh, peak[group : group + 1, start:])
            peak[group : group + 1, start:] = fresh

    @pl.loop(0, info[1])
    def _(device):
        for group, head in groups:
            scores = scores_of(keys_past[device], q[head, :], False)
            peak[group : group + 1, :] = jnp.maximum(
                peak[group : group + 1, :], jnp.max(scores, 0, keepdims=True)
            )

    def add(group, head, keys, values, start, masked, first):
        scores = scores_of(keys, q[head, start:], masked)
        exponent = jnp.exp(scores - peak[group : group + 1, start:])
        sums = jnp.sum(exponent, 0, keepdims=True)
        product = dot(values, exponent.astype(BF16), 1, 0)
        if first:
            total[group : group + 1, :] = sums
            mixed[head, :] = product
        else:
            total[group : group + 1, start:] += sums
            mixed[head, start:] += product

    for start in range(0, rows, block):
        part = slice(start, start + block)
        for group, head in groups:
            add(group, head, keys_own[part, :], v_own[:, part], start, True, start == 0)

    @pl.loop(0, info[1])
    def _(device):
        for group, head in groups:
            add(group, head, keys_past[device], v_past[device], 0, False, False)

    for group, head in groups:
        sums = total[group : group + 1, :]
        out[head, :] = (mixed[head, :] / sums).astype(BF16)
        lse[0, group : group + 1, :] = peak[group : group + 1, :] + jnp.log(sums)


def attention_specs(rows, past, base):
    hd = HEAD_DIM
    return [
        pl.BlockSpec((GROUP * hd, rows), lambda h, info: (base + h, 0)),
        pl.BlockSpec((hd, rows), lambda h, info: (QUERY_HEADS + base + h, 0)),
        pl.BlockSpec((hd, rows), lambda h, info: (QUERY_HEADS + KEY_HEADS + base + h, 0)),
        pl.BlockSpec((past, hd, rows), lambda h, info: (0, base + h, 0)),
        pl.BlockSpec((past, hd, rows), lambda h, info: (0, KEY_HEADS + base + h, 0)),
    ]


def attend(info, qkv, past, base, heads):
    rows = qkv.shape[1]
    count = past.shape[0]
    group = GROUP * HEAD_DIM
    return call(
        attend_kernel,
        "attend",
        (heads,),
        attention_specs(rows, count, base),
        [
            pl.BlockSpec((group, rows), lambda h, info: (h, 0)),
            pl.BlockSpec((1, 8, rows), lambda h, info: (h, 0, 0)),
        ],
        [shaped((heads * group, rows), BF16), shaped((heads, 8, rows), F32)],
        [
            pltpu.VMEM((rows, HEAD_DIM), BF16),
            pltpu.VMEM((count, rows, HEAD_DIM), BF16),
            pltpu.VMEM((8, rows), F32),
            pltpu.VMEM((8, rows), F32),
            pltpu.VMEM((GROUP * HEAD_DIM, rows), F32),
        ],
    )(info, qkv, qkv, qkv, past, past)


def mix_kernel(info, x, mixed, weight, gain, middle, normed):
    middle[...] = x[...].astype(F32) + dot(weight[...], mixed[...], 0, 0)
    values = middle[...]
    normed[...] = (values * scale_of(values) * gain[...]).astype(BF16)


def mix(info, x, mixed, weight, gain):
    width, rows = x.shape
    operands = (x, mixed, weight, gain)
    return call(
        mix_kernel,
        "mix",
        (1,),
        [whole(item.shape) for item in operands],
        [whole((width, rows)), whole((width, rows))],
        [shaped((width, rows), F32), shaped((width, rows), BF16)],
    )(info, *operands)


def activate(token_rows, gate_weight, up_weight, hidden, silu, slope):
    gate = dot(token_rows[...], gate_weight[...], 1, 0)
    up = dot(token_rows[...], up_weight[...], 1, 0)
    sigmoid = 0.5 * jnp.tanh(0.5 * gate) + 0.5
    active = gate * sigmoid
    hidden[...] = (active * up).astype(BF16)
    silu[...] = active.astype(BF16)
    slope[...] = (up * (sigmoid + active * (1.0 - sigmoid))).astype(BF16)


def expand_kernel(info, normed, gate_weight, up_weight, hidden, silu, slope, token_rows):
    @pl.when(pl.program_id(0) == 0)
    def _():
        token_rows[...] = normed[...].T

    activate(token_rows, gate_weight, up_weight, hidden, silu, slope)


def expand(info, normed, gate, up):
    width, rows = normed.shape
    ff = gate.shape[1]
    tile = ff // 5
    weight = pl.BlockSpec((width, tile), lambda t, info: (0, t))
    result = pl.BlockSpec((rows, tile), lambda t, info: (0, t))
    return call(
        expand_kernel,
        "expand",
        (ff // tile,),
        [whole((width, rows)), weight, weight],
        [result] * 3,
        [shaped((rows, ff), BF16)] * 3,
        [pltpu.VMEM((rows, width), BF16)],
    )(info, normed, gate, up)


def expand_first_kernel(info, normed, *refs):
    gate_parts, up_parts = refs[:5], refs[5:10]
    hidden, silu, slope, gate_weight, up_weight, token_rows = refs[10:]
    step = pl.program_id(0)
    steps = pl.num_programs(0)

    @pl.when(step == 0)
    def _():
        token_rows[...] = normed[...].T

    for (own, *pieces), target in ((gate_parts, gate_weight), (up_parts, up_weight)):
        half, quarter = own.shape[0], pieces[0].shape[0]
        target[pl.ds(pl.multiple_of(info[0] * half, half), half), :] = own[...]
        other = (1 - info[0]) * half
        near = pl.ds(pl.multiple_of(other + info[3] * quarter, quarter), quarter)
        far = pl.ds(pl.multiple_of(other + (1 - info[3]) * quarter, quarter), quarter)

        @pl.when(step < steps // 2)
        def _():
            target[near, :] = pieces[0][...]
            target[far, :] = pieces[1][...]

        @pl.when(step >= steps // 2)
        def _():
            target[near, :] = pieces[2][...]
            target[far, :] = pieces[3][...]

    activate(token_rows, gate_weight, up_weight, hidden, silu, slope)


def expand_first(info, normed, gate, up):
    width, rows = normed.shape
    half, ff = gate[0].shape
    steps = 4
    tile = ff // steps
    quarter = half // 2

    def column(t, info):
        own = info[2] * (steps // 2) + t
        return jnp.where(t < steps // 2, own, (1 - info[2]) * (steps // 2) + t - steps // 2)

    early = pl.BlockSpec((quarter, tile), lambda t, info: (0, jnp.minimum(t, steps // 2 - 1)))
    late = pl.BlockSpec((quarter, tile), lambda t, info: (0, jnp.maximum(t - steps // 2, 0)))
    parts = [pl.BlockSpec((half, tile), lambda t, info: (0, column(t, info)))]
    parts += [early, early, late, late]
    result = pl.BlockSpec((rows, tile), lambda t, info: (0, column(t, info)))
    weight = pl.BlockSpec((width, tile), lambda t, info: (0, column(t, info)))
    return call(
        expand_first_kernel,
        "expand_first",
        (steps,),
        [whole((width, rows))] + parts * 2,
        [result] * 3 + [weight] * 2,
        [shaped((rows, ff), BF16)] * 3 + [shaped((width, ff), BF16)] * 2,
        [pltpu.VMEM((rows, width), BF16)],
    )(info, normed, *gate, *up)


def shrink_kernel(info, middle, hidden, weight, out):
    out[...] = (middle[...] + dot(weight[...], hidden[...], 1, 1)).astype(out.dtype)


def shrink(info, middle, hidden, down, dtype, cost=None):
    width, rows = middle.shape
    ff = hidden.shape[1]
    tile = width // 2
    return call(
        shrink_kernel,
        "shrink",
        (width // tile,),
        [
            pl.BlockSpec((tile, rows), lambda t, info: (t, 0)),
            whole((rows, ff)),
            pl.BlockSpec((tile, ff), lambda t, info: (t, 0)),
        ],
        [pl.BlockSpec((tile, rows), lambda t, info: (t, 0))],
        [shaped((width, rows), dtype)],
        cost=cost,
    )(info, middle, hidden, down)[0]


def shrink_first_kernel(info, middle, hidden, own, near_0, far_0, near_1, far_1, out, weight):
    half, quarter = own.shape[1], near_0.shape[0]
    weight[:, pl.ds(pl.multiple_of(info[0] * half, half), half)] = own[...]
    other = pl.ds(pl.multiple_of((1 - info[0]) * half, half), half)
    at_near = pl.ds(pl.multiple_of(info[2] * quarter, quarter), quarter)
    at_far = pl.ds(pl.multiple_of((1 - info[2]) * quarter, quarter), quarter)
    for step, near, far in ((0, near_0, far_0), (1, near_1, far_1)):

        @pl.when(pl.program_id(0) == step)
        def _():
            weight[at_near, other] = near[...]
            weight[at_far, other] = far[...]

    out[...] = middle[...] + dot(weight[...], hidden[...], 1, 1)


def shrink_first(info, middle, hidden, parts):
    width, rows = middle.shape
    ff = hidden.shape[1]
    tile = width // 2
    own, first, second, third, fourth = parts

    def row(t, info):
        return jnp.where(t == 0, info[3], 1 - info[3])

    return call(
        shrink_first_kernel,
        "shrink_first",
        (2,),
        [
            pl.BlockSpec((tile, rows), lambda t, info: (row(t, info), 0)),
            whole((rows, ff)),
            pl.BlockSpec((tile, ff // 2), lambda t, info: (row(t, info), 0)),
        ]
        + [whole(first.shape)] * 4,
        [
            pl.BlockSpec((tile, rows), lambda t, info: (row(t, info), 0)),
            pl.BlockSpec((tile, ff), lambda t, info: (row(t, info), 0)),
        ],
        [shaped((width, rows), F32), shaped((width, ff), BF16)],
    )(info, middle, hidden, own, first, third, second, fourth)


def ffn_back_kernel(
    info,
    grad,
    middle,
    gain,
    silu,
    slope,
    down,
    gate,
    up,
    out_weight,
    gate_grad,
    up_grad,
    branch,
    grad_middle,
    attn_grad,
    mixed_grad,
    gain_grad,
    branch_rows,
    total,
):
    step = pl.program_id(0)
    steps = pl.num_programs(0)

    @pl.when(step == 0)
    def _():
        branch[...] = grad[...].astype(BF16)
        branch_rows[...] = branch[...].T
        total[...] = jnp.zeros_like(total)

    incoming = dot(branch_rows[...], down[...], 1, 0)
    gate_grad[...] = (incoming * slope[...].astype(F32)).astype(BF16)
    up_grad[...] = (incoming * silu[...].astype(F32)).astype(BF16)
    total[...] += dot(gate[...], gate_grad[...], 1, 1) + dot(up[...], up_grad[...], 1, 1)

    @pl.when(step == steps - 1)
    def _():
        back, gain_sum = norm_back(middle[...], gain[...], total[...])
        gain_grad[...] = gain_sum
        result = grad[...].astype(F32) + back
        grad_middle[...] = result
        attn_grad[...] = result.astype(BF16)
        mixed_grad[...] = dot(out_weight[...], attn_grad[...], 1, 0).astype(BF16)


def ffn_back(info, grad, middle, gain, silu, slope, down, gate, up, out_weight, cost=None):
    width, rows = middle.shape
    ff = silu.shape[1]
    tile = ff // 5
    heads = out_weight.shape[0]
    token = pl.BlockSpec((rows, tile), lambda t, info: (0, t))
    weight = pl.BlockSpec((width, tile), lambda t, info: (0, t))
    return call(
        ffn_back_kernel,
        "ffn_back",
        (ff // tile,),
        [
            whole((width, rows)),
            whole((width, rows)),
            whole((width, 1)),
            token,
            token,
            weight,
            weight,
            weight,
            whole((heads, width)),
        ],
        [
            token,
            token,
            whole((width, rows)),
            whole((width, rows)),
            whole((width, rows)),
            whole((heads, rows)),
            whole((width, 1)),
        ],
        [
            shaped((rows, ff), BF16),
            shaped((rows, ff), BF16),
            shaped((width, rows), BF16),
            shaped((width, rows), F32),
            shaped((width, rows), BF16),
            shaped((heads, rows), BF16),
            shaped((width, 1), F32),
        ],
        [pltpu.VMEM((rows, width), BF16), pltpu.VMEM((width, rows), F32)],
        cost=cost,
    )(info, grad, middle, gain, silu, slope, down, gate, up, out_weight)


def attend_back_kernel(
    info,
    q,
    k_own,
    v_own,
    k_past,
    v_past,
    mixed_grad,
    mixed,
    lse,
    cosine,
    sine,
    q_grad,
    own_grad,
    past_grad,
    keys_own,
    values_own,
    keys_past,
    values_past,
    inner,
    q_sum,
):
    rows = q.shape[1]
    block = min(256, rows)
    hd = HEAD_DIM
    groups = [(group, slice(group * hd, (group + 1) * hd)) for group in range(GROUP)]
    keys_own[...] = k_own[...].T
    values_own[...] = v_own[...].T

    @pl.loop(0, info[1])
    def _(device):
        keys_past[device] = k_past[device].T
        values_past[device] = v_past[device].T

    @pl.loop(info[1], past_grad.shape[0])
    def _(device):
        past_grad[device] = jnp.zeros_like(past_grad[device])

    for group, head in groups:
        product = mixed_grad[head, :].astype(F32) * mixed[head, :].astype(F32)
        inner[group : group + 1, :] = jnp.sum(product, 0, keepdims=True)

    def step(keys, key_rows, value_rows, start, masked, first):
        key_sum = value_sum = None
        for group, head in groups:
            query, incoming = q[head, start:], mixed_grad[head, start:]
            one = slice(group, group + 1)
            probs = jnp.exp(scores_of(key_rows, query, masked) - lse[0, one, start:])
            slopes = dot(value_rows, incoming, 1, 0)
            low = (probs * (slopes - inner[one, start:])).astype(BF16)
            value_part = dot(incoming, probs.astype(BF16), 1, 1)
            key_part = dot(query, low, 1, 1)
            key_sum = key_part if key_sum is None else key_sum + key_part
            value_sum = value_part if value_sum is None else value_sum + value_part
            query_part = dot(keys, low, 1, 0)
            if first:
                q_sum[head, :] = query_part
            else:
                q_sum[head, start:] += query_part
        return key_sum, value_sum

    for start in range(0, rows, block):
        part = slice(start, start + block)
        key_sum, value_sum = step(
            k_own[:, part], keys_own[part, :], values_own[part, :], start, True, start == 0
        )
        own_grad[0, :hd, part] = key_sum
        own_grad[0, hd:, part] = value_sum

    @pl.loop(0, info[1])
    def _(device):
        key_sum, value_sum = step(
            k_past[device], keys_past[device], values_past[device], 0, False, False
        )
        past_grad[device, 0, :hd, :] = key_sum.astype(past_grad.dtype)
        past_grad[device, 0, hd:, :] = value_sum.astype(past_grad.dtype)

    cos, sin = cosine[...], -sine[...]
    for group, head in groups:
        first, second = rotate(q_sum[head, :], cos, sin)
        at = group * hd
        q_grad[at : at + hd // 2, :] = (first * hd**-0.5).astype(BF16)
        q_grad[at + hd // 2 : at + hd, :] = (second * hd**-0.5).astype(BF16)


def attend_back(info, qkv, past, mixed_grad, mixed, lse, tables, base, heads, cost=None):
    rows = qkv.shape[1]
    count = past.shape[0]
    hd = HEAD_DIM
    group = pl.BlockSpec((GROUP * hd, rows), lambda h, info: (base + h, 0))
    return call(
        attend_back_kernel,
        "attend_back",
        (heads,),
        attention_specs(rows, count, base)
        + [
            group,
            group,
            pl.BlockSpec((1, 8, rows), lambda h, info: (base + h, 0, 0)),
            whole(tables[0].shape),
            whole(tables[1].shape),
        ],
        [
            pl.BlockSpec((GROUP * hd, rows), lambda h, info: (h, 0)),
            pl.BlockSpec((1, 2 * hd, rows), lambda h, info: (h, 0, 0)),
            pl.BlockSpec((count, 1, 2 * hd, rows), lambda h, info: (0, h, 0, 0)),
        ],
        [
            shaped((heads * GROUP * hd, rows), BF16),
            shaped((heads, 2 * hd, rows), F32),
            shaped((count, heads, 2 * hd, rows), BF16 if count == 1 else F32),
        ],
        [
            pltpu.VMEM((rows, hd), BF16),
            pltpu.VMEM((rows, hd), BF16),
            pltpu.VMEM((count, rows, hd), BF16),
            pltpu.VMEM((count, rows, hd), BF16),
            pltpu.VMEM((8, rows), F32),
            pltpu.VMEM((GROUP * hd, rows), F32),
        ],
        cost=cost,
    )(info, qkv, qkv, qkv, past, past, mixed_grad, mixed, lse, *tables)


def project_back_kernel(parts, info, x, gain, grad_middle, *refs):
    q_grads, own_grads, arrived = refs[:parts], refs[parts : 2 * parts], refs[2 * parts : 3 * parts]
    (
        q_weight,
        k_own,
        k_oth,
        v_own,
        v_oth,
        cosine,
        sine,
        q_grad,
        kv_grad,
        out,
        branch,
        gain_grad,
        total,
    ) = refs[3 * parts :]
    half = x.shape[0] // 2
    hd = HEAD_DIM
    kv = KEY_HEADS * hd
    cos, sin = cosine[...], -sine[...]
    head = 0
    for piece, own, far in zip(q_grads, own_grads, arrived):
        q_grad[head * GROUP * hd : head * GROUP * hd + piece.shape[0], :] = piece[...]
        for item in range(own.shape[0]):
            both = own[item] + far[item].astype(F32)
            first, second = rotate(both[:hd], cos, sin)
            at = head * hd
            kv_grad[at : at + hd // 2, :] = first.astype(BF16)
            kv_grad[at + hd // 2 : at + hd, :] = second.astype(BF16)
            kv_grad[kv + at : kv + at + hd, :] = both[hd:].astype(BF16)
            head += 1
    total[...] = dot(q_weight[...], q_grad[...], 1, 0)
    for mine, k, v in ((info[0], k_own, v_own), (1 - info[0], k_oth, v_oth)):
        total[pl.ds(pl.multiple_of(mine * half, half), half), :] += dot(
            k[...], kv_grad[:kv, :], 0, 0
        ) + dot(v[...], kv_grad[kv:, :], 0, 0)
    back, gain_sum = norm_back(x[...].astype(F32), gain[...], total[...])
    gain_grad[...] = gain_sum
    result = grad_middle[...] + back
    out[...] = result
    branch[...] = result.astype(BF16)


def project_back(info, x, gain, grad_middle, q_grads, own_grads, arrived, weights, tables, cost=None):
    width, rows = x.shape
    q, k, v = weights
    heads = q.shape[1]
    kv = 2 * KEY_HEADS * HEAD_DIM
    operands = (x, gain, grad_middle, *q_grads, *own_grads, *arrived, q, *k, *v, *tables)
    shapes = [
        shaped((heads, rows), BF16),
        shaped((kv, rows), BF16),
        shaped((width, rows), F32),
        shaped((width, rows), BF16),
        shaped((width, 1), F32),
    ]
    return call(
        functools.partial(project_back_kernel, len(q_grads)),
        "project_back",
        (1,),
        [whole(item.shape) for item in operands],
        [whole(item.shape) for item in shapes],
        shapes,
        [pltpu.VMEM((width, rows), F32)],
        cost=cost,
    )(info, *operands)


def order_rows(info, target, sources):
    rows = sources[0].shape[1]
    size = target.shape[0] // 4
    at = 0
    for core in (1 - info[2], info[2]):
        for half in (1 - info[0], info[0]):
            start = pl.multiple_of((2 * half + core) * size, size)
            for index, source in enumerate(sources):
                target[at : at + size, index * rows : (index + 1) * rows] = source[
                    pl.ds(start, size), :
                ]
            at += size


def order_halves(info, target, sources):
    rows = sources[0].shape[1]
    size = target.shape[0] // 2
    for at, core in ((0, 1 - info[2]), (size, info[2])):
        start = pl.multiple_of(core * size, size)
        for index, source in enumerate(sources):
            target[at : at + size, index * rows : (index + 1) * rows] = source[pl.ds(start, size), :]


def outer_kernel(split_columns, info, left_a, right_a, left_b, right_b, sent, kept, left, right):
    rows = left_a.shape[1]

    @pl.when(pl.program_id(0) == 0)
    def _():
        order = order_halves if split_columns else order_rows
        order(info, left, (left_a, left_b))

    right[:rows, :] = right_a[...]
    right[rows:, :] = right_b[...]
    count, size = sent.shape[0], sent.shape[1]
    for at, out in ((0, sent), (count * size, kept)):
        product = dot(left[at : at + count * size, :], right[...], 1, 0).astype(BF16)
        for index in range(count):
            out[index] = product[index * size : (index + 1) * size]


def outer(info, parts, split_columns, cost=None):
    left_a, right_a, left_b, right_b = parts
    width, rows = left_a.shape
    columns = right_a.shape[1]
    if split_columns:
        tile = columns // 4

        def column(t, info):
            return jnp.where(t < 2, (1 - info[0]) * 2 + t, info[0] * 2 + t - 2)

        right = pl.BlockSpec((rows, tile), lambda t, info: (0, column(t, info)))
        result = pl.BlockSpec((1, width // 2, tile), lambda t, info: (t // 2, 0, t % 2))
        shape = shaped((2, width // 2, columns // 2), BF16)
    else:
        tile = columns // 5
        right = pl.BlockSpec((rows, tile), lambda t, info: (0, t))
        result = pl.BlockSpec((2, width // 4, tile), lambda t, info: (0, 0, t))
        shape = shaped((2, width // 4, columns), BF16)
    return call(
        functools.partial(outer_kernel, split_columns),
        "outer",
        (columns // tile,),
        [whole((width, rows)), right, whole((width, rows)), right],
        [result, result],
        [shape, shape],
        [pltpu.VMEM((width, 2 * rows), BF16), pltpu.VMEM((2 * rows, tile), BF16)],
        cost=cost,
    )(info, *parts)


def pack_kernel(extra, info, left_a, *refs):
    sent, kept, left, right = refs[-4:]
    refs = refs[:-4]
    gains, refs = refs[len(refs) - extra :], refs[: len(refs) - extra]
    left_b, rights_a, rights_b = refs[0], refs[1::2], refs[2::2]
    rows = left_a.shape[1]
    order_rows(info, left, (left_a, left_b))
    at = 0
    for right_a, right_b in zip(rights_a, rights_b):
        right[at : at + right_a.shape[0], :rows] = right_a[...]
        right[at : at + right_a.shape[0], rows:] = right_b[...]
        at += right_a.shape[0]
    count, size = sent.shape[0], sent.shape[1]
    for base, core, out in ((0, 1 - info[2], sent), (count * size, info[2], kept)):
        for start, span in spans(right.shape[0], 512):
            product = dot(left[base : base + count * size, :], right[start : start + span, :], 1, 1)
            for index in range(count):
                out[index, :, start : start + span] = product[
                    index * size : (index + 1) * size
                ].astype(BF16)
        for index, half in enumerate((1 - info[0], info[0])):
            part = pl.ds(pl.multiple_of((2 * half + core) * size, size), size)
            for number in range(extra // 2):
                term = gains[2 * number][part, :] + gains[2 * number + 1][part, :]
                out[index, :, at + number : at + number + 1] = term.astype(BF16)
            if extra:
                out[index, :, at + extra // 2 :] = jnp.zeros((size, extra // 2), BF16)


def pack(info, left_a, left_b, rights, gains=(), cost=None):
    width, rows = left_a.shape
    columns = sum(item.shape[0] for item in rights[::2])
    operands = (left_a, left_b, *rights, *gains)
    shape = shaped((2, width // 4, columns + len(gains)), BF16)
    return call(
        functools.partial(pack_kernel, len(gains)),
        "pack",
        (1,),
        [whole(item.shape) for item in operands],
        [whole(shape.shape)] * 2,
        [shape, shape],
        [pltpu.VMEM((width, 2 * rows), BF16), pltpu.VMEM((columns, 2 * rows), BF16)],
        cost=cost,
    )(info, *operands)


def last_kernel(info, held, query, key, value, gains):
    width, narrow = query.shape[1], key.shape[0]
    values = held[...].astype(F32)
    query[...] = values[:, :width]
    key[...] = values[:, width : width + narrow].T
    value[...] = values[:, width + narrow : width + 2 * narrow].T
    gains[...] = values[:, width + 2 * narrow :]


def last(info, held, width, narrow):
    rows, columns = held.shape
    shapes = [
        shaped((rows, width), F32),
        shaped((narrow, rows), F32),
        shaped((narrow, rows), F32),
        shaped((rows, columns - width - 2 * narrow), F32),
    ]
    return call(last_kernel, "last", (1,), [None], [None] * 4, shapes)(info, held)


def column_split(columns):
    return columns // 2 // 128 * 128


def both_cores_kernel(info, *refs):
    pairs = list(zip(refs[:-4:2], refs[1:-4:2]))
    over_y, keep_y, over_x, keep_x = refs[-4:]
    half = over_x.shape[1]
    for index, out in ((0, over_y), (1, keep_y)):
        at_y = at_x = 0
        for kept, arrived in pairs:
            total = kept[index].astype(F32) + arrived[index].astype(F32)
            split = column_split(total.shape[1])
            out[:, at_y : at_y + split] = total[:, :split].astype(BF16)
            low, top = total[:half, split:], total[half:, split:]
            end = at_x + total.shape[1] - split
            keep_x[index, :, at_x:end] = jnp.where(info[3] == 0, low, top).astype(BF16)
            over_x[index, :, at_x:end] = jnp.where(info[3] == 0, top, low).astype(BF16)
            at_y, at_x = at_y + split, end
        if at_x < keep_x.shape[2]:
            rest = jnp.zeros((half, keep_x.shape[2] - at_x), BF16)
            keep_x[index, :, at_x:] = rest
            over_x[index, :, at_x:] = rest


def both_cores(info, pairs):
    rows = pairs[0][0].shape[1]
    columns = [kept.shape[2] for kept, _ in pairs]
    split = sum(column_split(item) for item in columns)
    rest = sum(columns) - split
    if len(pairs) > 1:
        rest = -(-(split + rest) // 512) * 512 - split
    first = shaped((rows, split), BF16)
    second = shaped((2, rows // 2, rest), BF16)
    shapes = [first, first, second, second]
    operands = [item for pair in pairs for item in pair]
    return call(both_cores_kernel, "both_cores", (1,), [None] * len(operands), [None] * 4, shapes)(
        info, *operands
    )


def split_pair_kernel(info, held, first, second):
    a, b = column_split(first.shape[1]), column_split(second.shape[1])
    values = held[...]
    first[:, :a] = values[:, :a].astype(F32)
    second[:, :b] = values[:, a : a + b].astype(F32)
    rest = a + b + first.shape[1] - a
    first[:, a:] = values[:, a + b : rest].astype(F32)
    second[:, b:] = values[:, rest : rest + second.shape[1] - b].astype(F32)


def split_pair(info, held, first, second):
    shapes = [shaped((held.shape[0], first), F32), shaped((held.shape[0], second), F32)]
    return call(split_pair_kernel, "split_pair", (1,), [None], [None] * 2, shapes)(info, held)


def cross_kernel(info, keep_y, from_y, keep_x, from_x, over_x, over_y, kept):
    split, half = over_x.shape[1], over_x.shape[0]
    total = keep_y[...].astype(F32) + from_y[...].astype(F32)
    low, top = total[:half], total[half:]
    over_x[...] = jnp.where(info[3] == 0, top, low).astype(BF16)
    kept[:, :split] = jnp.where(info[3] == 0, low, top).astype(BF16)
    over_y[...] = (keep_x[0].astype(F32) + from_x[0].astype(F32)).astype(BF16)
    kept[:, split:] = (keep_x[1].astype(F32) + from_x[1].astype(F32)).astype(BF16)


def cross(info, keep_y, from_y, keep_x, from_x):
    rows, split = keep_y.shape
    rest = keep_x.shape[2]
    shapes = [
        shaped((rows // 2, split), BF16),
        shaped((rows // 2, rest), BF16),
        shaped((rows // 2, split + rest), BF16),
    ]
    return call(cross_kernel, "cross", (1,), [None] * 4, [None] * 3, shapes)(
        info, keep_y, from_y, keep_x, from_x
    )


def chosen(values, number):
    result = values[0]
    for index in range(1, len(values)):
        result = jnp.where(number == index, values[index], result)
    return result


def cut_up(values, dim, count):
    size = values.shape[dim] // count
    if dim == 0:
        return [values[index * size : (index + 1) * size] for index in range(count)]
    return [values[:, index * size : (index + 1) * size] for index in range(count)]


def divide_kernel(dim, info, kept, from_x, from_y, *outs):
    split = from_x.shape[1]
    total = kept[...].astype(F32)
    total = jnp.concatenate(
        [total[:, :split] + from_x[...].astype(F32), total[:, split:] + from_y[...].astype(F32)], 1
    )
    parts = cut_up(total, dim, 4)
    for mask, out in enumerate(outs):
        order = [parts[index ^ mask] for index in range(4)]
        out[...] = chosen(order, info[4]).astype(BF16)


def divide(info, kept, from_x, from_y, dim):
    rows, columns = kept.shape
    shape = (rows // 4, columns) if dim == 0 else (rows, columns // 4)
    return call(
        functools.partial(divide_kernel, dim),
        "divide",
        (1,),
        [None] * 3,
        [None] * 4,
        [shaped(shape, BF16)] * 4,
    )(info, kept, from_x, from_y)


def sum_kernel(info, *refs):
    total = refs[0][...].astype(F32)
    for item in refs[1:-1]:
        total = total + item[...].astype(F32)
    refs[-1][...] = total.astype(BF16)


def sum_all(info, *parts):
    shape = shaped(parts[0].shape, BF16)
    return call(sum_kernel, "sum", (1,), [None] * len(parts), [None], [shape])(info, *parts)[0]


def unite_kernel(dim, place, info, *refs):
    values, out = [item[...].astype(F32) for item in refs[:-1]], refs[-1]
    number = info[place]
    ordered = [
        chosen([values[index ^ other] for other in range(len(values))], number)
        for index in range(len(values))
    ]
    out[...] = jnp.concatenate(ordered, dim).astype(out.dtype)


def unite(info, parts, dim, place, dtype):
    shape = list(parts[0].shape)
    shape[dim] *= len(parts)
    return call(
        functools.partial(unite_kernel, dim, place),
        "unite",
        (1,),
        [None] * len(parts),
        [None],
        [shaped(tuple(shape), dtype)],
    )(info, *parts)[0]


def swap(values, axis, bit):
    size = lax.axis_size(axis)
    return lax.ppermute(values, axis, [(i, i ^ bit) for i in range(size)])


def bits_of(axis):
    size = lax.axis_size(axis)
    assert size & (size - 1) == 0
    return [1 << i for i in range(size.bit_length() - 1)]


def high(axis, bit):
    return (lax.axis_index(axis) // bit) % 2


def halves(values, dim, which):
    half = values.shape[dim] // 2
    return lax.dynamic_slice_in_dim(values, which * half, half, dim)


def joined(mine, other, dim, which):
    return jnp.where(
        which == 0,
        jnp.concatenate([mine, other], dim),
        jnp.concatenate([other, mine], dim),
    )


def tied(values, others):
    return lax.optimization_barrier((values, others))[0]


def from_pieces(own, pieces, mine, core, low_batch):
    near = joined(pieces[0], pieces[2], 0, core)
    far = joined(pieces[1], pieces[3], 0, core)
    return joined(own, joined(near, far, 0, low_batch), 0, mine)


def split_dim(shape, parts):
    if shape[0] % (8 * parts) == 0:
        return 0
    if shape[1] % (128 * parts) == 0:
        return 1
    return 0 if shape[0] % parts == 0 else 1


class Order:
    def __init__(self, token):
        self.token = token

    def __call__(self, *values):
        self.token, *values = lax.optimization_barrier((self.token, *values))
        return values[0] if len(values) == 1 else values


def quarters(values, dim, number):
    quarter = values.shape[dim] // 4
    return lax.dynamic_slice_in_dim(values, number * quarter, quarter, dim)


class Chain:
    def __init__(self, order, pair, beside=()):
        self.order, self.pair, self.beside = order, pair, beside
        self.steps = [self.core, self.first, self.second]
        self.shares = [("seq", (1,), 0), ("batch", (1,), 0)]
        exchanges = [("seq", (bit,)) for bit in bits_of("seq")[1:]]
        bits = bits_of("batch")[1:]
        self.plain = not exchanges and len(bits) == 2
        while bits:
            exchanges.append(("batch", bits[:2]))
            bits = bits[2:]
        self.steps += [functools.partial(self.add, *item) for item in exchanges]
        self.steps += [self.share] * (2 + len(exchanges))
        self.waiting = None

    result_type = F32

    def send(self):
        self.waiting = self.steps.pop(0)()

    def core(self):
        away, kept = self.pair

        def finish(arrived):
            self.parts = both_cores(self.order.token, [(kept, arrived), *self.beside])

        return [swap(self.order(away), "seq", 1)], finish

    def first(self):
        over_y, keep_y, over_x, keep_x = self.parts
        over_y, over_x = self.order(over_y, over_x)

        def finish(from_y, from_x):
            self.parts = cross(self.order.token, keep_y, from_y, keep_x, from_x)

        return [swap(over_y, "fsdp", 1), swap(over_x, "batch", 1)], finish

    def second(self):
        over_x, over_y, kept = self.parts
        over_x, over_y = self.order(over_x, over_y)

        def finish(from_x, from_y):
            if self.plain:
                self.dim = split_dim(kept.shape, 4)
                self.held = divide(self.order.token, kept, from_x, from_y, self.dim)
                return
            arrived = jnp.concatenate([from_x, from_y], 1)
            self.held = (kept.astype(F32) + arrived.astype(F32)).astype(BF16)

        return [swap(over_x, "batch", 1), swap(over_y, "fsdp", 1)], finish

    def add(self, axis, bits):
        held = self.held
        if self.plain:
            own, *parts = held
            parts = self.order(*parts)
            arrived = [
                swap(part, axis, bits[0] * (mask & 1) + bits[1] * (mask >> 1))
                for mask, part in zip((1, 2, 3), parts)
            ]
            self.shares.append((axis, bits, self.dim))

            def finish(*values):
                self.held = sum_all(self.order.token, own, *values)

            return arrived, finish
        dim = split_dim(held.shape, 2 * len(bits))
        take = halves if len(bits) == 1 else quarters
        number = sum(high(axis, bit) << index for index, bit in enumerate(bits))
        masks = range(1, 1 << len(bits))
        parts = self.order(*[take(held, dim, number ^ mask) for mask in masks])
        parts = parts if len(bits) > 1 else [parts]
        arrived = [
            swap(part, axis, sum(bit for index, bit in enumerate(bits) if mask >> index & 1))
            for mask, part in zip(masks, parts)
        ]
        self.shares.append((axis, bits, dim))

        def finish(*values):
            total = take(held, dim, number).astype(F32)
            for item in values:
                total = total + item.astype(F32)
            self.held = total.astype(BF16)

        return arrived, finish

    def share(self):
        axis, bits, dim = self.shares.pop()
        held = self.order(self.held)
        masks = range(1, 1 << len(bits))
        arrived = [
            swap(held, axis, sum(bit for index, bit in enumerate(bits) if mask >> index & 1))
            for mask in masks
        ]

        def finish(*values):
            low = high(axis, bits[0])
            if self.plain:
                place = 4 if len(bits) == 2 else 3 if axis == "batch" else 2
                dtype = BF16 if self.shares else self.result_type
                self.held = unite(self.order.token, (held, *values), dim, place, dtype)
                return
            if len(bits) == 1:
                self.held = joined(held, values[0], dim, low)
                return
            near, far = joined(held, values[0], dim, low), joined(values[1], values[2], dim, low)
            self.held = joined(near, far, dim, high(axis, bits[1]))

        return arrived, finish

    def result(self):
        while self.waiting or self.steps:
            if self.waiting:
                take(self)
            else:
                self.send()
        return self.held.astype(self.result_type)


def take(*chains):
    flat = [item for chain in chains for item in chain.waiting[0]]
    values = chains[0].order(*flat)
    values = list(values) if len(flat) > 1 else [values]
    for chain in chains:
        arrived, finish = chain.waiting
        chain.waiting = None
        finish(*values[: len(arrived)])
        values = values[len(arrived) :]


def per_device(
    tokens,
    attn_gain,
    w_query,
    key_weight,
    value_weight,
    w_out,
    ffn_gain,
    w_gate,
    w_up,
    w_down,
    cotangent,
):
    assert tokens.shape[0] == 1 and lax.axis_size("fsdp") == 2
    mine, spot, core = lax.axis_index("fsdp"), lax.axis_index("seq"), high("seq", 1)
    low_batch = high("batch", 1)
    devices = lax.axis_size("seq")
    deep = lax.axis_index("batch") // 2 % 4
    info = jnp.stack([mine, spot, core, low_batch, deep]).astype(jnp.int32)
    start_in = tokens[0].T
    incoming = cotangent[0].T
    width, rows = start_in.shape

    key_weight, value_weight, w_down = key_weight.T, value_weight.T, w_down.T
    def fsdp(values):
        return swap(values, "fsdp", 1)

    def pair(values):
        return swap(values, "batch", 1)

    def cores(values):
        return swap(values, "seq", 1)

    q_piece = halves(halves(w_query, 0, low_batch), 0, core)
    kv_piece = halves(jnp.where(core == 0, key_weight, value_weight), 0, low_batch)
    q_0, kv_0 = fsdp(q_piece), fsdp(kv_piece)
    gains = jnp.stack([attn_gain, ffn_gain])
    far_gains = fsdp(tied(gains, q_0))
    gains = joined(gains, far_gains, 1, mine).astype(F32)[..., None]
    out_0 = fsdp(tied(halves(halves(w_out, 0, low_batch), 0, core), (q_0, kv_0)))
    q_1, kv_1, q_2, kv_2 = pair(q_0), pair(kv_0), cores(q_0), cores(kv_0)
    gate_0 = fsdp(tied(halves(halves(w_gate, 0, low_batch), 1, core), out_0))
    q_3, kv_3 = cores(q_1), cores(kv_1)
    q_weight = from_pieces(w_query, (q_0, q_1, q_2, q_3), mine, core, low_batch)
    held = joined(kv_0, kv_1, 0, low_batch)
    other = joined(kv_2, kv_3, 0, low_batch)
    k_oth, v_oth = jnp.where(core == 0, held, other), jnp.where(core == 0, other, held)
    qkv_weights = (q_weight, (key_weight, k_oth), (value_weight, v_oth))

    positions = (spot * rows + jnp.arange(rows, dtype=jnp.int32)).astype(F32)
    frequency = jnp.exp(
        jnp.arange(HEAD_DIM // 2, dtype=F32) * (-2.0 * math.log(10000.0) / HEAD_DIM)
    )
    angles = frequency[:, None] * positions[None, :]
    tables = (jnp.cos(angles), jnp.sin(angles))

    def gathered(qkv):
        kv = qkv[QUERY_HEADS * HEAD_DIM :]
        if devices == 2:
            return cores(kv)[None]
        return lax.all_gather(kv, "seq")

    low_normed, low_qkv = project(info, start_in, gains[0], qkv_weights, tables)
    low_past = gathered(low_qkv)
    ready = (low_qkv, gate_0)
    up_0 = fsdp(tied(halves(halves(w_up, 0, low_batch), 1, core), ready))
    down_0 = fsdp(tied(halves(halves(w_down, 0, low_batch), 0, core), ready))
    out_1, out_2 = pair(tied(out_0, (q_1, kv_1))), cores(out_0)
    gate_1, gate_2 = pair(tied(gate_0, (low_qkv, out_1))), cores(gate_0)
    out_3 = cores(out_1)
    out_weight = from_pieces(w_out, (out_0, out_1, out_2, out_3), mine, core, low_batch)
    low_mixed, low_lse = attend(info, low_qkv, tied(low_past, out_weight), 0, KEY_HEADS)
    low_mixed = tied(low_mixed, (up_0, gate_1))
    gate_3, up_1, up_2 = cores(gate_1), pair(tied(up_0, low_mixed)), cores(up_0)
    low_middle, low_normed_ffn = mix(info, start_in, low_mixed, out_weight, gains[1])
    up_3 = cores(tied(up_1, low_middle))
    down_1, down_2 = pair(tied(down_0, (up_1, low_middle))), cores(tied(down_0, low_middle))
    low_hidden, low_silu, low_slope, gate, up = expand_first(
        info,
        low_normed_ffn,
        (w_gate, gate_0, gate_1, gate_2, gate_3),
        (w_up, up_0, up_1, up_2, up_3),
    )
    down_3 = cores(tied(down_1, low_hidden))
    middle_in, down = shrink_first(
        info, low_middle, low_hidden, (w_down, down_0, down_1, down_2, down_3)
    )

    high_normed, high_qkv = project(info, middle_in, gains[0], qkv_weights, tables)
    high_past = gathered(high_qkv)
    high_mixed, high_lse = attend(info, high_qkv, high_past, 0, KEY_HEADS)
    high_middle, high_normed_ffn = mix(info, middle_in, high_mixed, out_weight, gains[1])
    high_hidden, high_silu, high_slope = expand(info, high_normed_ffn, gate, up)

    def attention_back(qkv, past, mixed_grad, mixed, lse, base, heads, cost=None):
        return attend_back(
            info, qkv, past, mixed_grad, mixed, lse, tables, base, heads, cost
        )

    def returned(past_grad):
        if devices == 2:
            return cores(past_grad[0])
        return lax.psum_scatter(past_grad, "seq", scatter_dimension=0)

    def to_input(x, grad_middle, parts, cost=None):
        return project_back(
            info, x, gains[0], grad_middle, *zip(*parts), qkv_weights, tables, cost
        )

    high_gate, high_up, high_branch, grad_middle, high_attn, mixed_grad, high_ffn_gain = ffn_back(
        info, incoming, high_middle, gains[1], high_silu, high_slope, down, gate, up, out_weight
    )
    parts = [
        attention_back(high_qkv, high_past, mixed_grad, high_mixed, high_lse, base, heads)
        for base, heads in ((0, 3), (3, 2))
    ]
    parts = [(*part[:2], returned(part[2])) for part in parts]
    high_q, high_kv, grad_between, low_branch, high_attn_gain = to_input(
        middle_in, grad_middle, parts
    )

    order = Order(tied(info, low_branch))
    down_terms = (high_branch, high_hidden, low_branch, low_hidden)
    down_g = Chain(order, outer(info, down_terms, True))
    down_g.send()
    final_out = order(shrink(info, order(high_middle), high_hidden, down, BF16))
    take(down_g)
    down_g.send()
    low_gate, low_up, _, grad_middle, low_attn, mixed_grad, low_ffn_gain = ffn_back(
        info, order(grad_between), low_middle, gains[1], low_silu, low_slope,
        down, gate, up, out_weight,
    )
    low_attn = order(low_attn)
    take(down_g)
    down_g.send()
    out_away, out_kept = pack(info, high_mixed, low_mixed, (high_attn, order(low_attn)))
    out_far = cores(order(out_away))
    gate_terms = (high_normed_ffn, high_gate, low_normed_ffn, order(low_gate))
    gate_g = Chain(order, outer(info, gate_terms, False))
    gate_g.result_type = BF16
    gate_g.send()
    take(down_g)
    down_g.send()
    gate_g.beside = ((out_kept, order(out_far)),)
    up_terms = (high_normed_ffn, high_up, low_normed_ffn, order(low_up))
    up_g = Chain(order, outer(info, up_terms, False, 14))
    up_g.send()
    take(gate_g)
    gate_g.send()
    parts = []

    def low_part(base, heads):
        mixed_now = order(mixed_grad)
        part = attention_back(low_qkv, low_past, mixed_now, low_mixed, low_lse, base, heads)
        parts.append((order(part[0]), *part[1:]))

    low_part(0, 2)
    take(up_g, gate_g, down_g)
    gate_g.send()
    up_g.send()
    down_g.send()
    low_part(2, 3)
    parts = [(*part[:2], returned(order(part[2]))) for part in parts]
    take(gate_g, up_g, down_g)
    up_g.send()
    gate_g.send()
    low_q, low_kv, grad_start, _, low_attn_gain = to_input(
        start_in, order(grad_middle), parts, 0
    )
    low_q = order(low_q)
    take(up_g, gate_g)
    gate_g.send()
    down_g.send()
    qkv_terms = (high_q, order(low_q), high_kv, low_kv)
    gain_terms = (high_attn_gain, low_attn_gain, high_ffn_gain, low_ffn_gain)
    qkv_g = Chain(order, pack(info, high_normed, low_normed, qkv_terms, gain_terms, 0))
    qkv_g.result_type = BF16
    qkv_g.send()
    take(gate_g, down_g)
    take(qkv_g)
    qkv_g.send()
    up_g.send()
    take(qkv_g, up_g)
    qkv_g.send()
    up_g.send()
    take(qkv_g, up_g)
    qkv_g.send()
    gate_g.send()
    down_g.send()
    take(qkv_g, gate_g, down_g)
    down_grad = down_g.result()
    qkv_g.send()
    up_g.send()
    gate_g.send()
    down_grad = order(down_grad)
    take(qkv_g, up_g, gate_g)
    qkv_g.send()
    up_g.send()
    gate_grad, out_grad = order(
        *split_pair(order.token, gate_g.result(), w_gate.shape[1], w_out.shape[1])
    )
    take(qkv_g, up_g)
    qkv_g.send()
    up_grad = order(up_g.result())
    held = order(qkv_g.result())
    narrow = KEY_HEADS * HEAD_DIM
    query_part, key_part, value_part, gain_grads = last(order.token, held, width, narrow)
    return (
        final_out.T[None],
        grad_start.T[None],
        gain_grads[:, 0],
        query_part,
        key_part.T,
        value_part.T,
        out_grad,
        gain_grads[:, 1],
        gate_grad,
        up_grad,
        down_grad.T,
    )


def solution(mesh):
    return jax.shard_map(
        per_device,
        mesh=mesh,
        in_specs=(
            P(("batch", "fsdp"), "seq", None),
            P("fsdp"),
            P("fsdp", None),
            P("fsdp", None),
            P("fsdp", None),
            P("fsdp", None),
            P("fsdp"),
            P("fsdp", None),
            P("fsdp", None),
            P("fsdp", None),
            P(("batch", "fsdp"), "seq", None),
        ),
        out_specs=(
            P(("batch", "fsdp"), "seq", None),
            P(("batch", "fsdp"), "seq", None),
            P("fsdp"),
            P("fsdp", None),
            P("fsdp", None),
            P("fsdp", None),
            P("fsdp", None),
            P("fsdp"),
            P("fsdp", None),
            P("fsdp", None),
            P("fsdp", None),
        ),
        check_vma=False,
    )
```
